32 devices in a mesh: ctx: 4 (over x, core), fsdp: 8 (over z, y).
Axes of the slice: x: 2, y: 2, z: 4, core: 2. Of those that a mesh axis runs over, the one named last changes fastest.
Arguments:
- inputs: bfloat16 [16, 1024, 1280], P('fsdp', 'ctx'), may hold values from -6 to 6
- targets: bfloat16 [16, 1024, 1280], P('fsdp', 'ctx'), may hold values from -6 to 6
- valid_counts: int32 [16], P('fsdp'), may hold values from 1 to 1024, as said below
- owners: int32 [96], replicated, may hold values from 0 to 7, as said below
- master: float32 [128, 80, 1280], P('fsdp', None, 'ctx'), may hold values from -0.15625 to 0.15625
- first_moment: float32 [128, 80, 1280], P('fsdp', None, 'ctx'), may hold values from -0.03125 to 0.03125
- second_moment: float32 [128, 80, 1280], P('fsdp', None, 'ctx'), may hold values from 1.6967773e-05 to 6.7749024e-05
- norm_gains: float32 [2, 1280], replicated, may hold values from 0.5 to 1.5
- gain_first: float32 [2, 1280], replicated, may hold values from -0.125 to 0.125
- gain_second: float32 [2, 1280], replicated, may hold values from 0.0002685547 to 0.0010864257
- query_scale: float32 [80], replicated, may hold values from 0.8 to 2
- scale_first: float32 [80], replicated, may hold values from -0.125 to 0.125
- scale_second: float32 [80], replicated, may hold values from 0.0002685547 to 0.0010864257
Outputs:
- block_out: float32 [16, 1024, 1280], P('fsdp', 'ctx')
- input_grad: float32 [16, 1024, 1280], P('fsdp', 'ctx')
- new_master: float32 [128, 80, 1280], P('fsdp', None, 'ctx')
- new_first: float32 [128, 80, 1280], P('fsdp', None, 'ctx')
- new_second: float32 [128, 80, 1280], P('fsdp', None, 'ctx')
- new_gains: float32 [2, 1280], replicated
- new_gain_first: float32 [2, 1280], replicated
- new_gain_second: float32 [2, 1280], replicated
- new_scale: float32 [80], replicated
- new_scale_first: float32 [80], replicated
- new_scale_second: float32 [80], replicated
The draws below stay inside these ranges and needn't reach their ends.
Inputs may be any that keep to these rules, and one draw needn't show every extreme that they name: `valid_counts`: among the 2 sequences of each index of fsdp one has all 1024 positions valid. `owners`: no owner has more than 16 matrices, and one has exactly 16.
All inputs are finite; a program needn't handle non-finite values.
Results may differ from the reference program's by a relative error of at most 0.018.
The reference program's roundings to bfloat16 on the way count: a program that leaves them out, or rounds other values in their place, can miss the bound.
Values may be sent and summed in bfloat16 or wider, within the bound.
No kernel may reach another device: no remote copies, remote signals or barrier semaphores. Data moves between devices by JAX's collectives and lax.ppermute only.
A program may use at most 384 MiB of HBM per device.

```python
import math
import jax
import jax.numpy as jnp
from jax import lax

D = 1280
H = 16
HD = 80
FF = 1280
SEQ_DEV = 2
STEP = 10
LEN = 1024
SEQS = 16
UNITS = 96
OWNERS = 8
SLOTS = 16
ROWS = 128


def draw_valid_counts(key, part):
    key = jax.random.fold_in(key, 7)
    subkeys = jax.random.split(key, 2)
    groups = SEQS // SEQ_DEV
    full_member = jax.random.randint(subkeys[0], (groups,), 0, SEQ_DEV)
    seq_index = jnp.arange(SEQS, dtype=jnp.int32)
    seq_group = seq_index // SEQ_DEV
    seq_member = seq_index % SEQ_DEV
    lower_len = LEN // 8 + LEN // 2 * seq_group // groups
    extra_len = jax.random.randint(subkeys[1], (SEQS,), 0, LEN // 4 + 1)
    partial_len = lower_len + extra_len
    return jnp.where(seq_member == full_member[seq_group], LEN, partial_len).astype(jnp.int32)


def draw_owners(key, part):
    key = jax.random.fold_in(key, 11)
    subkeys = jax.random.split(key, 3)
    full_owner = jax.random.randint(subkeys[0], (), 0, OWNERS)
    other_slots = jax.random.permutation(subkeys[1], (OWNERS - 1) * SLOTS)[:UNITS - SLOTS]
    other_owner = other_slots // SLOTS
    other_owner = other_owner + (other_owner >= full_owner).astype(jnp.int32)
    listed = jnp.concatenate([jnp.zeros((SLOTS,), jnp.int32) + full_owner, other_owner.astype(jnp.int32)])
    unit_order = jax.random.permutation(subkeys[2], UNITS)
    return listed[unit_order].astype(jnp.int32)


def block_levels(key, extent, pieces, smallest, top_value):
    factor_of = 1.0
    for position, blocks in pieces:
        heights = jax.random.uniform(jax.random.fold_in(jax.random.fold_in(key, 6), position), (blocks,), jnp.float32, smallest / len(pieces), top_value / len(pieces))
        factor_of = factor_of * jnp.repeat(jnp.exp(heights), extent[position] // blocks).reshape((-1,) + (1,) * (len(extent) - 1 - position))
    return factor_of


def centred(key, extent, scale, limit, cuts=(), held_as=jnp.bfloat16):
    entries = scale * jax.random.normal(key, extent, jnp.float32)
    if cuts:
        entries = entries * block_levels(key, extent, cuts, -0.22, 0.18)
    return jnp.clip(entries, -limit, limit).astype(held_as)


def setup_inputs(seed: int = 0) -> dict:
    seeds = jax.random.split(jax.random.key(seed), 14)
    return {
        "inputs": centred(seeds[0], (SEQS, LEN, D), 1.0, 6.0, ((0, 8), (1, 4))),
        "targets": centred(seeds[1], (SEQS, LEN, D), 1.0, 6.0, ((0, 8), (1, 4))),
        "valid_counts": draw_valid_counts(jax.random.fold_in(seeds[13], 71), 0),
        "owners": draw_owners(jax.random.fold_in(seeds[13], 71), 0),
        "master": centred(seeds[4], (ROWS, HD, D), D ** -0.5, 0.15625, ((0, 8), (2, 4)), jnp.float32),
        "first_moment": centred(seeds[5], (ROWS, HD, D), (0.255 / (SEQS * LEN) ** 0.5), 0.03125, ((0, 8), (2, 4)), jnp.float32),
        "second_moment": jnp.clip(jnp.exp(math.log(6.774902431061491e-05) - 1.3844942 * jax.random.uniform(seeds[6], (ROWS, HD, D), jnp.float32) ** block_levels(seeds[6], (ROWS, HD, D), ((0, 8), (2, 4)), -0.2, 0.2)), 1.6967773262877017e-05, 6.774902431061491e-05),
        "norm_gains": jnp.clip(1.0 + 0.1 * jax.random.normal(seeds[7], (2, D), jnp.float32), 0.5, 1.5),
        "gain_first": centred(seeds[8], (2, D), (1.0 / (SEQS * LEN) ** 0.5), 0.125, (), jnp.float32),
        "gain_second": jnp.clip(jnp.exp(jax.random.uniform(seeds[9], (2, D), jnp.float32, math.log(0.0002685547), math.log(0.0010864257))), 0.0002685547, 0.0010864257),
        "query_scale": jnp.clip(jax.random.uniform(seeds[10], (HD,), jnp.float32, 0.8, 2.0), 0.8, 2.0),
        "scale_first": centred(seeds[11], (HD,), (1.0 / (SEQS * LEN) ** 0.5), 0.125, (), jnp.float32),
        "scale_second": jnp.clip(jnp.exp(jax.random.uniform(seeds[12], (HD,), jnp.float32, math.log(0.0002685547), math.log(0.0010864257))), 0.0002685547, 0.0010864257),
    }


@jax.custom_vjp
def low(v):
    return lax.optimization_barrier(v.astype(jnp.bfloat16)).astype(jnp.float32)

@jax.custom_vjp
def low_back(v):
    return v

def low_keep(v):
    return (low(v), None)

def low_pass(kept, grad):
    return (grad,)

def back_keep(v):
    return (v, None)

def back_low(kept, grad):
    return (low(grad),)
low.defvjp(low_keep, low_pass)
low_back.defvjp(back_keep, back_low)
norm_eps = 1e-06
beta_first = 0.9
beta_second = 0.95
adam_eps = 1e-08
decay_rate = 0.1
master_rate = 0.05
gain_rate = 2.0
scale_rate = 2.0
score_base = 1.442695041
masked_score = -1e+30
highest = lax.Precision.HIGHEST

def unit_rows(owners, slot_count):
    unit_count = owners.shape[0]
    unit_order = jnp.arange(unit_count, dtype=jnp.int32)
    same_owner = owners[:, None] == owners[None, :]
    earlier = unit_order[None, :] < unit_order[:, None]
    slot_rank = lax.optimization_barrier(jnp.sum((same_owner & earlier).astype(jnp.int32), axis=1))
    return (owners * slot_count + slot_rank).astype(jnp.int32)

def rms_norm(values, gain):
    return values * lax.rsqrt(lax.optimization_barrier(jnp.mean(values * values, axis=-1, keepdims=True)) + norm_eps) * gain

def attention(query, key_all, value_all):
    length = query.shape[1]
    block = math.gcd(length, 512)
    positions = jnp.arange(length, dtype=jnp.int32)

    def one_block(offset):
        query_rows = lax.dynamic_slice_in_dim(query, offset, block, 1)
        scores = low_back(jnp.einsum('hqe,hke->hqk', query_rows, key_all, precision=highest))
        row_pos = offset + jnp.arange(block, dtype=jnp.int32)
        allowed = row_pos[:, None] >= positions[None, :]
        scores = jnp.where(allowed, scores, masked_score)
        attn_probs = low(jax.nn.softmax(scores, axis=-1))
        return jnp.einsum('hqk,hke->hqe', attn_probs, value_all, precision=highest)
    offsets = jnp.arange(length // block, dtype=jnp.int32) * block
    outputs = lax.map(jax.checkpoint(one_block), offsets)
    return jnp.transpose(outputs, (1, 0, 2, 3)).reshape(query.shape)

def sequence_loss(values_in, seq_target, seq_mask, weights, norm_gains, query_scale):
    ff_blocks = FF // HD
    w_query = weights[0:H]
    w_key = weights[H:2 * H]
    w_value = weights[2 * H:3 * H]
    w_out = weights[3 * H:4 * H]
    w_up = weights[4 * H:4 * H + ff_blocks]
    w_down = weights[4 * H + ff_blocks:]
    normed = low(rms_norm(values_in, norm_gains[0]))
    query_pre = low_back(jnp.einsum('td,hed->hte', normed, w_query, precision=highest))
    multiplier = jax.nn.softplus(query_scale) * (score_base / math.sqrt(HD))
    query = low(query_pre * multiplier)
    key_all = low(low_back(jnp.einsum('td,hed->hte', normed, w_key, precision=highest)))
    value_all = low(low_back(jnp.einsum('td,hed->hte', normed, w_value, precision=highest)))
    attended = low(low_back(attention(query, key_all, value_all)))
    branch = low_back(jnp.einsum('hte,hed->td', attended, w_out, precision=highest))
    middle = values_in + branch
    normed_mid = low(rms_norm(middle, norm_gains[1]))
    hidden = low_back(jnp.einsum('td,fed->tfe', normed_mid, w_up, precision=highest))
    active = low(jax.nn.silu(hidden))
    branch_two = low_back(jnp.einsum('tfe,fed->td', active, w_down, precision=highest))
    result = middle + branch_two
    error = jnp.sum(seq_mask[:, None] * (result - seq_target) ** 2)
    return (error, result)

def adam_step(values, moment_one, moment_two, gradient, step_rate, weight_decay):
    moment_one = beta_first * moment_one + (1.0 - beta_first) * gradient
    moment_two = beta_second * moment_two + (1.0 - beta_second) * gradient * gradient
    first_hat = moment_one / (1.0 - beta_first ** STEP)
    second_hat = moment_two / (1.0 - beta_second ** STEP)
    values = values - step_rate * (first_hat / (jnp.sqrt(second_hat) + adam_eps) + weight_decay * values)
    return (values, moment_one, moment_two)

def reference(inputs, targets, valid_counts, owners, master, first_moment, second_moment, norm_gains, gain_first, gain_second, query_scale, scale_first, scale_second):
    length = inputs.shape[1]
    slot_count = master.shape[0] // OWNERS
    slot_rows = unit_rows(owners, slot_count)
    weights = low(master[slot_rows])
    positions = jnp.arange(length, dtype=jnp.int32)
    masks = (positions[None, :] >= (length - valid_counts)[:, None]).astype(jnp.float32)

    def one_sequence(totals, seq_item):
        seq_in, seq_target, seq_mask = seq_item

        def loss_of(x_val, w_val, g_val, q_val):
            return sequence_loss(x_val, seq_target.astype(jnp.float32), seq_mask, w_val, g_val, q_val)
        seq_loss, pullback, result = jax.vjp(loss_of, seq_in.astype(jnp.float32), weights, norm_gains, query_scale, has_aux=True)
        grad_in, grad_w, grad_g, grad_q = pullback(jnp.ones((), jnp.float32))
        totals = (totals[0] + grad_w, totals[1] + grad_g, totals[2] + grad_q)
        return (totals, (result, grad_in))
    zero_grads = (jnp.zeros_like(weights), jnp.zeros_like(norm_gains), jnp.zeros_like(query_scale))
    totals, outputs = lax.scan(one_sequence, zero_grads, (inputs, targets, masks))
    block_out, input_grad = outputs
    count = jnp.sum(valid_counts).astype(jnp.float32)
    slot_grad = jnp.zeros_like(master).at[slot_rows].set(totals[0] / count)
    new_master, new_first, new_second = adam_step(master, first_moment, second_moment, slot_grad, master_rate, decay_rate)
    new_gains, new_gain_first, new_gain_second = adam_step(norm_gains, gain_first, gain_second, totals[1] / count, gain_rate, 0.0)
    new_scale, new_scale_first, new_scale_second = adam_step(query_scale, scale_first, scale_second, totals[2] / count, scale_rate, 0.0)
    return (block_out, input_grad, new_master, new_first, new_second, new_gains, new_gain_first, new_gain_second, new_scale, new_scale_first, new_scale_second)
```

```python
import functools
import math

import jax
import jax.numpy as jnp
from jax import lax
from jax.experimental import pallas as pl
from jax.experimental.pallas import tpu as pltpu
from jax.sharding import PartitionSpec as P

H = 16
FF = 1280
STEP = 10


norm_eps = 1e-06
beta_first = 0.9
beta_second = 0.95
adam_eps = 1e-08
decay_rate = 0.1
master_rate = 0.05
gain_rate = 2.0
scale_rate = 2.0
score_base = 1.442695041
masked_score = -1e30


def from_behind(block, axis, distance):
    devices = range(lax.axis_size(axis))
    route = [(i - distance, i) for i in devices if i - distance in devices]
    return lax.ppermute(block, axis, route)


def shifted(array, axis, by):
    count = lax.axis_size(axis)
    return lax.ppermute(array, axis, [(i, (i + by) % count) for i in range(count)])


def unit_rows(owners, slot_count):
    unit_count = owners.shape[0]
    unit_order = jnp.arange(unit_count, dtype=jnp.int32)
    same_owner = owners[:, None] == owners[None, :]
    earlier = unit_order[None, :] < unit_order[:, None]
    slot_rank = jnp.sum((same_owner & earlier).astype(jnp.int32), axis=1)
    return owners * slot_count + slot_rank


def inverse_rms(values):
    return lax.rsqrt(jnp.mean(values * values, axis=-1, keepdims=True) + norm_eps)


def norm_back(values, gain, grad_normed):
    inverse = inverse_rms(values)
    scaled = grad_normed * gain
    grad_values = inverse * scaled - values * inverse**3 * jnp.mean(
        scaled * values, axis=-1, keepdims=True
    )
    grad_gain = jnp.sum(grad_normed * values * inverse, axis=(0, 1))
    return (grad_values, grad_gain)


def adam_step(values, moment_one, moment_two, gradient, step_rate, weight_decay):
    moment_one = beta_first * moment_one + (1.0 - beta_first) * gradient
    moment_two = beta_second * moment_two + (1.0 - beta_second) * gradient * gradient
    first_hat = moment_one / (1.0 - beta_first**STEP)
    second_hat = moment_two / (1.0 - beta_second**STEP)
    values = values - step_rate * (
        first_hat / (jnp.sqrt(second_hat) + adam_eps) + weight_decay * values
    )
    return (values, moment_one, moment_two)


def general_layer(
    inputs,
    targets,
    valid_counts,
    owners,
    master,
    first_moment,
    second_moment,
    norm_gains,
    gain_first,
    gain_second,
    query_scale,
    scale_first,
    scale_second,
):
    seq_local, block_rows, width = inputs.shape
    slot_count, head_dim, column_count = master.shape
    ff_blocks = FF // head_dim
    ctx_size = lax.axis_size("ctx")
    ctx_index = lax.axis_index("ctx")
    slot_rows = unit_rows(owners, slot_count)
    owner_table = lax.all_gather(master.astype(jnp.bfloat16), "fsdp", axis=0, tiled=True)
    picked = owner_table[slot_rows]
    weights = lax.all_gather(picked, "ctx", axis=2, tiled=True)
    w_qkv = weights[0 : 3 * H]
    w_out = weights[3 * H : 4 * H]
    w_up = weights[4 * H : 4 * H + ff_blocks]
    w_down = weights[4 * H + ff_blocks :]
    values_in = inputs.astype(jnp.float32)
    normed_b = (values_in * inverse_rms(values_in) * norm_gains[0]).astype(jnp.bfloat16)
    projected = jnp.einsum("sbd,hed->shbe", normed_b, w_qkv, preferred_element_type=jnp.float32)
    query_pre = projected[:, 0:H]
    multiplier = jax.nn.softplus(query_scale) * (score_base / math.sqrt(head_dim))
    query_b = (query_pre * multiplier).astype(jnp.bfloat16)
    key_b = projected[:, H : 2 * H].astype(jnp.bfloat16)
    value_b = projected[:, 2 * H : 3 * H].astype(jnp.bfloat16)
    query_rows = ctx_index * block_rows + jnp.arange(block_rows, dtype=jnp.int32)
    last_row = ctx_index * block_rows + block_rows - 1
    start_state = (
        jnp.full(query_pre.shape[:3], masked_score, jnp.float32),
        jnp.zeros(query_pre.shape[:3], jnp.float32),
        jnp.zeros(query_pre.shape, jnp.float32),
    )
    key_part = lax.all_gather(key_b, "ctx", axis=2, tiled=True)
    value_part = lax.all_gather(value_b, "ctx", axis=2, tiled=True)
    key_count = key_part.shape[2]

    def update(current):
        run_max, run_sum, accum = current
        key_rows = jnp.arange(key_count, dtype=jnp.int32)
        allowed = query_rows[:, None] >= key_rows[None, :]
        scores = jnp.einsum(
            "shqe,shke->shqk", query_b, key_part, preferred_element_type=jnp.float32
        )
        scores = jnp.where(allowed, scores, masked_score)
        new_max = jnp.maximum(run_max, jnp.max(scores, axis=-1))
        attn_probs = jnp.where(allowed, jnp.exp(scores - new_max[..., None]), 0.0)
        run_sum = jnp.sum(attn_probs, axis=-1)
        accum = jnp.einsum(
            "shqk,shke->shqe",
            attn_probs.astype(jnp.bfloat16),
            value_part,
            preferred_element_type=jnp.float32,
        )
        return (new_max, run_sum, accum)

    run_max, run_sum, accum = lax.cond(
        jnp.int32(0) <= last_row, update, lambda current: current, start_state
    )
    attended = accum / run_sum[..., None]
    log_total = run_max + jnp.log(run_sum)
    attended_b = attended.astype(jnp.bfloat16)
    branch = jnp.einsum("shbe,hed->sbd", attended_b, w_out, preferred_element_type=jnp.float32)
    middle = values_in + branch
    normed_mid_b = (middle * inverse_rms(middle) * norm_gains[1]).astype(jnp.bfloat16)
    hidden = jnp.einsum("sbd,fed->sbfe", normed_mid_b, w_up, preferred_element_type=jnp.float32)
    active_b = jax.nn.silu(hidden).astype(jnp.bfloat16)
    block_out = middle + jnp.einsum(
        "sbfe,fed->sbd", active_b, w_down, preferred_element_type=jnp.float32
    )
    seq_length = block_rows * ctx_size
    counted = (query_rows[None, :] >= (seq_length - valid_counts)[:, None]).astype(jnp.float32)
    count_term = jnp.sum(counted)
    out_grad = 2.0 * (block_out - targets.astype(jnp.float32)) * counted[..., None]
    out_grad_b = out_grad.astype(jnp.bfloat16)
    grad_down = jnp.einsum(
        "sbfe,sbd->fed", active_b, out_grad_b, preferred_element_type=jnp.float32
    )
    grad_active = jnp.einsum(
        "sbd,fed->sbfe", out_grad_b, w_down, preferred_element_type=jnp.float32
    )
    sigma = jax.nn.sigmoid(hidden)
    grad_hidden_b = (grad_active * sigma * (1.0 + hidden * (1.0 - sigma))).astype(jnp.bfloat16)
    grad_up = jnp.einsum(
        "sbfe,sbd->fed", grad_hidden_b, normed_mid_b, preferred_element_type=jnp.float32
    )
    grad_normed_mid = jnp.einsum(
        "sbfe,fed->sbd", grad_hidden_b, w_up, preferred_element_type=jnp.float32
    )
    grad_middle_norm, grad_gain_two = norm_back(middle, norm_gains[1], grad_normed_mid)
    grad_middle = out_grad + grad_middle_norm
    grad_middle_b = grad_middle.astype(jnp.bfloat16)
    grad_out = jnp.einsum(
        "shbe,sbd->hed", attended_b, grad_middle_b, preferred_element_type=jnp.float32
    )
    grad_attended_b = jnp.einsum(
        "sbd,hed->shbe", grad_middle_b, w_out, preferred_element_type=jnp.float32
    ).astype(jnp.bfloat16)
    delta = jnp.sum(grad_attended_b.astype(jnp.float32) * attended, axis=-1)

    def block_grads(source, key_cur, value_cur, partial_grads):
        grad_key, grad_value, grad_query = partial_grads
        key_rows = source * block_rows + jnp.arange(block_rows, dtype=jnp.int32)
        allowed = query_rows[:, None] >= key_rows[None, :]
        scores = jnp.einsum("shqe,shke->shqk", query_b, key_cur, preferred_element_type=jnp.float32)
        scores = jnp.where(allowed, scores, masked_score)
        attn_probs = jnp.exp(scores - log_total[..., None])
        grad_value = grad_value + jnp.einsum(
            "shqk,shqe->shke",
            attn_probs.astype(jnp.bfloat16),
            grad_attended_b,
            preferred_element_type=jnp.float32,
        )
        grad_probs = jnp.einsum(
            "shqe,shke->shqk", grad_attended_b, value_cur, preferred_element_type=jnp.float32
        )
        grad_scores_b = (attn_probs * (grad_probs - delta[..., None])).astype(jnp.bfloat16)
        grad_query = grad_query + jnp.einsum(
            "shqk,shke->shqe", grad_scores_b, key_cur, preferred_element_type=jnp.float32
        )
        grad_key = grad_key + jnp.einsum(
            "shqk,shqe->shke", grad_scores_b, query_b, preferred_element_type=jnp.float32
        )
        return (grad_key, grad_value, grad_query)

    zero_heads = jnp.zeros(query_pre.shape, jnp.float32)

    def back_turn(which_turn, current):
        key_cur, value_cur, grad_key, grad_value, grad_query = current
        source = (ctx_index - which_turn) % ctx_size
        grad_key, grad_value, grad_query = lax.cond(
            source <= ctx_index,
            lambda parts: block_grads(source, key_cur, value_cur, parts),
            lambda parts: parts,
            (grad_key, grad_value, grad_query),
        )
        key_cur, value_cur = from_behind((key_cur, value_cur), "ctx", 1)
        grad_key, grad_value = (
            shifted(grad_key.astype(jnp.bfloat16), "ctx", 1).astype(grad_key.dtype),
            shifted(grad_value.astype(jnp.bfloat16), "ctx", 1).astype(grad_value.dtype),
        )
        return (key_cur, value_cur, grad_key, grad_value, grad_query)

    back_state = (key_b, value_b, zero_heads, zero_heads, zero_heads)
    back_state = lax.fori_loop(0, ctx_size, back_turn, back_state)
    grad_key, grad_value, grad_query = (back_state[2], back_state[3], back_state[4])
    grad_proj_b = jnp.concatenate([grad_query * multiplier, grad_key, grad_value], axis=1).astype(
        jnp.bfloat16
    )
    grad_qkv = jnp.einsum(
        "shbe,sbd->hed", grad_proj_b, normed_b, preferred_element_type=jnp.float32
    )
    grad_normed_in = jnp.einsum(
        "shbe,hed->sbd", grad_proj_b, w_qkv, preferred_element_type=jnp.float32
    )
    grad_input_norm, grad_gain_one = norm_back(values_in, norm_gains[0], grad_normed_in)
    input_grad = grad_middle + grad_input_norm
    scale_term = (
        jnp.sum(grad_query * query_pre, axis=(0, 1, 2))
        * (score_base / math.sqrt(head_dim))
        * jax.nn.sigmoid(query_scale)
    )
    unit_grads = jnp.concatenate([grad_qkv, grad_out, grad_up, grad_down], axis=0)
    owner_total = lax.axis_size("fsdp") * slot_count
    table_grads = (
        jnp.zeros((owner_total, head_dim, width), jnp.float32).at[slot_rows].set(unit_grads)
    )
    owned = lax.psum_scatter(
        table_grads.astype(jnp.bfloat16), "fsdp", scatter_dimension=0, tiled=True
    )
    slot_sums = lax.psum_scatter(owned, "ctx", scatter_dimension=2, tiled=True).astype(jnp.float32)
    gain_sums, scale_sums, count = lax.psum(
        (jnp.stack([grad_gain_one, grad_gain_two]), scale_term, count_term), ("ctx", "fsdp")
    )
    new_master, new_first, new_second = adam_step(
        master, first_moment, second_moment, slot_sums / count, master_rate, decay_rate
    )
    new_gains, new_gain_first, new_gain_second = adam_step(
        norm_gains, gain_first, gain_second, gain_sums / count, gain_rate, 0.0
    )
    new_scale, new_scale_first, new_scale_second = adam_step(
        query_scale, scale_first, scale_second, scale_sums / count, scale_rate, 0.0
    )
    return (
        block_out,
        input_grad,
        new_master,
        new_first,
        new_second,
        new_gains,
        new_gain_first,
        new_gain_second,
        new_scale,
        new_scale_first,
        new_scale_second,
    )


def swapped(array, axis, distance):
    return lax.ppermute(
        array, axis, [(i, i ^ distance) for i in range(lax.axis_size(axis))]
    )


def dot(left, right, left_dim, right_dim):
    return lax.dot_general(
        left,
        right,
        (((left_dim,), (right_dim,)), ((), ())),
        preferred_element_type=jnp.float32,
    )


def copy_rows_kernel(sizes, offsets, width, from_ref, row_ref, *refs):
    sources = refs[: len(offsets)]
    outs = refs[len(offsets) : -1]
    sems = refs[-1]
    start = 0
    for place, (out, size) in enumerate(zip(outs, sizes)):

        @pl.loop(0, size)
        def copy_row(i, start=start, place=place, out=out):
            which = from_ref[start + i]
            row = row_ref[start + i]
            for number, (source, offset) in enumerate(zip(sources, offsets)):

                @pl.when(which == number)
                def begin(source=source, offset=offset):
                    pltpu.make_async_copy(
                        source.at[row, :, pl.ds(offset, width)], out.at[i], sems.at[place]
                    ).start()

        start += size
    for place, out in enumerate(outs):
        pltpu.make_async_copy(out, out, sems.at[place]).wait()


def copy_rows(sources, offsets, width, pick_from, pick_row, sizes):
    rows = sources[0].shape[1]
    total = sum(sizes)
    return pl.pallas_call(
        functools.partial(copy_rows_kernel, tuple(sizes), tuple(offsets), width),
        out_shape=[jax.ShapeDtypeStruct((size, rows, width), sources[0].dtype) for size in sizes],
        grid_spec=pltpu.PrefetchScalarGridSpec(
            num_scalar_prefetch=2,
            grid=(1,),
            in_specs=[pl.BlockSpec(memory_space=pl.ANY)] * len(sources),
            out_specs=[pl.BlockSpec(memory_space=pl.ANY)] * len(sizes),
            scratch_shapes=[pltpu.SemaphoreType.DMA((len(sizes),))],
        ),
        cost_estimate=pl.CostEstimate(
            flops=0, bytes_accessed=total * rows * width * 4, transcendentals=0
        ),
        name="copy_rows",
    )(pick_from, pick_row, *sources)


def place_pieces_kernel(places, *refs):
    pieces = refs[: len(places)]
    outs = refs[len(places) : -1]
    sems = refs[-1]
    copies = []
    for number, (piece, (first, count, out, row, column)) in enumerate(zip(pieces, places)):
        copies.append(
            pltpu.make_async_copy(
                piece.at[pl.ds(first, count)],
                outs[out].at[pl.ds(row, count), :, pl.ds(column, piece.shape[2])],
                sems.at[number],
            )
        )
    for copy in copies:
        copy.start()
    for copy in copies:
        copy.wait()


def place_pieces(pieces, places, shapes):
    moved = sum(math.prod(shape) for shape in shapes)
    return pl.pallas_call(
        functools.partial(place_pieces_kernel, tuple(places)),
        out_shape=[jax.ShapeDtypeStruct(shape, pieces[0].dtype) for shape in shapes],
        in_specs=[pl.BlockSpec(memory_space=pl.ANY)] * len(pieces),
        out_specs=[pl.BlockSpec(memory_space=pl.ANY)] * len(shapes),
        scratch_shapes=[pltpu.SemaphoreType.DMA((len(pieces),))],
        cost_estimate=pl.CostEstimate(flops=0, bytes_accessed=4 * moved, transcendentals=0),
        name="place_pieces",
    )(*pieces)


def attend_kernel(blocks, order_ref, q_ref, k_ref, v_ref, out_ref, log_ref, key_rows, value_cols):
    size = q_ref.shape[1] // blocks
    at = [pl.multiple_of(order_ref[i] * size, size) for i in range(blocks)]
    for i in range(blocks):
        key_rows[i * size : (i + 1) * size, :] = k_ref[:, pl.ds(at[i], size)].T
        value_cols[:, i * size : (i + 1) * size] = v_ref[:, pl.ds(at[i], size)]
    key_pos = lax.broadcasted_iota(jnp.int32, (size, size), 0)
    query_pos = lax.broadcasted_iota(jnp.int32, (size, size), 1)
    seen = key_pos <= query_pos
    for i in range(blocks):
        past = i * size
        query = q_ref[:, pl.ds(at[i], size)]
        near = jnp.where(
            seen, dot(key_rows[past : past + size, :], query, 1, 0), masked_score
        )
        top = jnp.max(near, axis=0, keepdims=True)
        if i:
            far = dot(key_rows[:past, :], query, 1, 0)
            top = jnp.maximum(top, jnp.max(far, axis=0, keepdims=True))
        near = jnp.exp(near - top)
        total = jnp.sum(near, axis=0, keepdims=True)
        value = dot(value_cols[:, past : past + size], near.astype(jnp.bfloat16), 1, 0)
        if i:
            far = jnp.exp(far - top)
            total = total + jnp.sum(far, axis=0, keepdims=True)
            value = value + dot(value_cols[:, :past], far.astype(jnp.bfloat16), 1, 0)
        out_ref[:, pl.ds(at[i], size)] = (value / total).astype(jnp.bfloat16)
        log_ref[0, :, pl.ds(at[i], size)] = top + jnp.log(total)


def attend(projected, order, heads, head_dim):
    tokens = projected.shape[1]
    blocks = order.shape[0]

    def part(first):
        return pl.BlockSpec((head_dim, tokens), lambda h, order, first=first: (first + h, 0))

    return pl.pallas_call(
        functools.partial(attend_kernel, blocks),
        out_shape=[
            jax.ShapeDtypeStruct((heads * head_dim, tokens), jnp.bfloat16),
            jax.ShapeDtypeStruct((heads, 1, tokens), jnp.float32),
        ],
        grid_spec=pltpu.PrefetchScalarGridSpec(
            num_scalar_prefetch=1,
            grid=(heads,),
            in_specs=[part(0), part(heads), part(2 * heads)],
            out_specs=[
                pl.BlockSpec((head_dim, tokens), lambda h, order: (h, 0)),
                pl.BlockSpec((1, 1, tokens), lambda h, order: (h, 0, 0)),
            ],
            scratch_shapes=[
                pltpu.VMEM((tokens, head_dim), jnp.bfloat16),
                pltpu.VMEM((head_dim, tokens), jnp.bfloat16),
            ],
        ),
        compiler_params=pltpu.CompilerParams(vmem_limit_bytes=40 * 1024 * 1024),
        cost_estimate=pl.CostEstimate(
            flops=heads * tokens * tokens * head_dim * 4,
            bytes_accessed=heads * head_dim * tokens * 8,
            transcendentals=heads * tokens * tokens,
        ),
        name="attend",
    )(order, projected, projected, projected)


def attend_back_kernel(
    blocks,
    order_ref,
    q_ref,
    k_ref,
    v_ref,
    grad_ref,
    log_ref,
    scale_ref,
    out_ref,
    term_ref,
    key_rows,
    key_cols,
    value_rows,
    key_sum,
    value_sum,
):
    size = q_ref.shape[1] // blocks
    at = [pl.multiple_of(order_ref[i] * size, size) for i in range(blocks)]
    for i in range(blocks):
        here = slice(i * size, (i + 1) * size)
        key = k_ref[:, pl.ds(at[i], size)]
        key_rows[here, :] = key.T
        key_cols[:, here] = key
        value_rows[here, :] = v_ref[:, pl.ds(at[i], size)].T
    key_sum[...] = jnp.zeros_like(key_sum)
    value_sum[...] = jnp.zeros_like(value_sum)
    key_pos = lax.broadcasted_iota(jnp.int32, (size, size), 0)
    query_pos = lax.broadcasted_iota(jnp.int32, (size, size), 1)
    seen = key_pos <= query_pos
    term = jnp.zeros((q_ref.shape[0], 1), jnp.float32)
    for i in range(blocks):
        past = i * size
        query = q_ref[:, pl.ds(at[i], size)]
        grad = grad_ref[:, pl.ds(at[i], size)]
        log_total = log_ref[0, :, pl.ds(at[i], size)]
        parts = [(past, size)] + ([(0, past)] if i else [])
        probs, grads = [], []
        delta = jnp.zeros((1, size), jnp.float32)
        for first, count in parts:
            prob = jnp.exp(dot(key_rows[first : first + count, :], query, 1, 0) - log_total)
            if first == past:
                prob = jnp.where(seen, prob, 0.0)
            grad_prob = dot(value_rows[first : first + count, :], grad, 1, 0)
            delta = delta + jnp.sum(prob * grad_prob, axis=0, keepdims=True)
            probs.append(prob)
            grads.append(grad_prob)
        grad_query = jnp.zeros(query.shape, jnp.float32)
        for (first, count), prob, grad_prob in zip(parts, probs, grads):
            cols = slice(first, first + count)
            grad_score = (prob * (grad_prob - delta)).astype(jnp.bfloat16)
            value_sum[:, cols] += dot(grad, prob.astype(jnp.bfloat16), 1, 1)
            key_sum[:, cols] += dot(query, grad_score, 1, 1)
            grad_query = grad_query + dot(key_cols[:, cols], grad_score, 1, 0)
        term = term + jnp.sum(
            grad_query * query.astype(jnp.float32), axis=1, keepdims=True
        )
        out_ref[0, :, pl.ds(at[i], size)] = (grad_query * scale_ref[...]).astype(jnp.bfloat16)
    for i in range(blocks):
        here = slice(i * size, (i + 1) * size)
        out_ref[1, :, pl.ds(at[i], size)] = key_sum[:, here].astype(jnp.bfloat16)
        out_ref[2, :, pl.ds(at[i], size)] = value_sum[:, here].astype(jnp.bfloat16)
    term_ref[0] = term


def attend_back(projected, grad_attended, log_total, multiplier, order, heads, head_dim):
    tokens = projected.shape[1]
    blocks = order.shape[0]

    def part(first):
        return pl.BlockSpec((head_dim, tokens), lambda h, order, first=first: (first + h, 0))

    return pl.pallas_call(
        functools.partial(attend_back_kernel, blocks),
        out_shape=[
            jax.ShapeDtypeStruct((3, heads * head_dim, tokens), jnp.bfloat16),
            jax.ShapeDtypeStruct((heads, head_dim, 1), jnp.float32),
        ],
        grid_spec=pltpu.PrefetchScalarGridSpec(
            num_scalar_prefetch=1,
            grid=(heads,),
            in_specs=[
                part(0),
                part(heads),
                part(2 * heads),
                part(0),
                pl.BlockSpec((1, 1, tokens), lambda h, order: (h, 0, 0)),
                pl.BlockSpec((head_dim, 1), lambda h, order: (0, 0)),
            ],
            out_specs=[
                pl.BlockSpec((3, head_dim, tokens), lambda h, order: (0, h, 0)),
                pl.BlockSpec((1, head_dim, 1), lambda h, order: (h, 0, 0)),
            ],
            scratch_shapes=[
                pltpu.VMEM((tokens, head_dim), jnp.bfloat16),
                pltpu.VMEM((head_dim, tokens), jnp.bfloat16),
                pltpu.VMEM((tokens, head_dim), jnp.bfloat16),
                pltpu.VMEM((head_dim, tokens), jnp.float32),
                pltpu.VMEM((head_dim, tokens), jnp.float32),
            ],
        ),
        compiler_params=pltpu.CompilerParams(vmem_limit_bytes=48 * 1024 * 1024),
        cost_estimate=pl.CostEstimate(
            flops=heads * tokens * tokens * head_dim * 10,
            bytes_accessed=heads * head_dim * tokens * 14,
            transcendentals=heads * tokens * tokens,
        ),
        name="attend_back",
    )(order, projected, projected, projected, grad_attended, log_total, multiplier)


def paired_layer(
    inputs,
    targets,
    valid_counts,
    owners,
    master,
    first_moment,
    second_moment,
    norm_gains,
    gain_first,
    gain_second,
    query_scale,
    scale_first,
    scale_second,
):
    bf16 = jnp.bfloat16
    f32 = jnp.float32
    seq_local, block_rows, width = inputs.shape
    slot_count, head_dim, column_count = master.shape
    ff_blocks = FF // head_dim
    owner_count = lax.axis_size("fsdp")
    device = lax.axis_index("ctx")
    chip, core = device // 2, device % 2
    owner_here = lax.axis_index("fsdp")
    low_here = owner_here % 2
    low_groups = [list(range(low, owner_count, 2)) for low in range(2)]
    high_count = owner_count // 2
    half_width = width // 2
    half_slots = slot_count // 2
    half_rows = seq_local * block_rows
    half_heads = H // 2
    half_blocks = ff_blocks // 2
    set_units = 4 * half_heads + 2 * half_blocks
    first_chip, first_core = chip == 0, core == 0

    def columns_here(array):
        return jnp.where(first_chip, array, jnp.roll(array, half_width, axis=-1))

    def sequence_rows(array):
        own = jnp.where(first_chip, array[0], array[1])
        got = swapped(jnp.where(first_chip, array[1], array[0]), "ctx", 2)
        return jnp.where(
            first_chip, jnp.concatenate([own, got]), jnp.concatenate([got, own])
        )

    def rows_home(array):
        array = columns_here(array)
        first, last = array[:block_rows], array[block_rows:]
        own = jnp.where(first_chip, first, last)
        got = swapped(jnp.where(first_chip, last, first).astype(bf16), "ctx", 2).astype(f32)
        return jnp.where(first_chip, jnp.stack([own, got]), jnp.stack([got, own]))

    slot_rows = unit_rows(owners, slot_count)
    unit_total = owners.shape[0]
    kind_sizes = [H, H, H, H, ff_blocks, ff_blocks]
    kind_starts = [sum(kind_sizes[:i]) for i in range(6)]

    def unit_list(kinds, which):
        return jnp.concatenate(
            [
                kind_starts[k] + which * (kind_sizes[k] // 2) + jnp.arange(kind_sizes[k] // 2)
                for k in kinds
            ]
        ).astype(jnp.int32)

    wanted = jnp.concatenate(
        [unit_list(range(6), core), unit_list((4, 5), 1 - core)]
    )
    wanted_rows = slot_rows[wanted]
    wanted_owner, wanted_slot = wanted_rows // slot_count, wanted_rows % slot_count
    weight_from = 2 * (wanted_slot // half_slots != core) + (wanted_owner % 2 != low_here)
    weight_row = (wanted_owner // 2) * half_slots + wanted_slot % half_slots
    weight_sizes = [3 * half_heads, half_heads, 2 * half_blocks, 2 * half_blocks]

    chunks = []
    start = 0
    for size in (256, 256, 128):
        chunks.append((start, size))
        start += size
    shard = master.astype(bf16)
    own_half = jnp.where(first_core, shard[:half_slots], shard[half_slots:])
    got_half = swapped(jnp.where(first_core, shard[half_slots:], shard[:half_slots]), "ctx", 1)
    shard = jnp.where(
        first_core,
        jnp.concatenate([own_half, got_half], axis=2),
        jnp.concatenate([got_half, own_half], axis=2),
    )
    qkv_pieces, out_pieces, near_pieces, far_pieces = [], [], [], []
    for start, size in chunks:
        high = lax.all_gather(
            shard[:, :, start : start + size],
            "fsdp",
            axis=0,
            axis_index_groups=low_groups,
            tiled=True,
        )
        low = swapped(high, "fsdp", 1)
        sources = [high, low, swapped(high, "ctx", 1), swapped(low, "ctx", 1)]
        qkv, out, near, far = copy_rows(
            sources, [0] * 4, size, weight_from.astype(jnp.int32), weight_row, weight_sizes
        )
        near_got = swapped(near, "ctx", 2)
        for pieces, own, got in (
            (qkv_pieces, qkv, swapped(qkv, "ctx", 2)),
            (out_pieces, out, swapped(out, "ctx", 2)),
            (near_pieces, near, near_got),
            (far_pieces, far, swapped(near_got, "ctx", 1)),
        ):
            pieces.append((own, start))
            pieces.append((got, half_width + start))
    (w_qkv,) = place_pieces(
        [piece for piece, _ in qkv_pieces],
        [(0, 3 * half_heads, 0, 0, column) for _, column in qkv_pieces],
        [(3 * half_heads, head_dim, width)],
    )
    (w_out,) = place_pieces(
        [piece for piece, _ in out_pieces],
        [(0, half_heads, 0, 0, column) for _, column in out_pieces],
        [(half_heads, head_dim, width)],
    )
    mlp_pieces, mlp_places = [], []
    for row, pieces in ((0, near_pieces), (half_blocks, far_pieces)):
        for piece, column in pieces:
            for kind in range(2):
                mlp_pieces.append(piece)
                mlp_places.append((kind * half_blocks, half_blocks, kind, row, column))
    w_up, w_down = place_pieces(
        mlp_pieces, mlp_places, [(ff_blocks, head_dim, width)] * 2
    )
    w_qkv = w_qkv.reshape(-1, width)
    w_out = w_out.reshape(-1, width)
    w_up = w_up.reshape(-1, width)
    w_down = w_down.reshape(-1, width)

    gains = columns_here(norm_gains)
    values_b = columns_here(sequence_rows(inputs))
    targets_b = columns_here(sequence_rows(targets))
    values_in = values_b.astype(f32)
    normed_own = (values_in * inverse_rms(values_in) * gains[0]).astype(bf16)
    normed_b = jnp.concatenate([normed_own, swapped(normed_own, "ctx", 1)])
    base = score_base / math.sqrt(head_dim)
    multiplier = jax.nn.softplus(query_scale) * base
    row_scale = jnp.concatenate(
        [jnp.tile(multiplier, half_heads), jnp.ones((2 * half_heads * head_dim,), f32)]
    )
    projected = (dot(w_qkv, normed_b, 1, 1) * row_scale[:, None]).astype(bf16)
    positions = jnp.arange(4, dtype=jnp.int32)
    order = jnp.where(positions % 2 == core, 0, 2) + positions // 2
    order = order.astype(jnp.int32)
    attended, log_total = attend(projected, order, half_heads, head_dim)
    branch_far = dot(attended[:, half_rows:], w_out, 0, 0).astype(bf16)
    branch_got = swapped(branch_far, "ctx", 1)
    branch_own = dot(attended[:, :half_rows], w_out, 0, 0)
    middle = values_in + (branch_own + branch_got.astype(f32))
    normed_mid_b = (middle * inverse_rms(middle) * gains[1]).astype(bf16)
    hidden = dot(normed_mid_b, w_up, 1, 1)
    active_b = jax.nn.silu(hidden).astype(bf16)
    block_out = middle + dot(active_b, w_down, 1, 0)
    seq_length = 2 * half_rows
    row = jnp.arange(half_rows, dtype=jnp.int32)
    row_pos = (core + 2 * (row // block_rows)) * block_rows + row % block_rows
    valid = jnp.where(first_chip, valid_counts[0], valid_counts[1])
    counted = (row_pos >= seq_length - valid).astype(f32)
    count_term = jnp.sum(counted)

    out_grad = 2.0 * (block_out - targets_b.astype(f32)) * counted[:, None]
    out_grad_b = out_grad.astype(bf16)
    grad_active = dot(out_grad_b, w_down, 1, 1)
    sigma = jax.nn.sigmoid(hidden)
    grad_hidden_b = (grad_active * sigma * (1.0 + hidden * (1.0 - sigma))).astype(bf16)
    grad_normed_mid = dot(grad_hidden_b, w_up, 1, 0)
    inverse = inverse_rms(middle)
    scaled = grad_normed_mid * gains[1]
    grad_middle = out_grad + (
        inverse * scaled
        - middle * inverse**3 * jnp.mean(scaled * middle, axis=-1, keepdims=True)
    )
    grad_gain_two = jnp.sum(grad_normed_mid * middle * inverse, axis=0)
    grad_middle_own = grad_middle.astype(bf16)
    grad_middle_b = jnp.concatenate([grad_middle_own, swapped(grad_middle_own, "ctx", 1)])
    grad_attended = dot(w_out, grad_middle_b, 1, 1).astype(bf16)
    far_blocks = half_blocks * head_dim

    def block_pieces(left, right):
        far = dot(left[:, far_blocks:], right, 0, 0).astype(bf16)
        got = swapped(far, "ctx", 1)
        total = (dot(left[:, :far_blocks], right, 0, 0) + got.astype(f32)).astype(bf16)
        return across_chips(total[:, half_width:], total[:, :half_width], half_blocks)

    def across_chips(far, own, units):
        got = swapped(far.reshape(units, head_dim, -1), "ctx", 2)
        total = (own.reshape(got.shape).astype(f32) + got.astype(f32)).astype(bf16)
        return (total, swapped(total, "ctx", 1))

    early = [
        across_chips(
            dot(attended, grad_middle_b[:, half_width:], 1, 0).astype(bf16),
            dot(attended, grad_middle_b[:, :half_width], 1, 0),
            half_heads,
        ),
        block_pieces(grad_hidden_b, normed_mid_b),
        block_pieces(active_b, out_grad_b),
    ]
    grad_proj, grad_scale = attend_back(
        projected, grad_attended, log_total, multiplier[:, None], order, half_heads, head_dim
    )
    grad_proj = grad_proj.reshape(-1, grad_proj.shape[2])
    scale_term = (
        jnp.sum(grad_scale[:, :, 0], axis=0) / multiplier * base * jax.nn.sigmoid(query_scale)
    )

    low_order = jnp.stack([low_here, 1 - low_here])
    table_slots = (
        (2 * jnp.arange(high_count)[None, :, None] + low_order[:, None, None]) * slot_count
        + core * half_slots
        + jnp.arange(half_slots)[None, None, :]
    ).reshape(-1)
    holds = table_slots[:, None] == slot_rows[None, :]
    unit_order = jnp.arange(unit_total, dtype=jnp.int32)
    slot_unit = jnp.sum(jnp.where(holds, unit_order[None, :] + 1, 0), axis=1) - 1
    kind = jnp.where(
        slot_unit < 4 * H, slot_unit // H, 4 + (slot_unit - 4 * H) // ff_blocks
    )
    kind_size = jnp.where(kind < 4, H, ff_blocks)
    within = jnp.where(kind < 4, slot_unit % H, (slot_unit - 4 * H) % ff_blocks)
    other_set = (within // (kind_size // 2) != core).astype(jnp.int32)
    rank = within % (kind_size // 2)
    array_of = jnp.where(kind < 3, 0, kind - 2)
    grad_row = jnp.where(kind < 3, kind * half_heads + rank, rank)
    empty = slot_unit < 0
    grad_from = jnp.where(empty, 8, 2 * array_of + other_set).astype(jnp.int32)
    grad_row = jnp.where(empty, 0, grad_row).astype(jnp.int32)
    late = []
    for start, size in chunks:
        far = slice(half_width + start, half_width + start + size)
        near = slice(start, start + size)
        late.append(
            across_chips(
                dot(grad_proj, normed_b[:, far], 1, 0).astype(bf16),
                dot(grad_proj, normed_b[:, near], 1, 0),
                3 * half_heads,
            )
        )
    owned = []
    for (start, size), (qkv_own, qkv_got) in zip(chunks, late):
        zero = jnp.zeros((1, head_dim, size), bf16)
        sources = [qkv_own, qkv_got] + [part for pair in early for part in pair] + [zero]
        offsets = [0, 0] + [start] * 6 + [0]
        keep, send = copy_rows(
            sources, offsets, size, grad_from, grad_row, [high_count * half_slots] * 2
        )
        got = swapped(send, "fsdp", 1)
        table = (keep.astype(f32) + got.astype(f32)).astype(bf16)
        owned.append(
            lax.psum_scatter(
                table,
                "fsdp",
                scatter_dimension=0,
                axis_index_groups=low_groups,
                tiled=True,
            )
        )

    normed_far = dot(grad_proj[:, half_rows:], w_qkv, 0, 0).astype(bf16)
    normed_got = swapped(normed_far, "ctx", 1)
    grad_normed_in = dot(grad_proj[:, :half_rows], w_qkv, 0, 0) + normed_got.astype(f32)
    inverse = inverse_rms(values_in)
    scaled = grad_normed_in * gains[0]
    input_grad = grad_middle + (
        inverse * scaled
        - values_in * inverse**3 * jnp.mean(scaled * values_in, axis=-1, keepdims=True)
    )
    grad_gain_one = jnp.sum(grad_normed_in * values_in * inverse, axis=0)

    gain_terms = columns_here(jnp.stack([grad_gain_one, grad_gain_two]))
    small = jnp.concatenate([gain_terms.reshape(-1), scale_term, count_term[None]])
    small = jnp.pad(small, (0, -small.shape[0] % 1024)).reshape(1, -1)
    small = jnp.sum(lax.all_gather(small, ("ctx", "fsdp"), axis=0, tiled=True), axis=0)
    gain_sums = small[: 2 * width].reshape(2, width)
    scale_sums = small[2 * width : 2 * width + head_dim]
    count = small[2 * width + head_dim]

    owned = jnp.concatenate(owned, axis=2).reshape(half_slots, head_dim, 2, column_count)
    kept = jnp.where(first_core, owned[:, :, 0], owned[:, :, 1])
    sent = swapped(jnp.where(first_core, owned[:, :, 1], owned[:, :, 0]), "ctx", 1)
    slot_sums = jnp.where(
        first_core, jnp.concatenate([kept, sent]), jnp.concatenate([sent, kept])
    ).astype(f32)
    new_master, new_first, new_second = adam_step(
        master, first_moment, second_moment, slot_sums / count, master_rate, decay_rate
    )
    new_gains, new_gain_first, new_gain_second = adam_step(
        norm_gains, gain_first, gain_second, gain_sums / count, gain_rate, 0.0
    )
    new_scale, new_scale_first, new_scale_second = adam_step(
        query_scale, scale_first, scale_second, scale_sums / count, scale_rate, 0.0
    )
    return (
        rows_home(block_out),
        rows_home(input_grad),
        new_master,
        new_first,
        new_second,
        new_gains,
        new_gain_first,
        new_gain_second,
        new_scale,
        new_scale_first,
        new_scale_second,
    )


def on_device(*arguments):
    paired = (
        lax.axis_size("ctx") == 4
        and lax.axis_size("fsdp") % 2 == 0
        and arguments[0].shape[0] == 2
    )
    return (paired_layer if paired else general_layer)(*arguments)


def solution(mesh):
    in_specs = (
        P("fsdp", "ctx", None),
        P("fsdp", "ctx", None),
        P("fsdp"),
        P(),
        P("fsdp", None, "ctx"),
        P("fsdp", None, "ctx"),
        P("fsdp", None, "ctx"),
        P(),
        P(),
        P(),
        P(),
        P(),
        P(),
    )
    out_specs = (
        P("fsdp", "ctx", None),
        P("fsdp", "ctx", None),
        P("fsdp", None, "ctx"),
        P("fsdp", None, "ctx"),
        P("fsdp", None, "ctx"),
        P(),
        P(),
        P(),
        P(),
        P(),
        P(),
    )
    return jax.shard_map(
        on_device, mesh=mesh, in_specs=in_specs, out_specs=out_specs, check_vma=False
    )
```

```python
import functools
import math

import jax
import jax.numpy as jnp
from jax import lax
from jax.experimental import pallas as pl
from jax.experimental.pallas import tpu as pltpu
from jax.sharding import PartitionSpec as P

H = 16
FF = 1280
STEP = 10


norm_eps = 1e-06
beta_first = 0.9
beta_second = 0.95
adam_eps = 1e-08
decay_rate = 0.1
master_rate = 0.05
gain_rate = 2.0
scale_rate = 2.0
score_base = 1.442695041
masked_score = -1e30


def from_behind(block, axis, distance):
    devices = range(lax.axis_size(axis))
    route = [(i - distance, i) for i in devices if i - distance in devices]
    return lax.ppermute(block, axis, route)


def shifted(array, axis, by):
    count = lax.axis_size(axis)
    return lax.ppermute(array, axis, [(i, (i + by) % count) for i in range(count)])


def unit_rows(owners, slot_count):
    unit_count = owners.shape[0]
    unit_order = jnp.arange(unit_count, dtype=jnp.int32)
    same_owner = owners[:, None] == owners[None, :]
    earlier = unit_order[None, :] < unit_order[:, None]
    slot_rank = jnp.sum((same_owner & earlier).astype(jnp.int32), axis=1)
    return owners * slot_count + slot_rank


def inverse_rms(values):
    return lax.rsqrt(jnp.mean(values * values, axis=-1, keepdims=True) + norm_eps)


def norm_back(values, gain, grad_normed):
    inverse = inverse_rms(values)
    scaled = grad_normed * gain
    grad_values = inverse * scaled - values * inverse**3 * jnp.mean(
        scaled * values, axis=-1, keepdims=True
    )
    grad_gain = jnp.sum(grad_normed * values * inverse, axis=(0, 1))
    return (grad_values, grad_gain)


def adam_step(values, moment_one, moment_two, gradient, step_rate, weight_decay):
    moment_one = beta_first * moment_one + (1.0 - beta_first) * gradient
    moment_two = beta_second * moment_two + (1.0 - beta_second) * gradient * gradient
    first_hat = moment_one / (1.0 - beta_first**STEP)
    second_hat = moment_two / (1.0 - beta_second**STEP)
    values = values - step_rate * (
        first_hat / (jnp.sqrt(second_hat) + adam_eps) + weight_decay * values
    )
    return (values, moment_one, moment_two)


def general_layer(
    inputs,
    targets,
    valid_counts,
    owners,
    master,
    first_moment,
    second_moment,
    norm_gains,
    gain_first,
    gain_second,
    query_scale,
    scale_first,
    scale_second,
):
    seq_local, block_rows, width = inputs.shape
    slot_count, head_dim, column_count = master.shape
    ff_blocks = FF // head_dim
    ctx_size = lax.axis_size("ctx")
    ctx_index = lax.axis_index("ctx")
    slot_rows = unit_rows(owners, slot_count)
    owner_table = lax.all_gather(master.astype(jnp.bfloat16), "fsdp", axis=0, tiled=True)
    picked = owner_table[slot_rows]
    weights = lax.all_gather(picked, "ctx", axis=2, tiled=True)
    w_qkv = weights[0 : 3 * H]
    w_out = weights[3 * H : 4 * H]
    w_up = weights[4 * H : 4 * H + ff_blocks]
    w_down = weights[4 * H + ff_blocks :]
    values_in = inputs.astype(jnp.float32)
    normed_b = (values_in * inverse_rms(values_in) * norm_gains[0]).astype(jnp.bfloat16)
    projected = jnp.einsum("sbd,hed->shbe", normed_b, w_qkv, preferred_element_type=jnp.float32)
    query_pre = projected[:, 0:H]
    multiplier = jax.nn.softplus(query_scale) * (score_base / math.sqrt(head_dim))
    query_b = (query_pre * multiplier).astype(jnp.bfloat16)
    key_b = projected[:, H : 2 * H].astype(jnp.bfloat16)
    value_b = projected[:, 2 * H : 3 * H].astype(jnp.bfloat16)
    query_rows = ctx_index * block_rows + jnp.arange(block_rows, dtype=jnp.int32)
    last_row = ctx_index * block_rows + block_rows - 1
    start_state = (
        jnp.full(query_pre.shape[:3], masked_score, jnp.float32),
        jnp.zeros(query_pre.shape[:3], jnp.float32),
        jnp.zeros(query_pre.shape, jnp.float32),
    )
    key_part = lax.all_gather(key_b, "ctx", axis=2, tiled=True)
    value_part = lax.all_gather(value_b, "ctx", axis=2, tiled=True)
    key_count = key_part.shape[2]

    def update(current):
        run_max, run_sum, accum = current
        key_rows = jnp.arange(key_count, dtype=jnp.int32)
        allowed = query_rows[:, None] >= key_rows[None, :]
        scores = jnp.einsum(
            "shqe,shke->shqk", query_b, key_part, preferred_element_type=jnp.float32
        )
        scores = jnp.where(allowed, scores, masked_score)
        new_max = jnp.maximum(run_max, jnp.max(scores, axis=-1))
        attn_probs = jnp.where(allowed, jnp.exp(scores - new_max[..., None]), 0.0)
        run_sum = jnp.sum(attn_probs, axis=-1)
        accum = jnp.einsum(
            "shqk,shke->shqe",
            attn_probs.astype(jnp.bfloat16),
            value_part,
            preferred_element_type=jnp.float32,
        )
        return (new_max, run_sum, accum)

    run_max, run_sum, accum = lax.cond(
        jnp.int32(0) <= last_row, update, lambda current: current, start_state
    )
    attended = accum / run_sum[..., None]
    log_total = run_max + jnp.log(run_sum)
    attended_b = attended.astype(jnp.bfloat16)
    branch = jnp.einsum("shbe,hed->sbd", attended_b, w_out, preferred_element_type=jnp.float32)
    middle = values_in + branch
    normed_mid_b = (middle * inverse_rms(middle) * norm_gains[1]).astype(jnp.bfloat16)
    hidden = jnp.einsum("sbd,fed->sbfe", normed_mid_b, w_up, preferred_element_type=jnp.float32)
    active_b = jax.nn.silu(hidden).astype(jnp.bfloat16)
    block_out = middle + jnp.einsum(
        "sbfe,fed->sbd", active_b, w_down, preferred_element_type=jnp.float32
    )
    seq_length = block_rows * ctx_size
    counted = (query_rows[None, :] >= (seq_length - valid_counts)[:, None]).astype(jnp.float32)
    count_term = jnp.sum(counted)
    out_grad = 2.0 * (block_out - targets.astype(jnp.float32)) * counted[..., None]
    out_grad_b = out_grad.astype(jnp.bfloat16)
    grad_down = jnp.einsum(
        "sbfe,sbd->fed", active_b, out_grad_b, preferred_element_type=jnp.float32
    )
    grad_active = jnp.einsum(
        "sbd,fed->sbfe", out_grad_b, w_down, preferred_element_type=jnp.float32
    )
    sigma = jax.nn.sigmoid(hidden)
    grad_hidden_b = (grad_active * sigma * (1.0 + hidden * (1.0 - sigma))).astype(jnp.bfloat16)
    grad_up = jnp.einsum(
        "sbfe,sbd->fed", grad_hidden_b, normed_mid_b, preferred_element_type=jnp.float32
    )
    grad_normed_mid = jnp.einsum(
        "sbfe,fed->sbd", grad_hidden_b, w_up, preferred_element_type=jnp.float32
    )
    grad_middle_norm, grad_gain_two = norm_back(middle, norm_gains[1], grad_normed_mid)
    grad_middle = out_grad + grad_middle_norm
    grad_middle_b = grad_middle.astype(jnp.bfloat16)
    grad_out = jnp.einsum(
        "shbe,sbd->hed", attended_b, grad_middle_b, preferred_element_type=jnp.float32
    )
    grad_attended_b = jnp.einsum(
        "sbd,hed->shbe", grad_middle_b, w_out, preferred_element_type=jnp.float32
    ).astype(jnp.bfloat16)
    delta = jnp.sum(grad_attended_b.astype(jnp.float32) * attended, axis=-1)

    def block_grads(source, key_cur, value_cur, partial_grads):
        grad_key, grad_value, grad_query = partial_grads
        key_rows = source * block_rows + jnp.arange(block_rows, dtype=jnp.int32)
        allowed = query_rows[:, None] >= key_rows[None, :]
        scores = jnp.einsum("shqe,shke->shqk", query_b, key_cur, preferred_element_type=jnp.float32)
        scores = jnp.where(allowed, scores, masked_score)
        attn_probs = jnp.exp(scores - log_total[..., None])
        grad_value = grad_value + jnp.einsum(
            "shqk,shqe->shke",
            attn_probs.astype(jnp.bfloat16),
            grad_attended_b,
            preferred_element_type=jnp.float32,
        )
        grad_probs = jnp.einsum(
            "shqe,shke->shqk", grad_attended_b, value_cur, preferred_element_type=jnp.float32
        )
        grad_scores_b = (attn_probs * (grad_probs - delta[..., None])).astype(jnp.bfloat16)
        grad_query = grad_query + jnp.einsum(
            "shqk,shke->shqe", grad_scores_b, key_cur, preferred_element_type=jnp.float32
        )
        grad_key = grad_key + jnp.einsum(
            "shqk,shqe->shke", grad_scores_b, query_b, preferred_element_type=jnp.float32
        )
        return (grad_key, grad_value, grad_query)

    zero_heads = jnp.zeros(query_pre.shape, jnp.float32)

    def back_turn(which_turn, current):
        key_cur, value_cur, grad_key, grad_value, grad_query = current
        source = (ctx_index - which_turn) % ctx_size
        grad_key, grad_value, grad_query = lax.cond(
            source <= ctx_index,
            lambda parts: block_grads(source, key_cur, value_cur, parts),
            lambda parts: parts,
            (grad_key, grad_value, grad_query),
        )
        key_cur, value_cur = from_behind((key_cur, value_cur), "ctx", 1)
        grad_key, grad_value = (
            shifted(grad_key.astype(jnp.bfloat16), "ctx", 1).astype(grad_key.dtype),
            shifted(grad_value.astype(jnp.bfloat16), "ctx", 1).astype(grad_value.dtype),
        )
        return (key_cur, value_cur, grad_key, grad_value, grad_query)

    back_state = (key_b, value_b, zero_heads, zero_heads, zero_heads)
    back_state = lax.fori_loop(0, ctx_size, back_turn, back_state)
    grad_key, grad_value, grad_query = (back_state[2], back_state[3], back_state[4])
    grad_proj_b = jnp.concatenate([grad_query * multiplier, grad_key, grad_value], axis=1).astype(
        jnp.bfloat16
    )
    grad_qkv = jnp.einsum(
        "shbe,sbd->hed", grad_proj_b, normed_b, preferred_element_type=jnp.float32
    )
    grad_normed_in = jnp.einsum(
        "shbe,hed->sbd", grad_proj_b, w_qkv, preferred_element_type=jnp.float32
    )
    grad_input_norm, grad_gain_one = norm_back(values_in, norm_gains[0], grad_normed_in)
    input_grad = grad_middle + grad_input_norm
    scale_term = (
        jnp.sum(grad_query * query_pre, axis=(0, 1, 2))
        * (score_base / math.sqrt(head_dim))
        * jax.nn.sigmoid(query_scale)
    )
    unit_grads = jnp.concatenate([grad_qkv, grad_out, grad_up, grad_down], axis=0)
    owner_total = lax.axis_size("fsdp") * slot_count
    table_grads = (
        jnp.zeros((owner_total, head_dim, width), jnp.float32).at[slot_rows].set(unit_grads)
    )
    owned = lax.psum_scatter(
        table_grads.astype(jnp.bfloat16), "fsdp", scatter_dimension=0, tiled=True
    )
    slot_sums = lax.psum_scatter(owned, "ctx", scatter_dimension=2, tiled=True).astype(jnp.float32)
    gain_sums, scale_sums, count = lax.psum(
        (jnp.stack([grad_gain_one, grad_gain_two]), scale_term, count_term), ("ctx", "fsdp")
    )
    new_master, new_first, new_second = adam_step(
        master, first_moment, second_moment, slot_sums / count, master_rate, decay_rate
    )
    new_gains, new_gain_first, new_gain_second = adam_step(
        norm_gains, gain_first, gain_second, gain_sums / count, gain_rate, 0.0
    )
    new_scale, new_scale_first, new_scale_second = adam_step(
        query_scale, scale_first, scale_second, scale_sums / count, scale_rate, 0.0
    )
    return (
        block_out,
        input_grad,
        new_master,
        new_first,
        new_second,
        new_gains,
        new_gain_first,
        new_gain_second,
        new_scale,
        new_scale_first,
        new_scale_second,
    )


def swapped(array, axis, distance):
    return lax.ppermute(
        array, axis, [(i, i ^ distance) for i in range(lax.axis_size(axis))]
    )


def summed(array, axis):
    size = lax.axis_size(axis)
    if size & (size - 1):
        return lax.psum(array, axis)
    distance = 1
    while distance < size:
        array = array + swapped(array, axis, distance)
        distance *= 2
    return array


def dot(left, right, left_dim, right_dim):
    return lax.dot_general(
        left,
        right,
        (((left_dim,), (right_dim,)), ((), ())),
        preferred_element_type=jnp.float32,
    )


def copy_rows_kernel(sizes, offsets, width, from_ref, row_ref, *refs):
    sources = refs[: len(offsets)]
    outs = refs[len(offsets) : -1]
    sems = refs[-1]
    start = 0
    for place, (out, size) in enumerate(zip(outs, sizes)):

        @pl.loop(0, size)
        def copy_row(i, start=start, place=place, out=out):
            which = from_ref[start + i]
            row = row_ref[start + i]
            for number, (source, offset) in enumerate(zip(sources, offsets)):

                @pl.when(which == number)
                def begin(source=source, offset=offset):
                    pltpu.make_async_copy(
                        source.at[row, :, pl.ds(offset, width)], out.at[i], sems.at[place]
                    ).start()

        start += size
    for place, out in enumerate(outs):
        pltpu.make_async_copy(out, out, sems.at[place]).wait()


def copy_rows(sources, offsets, width, pick_from, pick_row, sizes):
    rows = sources[0].shape[1]
    total = sum(sizes)
    return pl.pallas_call(
        functools.partial(copy_rows_kernel, tuple(sizes), tuple(offsets), width),
        out_shape=[jax.ShapeDtypeStruct((size, rows, width), sources[0].dtype) for size in sizes],
        grid_spec=pltpu.PrefetchScalarGridSpec(
            num_scalar_prefetch=2,
            grid=(1,),
            in_specs=[pl.BlockSpec(memory_space=pl.ANY)] * len(sources),
            out_specs=[
                pl.BlockSpec((size, rows, width), lambda g, f, r: (0, 0, 0)) for size in sizes
            ],
            scratch_shapes=[pltpu.SemaphoreType.DMA((len(sizes),))],
        ),
        compiler_params=pltpu.CompilerParams(vmem_limit_bytes=40 * 1024 * 1024),
        cost_estimate=pl.CostEstimate(
            flops=0, bytes_accessed=total * rows * width * 4, transcendentals=0
        ),
        name="copy_rows",
    )(pick_from, pick_row, *sources)


def place_pieces_kernel(places, *refs):
    pieces = refs[: len(places)]
    outs = refs[len(places) : -1]
    sems = refs[-1]
    copies = []
    for number, (piece, (first, count, out, row, column)) in enumerate(zip(pieces, places)):
        copies.append(
            pltpu.make_async_copy(
                piece.at[pl.ds(first, count)],
                outs[out].at[pl.ds(row, count), :, pl.ds(column, piece.shape[2])],
                sems.at[number],
            )
        )
    for copy in copies:
        copy.start()
    for copy in copies:
        copy.wait()


def place_pieces(pieces, places, shapes):
    moved = sum(math.prod(shape) for shape in shapes)
    return pl.pallas_call(
        functools.partial(place_pieces_kernel, tuple(places)),
        out_shape=[jax.ShapeDtypeStruct(shape, pieces[0].dtype) for shape in shapes],
        in_specs=[pl.BlockSpec(memory_space=pl.ANY)] * len(pieces),
        out_specs=[pl.BlockSpec(memory_space=pltpu.VMEM)] * len(shapes),
        scratch_shapes=[pltpu.SemaphoreType.DMA((len(pieces),))],
        compiler_params=pltpu.CompilerParams(vmem_limit_bytes=40 * 1024 * 1024),
        cost_estimate=pl.CostEstimate(flops=0, bytes_accessed=4 * moved, transcendentals=0),
        name="place_pieces",
    )(*pieces)


def attend_kernel(blocks, order_ref, q_ref, k_ref, v_ref, out_ref, log_ref, key_rows, value_cols):
    size = q_ref.shape[1] // blocks
    at = [pl.multiple_of(order_ref[i] * size, size) for i in range(blocks)]
    for i in range(blocks):
        key_rows[i * size : (i + 1) * size, :] = k_ref[:, pl.ds(at[i], size)].T
        value_cols[:, i * size : (i + 1) * size] = v_ref[:, pl.ds(at[i], size)]
    key_pos = lax.broadcasted_iota(jnp.int32, (size, size), 0)
    query_pos = lax.broadcasted_iota(jnp.int32, (size, size), 1)
    seen = key_pos <= query_pos
    for i in range(blocks):
        past = i * size
        query = q_ref[:, pl.ds(at[i], size)]
        near = jnp.where(
            seen, dot(key_rows[past : past + size, :], query, 1, 0), masked_score
        )
        top = jnp.max(near, axis=0, keepdims=True)
        if i:
            far = dot(key_rows[:past, :], query, 1, 0)
            top = jnp.maximum(top, jnp.max(far, axis=0, keepdims=True))
        near = jnp.exp(near - top)
        total = jnp.sum(near, axis=0, keepdims=True)
        value = dot(value_cols[:, past : past + size], near.astype(jnp.bfloat16), 1, 0)
        if i:
            far = jnp.exp(far - top)
            total = total + jnp.sum(far, axis=0, keepdims=True)
            value = value + dot(value_cols[:, :past], far.astype(jnp.bfloat16), 1, 0)
        out_ref[:, pl.ds(at[i], size)] = (value / total).astype(jnp.bfloat16)
        log_ref[0, :, pl.ds(at[i], size)] = top + jnp.log(total)


def attend(projected, order, heads, head_dim):
    tokens = projected.shape[1]
    blocks = order.shape[0]

    def part(first):
        return pl.BlockSpec((head_dim, tokens), lambda h, order, first=first: (first + h, 0))

    return pl.pallas_call(
        functools.partial(attend_kernel, blocks),
        out_shape=[
            jax.ShapeDtypeStruct((heads * head_dim, tokens), jnp.bfloat16),
            jax.ShapeDtypeStruct((heads, 1, tokens), jnp.float32),
        ],
        grid_spec=pltpu.PrefetchScalarGridSpec(
            num_scalar_prefetch=1,
            grid=(heads,),
            in_specs=[part(0), part(heads), part(2 * heads)],
            out_specs=[
                pl.BlockSpec((head_dim, tokens), lambda h, order: (h, 0)),
                pl.BlockSpec((1, 1, tokens), lambda h, order: (h, 0, 0)),
            ],
            scratch_shapes=[
                pltpu.VMEM((tokens, head_dim), jnp.bfloat16),
                pltpu.VMEM((head_dim, tokens), jnp.bfloat16),
            ],
        ),
        compiler_params=pltpu.CompilerParams(vmem_limit_bytes=40 * 1024 * 1024),
        cost_estimate=pl.CostEstimate(
            flops=heads * tokens * tokens * head_dim * 4,
            bytes_accessed=heads * head_dim * tokens * 8,
            transcendentals=heads * tokens * tokens,
        ),
        name="attend",
    )(order, projected, projected, projected)


def attend_back_kernel(
    blocks,
    order_ref,
    q_ref,
    k_ref,
    v_ref,
    grad_ref,
    log_ref,
    scale_ref,
    out_ref,
    term_ref,
    key_rows,
    key_cols,
    value_rows,
    key_sum,
    value_sum,
):
    size = q_ref.shape[1] // blocks
    at = [pl.multiple_of(order_ref[i] * size, size) for i in range(blocks)]
    for i in range(blocks):
        here = slice(i * size, (i + 1) * size)
        key = k_ref[:, pl.ds(at[i], size)]
        key_rows[here, :] = key.T
        key_cols[:, here] = key
        value_rows[here, :] = v_ref[:, pl.ds(at[i], size)].T
    key_sum[...] = jnp.zeros_like(key_sum)
    value_sum[...] = jnp.zeros_like(value_sum)
    key_pos = lax.broadcasted_iota(jnp.int32, (size, size), 0)
    query_pos = lax.broadcasted_iota(jnp.int32, (size, size), 1)
    seen = key_pos <= query_pos
    term = jnp.zeros((q_ref.shape[0], 1), jnp.float32)
    for i in range(blocks):
        past = i * size
        query = q_ref[:, pl.ds(at[i], size)]
        grad = grad_ref[:, pl.ds(at[i], size)]
        log_total = log_ref[0, :, pl.ds(at[i], size)]
        parts = [(past, size)] + ([(0, past)] if i else [])
        probs, grads = [], []
        delta = jnp.zeros((1, size), jnp.float32)
        for first, count in parts:
            prob = jnp.exp(dot(key_rows[first : first + count, :], query, 1, 0) - log_total)
            if first == past:
                prob = jnp.where(seen, prob, 0.0)
            grad_prob = dot(value_rows[first : first + count, :], grad, 1, 0)
            delta = delta + jnp.sum(prob * grad_prob, axis=0, keepdims=True)
            probs.append(prob)
            grads.append(grad_prob)
        grad_query = jnp.zeros(query.shape, jnp.float32)
        for (first, count), prob, grad_prob in zip(parts, probs, grads):
            cols = slice(first, first + count)
            grad_score = (prob * (grad_prob - delta)).astype(jnp.bfloat16)
            value_sum[:, cols] += dot(grad, prob.astype(jnp.bfloat16), 1, 1)
            key_sum[:, cols] += dot(query, grad_score, 1, 1)
            grad_query = grad_query + dot(key_cols[:, cols], grad_score, 1, 0)
        term = term + jnp.sum(
            grad_query * query.astype(jnp.float32), axis=1, keepdims=True
        )
        out_ref[0, :, pl.ds(at[i], size)] = (grad_query * scale_ref[...]).astype(jnp.bfloat16)
    for i in range(blocks):
        here = slice(i * size, (i + 1) * size)
        out_ref[1, :, pl.ds(at[i], size)] = key_sum[:, here].astype(jnp.bfloat16)
        out_ref[2, :, pl.ds(at[i], size)] = value_sum[:, here].astype(jnp.bfloat16)
    term_ref[0] = term


def attend_back(projected, grad_attended, log_total, multiplier, order, heads, head_dim):
    tokens = projected.shape[1]
    blocks = order.shape[0]

    def part(first):
        return pl.BlockSpec((head_dim, tokens), lambda h, order, first=first: (first + h, 0))

    return pl.pallas_call(
        functools.partial(attend_back_kernel, blocks),
        out_shape=[
            jax.ShapeDtypeStruct((3, heads * head_dim, tokens), jnp.bfloat16),
            jax.ShapeDtypeStruct((heads, head_dim, 1), jnp.float32),
        ],
        grid_spec=pltpu.PrefetchScalarGridSpec(
            num_scalar_prefetch=1,
            grid=(heads,),
            in_specs=[
                part(0),
                part(heads),
                part(2 * heads),
                part(0),
                pl.BlockSpec((1, 1, tokens), lambda h, order: (h, 0, 0)),
                pl.BlockSpec((head_dim, 1), lambda h, order: (0, 0)),
            ],
            out_specs=[
                pl.BlockSpec((3, head_dim, tokens), lambda h, order: (0, h, 0)),
                pl.BlockSpec((1, head_dim, 1), lambda h, order: (h, 0, 0)),
            ],
            scratch_shapes=[
                pltpu.VMEM((tokens, head_dim), jnp.bfloat16),
                pltpu.VMEM((head_dim, tokens), jnp.bfloat16),
                pltpu.VMEM((tokens, head_dim), jnp.bfloat16),
                pltpu.VMEM((head_dim, tokens), jnp.float32),
                pltpu.VMEM((head_dim, tokens), jnp.float32),
            ],
        ),
        compiler_params=pltpu.CompilerParams(vmem_limit_bytes=48 * 1024 * 1024),
        cost_estimate=pl.CostEstimate(
            flops=heads * tokens * tokens * head_dim * 10,
            bytes_accessed=heads * head_dim * tokens * 14,
            transcendentals=heads * tokens * tokens,
        ),
        name="attend_back",
    )(order, projected, projected, projected, grad_attended, log_total, multiplier)


def paired_layer(
    inputs,
    targets,
    valid_counts,
    owners,
    master,
    first_moment,
    second_moment,
    norm_gains,
    gain_first,
    gain_second,
    query_scale,
    scale_first,
    scale_second,
):
    bf16 = jnp.bfloat16
    f32 = jnp.float32
    seq_local, block_rows, width = inputs.shape
    slot_count, head_dim, column_count = master.shape
    ff_blocks = FF // head_dim
    owner_count = lax.axis_size("fsdp")
    device = lax.axis_index("ctx")
    chip, core = device // 2, device % 2
    owner_here = lax.axis_index("fsdp")
    low_here = owner_here % 2
    low_groups = [list(range(low, owner_count, 2)) for low in range(2)]
    high_count = owner_count // 2
    half_width = width // 2
    half_slots = slot_count // 2
    half_rows = seq_local * block_rows
    half_heads = H // 2
    half_blocks = ff_blocks // 2
    set_units = 4 * half_heads + 2 * half_blocks
    first_chip, first_core = chip == 0, core == 0

    def columns_here(array):
        return jnp.where(first_chip, array, jnp.roll(array, half_width, axis=-1))

    def sequence_rows(array):
        own = jnp.where(first_chip, array[0], array[1])
        got = swapped(jnp.where(first_chip, array[1], array[0]), "ctx", 2)
        return jnp.where(
            first_chip, jnp.concatenate([own, got]), jnp.concatenate([got, own])
        )

    def rows_home(array):
        array = columns_here(array)
        first, last = array[:block_rows], array[block_rows:]
        own = jnp.where(first_chip, first, last)
        got = swapped(jnp.where(first_chip, last, first).astype(bf16), "ctx", 2).astype(f32)
        return jnp.where(first_chip, jnp.stack([own, got]), jnp.stack([got, own]))

    slot_rows = unit_rows(owners, slot_count)
    unit_total = owners.shape[0]
    kind_sizes = [H, H, H, H, ff_blocks, ff_blocks]
    kind_starts = [sum(kind_sizes[:i]) for i in range(6)]

    def unit_list(kinds, which):
        return jnp.concatenate(
            [
                kind_starts[k] + which * (kind_sizes[k] // 2) + jnp.arange(kind_sizes[k] // 2)
                for k in kinds
            ]
        ).astype(jnp.int32)

    wanted = jnp.concatenate(
        [unit_list(range(6), core), unit_list((4, 5), 1 - core)]
    )
    wanted_rows = slot_rows[wanted]
    wanted_owner, wanted_slot = wanted_rows // slot_count, wanted_rows % slot_count
    weight_from = 2 * (wanted_slot // half_slots != core) + (wanted_owner % 2 != low_here)
    weight_row = (wanted_owner // 2) * half_slots + wanted_slot % half_slots
    weight_sizes = [3 * half_heads, half_heads, 2 * half_blocks, 2 * half_blocks]

    chunks = []
    start = 0
    for size in (256, 256, 128):
        chunks.append((start, size))
        start += size
    shard = master.astype(bf16)
    own_half = jnp.where(first_core, shard[:half_slots], shard[half_slots:])
    got_half = swapped(jnp.where(first_core, shard[half_slots:], shard[:half_slots]), "ctx", 1)
    shard = jnp.where(
        first_core,
        jnp.concatenate([own_half, got_half], axis=2),
        jnp.concatenate([got_half, own_half], axis=2),
    )
    qkv_pieces, out_pieces, near_pieces, far_pieces = [], [], [], []
    for start, size in chunks:
        high = lax.all_gather(
            shard[:, :, start : start + size],
            "fsdp",
            axis=0,
            axis_index_groups=low_groups,
            tiled=True,
        )
        low = swapped(high, "fsdp", 1)
        sources = [high, low, swapped(high, "ctx", 1), swapped(low, "ctx", 1)]
        qkv, out, near, far = copy_rows(
            sources, [0] * 4, size, weight_from.astype(jnp.int32), weight_row, weight_sizes
        )
        near_got = swapped(near, "ctx", 2)
        for pieces, own, got in (
            (qkv_pieces, qkv, swapped(qkv, "ctx", 2)),
            (out_pieces, out, swapped(out, "ctx", 2)),
            (near_pieces, near, near_got),
            (far_pieces, far, swapped(near_got, "ctx", 1)),
        ):
            pieces.append((own, start))
            pieces.append((got, half_width + start))
    (w_qkv,) = place_pieces(
        [piece for piece, _ in qkv_pieces],
        [(0, 3 * half_heads, 0, 0, column) for _, column in qkv_pieces],
        [(3 * half_heads, head_dim, width)],
    )
    (w_out,) = place_pieces(
        [piece for piece, _ in out_pieces],
        [(0, half_heads, 0, 0, column) for _, column in out_pieces],
        [(half_heads, head_dim, width)],
    )
    mlp_pieces, mlp_places = [], []
    for row, pieces in ((0, near_pieces), (half_blocks, far_pieces)):
        for piece, column in pieces:
            for kind in range(2):
                mlp_pieces.append(piece)
                mlp_places.append((kind * half_blocks, half_blocks, kind, row, column))
    w_up, w_down = place_pieces(
        mlp_pieces, mlp_places, [(ff_blocks, head_dim, width)] * 2
    )
    w_qkv = w_qkv.reshape(-1, width)
    w_out = w_out.reshape(-1, width)
    w_up = w_up.reshape(-1, width)
    w_down = w_down.reshape(-1, width)

    gains = columns_here(norm_gains)
    values_b = columns_here(sequence_rows(inputs))
    targets_b = columns_here(sequence_rows(targets))
    values_in = values_b.astype(f32)
    normed_own = (values_in * inverse_rms(values_in) * gains[0]).astype(bf16)
    normed_b = jnp.concatenate([normed_own, swapped(normed_own, "ctx", 1)])
    base = score_base / math.sqrt(head_dim)
    multiplier = jax.nn.softplus(query_scale) * base
    row_scale = jnp.concatenate(
        [jnp.tile(multiplier, half_heads), jnp.ones((2 * half_heads * head_dim,), f32)]
    )
    projected = (dot(w_qkv, normed_b, 1, 1) * row_scale[:, None]).astype(bf16)
    positions = jnp.arange(4, dtype=jnp.int32)
    order = jnp.where(positions % 2 == core, 0, 2) + positions // 2
    order = order.astype(jnp.int32)
    attended, log_total = attend(projected, order, half_heads, head_dim)
    branch_far = dot(attended[:, half_rows:], w_out, 0, 0).astype(bf16)
    branch_got = swapped(branch_far, "ctx", 1)
    branch_own = dot(attended[:, :half_rows], w_out, 0, 0)
    middle = values_in + (branch_own + branch_got.astype(f32))
    normed_mid_b = (middle * inverse_rms(middle) * gains[1]).astype(bf16)
    hidden = dot(normed_mid_b, w_up, 1, 1)
    active_b = jax.nn.silu(hidden).astype(bf16)
    block_out = middle + dot(active_b, w_down, 1, 0)
    seq_length = 2 * half_rows
    row = jnp.arange(half_rows, dtype=jnp.int32)
    row_pos = (core + 2 * (row // block_rows)) * block_rows + row % block_rows
    valid = jnp.where(first_chip, valid_counts[0], valid_counts[1])
    counted = (row_pos >= seq_length - valid).astype(f32)
    count_term = jnp.sum(counted)

    out_grad = 2.0 * (block_out - targets_b.astype(f32)) * counted[:, None]
    out_grad_b = out_grad.astype(bf16)
    grad_active = dot(out_grad_b, w_down, 1, 1)
    sigma = jax.nn.sigmoid(hidden)
    grad_hidden_b = (grad_active * sigma * (1.0 + hidden * (1.0 - sigma))).astype(bf16)
    grad_normed_mid = dot(grad_hidden_b, w_up, 1, 0)
    inverse = inverse_rms(middle)
    scaled = grad_normed_mid * gains[1]
    grad_middle = out_grad + (
        inverse * scaled
        - middle * inverse**3 * jnp.mean(scaled * middle, axis=-1, keepdims=True)
    )
    grad_gain_two = jnp.sum(grad_normed_mid * middle * inverse, axis=0)
    grad_middle_own = grad_middle.astype(bf16)
    grad_middle_b = jnp.concatenate([grad_middle_own, swapped(grad_middle_own, "ctx", 1)])
    grad_attended = dot(w_out, grad_middle_b, 1, 1).astype(bf16)
    far_blocks = half_blocks * head_dim

    def block_pieces(left, right):
        far = dot(left[:, far_blocks:], right, 0, 0).astype(bf16)
        got = swapped(far, "ctx", 1)
        total = (dot(left[:, :far_blocks], right, 0, 0) + got.astype(f32)).astype(bf16)
        return across_chips(total[:, half_width:], total[:, :half_width], half_blocks)

    def across_chips(far, own, units):
        got = swapped(far.reshape(units, head_dim, -1), "ctx", 2)
        total = (own.reshape(got.shape).astype(f32) + got.astype(f32)).astype(bf16)
        return (total, swapped(total, "ctx", 1))

    early = [
        across_chips(
            dot(attended, grad_middle_b[:, half_width:], 1, 0).astype(bf16),
            dot(attended, grad_middle_b[:, :half_width], 1, 0),
            half_heads,
        ),
        block_pieces(grad_hidden_b, normed_mid_b),
        block_pieces(active_b, out_grad_b),
    ]
    grad_proj, grad_scale = attend_back(
        projected, grad_attended, log_total, multiplier[:, None], order, half_heads, head_dim
    )
    grad_proj = grad_proj.reshape(-1, grad_proj.shape[2])
    scale_term = (
        jnp.sum(grad_scale[:, :, 0], axis=0) / multiplier * base * jax.nn.sigmoid(query_scale)
    )

    low_order = jnp.stack([low_here, 1 - low_here])
    table_slots = (
        (2 * jnp.arange(high_count)[None, :, None] + low_order[:, None, None]) * slot_count
        + core * half_slots
        + jnp.arange(half_slots)[None, None, :]
    ).reshape(-1)
    holds = table_slots[:, None] == slot_rows[None, :]
    unit_order = jnp.arange(unit_total, dtype=jnp.int32)
    slot_unit = jnp.sum(jnp.where(holds, unit_order[None, :] + 1, 0), axis=1) - 1
    kind = jnp.where(
        slot_unit < 4 * H, slot_unit // H, 4 + (slot_unit - 4 * H) // ff_blocks
    )
    kind_size = jnp.where(kind < 4, H, ff_blocks)
    within = jnp.where(kind < 4, slot_unit % H, (slot_unit - 4 * H) % ff_blocks)
    other_set = (within // (kind_size // 2) != core).astype(jnp.int32)
    rank = within % (kind_size // 2)
    array_of = jnp.where(kind < 3, 0, kind - 2)
    grad_row = jnp.where(kind < 3, kind * half_heads + rank, rank)
    empty = slot_unit < 0
    grad_from = jnp.where(empty, 8, 2 * array_of + other_set).astype(jnp.int32)
    grad_row = jnp.where(empty, 0, grad_row).astype(jnp.int32)
    late = []
    for start, size in chunks:
        far = slice(half_width + start, half_width + start + size)
        near = slice(start, start + size)
        late.append(
            across_chips(
                dot(grad_proj, normed_b[:, far], 1, 0).astype(bf16),
                dot(grad_proj, normed_b[:, near], 1, 0),
                3 * half_heads,
            )
        )
    owned = []
    for (start, size), (qkv_own, qkv_got) in zip(chunks, late):
        zero = jnp.zeros((1, head_dim, size), bf16)
        sources = [qkv_own, qkv_got] + [part for pair in early for part in pair] + [zero]
        offsets = [0, 0] + [start] * 6 + [0]
        keep, send = copy_rows(
            sources, offsets, size, grad_from, grad_row, [high_count * half_slots] * 2
        )
        got = swapped(send, "fsdp", 1)
        table = (keep.astype(f32) + got.astype(f32)).astype(bf16)
        owned.append(
            lax.psum_scatter(
                table,
                "fsdp",
                scatter_dimension=0,
                axis_index_groups=low_groups,
                tiled=True,
            )
        )

    normed_far = dot(grad_proj[:, half_rows:], w_qkv, 0, 0).astype(bf16)
    normed_got = swapped(normed_far, "ctx", 1)
    grad_normed_in = dot(grad_proj[:, :half_rows], w_qkv, 0, 0) + normed_got.astype(f32)
    inverse = inverse_rms(values_in)
    scaled = grad_normed_in * gains[0]
    input_grad = grad_middle + (
        inverse * scaled
        - values_in * inverse**3 * jnp.mean(scaled * values_in, axis=-1, keepdims=True)
    )
    grad_gain_one = jnp.sum(grad_normed_in * values_in * inverse, axis=0)

    gain_terms = columns_here(jnp.stack([grad_gain_one, grad_gain_two]))
    small = jnp.concatenate([gain_terms.reshape(-1), scale_term, count_term[None]])
    small = jnp.pad(small, (0, -small.shape[0] % 1024))
    small = summed(summed(small, "ctx"), "fsdp")
    gain_sums = small[: 2 * width].reshape(2, width)
    scale_sums = small[2 * width : 2 * width + head_dim]
    count = small[2 * width + head_dim]

    owned = jnp.concatenate(owned, axis=2).reshape(half_slots, head_dim, 2, column_count)
    kept = jnp.where(first_core, owned[:, :, 0], owned[:, :, 1])
    sent = swapped(jnp.where(first_core, owned[:, :, 1], owned[:, :, 0]), "ctx", 1)
    slot_sums = jnp.where(
        first_core, jnp.concatenate([kept, sent]), jnp.concatenate([sent, kept])
    ).astype(f32)
    new_master, new_first, new_second = adam_step(
        master, first_moment, second_moment, slot_sums / count, master_rate, decay_rate
    )
    new_gains, new_gain_first, new_gain_second = adam_step(
        norm_gains, gain_first, gain_second, gain_sums / count, gain_rate, 0.0
    )
    new_scale, new_scale_first, new_scale_second = adam_step(
        query_scale, scale_first, scale_second, scale_sums / count, scale_rate, 0.0
    )
    return (
        rows_home(block_out),
        rows_home(input_grad),
        new_master,
        new_first,
        new_second,
        new_gains,
        new_gain_first,
        new_gain_second,
        new_scale,
        new_scale_first,
        new_scale_second,
    )


def on_device(*arguments):
    paired = (
        lax.axis_size("ctx") == 4
        and lax.axis_size("fsdp") % 2 == 0
        and arguments[0].shape[0] == 2
    )
    return (paired_layer if paired else general_layer)(*arguments)


def solution(mesh):
    in_specs = (
        P("fsdp", "ctx", None),
        P("fsdp", "ctx", None),
        P("fsdp"),
        P(),
        P("fsdp", None, "ctx"),
        P("fsdp", None, "ctx"),
        P("fsdp", None, "ctx"),
        P(),
        P(),
        P(),
        P(),
        P(),
        P(),
    )
    out_specs = (
        P("fsdp", "ctx", None),
        P("fsdp", "ctx", None),
        P("fsdp", None, "ctx"),
        P("fsdp", None, "ctx"),
        P("fsdp", None, "ctx"),
        P(),
        P(),
        P(),
        P(),
        P(),
        P(),
    )
    return jax.shard_map(
        on_device, mesh=mesh, in_specs=in_specs, out_specs=out_specs, check_vma=False
    )
```

```python
import functools
import math

import jax
import jax.numpy as jnp
from jax import lax
from jax.experimental import pallas as pl
from jax.experimental.pallas import tpu as pltpu
from jax.sharding import PartitionSpec as P

H = 16
FF = 1280
STEP = 10


norm_eps = 1e-06
beta_first = 0.9
beta_second = 0.95
adam_eps = 1e-08
decay_rate = 0.1
master_rate = 0.05
gain_rate = 2.0
scale_rate = 2.0
score_base = 1.442695041
masked_score = -1e30


def from_behind(block, axis, distance):
    devices = range(lax.axis_size(axis))
    route = [(i - distance, i) for i in devices if i - distance in devices]
    return lax.ppermute(block, axis, route)


def shifted(array, axis, by):
    count = lax.axis_size(axis)
    return lax.ppermute(array, axis, [(i, (i + by) % count) for i in range(count)])


def unit_rows(owners, slot_count):
    unit_count = owners.shape[0]
    unit_order = jnp.arange(unit_count, dtype=jnp.int32)
    same_owner = owners[:, None] == owners[None, :]
    earlier = unit_order[None, :] < unit_order[:, None]
    slot_rank = jnp.sum((same_owner & earlier).astype(jnp.int32), axis=1)
    return owners * slot_count + slot_rank


def inverse_rms(values):
    return lax.rsqrt(jnp.mean(values * values, axis=-1, keepdims=True) + norm_eps)


def norm_back(values, gain, grad_normed):
    inverse = inverse_rms(values)
    scaled = grad_normed * gain
    grad_values = inverse * scaled - values * inverse**3 * jnp.mean(
        scaled * values, axis=-1, keepdims=True
    )
    grad_gain = jnp.sum(grad_normed * values * inverse, axis=(0, 1))
    return (grad_values, grad_gain)


def adam_step(values, moment_one, moment_two, gradient, step_rate, weight_decay):
    moment_one = beta_first * moment_one + (1.0 - beta_first) * gradient
    moment_two = beta_second * moment_two + (1.0 - beta_second) * gradient * gradient
    first_hat = moment_one / (1.0 - beta_first**STEP)
    second_hat = moment_two / (1.0 - beta_second**STEP)
    values = values - step_rate * (
        first_hat / (jnp.sqrt(second_hat) + adam_eps) + weight_decay * values
    )
    return (values, moment_one, moment_two)


def general_layer(
    inputs,
    targets,
    valid_counts,
    owners,
    master,
    first_moment,
    second_moment,
    norm_gains,
    gain_first,
    gain_second,
    query_scale,
    scale_first,
    scale_second,
):
    seq_local, block_rows, width = inputs.shape
    slot_count, head_dim, column_count = master.shape
    ff_blocks = FF // head_dim
    ctx_size = lax.axis_size("ctx")
    ctx_index = lax.axis_index("ctx")
    slot_rows = unit_rows(owners, slot_count)
    owner_table = lax.all_gather(master.astype(jnp.bfloat16), "fsdp", axis=0, tiled=True)
    picked = owner_table[slot_rows]
    weights = lax.all_gather(picked, "ctx", axis=2, tiled=True)
    w_qkv = weights[0 : 3 * H]
    w_out = weights[3 * H : 4 * H]
    w_up = weights[4 * H : 4 * H + ff_blocks]
    w_down = weights[4 * H + ff_blocks :]
    values_in = inputs.astype(jnp.float32)
    normed_b = (values_in * inverse_rms(values_in) * norm_gains[0]).astype(jnp.bfloat16)
    projected = jnp.einsum("sbd,hed->shbe", normed_b, w_qkv, preferred_element_type=jnp.float32)
    query_pre = projected[:, 0:H]
    multiplier = jax.nn.softplus(query_scale) * (score_base / math.sqrt(head_dim))
    query_b = (query_pre * multiplier).astype(jnp.bfloat16)
    key_b = projected[:, H : 2 * H].astype(jnp.bfloat16)
    value_b = projected[:, 2 * H : 3 * H].astype(jnp.bfloat16)
    query_rows = ctx_index * block_rows + jnp.arange(block_rows, dtype=jnp.int32)
    last_row = ctx_index * block_rows + block_rows - 1
    start_state = (
        jnp.full(query_pre.shape[:3], masked_score, jnp.float32),
        jnp.zeros(query_pre.shape[:3], jnp.float32),
        jnp.zeros(query_pre.shape, jnp.float32),
    )
    key_part = lax.all_gather(key_b, "ctx", axis=2, tiled=True)
    value_part = lax.all_gather(value_b, "ctx", axis=2, tiled=True)
    key_count = key_part.shape[2]

    def update(current):
        run_max, run_sum, accum = current
        key_rows = jnp.arange(key_count, dtype=jnp.int32)
        allowed = query_rows[:, None] >= key_rows[None, :]
        scores = jnp.einsum(
            "shqe,shke->shqk", query_b, key_part, preferred_element_type=jnp.float32
        )
        scores = jnp.where(allowed, scores, masked_score)
        new_max = jnp.maximum(run_max, jnp.max(scores, axis=-1))
        attn_probs = jnp.where(allowed, jnp.exp(scores - new_max[..., None]), 0.0)
        run_sum = jnp.sum(attn_probs, axis=-1)
        accum = jnp.einsum(
            "shqk,shke->shqe",
            attn_probs.astype(jnp.bfloat16),
            value_part,
            preferred_element_type=jnp.float32,
        )
        return (new_max, run_sum, accum)

    run_max, run_sum, accum = lax.cond(
        jnp.int32(0) <= last_row, update, lambda current: current, start_state
    )
    attended = accum / run_sum[..., None]
    log_total = run_max + jnp.log(run_sum)
    attended_b = attended.astype(jnp.bfloat16)
    branch = jnp.einsum("shbe,hed->sbd", attended_b, w_out, preferred_element_type=jnp.float32)
    middle = values_in + branch
    normed_mid_b = (middle * inverse_rms(middle) * norm_gains[1]).astype(jnp.bfloat16)
    hidden = jnp.einsum("sbd,fed->sbfe", normed_mid_b, w_up, preferred_element_type=jnp.float32)
    active_b = jax.nn.silu(hidden).astype(jnp.bfloat16)
    block_out = middle + jnp.einsum(
        "sbfe,fed->sbd", active_b, w_down, preferred_element_type=jnp.float32
    )
    seq_length = block_rows * ctx_size
    counted = (query_rows[None, :] >= (seq_length - valid_counts)[:, None]).astype(jnp.float32)
    count_term = jnp.sum(counted)
    out_grad = 2.0 * (block_out - targets.astype(jnp.float32)) * counted[..., None]
    out_grad_b = out_grad.astype(jnp.bfloat16)
    grad_down = jnp.einsum(
        "sbfe,sbd->fed", active_b, out_grad_b, preferred_element_type=jnp.float32
    )
    grad_active = jnp.einsum(
        "sbd,fed->sbfe", out_grad_b, w_down, preferred_element_type=jnp.float32
    )
    sigma = jax.nn.sigmoid(hidden)
    grad_hidden_b = (grad_active * sigma * (1.0 + hidden * (1.0 - sigma))).astype(jnp.bfloat16)
    grad_up = jnp.einsum(
        "sbfe,sbd->fed", grad_hidden_b, normed_mid_b, preferred_element_type=jnp.float32
    )
    grad_normed_mid = jnp.einsum(
        "sbfe,fed->sbd", grad_hidden_b, w_up, preferred_element_type=jnp.float32
    )
    grad_middle_norm, grad_gain_two = norm_back(middle, norm_gains[1], grad_normed_mid)
    grad_middle = out_grad + grad_middle_norm
    grad_middle_b = grad_middle.astype(jnp.bfloat16)
    grad_out = jnp.einsum(
        "shbe,sbd->hed", attended_b, grad_middle_b, preferred_element_type=jnp.float32
    )
    grad_attended_b = jnp.einsum(
        "sbd,hed->shbe", grad_middle_b, w_out, preferred_element_type=jnp.float32
    ).astype(jnp.bfloat16)
    delta = jnp.sum(grad_attended_b.astype(jnp.float32) * attended, axis=-1)

    def block_grads(source, key_cur, value_cur, partial_grads):
        grad_key, grad_value, grad_query = partial_grads
        key_rows = source * block_rows + jnp.arange(block_rows, dtype=jnp.int32)
        allowed = query_rows[:, None] >= key_rows[None, :]
        scores = jnp.einsum("shqe,shke->shqk", query_b, key_cur, preferred_element_type=jnp.float32)
        scores = jnp.where(allowed, scores, masked_score)
        attn_probs = jnp.exp(scores - log_total[..., None])
        grad_value = grad_value + jnp.einsum(
            "shqk,shqe->shke",
            attn_probs.astype(jnp.bfloat16),
            grad_attended_b,
            preferred_element_type=jnp.float32,
        )
        grad_probs = jnp.einsum(
            "shqe,shke->shqk", grad_attended_b, value_cur, preferred_element_type=jnp.float32
        )
        grad_scores_b = (attn_probs * (grad_probs - delta[..., None])).astype(jnp.bfloat16)
        grad_query = grad_query + jnp.einsum(
            "shqk,shke->shqe", grad_scores_b, key_cur, preferred_element_type=jnp.float32
        )
        grad_key = grad_key + jnp.einsum(
            "shqk,shqe->shke", grad_scores_b, query_b, preferred_element_type=jnp.float32
        )
        return (grad_key, grad_value, grad_query)

    zero_heads = jnp.zeros(query_pre.shape, jnp.float32)

    def back_turn(which_turn, current):
        key_cur, value_cur, grad_key, grad_value, grad_query = current
        source = (ctx_index - which_turn) % ctx_size
        grad_key, grad_value, grad_query = lax.cond(
            source <= ctx_index,
            lambda parts: block_grads(source, key_cur, value_cur, parts),
            lambda parts: parts,
            (grad_key, grad_value, grad_query),
        )
        key_cur, value_cur = from_behind((key_cur, value_cur), "ctx", 1)
        grad_key, grad_value = (
            shifted(grad_key.astype(jnp.bfloat16), "ctx", 1).astype(grad_key.dtype),
            shifted(grad_value.astype(jnp.bfloat16), "ctx", 1).astype(grad_value.dtype),
        )
        return (key_cur, value_cur, grad_key, grad_value, grad_query)

    back_state = (key_b, value_b, zero_heads, zero_heads, zero_heads)
    back_state = lax.fori_loop(0, ctx_size, back_turn, back_state)
    grad_key, grad_value, grad_query = (back_state[2], back_state[3], back_state[4])
    grad_proj_b = jnp.concatenate([grad_query * multiplier, grad_key, grad_value], axis=1).astype(
        jnp.bfloat16
    )
    grad_qkv = jnp.einsum(
        "shbe,sbd->hed", grad_proj_b, normed_b, preferred_element_type=jnp.float32
    )
    grad_normed_in = jnp.einsum(
        "shbe,hed->sbd", grad_proj_b, w_qkv, preferred_element_type=jnp.float32
    )
    grad_input_norm, grad_gain_one = norm_back(values_in, norm_gains[0], grad_normed_in)
    input_grad = grad_middle + grad_input_norm
    scale_term = (
        jnp.sum(grad_query * query_pre, axis=(0, 1, 2))
        * (score_base / math.sqrt(head_dim))
        * jax.nn.sigmoid(query_scale)
    )
    unit_grads = jnp.concatenate([grad_qkv, grad_out, grad_up, grad_down], axis=0)
    owner_total = lax.axis_size("fsdp") * slot_count
    table_grads = (
        jnp.zeros((owner_total, head_dim, width), jnp.float32).at[slot_rows].set(unit_grads)
    )
    owned = lax.psum_scatter(
        table_grads.astype(jnp.bfloat16), "fsdp", scatter_dimension=0, tiled=True
    )
    slot_sums = lax.psum_scatter(owned, "ctx", scatter_dimension=2, tiled=True).astype(jnp.float32)
    gain_sums, scale_sums, count = lax.psum(
        (jnp.stack([grad_gain_one, grad_gain_two]), scale_term, count_term), ("ctx", "fsdp")
    )
    new_master, new_first, new_second = adam_step(
        master, first_moment, second_moment, slot_sums / count, master_rate, decay_rate
    )
    new_gains, new_gain_first, new_gain_second = adam_step(
        norm_gains, gain_first, gain_second, gain_sums / count, gain_rate, 0.0
    )
    new_scale, new_scale_first, new_scale_second = adam_step(
        query_scale, scale_first, scale_second, scale_sums / count, scale_rate, 0.0
    )
    return (
        block_out,
        input_grad,
        new_master,
        new_first,
        new_second,
        new_gains,
        new_gain_first,
        new_gain_second,
        new_scale,
        new_scale_first,
        new_scale_second,
    )


def swapped(array, axis, distance):
    return lax.ppermute(
        array, axis, [(i, i ^ distance) for i in range(lax.axis_size(axis))]
    )


def summed(array, axis):
    size = lax.axis_size(axis)
    if size & (size - 1):
        return lax.psum(array, axis)
    distance = 1
    while distance < size:
        array = array + swapped(array, axis, distance)
        distance *= 2
    return array


def together(array, piece):
    array, first = lax.optimization_barrier((array, piece[0]))
    return (array, (first, *piece[1:]))


def dot(left, right, left_dim, right_dim):
    return lax.dot_general(
        left,
        right,
        (((left_dim,), (right_dim,)), ((), ())),
        preferred_element_type=jnp.float32,
    )


def copy_rows_kernel(sizes, offsets, width, from_ref, row_ref, *refs):
    sources = refs[: len(offsets)]
    outs = refs[-1 - len(sizes) : -1]
    sems = refs[-1]
    start = 0
    for place, (out, size) in enumerate(zip(outs, sizes)):

        @pl.loop(0, size)
        def copy_row(i, start=start, place=place, out=out):
            which = from_ref[start + i]
            row = row_ref[start + i]
            for number, (source, offset) in enumerate(zip(sources, offsets)):

                @pl.when(which == number)
                def begin(source=source, offset=offset):
                    pltpu.make_async_copy(
                        source.at[row, :, pl.ds(offset, width)], out.at[i], sems.at[place]
                    ).start()

        start += size
    for place, out in enumerate(outs):
        pltpu.make_async_copy(out, out, sems.at[place]).wait()


def copy_rows(sources, offsets, width, pick_from, pick_row, sizes, events=()):
    rows = sources[0].shape[1]
    total = sum(sizes)
    return pl.pallas_call(
        functools.partial(copy_rows_kernel, tuple(sizes), tuple(offsets), width),
        out_shape=[jax.ShapeDtypeStruct((size, rows, width), sources[0].dtype) for size in sizes],
        grid_spec=pltpu.PrefetchScalarGridSpec(
            num_scalar_prefetch=2,
            grid=(1,),
            in_specs=[pl.BlockSpec(memory_space=pl.ANY)] * (len(sources) + len(events)),
            out_specs=[
                pl.BlockSpec((size, rows, width), lambda g, f, r: (0, 0, 0)) for size in sizes
            ],
            scratch_shapes=[pltpu.SemaphoreType.DMA((len(sizes),))],
        ),
        compiler_params=pltpu.CompilerParams(vmem_limit_bytes=40 * 1024 * 1024),
        cost_estimate=pl.CostEstimate(
            flops=0, bytes_accessed=total * rows * width * 4, transcendentals=0
        ),
        name="copy_rows",
    )(pick_from, pick_row, *sources, *events)


def place_pieces_kernel(places, *refs):
    pieces = refs[: len(places)]
    outs = refs[len(places) : -1]
    sems = refs[-1]
    copies = []
    for number, (piece, place) in enumerate(zip(pieces, places)):
        first, count, begin, size, column, out, row = place
        copies.append(
            pltpu.make_async_copy(
                piece.at[pl.ds(first, count), :, pl.ds(begin, size)],
                outs[out].at[pl.ds(row, count), :, pl.ds(column, size)],
                sems.at[number],
            )
        )
    for copy in copies:
        copy.start()
    for copy in copies:
        copy.wait()


def place_pieces(pieces, places, shapes):
    moved = sum(math.prod(shape) for shape in shapes)
    return pl.pallas_call(
        functools.partial(place_pieces_kernel, tuple(places)),
        out_shape=[jax.ShapeDtypeStruct(shape, pieces[0].dtype) for shape in shapes],
        in_specs=[pl.BlockSpec(memory_space=pl.ANY)] * len(pieces),
        out_specs=[pl.BlockSpec(memory_space=pltpu.VMEM)] * len(shapes),
        scratch_shapes=[pltpu.SemaphoreType.DMA((len(pieces),))],
        compiler_params=pltpu.CompilerParams(vmem_limit_bytes=40 * 1024 * 1024),
        cost_estimate=pl.CostEstimate(flops=0, bytes_accessed=4 * moved, transcendentals=0),
        name="place_pieces",
    )(*pieces)


def attend_kernel(blocks, order_ref, q_ref, k_ref, v_ref, out_ref, log_ref, key_rows, value_cols):
    size = q_ref.shape[1] // blocks
    at = [pl.multiple_of(order_ref[i] * size, size) for i in range(blocks)]
    for i in range(blocks):
        key_rows[i * size : (i + 1) * size, :] = k_ref[:, pl.ds(at[i], size)].T
        value_cols[:, i * size : (i + 1) * size] = v_ref[:, pl.ds(at[i], size)]
    key_pos = lax.broadcasted_iota(jnp.int32, (size, size), 0)
    query_pos = lax.broadcasted_iota(jnp.int32, (size, size), 1)
    seen = key_pos <= query_pos
    for i in range(blocks):
        past = i * size
        query = q_ref[:, pl.ds(at[i], size)]
        near = jnp.where(
            seen, dot(key_rows[past : past + size, :], query, 1, 0), masked_score
        )
        top = jnp.max(near, axis=0, keepdims=True)
        if i:
            far = dot(key_rows[:past, :], query, 1, 0)
            top = jnp.maximum(top, jnp.max(far, axis=0, keepdims=True))
        near = jnp.exp(near - top)
        total = jnp.sum(near, axis=0, keepdims=True)
        value = dot(value_cols[:, past : past + size], near.astype(jnp.bfloat16), 1, 0)
        if i:
            far = jnp.exp(far - top)
            total = total + jnp.sum(far, axis=0, keepdims=True)
            value = value + dot(value_cols[:, :past], far.astype(jnp.bfloat16), 1, 0)
        out_ref[:, pl.ds(at[i], size)] = (value / total).astype(jnp.bfloat16)
        log_ref[0, :, pl.ds(at[i], size)] = top + jnp.log(total)


def attend(projected, order, heads, head_dim):
    tokens = projected.shape[1]
    blocks = order.shape[0]

    def part(first):
        return pl.BlockSpec((head_dim, tokens), lambda h, order, first=first: (first + h, 0))

    return pl.pallas_call(
        functools.partial(attend_kernel, blocks),
        out_shape=[
            jax.ShapeDtypeStruct((heads * head_dim, tokens), jnp.bfloat16),
            jax.ShapeDtypeStruct((heads, 1, tokens), jnp.float32),
        ],
        grid_spec=pltpu.PrefetchScalarGridSpec(
            num_scalar_prefetch=1,
            grid=(heads,),
            in_specs=[part(0), part(heads), part(2 * heads)],
            out_specs=[
                pl.BlockSpec((head_dim, tokens), lambda h, order: (h, 0)),
                pl.BlockSpec((1, 1, tokens), lambda h, order: (h, 0, 0)),
            ],
            scratch_shapes=[
                pltpu.VMEM((tokens, head_dim), jnp.bfloat16),
                pltpu.VMEM((head_dim, tokens), jnp.bfloat16),
            ],
        ),
        compiler_params=pltpu.CompilerParams(vmem_limit_bytes=40 * 1024 * 1024),
        cost_estimate=pl.CostEstimate(
            flops=heads * tokens * tokens * head_dim * 4,
            bytes_accessed=heads * head_dim * tokens * 8,
            transcendentals=heads * tokens * tokens,
        ),
        name="attend",
    )(order, projected, projected, projected)


def attend_back_kernel(
    blocks,
    order_ref,
    q_ref,
    k_ref,
    v_ref,
    grad_ref,
    log_ref,
    scale_ref,
    *refs,
):
    out_ref, term_ref, key_rows, key_cols, value_rows, key_sum, value_sum = refs[-7:]
    size = q_ref.shape[1] // blocks
    at = [pl.multiple_of(order_ref[i] * size, size) for i in range(blocks)]
    for i in range(blocks):
        here = slice(i * size, (i + 1) * size)
        key = k_ref[:, pl.ds(at[i], size)]
        key_rows[here, :] = key.T
        key_cols[:, here] = key
        value_rows[here, :] = v_ref[:, pl.ds(at[i], size)].T
    key_sum[...] = jnp.zeros_like(key_sum)
    value_sum[...] = jnp.zeros_like(value_sum)
    key_pos = lax.broadcasted_iota(jnp.int32, (size, size), 0)
    query_pos = lax.broadcasted_iota(jnp.int32, (size, size), 1)
    seen = key_pos <= query_pos
    term = jnp.zeros((q_ref.shape[0], 1), jnp.float32)
    for i in range(blocks):
        past = i * size
        query = q_ref[:, pl.ds(at[i], size)]
        grad = grad_ref[:, pl.ds(at[i], size)]
        log_total = log_ref[0, :, pl.ds(at[i], size)]
        parts = [(past, size)] + ([(0, past)] if i else [])
        probs, grads = [], []
        delta = jnp.zeros((1, size), jnp.float32)
        for first, count in parts:
            prob = jnp.exp(dot(key_rows[first : first + count, :], query, 1, 0) - log_total)
            if first == past:
                prob = jnp.where(seen, prob, 0.0)
            grad_prob = dot(value_rows[first : first + count, :], grad, 1, 0)
            delta = delta + jnp.sum(prob * grad_prob, axis=0, keepdims=True)
            probs.append(prob)
            grads.append(grad_prob)
        grad_query = jnp.zeros(query.shape, jnp.float32)
        for (first, count), prob, grad_prob in zip(parts, probs, grads):
            cols = slice(first, first + count)
            grad_score = (prob * (grad_prob - delta)).astype(jnp.bfloat16)
            value_sum[:, cols] += dot(grad, prob.astype(jnp.bfloat16), 1, 1)
            key_sum[:, cols] += dot(query, grad_score, 1, 1)
            grad_query = grad_query + dot(key_cols[:, cols], grad_score, 1, 0)
        term = term + jnp.sum(
            grad_query * query.astype(jnp.float32), axis=1, keepdims=True
        )
        out_ref[0, :, pl.ds(at[i], size)] = (grad_query * scale_ref[...]).astype(jnp.bfloat16)
    for i in range(blocks):
        here = slice(i * size, (i + 1) * size)
        out_ref[1, :, pl.ds(at[i], size)] = key_sum[:, here].astype(jnp.bfloat16)
        out_ref[2, :, pl.ds(at[i], size)] = value_sum[:, here].astype(jnp.bfloat16)
    term_ref[0] = term


def attend_back(
    projected, grad_attended, log_total, multiplier, order, heads, head_dim, events=()
):
    tokens = projected.shape[1]
    blocks = order.shape[0]

    def part(first):
        return pl.BlockSpec((head_dim, tokens), lambda h, order, first=first: (first + h, 0))

    return pl.pallas_call(
        functools.partial(attend_back_kernel, blocks),
        out_shape=[
            jax.ShapeDtypeStruct((3, heads * head_dim, tokens), jnp.bfloat16),
            jax.ShapeDtypeStruct((heads, head_dim, 1), jnp.float32),
        ],
        grid_spec=pltpu.PrefetchScalarGridSpec(
            num_scalar_prefetch=1,
            grid=(heads,),
            in_specs=[
                part(0),
                part(heads),
                part(2 * heads),
                part(0),
                pl.BlockSpec((1, 1, tokens), lambda h, order: (h, 0, 0)),
                pl.BlockSpec((head_dim, 1), lambda h, order: (0, 0)),
            ]
            + [pl.BlockSpec(memory_space=pl.ANY)] * len(events),
            out_specs=[
                pl.BlockSpec((3, head_dim, tokens), lambda h, order: (0, h, 0)),
                pl.BlockSpec((1, head_dim, 1), lambda h, order: (h, 0, 0)),
            ],
            scratch_shapes=[
                pltpu.VMEM((tokens, head_dim), jnp.bfloat16),
                pltpu.VMEM((head_dim, tokens), jnp.bfloat16),
                pltpu.VMEM((tokens, head_dim), jnp.bfloat16),
                pltpu.VMEM((head_dim, tokens), jnp.float32),
                pltpu.VMEM((head_dim, tokens), jnp.float32),
            ],
        ),
        compiler_params=pltpu.CompilerParams(vmem_limit_bytes=48 * 1024 * 1024),
        cost_estimate=pl.CostEstimate(
            flops=heads * tokens * tokens * head_dim * 10,
            bytes_accessed=heads * head_dim * tokens * 14,
            transcendentals=heads * tokens * tokens,
        ),
        name="attend_back",
    )(order, projected, projected, projected, grad_attended, log_total, multiplier, *events)


def paired_layer(
    inputs,
    targets,
    valid_counts,
    owners,
    master,
    first_moment,
    second_moment,
    norm_gains,
    gain_first,
    gain_second,
    query_scale,
    scale_first,
    scale_second,
):
    bf16 = jnp.bfloat16
    f32 = jnp.float32
    seq_local, block_rows, width = inputs.shape
    slot_count, head_dim, column_count = master.shape
    ff_blocks = FF // head_dim
    owner_count = lax.axis_size("fsdp")
    device = lax.axis_index("ctx")
    chip, core = device // 2, device % 2
    owner_here = lax.axis_index("fsdp")
    low_here = owner_here % 2
    high_here = owner_here // 2
    high_count = owner_count // 2
    high_distances = range(1, high_count)
    half_width = width // 2
    half_slots = slot_count // 2
    half_rows = seq_local * block_rows
    half_heads = H // 2
    half_blocks = ff_blocks // 2
    set_units = 4 * half_heads + 2 * half_blocks
    first_chip, first_core = chip == 0, core == 0

    def columns_here(array):
        return jnp.where(first_chip, array, jnp.roll(array, half_width, axis=-1))

    def sequence_rows(array):
        own = jnp.where(first_chip, array[0], array[1])
        got = swapped(jnp.where(first_chip, array[1], array[0]), "ctx", 2)
        return jnp.where(
            first_chip, jnp.concatenate([own, got]), jnp.concatenate([got, own])
        )

    def rows_home(array):
        array = columns_here(array)
        first, last = array[:block_rows], array[block_rows:]
        own = jnp.where(first_chip, first, last)
        got = swapped(jnp.where(first_chip, last, first).astype(bf16), "ctx", 2).astype(f32)
        return jnp.where(first_chip, jnp.stack([own, got]), jnp.stack([got, own]))

    slot_rows = unit_rows(owners, slot_count)
    unit_total = owners.shape[0]
    kind_sizes = [H, H, H, H, ff_blocks, ff_blocks]
    kind_starts = [sum(kind_sizes[:i]) for i in range(6)]

    def unit_list(kinds, which):
        return jnp.concatenate(
            [
                kind_starts[k] + which * (kind_sizes[k] // 2) + jnp.arange(kind_sizes[k] // 2)
                for k in kinds
            ]
        ).astype(jnp.int32)

    wanted = jnp.concatenate(
        [unit_list(range(6), core), unit_list((4, 5), 1 - core)]
    )
    wanted_rows = slot_rows[wanted]
    wanted_owner, wanted_slot = wanted_rows // slot_count, wanted_rows % slot_count
    weight_from = 2 * (wanted_slot // half_slots != core) + (wanted_owner % 2 != low_here)
    weight_from = weight_from.astype(jnp.int32)
    weight_row = ((wanted_owner // 2) ^ high_here) * half_slots + wanted_slot % half_slots
    weight_sizes = [3 * half_heads, half_heads + 2 * half_blocks, 2 * half_blocks]

    lead = 256
    tail = half_width - 2 * lead
    shard = master.astype(bf16)
    own_half = jnp.where(first_core, shard[:half_slots], shard[half_slots:])
    got_half = swapped(jnp.where(first_core, shard[half_slots:], shard[:half_slots]), "ctx", 1)
    shard = jnp.where(
        first_core,
        jnp.concatenate([own_half, got_half], axis=2),
        jnp.concatenate([got_half, own_half], axis=2),
    )
    shard_last = shard[:, :, 2 * lead :]
    shards = [
        shard[:, :, :lead],
        shard[:, :, lead : 2 * lead],
        jnp.concatenate([shard_last, swapped(shard_last, "ctx", 2)], axis=2),
    ]
    values_b = columns_here(sequence_rows(inputs))
    targets_b = columns_here(sequence_rows(targets))
    qkv_pieces, rest_pieces, far_pieces = [], [], []
    events = [shards[2], values_b, targets_b]
    highs = [
        jnp.concatenate([part] + [swapped(part, "fsdp", 2 * d) for d in high_distances])
        for part in shards
    ]
    for number, part in enumerate(shards):
        size = part.shape[2]
        high = highs[number]
        low = swapped(high, "fsdp", 1)
        if number:
            low, far_pieces[-2] = together(low, far_pieces[-2])
            low, qkv_pieces[-1] = together(low, qkv_pieces[-1])
            events[0] = qkv_pieces[-1][0]
        if number < 2:
            low, highs[number + 1] = lax.optimization_barrier((low, highs[number + 1]))
        sources = [high, low, swapped(high, "ctx", 1), swapped(low, "ctx", 1)]
        qkv, rest, far = copy_rows(
            sources, [0] * 4, size, weight_from, weight_row, weight_sizes, events
        )
        if number == 2:
            for pieces, piece in ((qkv_pieces, qkv), (rest_pieces, rest), (far_pieces, far)):
                pieces.append((piece, 0, tail, 2 * lead))
                pieces.append((piece, tail, tail, half_width + 2 * lead))
            continue
        qkv_got = swapped(qkv, "ctx", 2)
        rest_got = swapped(rest, "ctx", 2)
        events = [qkv_got] if number == 0 else [qkv_got, rest_pieces[1][0]]
        far_got = swapped(rest_got, "ctx", 1)
        if number:
            events.append(far_pieces[1][0])
        start = number * lead
        qkv_pieces += [(qkv, 0, lead, start), (qkv_got, 0, lead, half_width + start)]
        rest_pieces += [(rest, 0, lead, start), (rest_got, 0, lead, half_width + start)]
        far_pieces += [(far, 0, lead, start), (far_got, 0, lead, half_width + start)]
    (w_qkv,) = place_pieces(
        [piece for piece, *_ in qkv_pieces],
        [(0, 3 * half_heads, *columns, 0, 0) for _, *columns in qkv_pieces],
        [(3 * half_heads, head_dim, width)],
    )
    (w_out,) = place_pieces(
        [piece for piece, *_ in rest_pieces],
        [(0, half_heads, *columns, 0, 0) for _, *columns in rest_pieces],
        [(half_heads, head_dim, width)],
    )
    mlp_pieces, mlp_places = [], []
    for row, pieces in ((0, rest_pieces), (half_blocks, far_pieces)):
        for piece, *columns in pieces:
            skipped = piece.shape[0] - 2 * half_blocks
            for kind in range(2):
                mlp_pieces.append(piece)
                mlp_places.append(
                    (skipped + kind * half_blocks, half_blocks, *columns, kind, row)
                )
    w_up, w_down = place_pieces(
        mlp_pieces, mlp_places, [(ff_blocks, head_dim, width)] * 2
    )
    w_qkv = w_qkv.reshape(-1, width)
    w_out = w_out.reshape(-1, width)
    w_up = w_up.reshape(-1, width)
    w_down = w_down.reshape(-1, width)

    gains = columns_here(norm_gains)
    values_in = values_b.astype(f32)
    normed_own = (values_in * inverse_rms(values_in) * gains[0]).astype(bf16)
    normed_b = jnp.concatenate([normed_own, swapped(normed_own, "ctx", 1)])
    base = score_base / math.sqrt(head_dim)
    multiplier = jax.nn.softplus(query_scale) * base
    row_scale = jnp.concatenate(
        [jnp.tile(multiplier, half_heads), jnp.ones((2 * half_heads * head_dim,), f32)]
    )
    projected = (dot(w_qkv, normed_b, 1, 1) * row_scale[:, None]).astype(bf16)
    positions = jnp.arange(4, dtype=jnp.int32)
    order = jnp.where(positions % 2 == core, 0, 2) + positions // 2
    order = order.astype(jnp.int32)
    attended, log_total = attend(projected, order, half_heads, head_dim)
    branch_far = dot(attended[:, half_rows:], w_out, 0, 0).astype(bf16)
    branch_got = swapped(branch_far, "ctx", 1)
    branch_own = dot(attended[:, :half_rows], w_out, 0, 0)
    middle = values_in + (branch_own + branch_got.astype(f32))
    normed_mid_b = (middle * inverse_rms(middle) * gains[1]).astype(bf16)
    hidden = dot(normed_mid_b, w_up, 1, 1)
    active_b = jax.nn.silu(hidden).astype(bf16)
    block_out = middle + dot(active_b, w_down, 1, 0)
    seq_length = 2 * half_rows
    row = jnp.arange(half_rows, dtype=jnp.int32)
    row_pos = (core + 2 * (row // block_rows)) * block_rows + row % block_rows
    valid = jnp.where(first_chip, valid_counts[0], valid_counts[1])
    counted = (row_pos >= seq_length - valid).astype(f32)
    count_term = jnp.sum(counted)

    out_grad = 2.0 * (block_out - targets_b.astype(f32)) * counted[:, None]
    out_grad_b = out_grad.astype(bf16)
    grad_active = dot(out_grad_b, w_down, 1, 1)
    sigma = jax.nn.sigmoid(hidden)
    grad_hidden_b = (grad_active * sigma * (1.0 + hidden * (1.0 - sigma))).astype(bf16)
    grad_normed_mid = dot(grad_hidden_b, w_up, 1, 0)
    inverse = inverse_rms(middle)
    scaled = grad_normed_mid * gains[1]
    grad_middle = out_grad + (
        inverse * scaled
        - middle * inverse**3 * jnp.mean(scaled * middle, axis=-1, keepdims=True)
    )
    grad_gain_two = jnp.sum(grad_normed_mid * middle * inverse, axis=0)
    grad_middle_own = grad_middle.astype(bf16)
    grad_middle_b = jnp.concatenate([grad_middle_own, swapped(grad_middle_own, "ctx", 1)])
    grad_attended = dot(w_out, grad_middle_b, 1, 1).astype(bf16)
    far_blocks = half_blocks * head_dim
    block_grads = []
    for left, right in ((grad_hidden_b, normed_mid_b), (active_b, out_grad_b)):
        got = swapped(dot(left[:, far_blocks:], right, 0, 0).astype(bf16), "ctx", 1)
        total = dot(left[:, :far_blocks], right, 0, 0) + got.astype(f32)
        block_grads.append(total.astype(bf16).reshape(half_blocks, head_dim, width))
    block_grads = jnp.concatenate(block_grads)
    far_lead = slice(half_width, half_width + 2 * lead)
    near_lead = slice(0, 2 * lead)

    def last_columns(array):
        return jnp.concatenate(
            [array[..., 2 * lead : half_width], array[..., half_width + 2 * lead :]], axis=-1
        )

    def with_chip(own, got):
        return (own.reshape(got.shape).astype(f32) + got.astype(f32)).astype(bf16)

    block_far = block_grads[:, :, far_lead]
    block_got = swapped(block_far, "ctx", 2)
    head_grads = dot(attended, grad_middle_b, 1, 0).astype(bf16)
    head_grads = head_grads.reshape(half_heads, head_dim, width)
    head_far = head_grads[:, :, far_lead]
    head_got = swapped(head_far, "ctx", 2)
    early_last = jnp.concatenate([last_columns(head_grads), last_columns(block_grads)])
    grad_proj, grad_scale = attend_back(
        projected,
        grad_attended,
        log_total,
        multiplier[:, None],
        order,
        half_heads,
        head_dim,
        [block_far, head_far, early_last],
    )
    grad_proj, block_got = lax.optimization_barrier((grad_proj, block_got))
    grad_proj = grad_proj.reshape(-1, grad_proj.shape[2])
    scale_term = (
        jnp.sum(grad_scale[:, :, 0], axis=0) / multiplier * base * jax.nn.sigmoid(query_scale)
    )

    low_order = jnp.stack([low_here, 1 - low_here])
    table_slots = (
        (2 * (jnp.arange(high_count) ^ high_here)[None, :, None] + low_order[:, None, None])
        * slot_count
        + core * half_slots
        + jnp.arange(half_slots)[None, None, :]
    ).reshape(-1)
    holds = table_slots[:, None] == slot_rows[None, :]
    unit_order = jnp.arange(unit_total, dtype=jnp.int32)
    slot_unit = jnp.sum(jnp.where(holds, unit_order[None, :] + 1, 0), axis=1) - 1
    kind = jnp.where(
        slot_unit < 4 * H, slot_unit // H, 4 + (slot_unit - 4 * H) // ff_blocks
    )
    kind_size = jnp.where(kind < 4, H, ff_blocks)
    within = jnp.where(kind < 4, slot_unit % H, (slot_unit - 4 * H) % ff_blocks)
    other_set = (within // (kind_size // 2) != core).astype(jnp.int32)
    rank = within % (kind_size // 2)
    early = (kind >= 3).astype(jnp.int32)
    grad_row = rank + jnp.where(
        kind <= 3, kind % 3 * half_heads, half_heads + (kind - 4) * half_blocks
    )
    empty = slot_unit < 0
    grad_from = jnp.where(empty, 4, 2 * early + other_set).astype(jnp.int32)
    grad_row = jnp.where(empty, 0, grad_row).astype(jnp.int32)
    zero = jnp.zeros((1, head_dim, lead), bf16)

    def at_peer(arrays):
        return [(array, swapped(array, "ctx", 1)) for array in arrays]

    def pick_table(pairs, offsets, events=()):
        return copy_rows(
            [part for pair in pairs for part in pair] + [zero],
            [offset for offset in offsets for _ in range(2)] + [0],
            lead,
            grad_from,
            grad_row,
            [high_count * half_slots] * 2,
            events,
        )

    def table_sums(keep, got):
        sums = []
        for d in range(high_count):
            rows = slice(d * half_slots, (d + 1) * half_slots)
            sums.append((keep[rows].astype(f32) + got[rows].astype(f32)).astype(bf16))
        return sums

    def from_owners(tables):
        return [swapped(tables[d], "fsdp", 2 * d) for d in high_distances]

    def owner_sum(table, got):
        total = table.astype(f32)
        for part in got:
            total = total + part.astype(f32)
        return total.astype(bf16)

    def proj_grad(columns):
        return dot(grad_proj, columns, 1, 0).astype(bf16).reshape(-1, head_dim, lead)

    proj_last = proj_grad(last_columns(normed_b))
    proj_got = [swapped(proj_grad(normed_b[:, half_width : half_width + lead]), "ctx", 2)]
    far_two = slice(half_width + lead, half_width + 2 * lead)
    proj_got.append(swapped(proj_grad(normed_b[:, far_two]), "ctx", 2))
    keep_last, send_last = pick_table(at_peer([proj_last, early_last]), [0, 0])
    low_last = swapped(send_last, "fsdp", 1)
    keep_last, grad_proj = lax.optimization_barrier((keep_last, grad_proj))
    low_last, proj_got[0], head_got = lax.optimization_barrier((low_last, proj_got[0], head_got))
    tables_last = table_sums(keep_last, low_last)
    high_last = from_owners(tables_last)
    early_pair = at_peer(
        [
            jnp.concatenate(
                [
                    with_chip(head_grads[:, :, near_lead], head_got),
                    with_chip(block_grads[:, :, near_lead], block_got),
                ]
            )
        ]
    )
    proj_near = [dot(grad_proj, normed_b[:, start : start + lead], 1, 0) for start in (0, lead)]
    pairs = at_peer([with_chip(proj_near[0], proj_got[0])]) + early_pair
    keep_one, send_one = pick_table(pairs, [0, 0], tables_last)
    keep_one, proj_got[1] = lax.optimization_barrier((keep_one, proj_got[1]))
    low_one = swapped(send_one, "fsdp", 1)
    low_one, high_last = lax.optimization_barrier((low_one, high_last))
    tables_one = table_sums(keep_one, low_one)
    high_one = from_owners(tables_one)
    pair_two = at_peer([with_chip(proj_near[1], proj_got[1])])

    normed_far = dot(grad_proj[:, half_rows:], w_qkv, 0, 0).astype(bf16)
    normed_got = swapped(normed_far, "ctx", 1)
    grad_normed_in = dot(grad_proj[:, :half_rows], w_qkv, 0, 0) + normed_got.astype(f32)
    inverse = inverse_rms(values_in)
    scaled = grad_normed_in * gains[0]
    input_grad = grad_middle + (
        inverse * scaled
        - values_in * inverse**3 * jnp.mean(scaled * values_in, axis=-1, keepdims=True)
    )
    grad_gain_one = jnp.sum(grad_normed_in * values_in * inverse, axis=0)

    gain_terms = columns_here(jnp.stack([grad_gain_one, grad_gain_two]))
    small = jnp.concatenate([gain_terms.reshape(-1), scale_term, count_term[None]])
    small = jnp.pad(small, (0, -small.shape[0] % 1024))
    keep_one, small = lax.optimization_barrier((keep_one, small))
    small = lax.psum(small, ("ctx", "fsdp"))
    keep_two, send_two = pick_table(
        pair_two + early_pair, [0, lead], tables_one + high_last + [small]
    )
    tables_two = table_sums(keep_two, swapped(send_two, "fsdp", 1))
    tables_two, high_one, block_out = lax.optimization_barrier((tables_two, high_one, block_out))
    high_two = from_owners(tables_two)
    owned_last = owner_sum(tables_last[0], high_last)
    owned_one = owner_sum(tables_one[0], high_one)
    owned_two = owner_sum(tables_two[0], high_two)
    gain_sums = small[: 2 * width].reshape(2, width)
    scale_sums = small[2 * width : 2 * width + head_dim]
    count = small[2 * width + head_dim]

    last_got = swapped(owned_last[:, :, tail:], "ctx", 2)
    owned_last = with_chip(owned_last[:, :, :tail], last_got)
    owned = jnp.concatenate([owned_one, owned_two, owned_last], axis=2).reshape(half_slots, head_dim, 2, column_count)
    kept = jnp.where(first_core, owned[:, :, 0], owned[:, :, 1])
    sent = swapped(jnp.where(first_core, owned[:, :, 1], owned[:, :, 0]), "ctx", 1)
    slot_sums = jnp.where(
        first_core, jnp.concatenate([kept, sent]), jnp.concatenate([sent, kept])
    ).astype(f32)
    new_master, new_first, new_second = adam_step(
        master, first_moment, second_moment, slot_sums / count, master_rate, decay_rate
    )
    new_gains, new_gain_first, new_gain_second = adam_step(
        norm_gains, gain_first, gain_second, gain_sums / count, gain_rate, 0.0
    )
    new_scale, new_scale_first, new_scale_second = adam_step(
        query_scale, scale_first, scale_second, scale_sums / count, scale_rate, 0.0
    )
    return (
        rows_home(block_out),
        rows_home(input_grad),
        new_master,
        new_first,
        new_second,
        new_gains,
        new_gain_first,
        new_gain_second,
        new_scale,
        new_scale_first,
        new_scale_second,
    )


def on_device(*arguments):
    paired = (
        lax.axis_size("ctx") == 4
        and lax.axis_size("fsdp") == 8
        and arguments[0].shape[0] == 2
    )
    return (paired_layer if paired else general_layer)(*arguments)


def solution(mesh):
    in_specs = (
        P("fsdp", "ctx", None),
        P("fsdp", "ctx", None),
        P("fsdp"),
        P(),
        P("fsdp", None, "ctx"),
        P("fsdp", None, "ctx"),
        P("fsdp", None, "ctx"),
        P(),
        P(),
        P(),
        P(),
        P(),
        P(),
    )
    out_specs = (
        P("fsdp", "ctx", None),
        P("fsdp", "ctx", None),
        P("fsdp", None, "ctx"),
        P("fsdp", None, "ctx"),
        P("fsdp", None, "ctx"),
        P(),
        P(),
        P(),
        P(),
        P(),
        P(),
    )
    return jax.shard_map(
        on_device, mesh=mesh, in_specs=in_specs, out_specs=out_specs, check_vma=False
    )
```

```python
import functools
import math

import jax
import jax.numpy as jnp
from jax import lax
from jax.experimental import pallas as pl
from jax.experimental.pallas import tpu as pltpu
from jax.sharding import PartitionSpec as P

H = 16
FF = 1280
STEP = 10


norm_eps = 1e-06
beta_first = 0.9
beta_second = 0.95
adam_eps = 1e-08
decay_rate = 0.1
master_rate = 0.05
gain_rate = 2.0
scale_rate = 2.0
score_base = 1.442695041
masked_score = -1e30


def from_behind(block, axis, distance):
    devices = range(lax.axis_size(axis))
    route = [(i - distance, i) for i in devices if i - distance in devices]
    return lax.ppermute(block, axis, route)


def shifted(array, axis, by):
    count = lax.axis_size(axis)
    return lax.ppermute(array, axis, [(i, (i + by) % count) for i in range(count)])


def unit_rows(owners, slot_count):
    unit_count = owners.shape[0]
    unit_order = jnp.arange(unit_count, dtype=jnp.int32)
    same_owner = owners[:, None] == owners[None, :]
    earlier = unit_order[None, :] < unit_order[:, None]
    slot_rank = jnp.sum((same_owner & earlier).astype(jnp.int32), axis=1)
    return owners * slot_count + slot_rank


def inverse_rms(values):
    return lax.rsqrt(jnp.mean(values * values, axis=-1, keepdims=True) + norm_eps)


def norm_back(values, gain, grad_normed):
    inverse = inverse_rms(values)
    scaled = grad_normed * gain
    grad_values = inverse * scaled - values * inverse**3 * jnp.mean(
        scaled * values, axis=-1, keepdims=True
    )
    grad_gain = jnp.sum(grad_normed * values * inverse, axis=(0, 1))
    return (grad_values, grad_gain)


def adam_step(values, moment_one, moment_two, gradient, step_rate, weight_decay):
    moment_one = beta_first * moment_one + (1.0 - beta_first) * gradient
    moment_two = beta_second * moment_two + (1.0 - beta_second) * gradient * gradient
    first_hat = moment_one / (1.0 - beta_first**STEP)
    second_hat = moment_two / (1.0 - beta_second**STEP)
    values = values - step_rate * (
        first_hat / (jnp.sqrt(second_hat) + adam_eps) + weight_decay * values
    )
    return (values, moment_one, moment_two)


def general_layer(
    inputs,
    targets,
    valid_counts,
    owners,
    master,
    first_moment,
    second_moment,
    norm_gains,
    gain_first,
    gain_second,
    query_scale,
    scale_first,
    scale_second,
):
    seq_local, block_rows, width = inputs.shape
    slot_count, head_dim, column_count = master.shape
    ff_blocks = FF // head_dim
    ctx_size = lax.axis_size("ctx")
    ctx_index = lax.axis_index("ctx")
    slot_rows = unit_rows(owners, slot_count)
    owner_table = lax.all_gather(master.astype(jnp.bfloat16), "fsdp", axis=0, tiled=True)
    picked = owner_table[slot_rows]
    weights = lax.all_gather(picked, "ctx", axis=2, tiled=True)
    w_qkv = weights[0 : 3 * H]
    w_out = weights[3 * H : 4 * H]
    w_up = weights[4 * H : 4 * H + ff_blocks]
    w_down = weights[4 * H + ff_blocks :]
    values_in = inputs.astype(jnp.float32)
    normed_b = (values_in * inverse_rms(values_in) * norm_gains[0]).astype(jnp.bfloat16)
    projected = jnp.einsum("sbd,hed->shbe", normed_b, w_qkv, preferred_element_type=jnp.float32)
    query_pre = projected[:, 0:H]
    multiplier = jax.nn.softplus(query_scale) * (score_base / math.sqrt(head_dim))
    query_b = (query_pre * multiplier).astype(jnp.bfloat16)
    key_b = projected[:, H : 2 * H].astype(jnp.bfloat16)
    value_b = projected[:, 2 * H : 3 * H].astype(jnp.bfloat16)
    query_rows = ctx_index * block_rows + jnp.arange(block_rows, dtype=jnp.int32)
    last_row = ctx_index * block_rows + block_rows - 1
    start_state = (
        jnp.full(query_pre.shape[:3], masked_score, jnp.float32),
        jnp.zeros(query_pre.shape[:3], jnp.float32),
        jnp.zeros(query_pre.shape, jnp.float32),
    )
    key_part = lax.all_gather(key_b, "ctx", axis=2, tiled=True)
    value_part = lax.all_gather(value_b, "ctx", axis=2, tiled=True)
    key_count = key_part.shape[2]

    def update(current):
        run_max, run_sum, accum = current
        key_rows = jnp.arange(key_count, dtype=jnp.int32)
        allowed = query_rows[:, None] >= key_rows[None, :]
        scores = jnp.einsum(
            "shqe,shke->shqk", query_b, key_part, preferred_element_type=jnp.float32
        )
        scores = jnp.where(allowed, scores, masked_score)
        new_max = jnp.maximum(run_max, jnp.max(scores, axis=-1))
        attn_probs = jnp.where(allowed, jnp.exp(scores - new_max[..., None]), 0.0)
        run_sum = jnp.sum(attn_probs, axis=-1)
        accum = jnp.einsum(
            "shqk,shke->shqe",
            attn_probs.astype(jnp.bfloat16),
            value_part,
            preferred_element_type=jnp.float32,
        )
        return (new_max, run_sum, accum)

    run_max, run_sum, accum = lax.cond(
        jnp.int32(0) <= last_row, update, lambda current: current, start_state
    )
    attended = accum / run_sum[..., None]
    log_total = run_max + jnp.log(run_sum)
    attended_b = attended.astype(jnp.bfloat16)
    branch = jnp.einsum("shbe,hed->sbd", attended_b, w_out, preferred_element_type=jnp.float32)
    middle = values_in + branch
    normed_mid_b = (middle * inverse_rms(middle) * norm_gains[1]).astype(jnp.bfloat16)
    hidden = jnp.einsum("sbd,fed->sbfe", normed_mid_b, w_up, preferred_element_type=jnp.float32)
    active_b = jax.nn.silu(hidden).astype(jnp.bfloat16)
    block_out = middle + jnp.einsum(
        "sbfe,fed->sbd", active_b, w_down, preferred_element_type=jnp.float32
    )
    seq_length = block_rows * ctx_size
    counted = (query_rows[None, :] >= (seq_length - valid_counts)[:, None]).astype(jnp.float32)
    count_term = jnp.sum(counted)
    out_grad = 2.0 * (block_out - targets.astype(jnp.float32)) * counted[..., None]
    out_grad_b = out_grad.astype(jnp.bfloat16)
    grad_down = jnp.einsum(
        "sbfe,sbd->fed", active_b, out_grad_b, preferred_element_type=jnp.float32
    )
    grad_active = jnp.einsum(
        "sbd,fed->sbfe", out_grad_b, w_down, preferred_element_type=jnp.float32
    )
    sigma = jax.nn.sigmoid(hidden)
    grad_hidden_b = (grad_active * sigma * (1.0 + hidden * (1.0 - sigma))).astype(jnp.bfloat16)
    grad_up = jnp.einsum(
        "sbfe,sbd->fed", grad_hidden_b, normed_mid_b, preferred_element_type=jnp.float32
    )
    grad_normed_mid = jnp.einsum(
        "sbfe,fed->sbd", grad_hidden_b, w_up, preferred_element_type=jnp.float32
    )
    grad_middle_norm, grad_gain_two = norm_back(middle, norm_gains[1], grad_normed_mid)
    grad_middle = out_grad + grad_middle_norm
    grad_middle_b = grad_middle.astype(jnp.bfloat16)
    grad_out = jnp.einsum(
        "shbe,sbd->hed", attended_b, grad_middle_b, preferred_element_type=jnp.float32
    )
    grad_attended_b = jnp.einsum(
        "sbd,hed->shbe", grad_middle_b, w_out, preferred_element_type=jnp.float32
    ).astype(jnp.bfloat16)
    delta = jnp.sum(grad_attended_b.astype(jnp.float32) * attended, axis=-1)

    def block_grads(source, key_cur, value_cur, partial_grads):
        grad_key, grad_value, grad_query = partial_grads
        key_rows = source * block_rows + jnp.arange(block_rows, dtype=jnp.int32)
        allowed = query_rows[:, None] >= key_rows[None, :]
        scores = jnp.einsum("shqe,shke->shqk", query_b, key_cur, preferred_element_type=jnp.float32)
        scores = jnp.where(allowed, scores, masked_score)
        attn_probs = jnp.exp(scores - log_total[..., None])
        grad_value = grad_value + jnp.einsum(
            "shqk,shqe->shke",
            attn_probs.astype(jnp.bfloat16),
            grad_attended_b,
            preferred_element_type=jnp.float32,
        )
        grad_probs = jnp.einsum(
            "shqe,shke->shqk", grad_attended_b, value_cur, preferred_element_type=jnp.float32
        )
        grad_scores_b = (attn_probs * (grad_probs - delta[..., None])).astype(jnp.bfloat16)
        grad_query = grad_query + jnp.einsum(
            "shqk,shke->shqe", grad_scores_b, key_cur, preferred_element_type=jnp.float32
        )
        grad_key = grad_key + jnp.einsum(
            "shqk,shqe->shke", grad_scores_b, query_b, preferred_element_type=jnp.float32
        )
        return (grad_key, grad_value, grad_query)

    zero_heads = jnp.zeros(query_pre.shape, jnp.float32)

    def back_turn(which_turn, current):
        key_cur, value_cur, grad_key, grad_value, grad_query = current
        source = (ctx_index - which_turn) % ctx_size
        grad_key, grad_value, grad_query = lax.cond(
            source <= ctx_index,
            lambda parts: block_grads(source, key_cur, value_cur, parts),
            lambda parts: parts,
            (grad_key, grad_value, grad_query),
        )
        key_cur, value_cur = from_behind((key_cur, value_cur), "ctx", 1)
        grad_key, grad_value = (
            shifted(grad_key.astype(jnp.bfloat16), "ctx", 1).astype(grad_key.dtype),
            shifted(grad_value.astype(jnp.bfloat16), "ctx", 1).astype(grad_value.dtype),
        )
        return (key_cur, value_cur, grad_key, grad_value, grad_query)

    back_state = (key_b, value_b, zero_heads, zero_heads, zero_heads)
    back_state = lax.fori_loop(0, ctx_size, back_turn, back_state)
    grad_key, grad_value, grad_query = (back_state[2], back_state[3], back_state[4])
    grad_proj_b = jnp.concatenate([grad_query * multiplier, grad_key, grad_value], axis=1).astype(
        jnp.bfloat16
    )
    grad_qkv = jnp.einsum(
        "shbe,sbd->hed", grad_proj_b, normed_b, preferred_element_type=jnp.float32
    )
    grad_normed_in = jnp.einsum(
        "shbe,hed->sbd", grad_proj_b, w_qkv, preferred_element_type=jnp.float32
    )
    grad_input_norm, grad_gain_one = norm_back(values_in, norm_gains[0], grad_normed_in)
    input_grad = grad_middle + grad_input_norm
    scale_term = (
        jnp.sum(grad_query * query_pre, axis=(0, 1, 2))
        * (score_base / math.sqrt(head_dim))
        * jax.nn.sigmoid(query_scale)
    )
    unit_grads = jnp.concatenate([grad_qkv, grad_out, grad_up, grad_down], axis=0)
    owner_total = lax.axis_size("fsdp") * slot_count
    table_grads = (
        jnp.zeros((owner_total, head_dim, width), jnp.float32).at[slot_rows].set(unit_grads)
    )
    owned = lax.psum_scatter(
        table_grads.astype(jnp.bfloat16), "fsdp", scatter_dimension=0, tiled=True
    )
    slot_sums = lax.psum_scatter(owned, "ctx", scatter_dimension=2, tiled=True).astype(jnp.float32)
    gain_sums, scale_sums, count = lax.psum(
        (jnp.stack([grad_gain_one, grad_gain_two]), scale_term, count_term), ("ctx", "fsdp")
    )
    new_master, new_first, new_second = adam_step(
        master, first_moment, second_moment, slot_sums / count, master_rate, decay_rate
    )
    new_gains, new_gain_first, new_gain_second = adam_step(
        norm_gains, gain_first, gain_second, gain_sums / count, gain_rate, 0.0
    )
    new_scale, new_scale_first, new_scale_second = adam_step(
        query_scale, scale_first, scale_second, scale_sums / count, scale_rate, 0.0
    )
    return (
        block_out,
        input_grad,
        new_master,
        new_first,
        new_second,
        new_gains,
        new_gain_first,
        new_gain_second,
        new_scale,
        new_scale_first,
        new_scale_second,
    )


def swapped(array, axis, distance):
    return lax.ppermute(
        array, axis, [(i, i ^ distance) for i in range(lax.axis_size(axis))]
    )


def summed(array, axis):
    size = lax.axis_size(axis)
    if size & (size - 1):
        return lax.psum(array, axis)
    distance = 1
    while distance < size:
        array = array + swapped(array, axis, distance)
        distance *= 2
    return array


def dot(left, right, left_dim, right_dim):
    return lax.dot_general(
        left,
        right,
        (((left_dim,), (right_dim,)), ((), ())),
        preferred_element_type=jnp.float32,
    )


def copy_rows_kernel(sizes, offsets, width, bound_ref, place_ref, row_ref, *refs):
    sources = refs[: len(offsets)]
    outs = refs[-2 - len(sizes) : -2]
    rows, sems = refs[-2:]
    for number, (source, offset) in enumerate(zip(sources, offsets)):

        @pl.loop(bound_ref[number], bound_ref[number + 1])
        def copy_row(i, source=source, offset=offset):
            pltpu.make_async_copy(
                source.at[row_ref[i], :, pl.ds(offset, width)],
                rows.at[place_ref[i]],
                sems.at[len(sizes)],
            ).start()

    pltpu.make_async_copy(rows, rows, sems.at[len(sizes)]).wait()
    copies, start = [], 0
    for place, (out, size) in enumerate(zip(outs, sizes)):
        copies.append(
            pltpu.make_async_copy(rows.at[pl.ds(start, size)], out, sems.at[place])
        )
        start += size
    for copy in copies:
        copy.start()
    for copy in copies:
        copy.wait()


def copy_plan(pick_from, pick_row, source_count):
    number = jnp.arange(pick_from.shape[0], dtype=jnp.int32)
    before = pick_from[None, :] < pick_from[:, None]
    same = (pick_from[None, :] == pick_from[:, None]) & (number[None, :] < number[:, None])
    rank = jnp.sum((before | same).astype(jnp.int32), axis=1)
    here = rank[None, :] == number[:, None]
    place = jnp.sum(jnp.where(here, number[None, :], 0), axis=1)
    row = jnp.sum(jnp.where(here, pick_row[None, :], 0), axis=1)
    bounds = jnp.sum(
        (pick_from[None, :] < jnp.arange(source_count + 1)[:, None]).astype(jnp.int32), axis=1
    )
    return (bounds.astype(jnp.int32), place.astype(jnp.int32), row.astype(jnp.int32))


def copy_rows(sources, offsets, width, plan, sizes, events=()):
    rows = sources[0].shape[1]
    total = sum(sizes)
    return pl.pallas_call(
        functools.partial(copy_rows_kernel, tuple(sizes), tuple(offsets), width),
        out_shape=[jax.ShapeDtypeStruct((size, rows, width), sources[0].dtype) for size in sizes],
        grid_spec=pltpu.PrefetchScalarGridSpec(
            num_scalar_prefetch=3,
            grid=(1,),
            in_specs=[pl.BlockSpec(memory_space=pl.ANY)] * (len(sources) + len(events)),
            out_specs=[pl.BlockSpec(memory_space=pl.ANY)] * len(sizes),
            scratch_shapes=[
                pltpu.VMEM((total, rows, width), sources[0].dtype),
                pltpu.SemaphoreType.DMA((len(sizes) + 1,)),
            ],
        ),
        compiler_params=pltpu.CompilerParams(vmem_limit_bytes=40 * 1024 * 1024),
        cost_estimate=pl.CostEstimate(flops=0, bytes_accessed=1024, transcendentals=0),
        name="copy_rows",
    )(*plan, *sources, *events)


def place_pieces_kernel(places, count_outs, *refs):
    pieces = refs[: len(places)]
    outs = refs[-1 - count_outs : -1]
    sems = refs[-1]
    copies = []
    for number, (piece, place) in enumerate(zip(pieces, places)):
        first, count, begin, size, column, out, row = place
        copies.append(
            pltpu.make_async_copy(
                piece.at[pl.ds(first, count), :, pl.ds(begin, size)],
                outs[out].at[pl.ds(row, count), :, pl.ds(column, size)],
                sems.at[number],
            )
        )
    for copy in copies:
        copy.start()
    for copy in copies:
        copy.wait()


def place_pieces(pieces, places, shapes, events=()):
    return pl.pallas_call(
        functools.partial(place_pieces_kernel, tuple(places), len(shapes)),
        out_shape=[jax.ShapeDtypeStruct(shape, pieces[0].dtype) for shape in shapes],
        in_specs=[pl.BlockSpec(memory_space=pl.ANY)] * (len(pieces) + len(events)),
        out_specs=[pl.BlockSpec(memory_space=pltpu.VMEM)] * len(shapes),
        scratch_shapes=[pltpu.SemaphoreType.DMA((len(pieces),))],
        compiler_params=pltpu.CompilerParams(vmem_limit_bytes=40 * 1024 * 1024),
        cost_estimate=pl.CostEstimate(flops=0, bytes_accessed=1024, transcendentals=0),
        name="place_pieces",
    )(*pieces, *events)


def attend_kernel(blocks, order_ref, q_ref, k_ref, v_ref, out_ref, log_ref, key_rows, value_cols):
    size = q_ref.shape[1] // blocks
    at = [pl.multiple_of(order_ref[i] * size, size) for i in range(blocks)]
    for i in range(blocks):
        key_rows[i * size : (i + 1) * size, :] = k_ref[:, pl.ds(at[i], size)].T
        value_cols[:, i * size : (i + 1) * size] = v_ref[:, pl.ds(at[i], size)]
    key_pos = lax.broadcasted_iota(jnp.int32, (size, size), 0)
    query_pos = lax.broadcasted_iota(jnp.int32, (size, size), 1)
    seen = key_pos <= query_pos
    for i in range(blocks):
        past = i * size
        query = q_ref[:, pl.ds(at[i], size)]
        near = jnp.where(
            seen, dot(key_rows[past : past + size, :], query, 1, 0), masked_score
        )
        top = jnp.max(near, axis=0, keepdims=True)
        if i:
            far = dot(key_rows[:past, :], query, 1, 0)
            top = jnp.maximum(top, jnp.max(far, axis=0, keepdims=True))
        near = jnp.exp(near - top)
        total = jnp.sum(near, axis=0, keepdims=True)
        value = dot(value_cols[:, past : past + size], near.astype(jnp.bfloat16), 1, 0)
        if i:
            far = jnp.exp(far - top)
            total = total + jnp.sum(far, axis=0, keepdims=True)
            value = value + dot(value_cols[:, :past], far.astype(jnp.bfloat16), 1, 0)
        out_ref[:, pl.ds(at[i], size)] = (value / total).astype(jnp.bfloat16)
        log_ref[0, :, pl.ds(at[i], size)] = top + jnp.log(total)


def attend(projected, order, heads, head_dim):
    tokens = projected.shape[1]
    blocks = order.shape[0]

    def part(first):
        return pl.BlockSpec((head_dim, tokens), lambda h, order, first=first: (first + h, 0))

    return pl.pallas_call(
        functools.partial(attend_kernel, blocks),
        out_shape=[
            jax.ShapeDtypeStruct((heads * head_dim, tokens), jnp.bfloat16),
            jax.ShapeDtypeStruct((heads, 1, tokens), jnp.float32),
        ],
        grid_spec=pltpu.PrefetchScalarGridSpec(
            num_scalar_prefetch=1,
            grid=(heads,),
            in_specs=[part(0), part(heads), part(2 * heads)],
            out_specs=[
                pl.BlockSpec((head_dim, tokens), lambda h, order: (h, 0)),
                pl.BlockSpec((1, 1, tokens), lambda h, order: (h, 0, 0)),
            ],
            scratch_shapes=[
                pltpu.VMEM((tokens, head_dim), jnp.bfloat16),
                pltpu.VMEM((head_dim, tokens), jnp.bfloat16),
            ],
        ),
        compiler_params=pltpu.CompilerParams(vmem_limit_bytes=40 * 1024 * 1024),
        cost_estimate=pl.CostEstimate(
            flops=heads * tokens * tokens * head_dim * 4,
            bytes_accessed=heads * head_dim * tokens * 8,
            transcendentals=heads * tokens * tokens,
        ),
        name="attend",
    )(order, projected, projected, projected)


def attend_back_kernel(
    blocks,
    order_ref,
    q_ref,
    k_ref,
    v_ref,
    grad_ref,
    log_ref,
    scale_ref,
    *refs,
):
    out_ref, term_ref, key_rows, key_cols, value_rows, key_sum, value_sum = refs[-7:]
    size = q_ref.shape[1] // blocks
    at = [pl.multiple_of(order_ref[i] * size, size) for i in range(blocks)]
    for i in range(blocks):
        here = slice(i * size, (i + 1) * size)
        key = k_ref[:, pl.ds(at[i], size)]
        key_rows[here, :] = key.T
        key_cols[:, here] = key
        value_rows[here, :] = v_ref[:, pl.ds(at[i], size)].T
    key_sum[...] = jnp.zeros_like(key_sum)
    value_sum[...] = jnp.zeros_like(value_sum)
    key_pos = lax.broadcasted_iota(jnp.int32, (size, size), 0)
    query_pos = lax.broadcasted_iota(jnp.int32, (size, size), 1)
    seen = key_pos <= query_pos
    term = jnp.zeros((q_ref.shape[0], 1), jnp.float32)
    for i in range(blocks):
        past = i * size
        query = q_ref[:, pl.ds(at[i], size)]
        grad = grad_ref[:, pl.ds(at[i], size)]
        log_total = log_ref[0, :, pl.ds(at[i], size)]
        parts = [(past, size)] + ([(0, past)] if i else [])
        probs, grads = [], []
        delta = jnp.zeros((1, size), jnp.float32)
        for first, count in parts:
            prob = jnp.exp(dot(key_rows[first : first + count, :], query, 1, 0) - log_total)
            if first == past:
                prob = jnp.where(seen, prob, 0.0)
            grad_prob = dot(value_rows[first : first + count, :], grad, 1, 0)
            delta = delta + jnp.sum(prob * grad_prob, axis=0, keepdims=True)
            probs.append(prob)
            grads.append(grad_prob)
        grad_query = jnp.zeros(query.shape, jnp.float32)
        for (first, count), prob, grad_prob in zip(parts, probs, grads):
            cols = slice(first, first + count)
            grad_score = (prob * (grad_prob - delta)).astype(jnp.bfloat16)
            value_sum[:, cols] += dot(grad, prob.astype(jnp.bfloat16), 1, 1)
            key_sum[:, cols] += dot(query, grad_score, 1, 1)
            grad_query = grad_query + dot(key_cols[:, cols], grad_score, 1, 0)
        term = term + jnp.sum(
            grad_query * query.astype(jnp.float32), axis=1, keepdims=True
        )
        out_ref[0, :, pl.ds(at[i], size)] = (grad_query * scale_ref[...]).astype(jnp.bfloat16)
    for i in range(blocks):
        here = slice(i * size, (i + 1) * size)
        out_ref[1, :, pl.ds(at[i], size)] = key_sum[:, here].astype(jnp.bfloat16)
        out_ref[2, :, pl.ds(at[i], size)] = value_sum[:, here].astype(jnp.bfloat16)
    term_ref[0] = term


def attend_back(
    projected, grad_attended, log_total, multiplier, order, heads, head_dim, events=()
):
    tokens = projected.shape[1]
    blocks = order.shape[0]

    def part(first):
        return pl.BlockSpec((head_dim, tokens), lambda h, order, first=first: (first + h, 0))

    return pl.pallas_call(
        functools.partial(attend_back_kernel, blocks),
        out_shape=[
            jax.ShapeDtypeStruct((3, heads * head_dim, tokens), jnp.bfloat16),
            jax.ShapeDtypeStruct((heads, head_dim, 1), jnp.float32),
        ],
        grid_spec=pltpu.PrefetchScalarGridSpec(
            num_scalar_prefetch=1,
            grid=(heads,),
            in_specs=[
                part(0),
                part(heads),
                part(2 * heads),
                part(0),
                pl.BlockSpec((1, 1, tokens), lambda h, order: (h, 0, 0)),
                pl.BlockSpec((head_dim, 1), lambda h, order: (0, 0)),
            ]
            + [pl.BlockSpec(memory_space=pl.ANY)] * len(events),
            out_specs=[
                pl.BlockSpec((3, head_dim, tokens), lambda h, order: (0, h, 0)),
                pl.BlockSpec((1, head_dim, 1), lambda h, order: (h, 0, 0)),
            ],
            scratch_shapes=[
                pltpu.VMEM((tokens, head_dim), jnp.bfloat16),
                pltpu.VMEM((head_dim, tokens), jnp.bfloat16),
                pltpu.VMEM((tokens, head_dim), jnp.bfloat16),
                pltpu.VMEM((head_dim, tokens), jnp.float32),
                pltpu.VMEM((head_dim, tokens), jnp.float32),
            ],
        ),
        compiler_params=pltpu.CompilerParams(vmem_limit_bytes=48 * 1024 * 1024),
        cost_estimate=pl.CostEstimate(
            flops=heads * tokens * tokens * head_dim * 10,
            bytes_accessed=heads * head_dim * tokens * 14,
            transcendentals=heads * tokens * tokens,
        ),
        name="attend_back",
    )(order, projected, projected, projected, grad_attended, log_total, multiplier, *events)


def paired_layer(
    inputs,
    targets,
    valid_counts,
    owners,
    master,
    first_moment,
    second_moment,
    norm_gains,
    gain_first,
    gain_second,
    query_scale,
    scale_first,
    scale_second,
):
    bf16 = jnp.bfloat16
    f32 = jnp.float32
    seq_local, block_rows, width = inputs.shape
    slot_count, head_dim, column_count = master.shape
    ff_blocks = FF // head_dim
    owner_count = lax.axis_size("fsdp")
    device = lax.axis_index("ctx")
    chip, core = device // 2, device % 2
    owner_here = lax.axis_index("fsdp")
    low_here = owner_here % 2
    high_here = owner_here // 2
    high_count = owner_count // 2
    high_distances = range(1, high_count)
    half_width = width // 2
    half_slots = slot_count // 2
    half_rows = seq_local * block_rows
    half_heads = H // 2
    half_blocks = ff_blocks // 2
    set_units = 4 * half_heads + 2 * half_blocks
    first_chip, first_core = chip == 0, core == 0

    def columns_here(array):
        return jnp.where(first_chip, array, jnp.roll(array, half_width, axis=-1))

    def sequence_rows(array):
        own = jnp.where(first_chip, array[0], array[1])
        got = swapped(jnp.where(first_chip, array[1], array[0]), "ctx", 2)
        return jnp.where(
            first_chip, jnp.concatenate([own, got]), jnp.concatenate([got, own])
        )

    def rows_home(array):
        array = columns_here(array)
        first, last = array[:block_rows], array[block_rows:]
        own = jnp.where(first_chip, first, last)
        got = swapped(jnp.where(first_chip, last, first).astype(bf16), "ctx", 2).astype(f32)
        return jnp.where(first_chip, jnp.stack([own, got]), jnp.stack([got, own]))

    slot_rows = unit_rows(owners, slot_count)
    unit_total = owners.shape[0]
    kind_sizes = [H, H, H, H, ff_blocks, ff_blocks]
    kind_starts = [sum(kind_sizes[:i]) for i in range(6)]

    def unit_list(kinds, which):
        return jnp.concatenate(
            [
                kind_starts[k] + which * (kind_sizes[k] // 2) + jnp.arange(kind_sizes[k] // 2)
                for k in kinds
            ]
        ).astype(jnp.int32)

    wanted = jnp.concatenate(
        [unit_list(range(6), core), unit_list((4, 5), 1 - core)]
    )
    wanted_rows = slot_rows[wanted]
    wanted_owner, wanted_slot = wanted_rows // slot_count, wanted_rows % slot_count
    weight_from = 2 * (wanted_slot // half_slots != core) + (wanted_owner % 2 != low_here)
    weight_from = weight_from.astype(jnp.int32)
    weight_row = ((wanted_owner // 2) ^ high_here) * half_slots + wanted_slot % half_slots
    weight_plan = copy_plan(weight_from, weight_row, 4)
    weight_sizes = [3 * half_heads, half_heads + 2 * half_blocks, 2 * half_blocks]

    lead = 256
    tail = half_width - 2 * lead
    shard = master.astype(bf16)
    own_half = jnp.where(first_core, shard[:half_slots], shard[half_slots:])
    got_half = swapped(jnp.where(first_core, shard[half_slots:], shard[:half_slots]), "ctx", 1)
    shard = jnp.where(
        first_core,
        jnp.concatenate([own_half, got_half], axis=2),
        jnp.concatenate([got_half, own_half], axis=2),
    )
    shard, inputs, targets = lax.optimization_barrier((shard, inputs, targets))
    values_b = columns_here(sequence_rows(inputs))
    targets_b = columns_here(sequence_rows(targets))
    shard_last = shard[:, :, 2 * lead :]
    shards = [
        shard[:, :, :lead],
        shard[:, :, lead : 2 * lead],
        jnp.concatenate([shard_last, swapped(shard_last, "ctx", 2)], axis=2),
    ]
    highs = []
    for number, part in enumerate(shards):
        if number:
            part, highs[-1] = lax.optimization_barrier((part, highs[-1]))
        highs.append(
            jnp.concatenate([part] + [swapped(part, "fsdp", 2 * d) for d in high_distances])
        )
    lows = [swapped(high, "fsdp", 1) for high in highs]
    own_units, rest_units = weight_sizes[0], weight_sizes[1]

    def pick_units(number, sizes, events):
        high, low = highs[number], lows[number]
        sources = [high, low, swapped(high, "ctx", 1), swapped(low, "ctx", 1)]
        return copy_rows(sources, [0] * 4, high.shape[2], weight_plan, sizes, events)

    lows[0], highs[1] = lax.optimization_barrier((lows[0], highs[1]))
    near_one, far_one = pick_units(
        0, [own_units + rest_units, weight_sizes[2]], [shards[2], values_b, targets_b]
    )
    got_one = swapped(near_one, "ctx", 2)
    lows[1], far_one, highs[2] = lax.optimization_barrier((lows[1], far_one, highs[2]))
    qkv_two, rest_two, far_two = pick_units(1, weight_sizes, [])
    qkv_got = swapped(qkv_two, "ctx", 2)
    rest_two, qkv_got = lax.optimization_barrier((rest_two, qkv_got))
    rest_got = swapped(rest_two, "ctx", 2)
    lows[2], far_two, got_one = lax.optimization_barrier((lows[2], far_two, got_one))
    qkv_last, rest_last, far_last = pick_units(2, weight_sizes, [qkv_got])
    far_got_one = swapped(got_one, "ctx", 1)
    far_got_two = swapped(rest_got, "ctx", 1)

    def columns_of(own_one, got_one, own_two, got_two, last):
        return [
            (own_one, 0, lead, 0),
            (own_two, 0, lead, lead),
            (last, 0, tail, 2 * lead),
            (got_one, 0, lead, half_width),
            (got_two, 0, lead, half_width + lead),
            (last, tail, tail, half_width + 2 * lead),
        ]

    qkv_pieces = columns_of(near_one, got_one, qkv_two, qkv_got, qkv_last)
    rest_pieces = columns_of(near_one, got_one, rest_two, rest_got, rest_last)
    far_pieces = columns_of(far_one, far_got_one, far_two, far_got_two, far_last)

    def placed(pieces, from_end, count, out, row):
        return [
            (piece.shape[0] - from_end if from_end else 0, count, *columns, out, row)
            for piece, *columns in pieces
        ]

    (w_qkv,) = place_pieces(
        [piece for piece, *_ in qkv_pieces],
        placed(qkv_pieces, 0, own_units, 0, 0),
        [(own_units, head_dim, width)],
    )
    w_qkv = w_qkv.reshape(-1, width)

    gains = columns_here(norm_gains)
    values_in = values_b.astype(f32)
    normed_own = (values_in * inverse_rms(values_in) * gains[0]).astype(bf16)
    normed_b = jnp.concatenate([normed_own, swapped(normed_own, "ctx", 1)])
    base = score_base / math.sqrt(head_dim)
    multiplier = jax.nn.softplus(query_scale) * base
    row_scale = jnp.concatenate(
        [jnp.tile(multiplier, half_heads), jnp.ones((2 * half_heads * head_dim,), f32)]
    )
    projected = (dot(w_qkv, normed_b, 1, 1) * row_scale[:, None]).astype(bf16)
    positions = jnp.arange(4, dtype=jnp.int32)
    order = jnp.where(positions % 2 == core, 0, 2) + positions // 2
    order = order.astype(jnp.int32)
    attended, log_total = attend(projected, order, half_heads, head_dim)
    (w_out,) = place_pieces(
        [piece for piece, *_ in rest_pieces],
        placed(rest_pieces, rest_units, half_heads, 0, 0),
        [(half_heads, head_dim, width)],
        [log_total],
    )
    mlp_pieces, mlp_places = [], []
    for row, pieces in ((0, rest_pieces), (half_blocks, far_pieces)):
        for kind in range(2):
            mlp_pieces += [piece for piece, *_ in pieces]
            mlp_places += placed(pieces, (2 - kind) * half_blocks, half_blocks, kind, row)
    w_up, w_down = place_pieces(
        mlp_pieces, mlp_places, [(ff_blocks, head_dim, width)] * 2, [log_total]
    )
    w_out = w_out.reshape(-1, width)
    w_up = w_up.reshape(-1, width)
    w_down = w_down.reshape(-1, width)
    branch_far = dot(attended[:, half_rows:], w_out, 0, 0).astype(bf16)
    branch_got = swapped(branch_far, "ctx", 1)
    branch_own = dot(attended[:, :half_rows], w_out, 0, 0)
    middle = values_in + (branch_own + branch_got.astype(f32))
    normed_mid_b = (middle * inverse_rms(middle) * gains[1]).astype(bf16)
    hidden = dot(normed_mid_b, w_up, 1, 1)
    active_b = jax.nn.silu(hidden).astype(bf16)
    block_out = middle + dot(active_b, w_down, 1, 0)
    seq_length = 2 * half_rows
    row = jnp.arange(half_rows, dtype=jnp.int32)
    row_pos = (core + 2 * (row // block_rows)) * block_rows + row % block_rows
    valid = jnp.where(first_chip, valid_counts[0], valid_counts[1])
    counted = (row_pos >= seq_length - valid).astype(f32)
    count = summed(jnp.sum(valid_counts)[None], "fsdp")

    out_grad = 2.0 * (block_out - targets_b.astype(f32)) * counted[:, None]
    out_grad_b = out_grad.astype(bf16)
    grad_active = dot(out_grad_b, w_down, 1, 1)
    sigma = jax.nn.sigmoid(hidden)
    grad_hidden_b = (grad_active * sigma * (1.0 + hidden * (1.0 - sigma))).astype(bf16)
    grad_normed_mid = dot(grad_hidden_b, w_up, 1, 0)
    inverse = inverse_rms(middle)
    scaled = grad_normed_mid * gains[1]
    grad_middle = out_grad + (
        inverse * scaled
        - middle * inverse**3 * jnp.mean(scaled * middle, axis=-1, keepdims=True)
    )
    grad_gain_two = jnp.sum(grad_normed_mid * middle * inverse, axis=0)
    grad_middle_own = grad_middle.astype(bf16)
    grad_middle_b = jnp.concatenate([grad_middle_own, swapped(grad_middle_own, "ctx", 1)])
    grad_attended = dot(w_out, grad_middle_b, 1, 1).astype(bf16)
    far_blocks = half_blocks * head_dim
    block_grads = []
    for left, right in ((grad_hidden_b, normed_mid_b), (active_b, out_grad_b)):
        got = swapped(dot(left[:, far_blocks:], right, 0, 0).astype(bf16), "ctx", 1)
        total = dot(left[:, :far_blocks], right, 0, 0) + got.astype(f32)
        block_grads.append(total.astype(bf16).reshape(half_blocks, head_dim, width))
    block_grads = jnp.concatenate(block_grads)
    far_lead = slice(half_width, half_width + 2 * lead)
    near_lead = slice(0, 2 * lead)

    def last_columns(array):
        return jnp.concatenate(
            [array[..., 2 * lead : half_width], array[..., half_width + 2 * lead :]], axis=-1
        )

    def with_chip(own, got):
        return (own.reshape(got.shape).astype(f32) + got.astype(f32)).astype(bf16)

    block_far = block_grads[:, :, far_lead]
    block_got = swapped(block_far, "ctx", 2)
    head_grads = dot(attended, grad_middle_b, 1, 0).astype(bf16)
    head_grads = head_grads.reshape(half_heads, head_dim, width)
    head_far = head_grads[:, :, far_lead]
    head_got = swapped(head_far, "ctx", 2)
    early_last = jnp.concatenate([last_columns(head_grads), last_columns(block_grads)])
    grad_proj, grad_scale = attend_back(
        projected,
        grad_attended,
        log_total,
        multiplier[:, None],
        order,
        half_heads,
        head_dim,
        [block_far, head_far, early_last, count],
    )
    grad_proj = grad_proj.reshape(-1, grad_proj.shape[2])
    scale_term = (
        jnp.sum(grad_scale[:, :, 0], axis=0) / multiplier * base * jax.nn.sigmoid(query_scale)
    )

    low_order = jnp.stack([low_here, 1 - low_here])
    table_slots = (
        (2 * (jnp.arange(high_count) ^ high_here)[None, :, None] + low_order[:, None, None])
        * slot_count
        + core * half_slots
        + jnp.arange(half_slots)[None, None, :]
    ).reshape(-1)
    holds = table_slots[:, None] == slot_rows[None, :]
    unit_order = jnp.arange(unit_total, dtype=jnp.int32)
    slot_unit = jnp.sum(jnp.where(holds, unit_order[None, :] + 1, 0), axis=1) - 1
    kind = jnp.where(
        slot_unit < 4 * H, slot_unit // H, 4 + (slot_unit - 4 * H) // ff_blocks
    )
    kind_size = jnp.where(kind < 4, H, ff_blocks)
    within = jnp.where(kind < 4, slot_unit % H, (slot_unit - 4 * H) % ff_blocks)
    other_set = (within // (kind_size // 2) != core).astype(jnp.int32)
    rank = within % (kind_size // 2)
    early = (kind >= 3).astype(jnp.int32)
    grad_row = rank + jnp.where(
        kind <= 3, kind % 3 * half_heads, half_heads + (kind - 4) * half_blocks
    )
    empty = slot_unit < 0
    grad_from = jnp.where(empty, 4, 2 * early + other_set).astype(jnp.int32)
    grad_row = jnp.where(empty, 0, grad_row).astype(jnp.int32)
    grad_plan = copy_plan(grad_from, grad_row, 5)
    zero = jnp.zeros((1, head_dim, lead), bf16)

    def at_peer(arrays):
        return [(array, swapped(array, "ctx", 1)) for array in arrays]

    def pick_table(pairs, offsets, events=()):
        return copy_rows(
            [part for pair in pairs for part in pair] + [zero],
            [offset for offset in offsets for _ in range(2)] + [0],
            lead,
            grad_plan,
            [high_count * half_slots] * 2,
            events,
        )

    def table_sums(keep, got):
        sums = []
        for d in range(high_count):
            rows = slice(d * half_slots, (d + 1) * half_slots)
            sums.append((keep[rows].astype(f32) + got[rows].astype(f32)).astype(bf16))
        return sums

    def from_owners(tables):
        return [swapped(tables[d], "fsdp", 2 * d) for d in high_distances]

    def owner_sum(table, got):
        total = table.astype(f32)
        for part in got:
            total = total + part.astype(f32)
        return total.astype(bf16)

    def proj_grad(columns):
        return dot(grad_proj, columns, 1, 0).astype(bf16).reshape(-1, head_dim, lead)

    proj_last = proj_grad(last_columns(normed_b))
    proj_last, block_got = lax.optimization_barrier((proj_last, block_got))
    proj_got = [swapped(proj_grad(normed_b[:, half_width : half_width + lead]), "ctx", 2)]
    far_two = slice(half_width + lead, half_width + 2 * lead)
    proj_got.append(swapped(proj_grad(normed_b[:, far_two]), "ctx", 2))
    keep_last, send_last = pick_table(at_peer([proj_last, early_last]), [0, 0])
    low_last = swapped(send_last, "fsdp", 1)
    keep_last, grad_proj = lax.optimization_barrier((keep_last, grad_proj))
    low_last, proj_got[0], head_got = lax.optimization_barrier((low_last, proj_got[0], head_got))
    tables_last = table_sums(keep_last, low_last)
    high_last = from_owners(tables_last)
    early_pair = at_peer(
        [
            jnp.concatenate(
                [
                    with_chip(head_grads[:, :, near_lead], head_got),
                    with_chip(block_grads[:, :, near_lead], block_got),
                ]
            )
        ]
    )
    proj_near = [dot(grad_proj, normed_b[:, start : start + lead], 1, 0) for start in (0, lead)]
    pairs = at_peer([with_chip(proj_near[0], proj_got[0])]) + early_pair
    keep_one, send_one = pick_table(pairs, [0, 0], tables_last)
    keep_one, proj_got[1] = lax.optimization_barrier((keep_one, proj_got[1]))
    low_one = swapped(send_one, "fsdp", 1)
    low_one, high_last = lax.optimization_barrier((low_one, high_last))
    tables_one = table_sums(keep_one, low_one)
    high_one = from_owners(tables_one)
    pair_two = at_peer([with_chip(proj_near[1], proj_got[1])])

    normed_far = dot(grad_proj[:, half_rows:], w_qkv, 0, 0).astype(bf16)
    normed_got = swapped(normed_far, "ctx", 1)
    grad_normed_in = dot(grad_proj[:, :half_rows], w_qkv, 0, 0) + normed_got.astype(f32)
    inverse = inverse_rms(values_in)
    scaled = grad_normed_in * gains[0]
    input_grad = grad_middle + (
        inverse * scaled
        - values_in * inverse**3 * jnp.mean(scaled * values_in, axis=-1, keepdims=True)
    )
    grad_gain_one = jnp.sum(grad_normed_in * values_in * inverse, axis=0)

    gain_terms = columns_here(jnp.stack([grad_gain_one, grad_gain_two]))
    small = jnp.concatenate([gain_terms.reshape(-1), scale_term])
    small = jnp.pad(small, (0, -small.shape[0] % 1024))
    keep_two, send_two = pick_table(
        pair_two + early_pair, [0, lead], tables_one + high_last
    )
    keep_two, small = lax.optimization_barrier((keep_two, small))
    tables_two = table_sums(keep_two, swapped(send_two, "fsdp", 1))
    small = small + swapped(small, "fsdp", 1)
    tables_two, high_one, block_out, small = lax.optimization_barrier(
        (tables_two, high_one, block_out, small)
    )
    high_two = from_owners(tables_two)
    small_got = from_owners([small] * high_count)
    high_two, small_got = lax.optimization_barrier((high_two, small_got))
    owned_last = owner_sum(tables_last[0], high_last)
    owned_one = owner_sum(tables_one[0], high_one)
    owned_two = owner_sum(tables_two[0], high_two)
    small = summed((small + small_got[0]) + (small_got[1] + small_got[2]), "ctx")
    gain_sums = small[: 2 * width].reshape(2, width)
    scale_sums = small[2 * width : 2 * width + head_dim]

    count = count[0].astype(f32)
    last_got = swapped(owned_last[:, :, tail:], "ctx", 2)
    owned_last = with_chip(owned_last[:, :, :tail], last_got)
    owned = jnp.concatenate([owned_one, owned_two, owned_last], axis=2).reshape(half_slots, head_dim, 2, column_count)
    kept = jnp.where(first_core, owned[:, :, 0], owned[:, :, 1])
    sent = swapped(jnp.where(first_core, owned[:, :, 1], owned[:, :, 0]), "ctx", 1)
    slot_sums = jnp.where(
        first_core, jnp.concatenate([kept, sent]), jnp.concatenate([sent, kept])
    ).astype(f32)
    new_master, new_first, new_second = adam_step(
        master, first_moment, second_moment, slot_sums / count, master_rate, decay_rate
    )
    new_gains, new_gain_first, new_gain_second = adam_step(
        norm_gains, gain_first, gain_second, gain_sums / count, gain_rate, 0.0
    )
    new_scale, new_scale_first, new_scale_second = adam_step(
        query_scale, scale_first, scale_second, scale_sums / count, scale_rate, 0.0
    )
    return (
        rows_home(block_out),
        rows_home(input_grad),
        new_master,
        new_first,
        new_second,
        new_gains,
        new_gain_first,
        new_gain_second,
        new_scale,
        new_scale_first,
        new_scale_second,
    )


def on_device(*arguments):
    paired = (
        lax.axis_size("ctx") == 4
        and lax.axis_size("fsdp") == 8
        and arguments[0].shape[0] == 2
    )
    return (paired_layer if paired else general_layer)(*arguments)


def solution(mesh):
    in_specs = (
        P("fsdp", "ctx", None),
        P("fsdp", "ctx", None),
        P("fsdp"),
        P(),
        P("fsdp", None, "ctx"),
        P("fsdp", None, "ctx"),
        P("fsdp", None, "ctx"),
        P(),
        P(),
        P(),
        P(),
        P(),
        P(),
    )
    out_specs = (
        P("fsdp", "ctx", None),
        P("fsdp", "ctx", None),
        P("fsdp", None, "ctx"),
        P("fsdp", None, "ctx"),
        P("fsdp", None, "ctx"),
        P(),
        P(),
        P(),
        P(),
        P(),
        P(),
    )
    return jax.shard_map(
        on_device, mesh=mesh, in_specs=in_specs, out_specs=out_specs, check_vma=False
    )
```

```python
import functools
import math

import jax
import jax.numpy as jnp
from jax import lax
from jax.experimental import pallas as pl
from jax.experimental.pallas import tpu as pltpu
from jax.sharding import PartitionSpec as P

H = 16
FF = 1280
STEP = 10


norm_eps = 1e-06
beta_first = 0.9
beta_second = 0.95
adam_eps = 1e-08
decay_rate = 0.1
master_rate = 0.05
gain_rate = 2.0
scale_rate = 2.0
score_base = 1.442695041
masked_score = -1e30


def from_behind(block, axis, distance):
    devices = range(lax.axis_size(axis))
    route = [(i - distance, i) for i in devices if i - distance in devices]
    return lax.ppermute(block, axis, route)


def shifted(array, axis, by):
    count = lax.axis_size(axis)
    return lax.ppermute(array, axis, [(i, (i + by) % count) for i in range(count)])


def unit_rows(owners, slot_count):
    unit_count = owners.shape[0]
    unit_order = jnp.arange(unit_count, dtype=jnp.int32)
    same_owner = owners[:, None] == owners[None, :]
    earlier = unit_order[None, :] < unit_order[:, None]
    slot_rank = jnp.sum((same_owner & earlier).astype(jnp.int32), axis=1)
    return owners * slot_count + slot_rank


def inverse_rms(values):
    return lax.rsqrt(jnp.mean(values * values, axis=-1, keepdims=True) + norm_eps)


def norm_back(values, gain, grad_normed):
    inverse = inverse_rms(values)
    scaled = grad_normed * gain
    grad_values = inverse * scaled - values * inverse**3 * jnp.mean(
        scaled * values, axis=-1, keepdims=True
    )
    grad_gain = jnp.sum(grad_normed * values * inverse, axis=(0, 1))
    return (grad_values, grad_gain)


def adam_step(values, moment_one, moment_two, gradient, step_rate, weight_decay):
    moment_one = beta_first * moment_one + (1.0 - beta_first) * gradient
    moment_two = beta_second * moment_two + (1.0 - beta_second) * gradient * gradient
    first_hat = moment_one / (1.0 - beta_first**STEP)
    second_hat = moment_two / (1.0 - beta_second**STEP)
    values = values - step_rate * (
        first_hat / (jnp.sqrt(second_hat) + adam_eps) + weight_decay * values
    )
    return (values, moment_one, moment_two)


def general_layer(
    inputs,
    targets,
    valid_counts,
    owners,
    master,
    first_moment,
    second_moment,
    norm_gains,
    gain_first,
    gain_second,
    query_scale,
    scale_first,
    scale_second,
):
    seq_local, block_rows, width = inputs.shape
    slot_count, head_dim, column_count = master.shape
    ff_blocks = FF // head_dim
    ctx_size = lax.axis_size("ctx")
    ctx_index = lax.axis_index("ctx")
    slot_rows = unit_rows(owners, slot_count)
    owner_table = lax.all_gather(master.astype(jnp.bfloat16), "fsdp", axis=0, tiled=True)
    picked = owner_table[slot_rows]
    weights = lax.all_gather(picked, "ctx", axis=2, tiled=True)
    w_qkv = weights[0 : 3 * H]
    w_out = weights[3 * H : 4 * H]
    w_up = weights[4 * H : 4 * H + ff_blocks]
    w_down = weights[4 * H + ff_blocks :]
    values_in = inputs.astype(jnp.float32)
    normed_b = (values_in * inverse_rms(values_in) * norm_gains[0]).astype(jnp.bfloat16)
    projected = jnp.einsum("sbd,hed->shbe", normed_b, w_qkv, preferred_element_type=jnp.float32)
    query_pre = projected[:, 0:H]
    multiplier = jax.nn.softplus(query_scale) * (score_base / math.sqrt(head_dim))
    query_b = (query_pre * multiplier).astype(jnp.bfloat16)
    key_b = projected[:, H : 2 * H].astype(jnp.bfloat16)
    value_b = projected[:, 2 * H : 3 * H].astype(jnp.bfloat16)
    query_rows = ctx_index * block_rows + jnp.arange(block_rows, dtype=jnp.int32)
    last_row = ctx_index * block_rows + block_rows - 1
    start_state = (
        jnp.full(query_pre.shape[:3], masked_score, jnp.float32),
        jnp.zeros(query_pre.shape[:3], jnp.float32),
        jnp.zeros(query_pre.shape, jnp.float32),
    )
    key_part = lax.all_gather(key_b, "ctx", axis=2, tiled=True)
    value_part = lax.all_gather(value_b, "ctx", axis=2, tiled=True)
    key_count = key_part.shape[2]

    def update(current):
        run_max, run_sum, accum = current
        key_rows = jnp.arange(key_count, dtype=jnp.int32)
        allowed = query_rows[:, None] >= key_rows[None, :]
        scores = jnp.einsum(
            "shqe,shke->shqk", query_b, key_part, preferred_element_type=jnp.float32
        )
        scores = jnp.where(allowed, scores, masked_score)
        new_max = jnp.maximum(run_max, jnp.max(scores, axis=-1))
        attn_probs = jnp.where(allowed, jnp.exp(scores - new_max[..., None]), 0.0)
        run_sum = jnp.sum(attn_probs, axis=-1)
        accum = jnp.einsum(
            "shqk,shke->shqe",
            attn_probs.astype(jnp.bfloat16),
            value_part,
            preferred_element_type=jnp.float32,
        )
        return (new_max, run_sum, accum)

    run_max, run_sum, accum = lax.cond(
        jnp.int32(0) <= last_row, update, lambda current: current, start_state
    )
    attended = accum / run_sum[..., None]
    log_total = run_max + jnp.log(run_sum)
    attended_b = attended.astype(jnp.bfloat16)
    branch = jnp.einsum("shbe,hed->sbd", attended_b, w_out, preferred_element_type=jnp.float32)
    middle = values_in + branch
    normed_mid_b = (middle * inverse_rms(middle) * norm_gains[1]).astype(jnp.bfloat16)
    hidden = jnp.einsum("sbd,fed->sbfe", normed_mid_b, w_up, preferred_element_type=jnp.float32)
    active_b = jax.nn.silu(hidden).astype(jnp.bfloat16)
    block_out = middle + jnp.einsum(
        "sbfe,fed->sbd", active_b, w_down, preferred_element_type=jnp.float32
    )
    seq_length = block_rows * ctx_size
    counted = (query_rows[None, :] >= (seq_length - valid_counts)[:, None]).astype(jnp.float32)
    count_term = jnp.sum(counted)
    out_grad = 2.0 * (block_out - targets.astype(jnp.float32)) * counted[..., None]
    out_grad_b = out_grad.astype(jnp.bfloat16)
    grad_down = jnp.einsum(
        "sbfe,sbd->fed", active_b, out_grad_b, preferred_element_type=jnp.float32
    )
    grad_active = jnp.einsum(
        "sbd,fed->sbfe", out_grad_b, w_down, preferred_element_type=jnp.float32
    )
    sigma = jax.nn.sigmoid(hidden)
    grad_hidden_b = (grad_active * sigma * (1.0 + hidden * (1.0 - sigma))).astype(jnp.bfloat16)
    grad_up = jnp.einsum(
        "sbfe,sbd->fed", grad_hidden_b, normed_mid_b, preferred_element_type=jnp.float32
    )
    grad_normed_mid = jnp.einsum(
        "sbfe,fed->sbd", grad_hidden_b, w_up, preferred_element_type=jnp.float32
    )
    grad_middle_norm, grad_gain_two = norm_back(middle, norm_gains[1], grad_normed_mid)
    grad_middle = out_grad + grad_middle_norm
    grad_middle_b = grad_middle.astype(jnp.bfloat16)
    grad_out = jnp.einsum(
        "shbe,sbd->hed", attended_b, grad_middle_b, preferred_element_type=jnp.float32
    )
    grad_attended_b = jnp.einsum(
        "sbd,hed->shbe", grad_middle_b, w_out, preferred_element_type=jnp.float32
    ).astype(jnp.bfloat16)
    delta = jnp.sum(grad_attended_b.astype(jnp.float32) * attended, axis=-1)

    def block_grads(source, key_cur, value_cur, partial_grads):
        grad_key, grad_value, grad_query = partial_grads
        key_rows = source * block_rows + jnp.arange(block_rows, dtype=jnp.int32)
        allowed = query_rows[:, None] >= key_rows[None, :]
        scores = jnp.einsum("shqe,shke->shqk", query_b, key_cur, preferred_element_type=jnp.float32)
        scores = jnp.where(allowed, scores, masked_score)
        attn_probs = jnp.exp(scores - log_total[..., None])
        grad_value = grad_value + jnp.einsum(
            "shqk,shqe->shke",
            attn_probs.astype(jnp.bfloat16),
            grad_attended_b,
            preferred_element_type=jnp.float32,
        )
        grad_probs = jnp.einsum(
            "shqe,shke->shqk", grad_attended_b, value_cur, preferred_element_type=jnp.float32
        )
        grad_scores_b = (attn_probs * (grad_probs - delta[..., None])).astype(jnp.bfloat16)
        grad_query = grad_query + jnp.einsum(
            "shqk,shke->shqe", grad_scores_b, key_cur, preferred_element_type=jnp.float32
        )
        grad_key = grad_key + jnp.einsum(
            "shqk,shqe->shke", grad_scores_b, query_b, preferred_element_type=jnp.float32
        )
        return (grad_key, grad_value, grad_query)

    zero_heads = jnp.zeros(query_pre.shape, jnp.float32)

    def back_turn(which_turn, current):
        key_cur, value_cur, grad_key, grad_value, grad_query = current
        source = (ctx_index - which_turn) % ctx_size
        grad_key, grad_value, grad_query = lax.cond(
            source <= ctx_index,
            lambda parts: block_grads(source, key_cur, value_cur, parts),
            lambda parts: parts,
            (grad_key, grad_value, grad_query),
        )
        key_cur, value_cur = from_behind((key_cur, value_cur), "ctx", 1)
        grad_key, grad_value = (
            shifted(grad_key.astype(jnp.bfloat16), "ctx", 1).astype(grad_key.dtype),
            shifted(grad_value.astype(jnp.bfloat16), "ctx", 1).astype(grad_value.dtype),
        )
        return (key_cur, value_cur, grad_key, grad_value, grad_query)

    back_state = (key_b, value_b, zero_heads, zero_heads, zero_heads)
    back_state = lax.fori_loop(0, ctx_size, back_turn, back_state)
    grad_key, grad_value, grad_query = (back_state[2], back_state[3], back_state[4])
    grad_proj_b = jnp.concatenate([grad_query * multiplier, grad_key, grad_value], axis=1).astype(
        jnp.bfloat16
    )
    grad_qkv = jnp.einsum(
        "shbe,sbd->hed", grad_proj_b, normed_b, preferred_element_type=jnp.float32
    )
    grad_normed_in = jnp.einsum(
        "shbe,hed->sbd", grad_proj_b, w_qkv, preferred_element_type=jnp.float32
    )
    grad_input_norm, grad_gain_one = norm_back(values_in, norm_gains[0], grad_normed_in)
    input_grad = grad_middle + grad_input_norm
    scale_term = (
        jnp.sum(grad_query * query_pre, axis=(0, 1, 2))
        * (score_base / math.sqrt(head_dim))
        * jax.nn.sigmoid(query_scale)
    )
    unit_grads = jnp.concatenate([grad_qkv, grad_out, grad_up, grad_down], axis=0)
    owner_total = lax.axis_size("fsdp") * slot_count
    table_grads = (
        jnp.zeros((owner_total, head_dim, width), jnp.float32).at[slot_rows].set(unit_grads)
    )
    owned = lax.psum_scatter(
        table_grads.astype(jnp.bfloat16), "fsdp", scatter_dimension=0, tiled=True
    )
    slot_sums = lax.psum_scatter(owned, "ctx", scatter_dimension=2, tiled=True).astype(jnp.float32)
    gain_sums, scale_sums, count = lax.psum(
        (jnp.stack([grad_gain_one, grad_gain_two]), scale_term, count_term), ("ctx", "fsdp")
    )
    new_master, new_first, new_second = adam_step(
        master, first_moment, second_moment, slot_sums / count, master_rate, decay_rate
    )
    new_gains, new_gain_first, new_gain_second = adam_step(
        norm_gains, gain_first, gain_second, gain_sums / count, gain_rate, 0.0
    )
    new_scale, new_scale_first, new_scale_second = adam_step(
        query_scale, scale_first, scale_second, scale_sums / count, scale_rate, 0.0
    )
    return (
        block_out,
        input_grad,
        new_master,
        new_first,
        new_second,
        new_gains,
        new_gain_first,
        new_gain_second,
        new_scale,
        new_scale_first,
        new_scale_second,
    )


def swapped(array, axis, distance):
    return lax.ppermute(
        array, axis, [(i, i ^ distance) for i in range(lax.axis_size(axis))]
    )


def summed(array, axis):
    size = lax.axis_size(axis)
    if size & (size - 1):
        return lax.psum(array, axis)
    distance = 1
    while distance < size:
        array = array + swapped(array, axis, distance)
        distance *= 2
    return array


def dot(left, right, left_dim, right_dim):
    return lax.dot_general(
        left,
        right,
        (((left_dim,), (right_dim,)), ((), ())),
        preferred_element_type=jnp.float32,
    )


def copy_rows_kernel(sizes, offsets, width, bound_ref, place_ref, row_ref, *refs):
    sources = refs[: len(offsets)]
    outs = refs[-2 - len(sizes) : -2]
    rows, sems = refs[-2:]
    for number, (source, offset) in enumerate(zip(sources, offsets)):

        @pl.loop(bound_ref[number], bound_ref[number + 1])
        def copy_row(i, source=source, offset=offset):
            pltpu.make_async_copy(
                source.at[row_ref[i], :, pl.ds(offset, width)],
                rows.at[place_ref[i]],
                sems.at[len(sizes)],
            ).start()

    pltpu.make_async_copy(rows, rows, sems.at[len(sizes)]).wait()
    copies, start = [], 0
    for place, (out, size) in enumerate(zip(outs, sizes)):
        copies.append(
            pltpu.make_async_copy(rows.at[pl.ds(start, size)], out, sems.at[place])
        )
        start += size
    for copy in copies:
        copy.start()
    for copy in copies:
        copy.wait()


def copy_plan(pick_from, pick_row, source_count):
    number = jnp.arange(pick_from.shape[0], dtype=jnp.int32)
    before = pick_from[None, :] < pick_from[:, None]
    same = (pick_from[None, :] == pick_from[:, None]) & (number[None, :] < number[:, None])
    rank = jnp.sum((before | same).astype(jnp.int32), axis=1)
    here = rank[None, :] == number[:, None]
    place = jnp.sum(jnp.where(here, number[None, :], 0), axis=1)
    row = jnp.sum(jnp.where(here, pick_row[None, :], 0), axis=1)
    bounds = jnp.sum(
        (pick_from[None, :] < jnp.arange(source_count + 1)[:, None]).astype(jnp.int32), axis=1
    )
    return (bounds.astype(jnp.int32), place.astype(jnp.int32), row.astype(jnp.int32))


def copy_rows(sources, offsets, width, plan, sizes, events=()):
    rows = sources[0].shape[1]
    total = sum(sizes)
    return pl.pallas_call(
        functools.partial(copy_rows_kernel, tuple(sizes), tuple(offsets), width),
        out_shape=[jax.ShapeDtypeStruct((size, rows, width), sources[0].dtype) for size in sizes],
        grid_spec=pltpu.PrefetchScalarGridSpec(
            num_scalar_prefetch=3,
            grid=(1,),
            in_specs=[pl.BlockSpec(memory_space=pl.ANY)] * (len(sources) + len(events)),
            out_specs=[pl.BlockSpec(memory_space=pl.ANY)] * len(sizes),
            scratch_shapes=[
                pltpu.VMEM((total, rows, width), sources[0].dtype),
                pltpu.SemaphoreType.DMA((len(sizes) + 1,)),
            ],
        ),
        compiler_params=pltpu.CompilerParams(vmem_limit_bytes=40 * 1024 * 1024),
        cost_estimate=pl.CostEstimate(flops=0, bytes_accessed=1024, transcendentals=0),
        name="copy_rows",
    )(*plan, *sources, *events)


def place_pieces_kernel(places, count_outs, *refs):
    pieces = refs[: len(places)]
    outs = refs[-1 - count_outs : -1]
    sems = refs[-1]
    copies = []
    for number, (piece, place) in enumerate(zip(pieces, places)):
        first, count, begin, size, column, out, row = place
        copies.append(
            pltpu.make_async_copy(
                piece.at[pl.ds(first, count), :, pl.ds(begin, size)],
                outs[out].at[pl.ds(row, count), :, pl.ds(column, size)],
                sems.at[number],
            )
        )
    for copy in copies:
        copy.start()
    for copy in copies:
        copy.wait()


def place_pieces(pieces, places, shapes, events=()):
    return pl.pallas_call(
        functools.partial(place_pieces_kernel, tuple(places), len(shapes)),
        out_shape=[jax.ShapeDtypeStruct(shape, pieces[0].dtype) for shape in shapes],
        in_specs=[pl.BlockSpec(memory_space=pl.ANY)] * (len(pieces) + len(events)),
        out_specs=[pl.BlockSpec(memory_space=pltpu.VMEM)] * len(shapes),
        scratch_shapes=[pltpu.SemaphoreType.DMA((len(pieces),))],
        compiler_params=pltpu.CompilerParams(vmem_limit_bytes=40 * 1024 * 1024),
        cost_estimate=pl.CostEstimate(flops=0, bytes_accessed=1024, transcendentals=0),
        name="place_pieces",
    )(*pieces, *events)


def attend_kernel(blocks, order_ref, q_ref, k_ref, v_ref, out_ref, log_ref, key_rows, value_cols):
    size = q_ref.shape[1] // blocks
    at = [pl.multiple_of(order_ref[i] * size, size) for i in range(blocks)]
    for i in range(blocks):
        key_rows[i * size : (i + 1) * size, :] = k_ref[:, pl.ds(at[i], size)].T
        value_cols[:, i * size : (i + 1) * size] = v_ref[:, pl.ds(at[i], size)]
    key_pos = lax.broadcasted_iota(jnp.int32, (size, size), 0)
    query_pos = lax.broadcasted_iota(jnp.int32, (size, size), 1)
    seen = key_pos <= query_pos
    for i in range(blocks):
        past = i * size
        query = q_ref[:, pl.ds(at[i], size)]
        near = jnp.where(
            seen, dot(key_rows[past : past + size, :], query, 1, 0), masked_score
        )
        top = jnp.max(near, axis=0, keepdims=True)
        if i:
            far = dot(key_rows[:past, :], query, 1, 0)
            top = jnp.maximum(top, jnp.max(far, axis=0, keepdims=True))
        near = jnp.exp(near - top)
        total = jnp.sum(near, axis=0, keepdims=True)
        value = dot(value_cols[:, past : past + size], near.astype(jnp.bfloat16), 1, 0)
        if i:
            far = jnp.exp(far - top)
            total = total + jnp.sum(far, axis=0, keepdims=True)
            value = value + dot(value_cols[:, :past], far.astype(jnp.bfloat16), 1, 0)
        out_ref[:, pl.ds(at[i], size)] = (value / total).astype(jnp.bfloat16)
        log_ref[0, :, pl.ds(at[i], size)] = top + jnp.log(total)


def attend(projected, order, heads, head_dim):
    tokens = projected.shape[1]
    blocks = order.shape[0]

    def part(first):
        return pl.BlockSpec((head_dim, tokens), lambda h, order, first=first: (first + h, 0))

    return pl.pallas_call(
        functools.partial(attend_kernel, blocks),
        out_shape=[
            jax.ShapeDtypeStruct((heads * head_dim, tokens), jnp.bfloat16),
            jax.ShapeDtypeStruct((heads, 1, tokens), jnp.float32),
        ],
        grid_spec=pltpu.PrefetchScalarGridSpec(
            num_scalar_prefetch=1,
            grid=(heads,),
            in_specs=[part(0), part(heads), part(2 * heads)],
            out_specs=[
                pl.BlockSpec((head_dim, tokens), lambda h, order: (h, 0)),
                pl.BlockSpec((1, 1, tokens), lambda h, order: (h, 0, 0)),
            ],
            scratch_shapes=[
                pltpu.VMEM((tokens, head_dim), jnp.bfloat16),
                pltpu.VMEM((head_dim, tokens), jnp.bfloat16),
            ],
        ),
        compiler_params=pltpu.CompilerParams(vmem_limit_bytes=40 * 1024 * 1024),
        cost_estimate=pl.CostEstimate(
            flops=heads * tokens * tokens * head_dim * 4,
            bytes_accessed=heads * head_dim * tokens * 8,
            transcendentals=heads * tokens * tokens,
        ),
        name="attend",
    )(order, projected, projected, projected)


def attend_back_kernel(
    blocks,
    order_ref,
    q_ref,
    k_ref,
    v_ref,
    grad_ref,
    log_ref,
    scale_ref,
    *refs,
):
    out_ref, term_ref, key_rows, key_cols, value_rows, key_sum, value_sum = refs[-7:]
    size = q_ref.shape[1] // blocks
    at = [pl.multiple_of(order_ref[i] * size, size) for i in range(blocks)]
    for i in range(blocks):
        here = slice(i * size, (i + 1) * size)
        key = k_ref[:, pl.ds(at[i], size)]
        key_rows[here, :] = key.T
        key_cols[:, here] = key
        value_rows[here, :] = v_ref[:, pl.ds(at[i], size)].T
    key_sum[...] = jnp.zeros_like(key_sum)
    value_sum[...] = jnp.zeros_like(value_sum)
    key_pos = lax.broadcasted_iota(jnp.int32, (size, size), 0)
    query_pos = lax.broadcasted_iota(jnp.int32, (size, size), 1)
    seen = key_pos <= query_pos
    term = jnp.zeros((q_ref.shape[0], 1), jnp.float32)
    for i in range(blocks):
        past = i * size
        query = q_ref[:, pl.ds(at[i], size)]
        grad = grad_ref[:, pl.ds(at[i], size)]
        log_total = log_ref[0, :, pl.ds(at[i], size)]
        parts = [(past, size)] + ([(0, past)] if i else [])
        probs, grads = [], []
        delta = jnp.zeros((1, size), jnp.float32)
        for first, count in parts:
            prob = jnp.exp(dot(key_rows[first : first + count, :], query, 1, 0) - log_total)
            if first == past:
                prob = jnp.where(seen, prob, 0.0)
            grad_prob = dot(value_rows[first : first + count, :], grad, 1, 0)
            delta = delta + jnp.sum(prob * grad_prob, axis=0, keepdims=True)
            probs.append(prob)
            grads.append(grad_prob)
        grad_query = jnp.zeros(query.shape, jnp.float32)
        for (first, count), prob, grad_prob in zip(parts, probs, grads):
            cols = slice(first, first + count)
            grad_score = (prob * (grad_prob - delta)).astype(jnp.bfloat16)
            value_sum[:, cols] += dot(grad, prob.astype(jnp.bfloat16), 1, 1)
            key_sum[:, cols] += dot(query, grad_score, 1, 1)
            grad_query = grad_query + dot(key_cols[:, cols], grad_score, 1, 0)
        term = term + jnp.sum(
            grad_query * query.astype(jnp.float32), axis=1, keepdims=True
        )
        out_ref[0, :, pl.ds(at[i], size)] = (grad_query * scale_ref[...]).astype(jnp.bfloat16)
    for i in range(blocks):
        here = slice(i * size, (i + 1) * size)
        out_ref[1, :, pl.ds(at[i], size)] = key_sum[:, here].astype(jnp.bfloat16)
        out_ref[2, :, pl.ds(at[i], size)] = value_sum[:, here].astype(jnp.bfloat16)
    term_ref[0] = term


def attend_back(
    projected, grad_attended, log_total, multiplier, order, heads, head_dim, events=()
):
    tokens = projected.shape[1]
    blocks = order.shape[0]

    def part(first):
        return pl.BlockSpec((head_dim, tokens), lambda h, order, first=first: (first + h, 0))

    return pl.pallas_call(
        functools.partial(attend_back_kernel, blocks),
        out_shape=[
            jax.ShapeDtypeStruct((3, heads * head_dim, tokens), jnp.bfloat16),
            jax.ShapeDtypeStruct((heads, head_dim, 1), jnp.float32),
        ],
        grid_spec=pltpu.PrefetchScalarGridSpec(
            num_scalar_prefetch=1,
            grid=(heads,),
            in_specs=[
                part(0),
                part(heads),
                part(2 * heads),
                part(0),
                pl.BlockSpec((1, 1, tokens), lambda h, order: (h, 0, 0)),
                pl.BlockSpec((head_dim, 1), lambda h, order: (0, 0)),
            ]
            + [pl.BlockSpec(memory_space=pl.ANY)] * len(events),
            out_specs=[
                pl.BlockSpec((3, head_dim, tokens), lambda h, order: (0, h, 0)),
                pl.BlockSpec((1, head_dim, 1), lambda h, order: (h, 0, 0)),
            ],
            scratch_shapes=[
                pltpu.VMEM((tokens, head_dim), jnp.bfloat16),
                pltpu.VMEM((head_dim, tokens), jnp.bfloat16),
                pltpu.VMEM((tokens, head_dim), jnp.bfloat16),
                pltpu.VMEM((head_dim, tokens), jnp.float32),
                pltpu.VMEM((head_dim, tokens), jnp.float32),
            ],
        ),
        compiler_params=pltpu.CompilerParams(vmem_limit_bytes=48 * 1024 * 1024),
        cost_estimate=pl.CostEstimate(
            flops=heads * tokens * tokens * head_dim * 10,
            bytes_accessed=heads * head_dim * tokens * 14,
            transcendentals=heads * tokens * tokens,
        ),
        name="attend_back",
    )(order, projected, projected, projected, grad_attended, log_total, multiplier, *events)


def paired_layer(
    inputs,
    targets,
    valid_counts,
    owners,
    master,
    first_moment,
    second_moment,
    norm_gains,
    gain_first,
    gain_second,
    query_scale,
    scale_first,
    scale_second,
):
    bf16 = jnp.bfloat16
    f32 = jnp.float32
    seq_local, block_rows, width = inputs.shape
    slot_count, head_dim, column_count = master.shape
    ff_blocks = FF // head_dim
    owner_count = lax.axis_size("fsdp")
    device = lax.axis_index("ctx")
    chip, core = device // 2, device % 2
    owner_here = lax.axis_index("fsdp")
    low_here = owner_here % 2
    high_here = owner_here // 2
    high_count = owner_count // 2
    high_distances = range(1, high_count)
    half_width = width // 2
    half_slots = slot_count // 2
    half_rows = seq_local * block_rows
    half_heads = H // 2
    half_blocks = ff_blocks // 2
    set_units = 4 * half_heads + 2 * half_blocks
    first_chip, first_core = chip == 0, core == 0

    def columns_here(array):
        return jnp.where(first_chip, array, jnp.roll(array, half_width, axis=-1))

    def sequence_rows(array):
        own = jnp.where(first_chip, array[0], array[1])
        got = swapped(jnp.where(first_chip, array[1], array[0]), "ctx", 2)
        return jnp.where(
            first_chip, jnp.concatenate([own, got]), jnp.concatenate([got, own])
        )

    def rows_home(array):
        array = columns_here(array)
        first, last = array[:block_rows], array[block_rows:]
        own = jnp.where(first_chip, first, last)
        got = swapped(jnp.where(first_chip, last, first).astype(bf16), "ctx", 2).astype(f32)
        return jnp.where(first_chip, jnp.stack([own, got]), jnp.stack([got, own]))

    slot_rows = unit_rows(owners, slot_count)
    unit_total = owners.shape[0]
    kind_sizes = [H, H, H, H, ff_blocks, ff_blocks]
    kind_starts = [sum(kind_sizes[:i]) for i in range(6)]

    def unit_list(kinds, which):
        return jnp.concatenate(
            [
                kind_starts[k] + which * (kind_sizes[k] // 2) + jnp.arange(kind_sizes[k] // 2)
                for k in kinds
            ]
        ).astype(jnp.int32)

    wanted = jnp.concatenate(
        [unit_list(range(6), core), unit_list((4, 5), 1 - core)]
    )
    wanted_rows = slot_rows[wanted]
    wanted_owner, wanted_slot = wanted_rows // slot_count, wanted_rows % slot_count
    weight_from = 2 * (wanted_slot // half_slots != core) + (wanted_owner % 2 != low_here)
    weight_from = weight_from.astype(jnp.int32)
    weight_row = ((wanted_owner // 2) ^ high_here) * half_slots + wanted_slot % half_slots
    weight_plan = copy_plan(weight_from, weight_row, 4)
    weight_sizes = [3 * half_heads, half_heads + 2 * half_blocks, 2 * half_blocks]

    chunks = [(0, 128), (128, 128), (256, 256)]
    lead = 512
    tail = half_width - lead
    shard = master.astype(bf16)
    own_half = jnp.where(first_core, shard[:half_slots], shard[half_slots:])
    got_half = swapped(jnp.where(first_core, shard[half_slots:], shard[:half_slots]), "ctx", 1)
    shard = jnp.where(
        first_core,
        jnp.concatenate([own_half, got_half], axis=2),
        jnp.concatenate([got_half, own_half], axis=2),
    )
    shard, inputs, targets = lax.optimization_barrier((shard, inputs, targets))
    values_b = columns_here(sequence_rows(inputs))
    targets_b = columns_here(sequence_rows(targets))
    shard_last = shard[:, :, lead:]
    shards = [shard[:, :, start : start + size] for start, size in chunks]
    shards.append(jnp.concatenate([shard_last, swapped(shard_last, "ctx", 2)], axis=2))
    highs, lows, firsts = [], [], []
    for number, part in enumerate(shards):
        if number:
            part, gathered = lax.optimization_barrier((part, gathered))
            highs[-1] = gathered
        pieces = [part] + [swapped(part, "fsdp", 2 * d) for d in high_distances]
        firsts.append(pieces[1])
        gathered = jnp.concatenate(pieces)
        highs.append(gathered)
    own_units, rest_units, far_units = weight_sizes
    near_units = own_units + rest_units

    def pick_units(number, sizes, events):
        high, low = highs[number], lows[number]
        sources = [high, low, swapped(high, "ctx", 1), swapped(low, "ctx", 1)]
        return copy_rows(sources, [0] * 4, high.shape[2], weight_plan, sizes, events)

    lows.append(swapped(highs[0], "fsdp", 1))
    lows[0], highs[1] = lax.optimization_barrier((lows[0], highs[1]))
    near_one, far_one = pick_units(0, [near_units, far_units], [firsts[2]])
    got_one = swapped(near_one, "ctx", 2)
    highs[1], far_one = lax.optimization_barrier((highs[1], far_one))
    highs[3], got_one = lax.optimization_barrier((highs[3], got_one))
    for number in range(1, 4):
        if number == 3:
            near_two, far_two = pick_units(1, [near_units, far_units], [values_b, got_one])
            highs[3], far_two = lax.optimization_barrier((highs[3], far_two))
        if number > 1:
            highs[number], lows[-1] = lax.optimization_barrier((highs[number], lows[-1]))
        lows.append(swapped(highs[number], "fsdp", 1))
    got_two = swapped(near_two, "ctx", 2)
    qkv_three, rest_three, far_three = pick_units(2, weight_sizes, [targets_b, got_two])
    qkv_got = swapped(qkv_three, "ctx", 2)
    rest_three, qkv_got = lax.optimization_barrier((rest_three, qkv_got))
    rest_got = swapped(rest_three, "ctx", 2)
    qkv_last, rest_last, far_last = pick_units(3, weight_sizes, [qkv_got])

    def columns_of(owns, gots, last):
        pieces = [(last, 0, tail, lead), (last, tail, tail, half_width + lead)]
        for (start, size), own, got in zip(chunks, owns, gots):
            pieces += [(own, 0, size, start), (got, 0, size, half_width + start)]
        return pieces

    def placed(pieces, from_end, count, out, row):
        return [
            (piece.shape[0] - from_end if from_end else 0, count, *columns, out, row)
            for piece, *columns in pieces
        ]

    qkv_pieces = columns_of(
        [near_one, near_two, qkv_three], [got_one, got_two, qkv_got], qkv_last
    )
    rest_pieces = columns_of(
        [near_one, near_two, rest_three], [got_one, got_two, rest_got], rest_last
    )
    far_pieces = columns_of(
        [far_one, far_two, far_three],
        [swapped(got, "ctx", 1) for got in (got_one, got_two, rest_got)],
        far_last,
    )
    (w_qkv,) = place_pieces(
        [piece for piece, *_ in qkv_pieces],
        placed(qkv_pieces, 0, own_units, 0, 0),
        [(own_units, head_dim, width)],
    )
    w_qkv = w_qkv.reshape(-1, width)

    gains = columns_here(norm_gains)
    values_in = values_b.astype(f32)
    normed_own = (values_in * inverse_rms(values_in) * gains[0]).astype(bf16)
    normed_b = jnp.concatenate([normed_own, swapped(normed_own, "ctx", 1)])
    base = score_base / math.sqrt(head_dim)
    multiplier = jax.nn.softplus(query_scale) * base
    row_scale = jnp.concatenate(
        [jnp.tile(multiplier, half_heads), jnp.ones((2 * half_heads * head_dim,), f32)]
    )
    projected = (dot(w_qkv, normed_b, 1, 1) * row_scale[:, None]).astype(bf16)
    positions = jnp.arange(4, dtype=jnp.int32)
    order = jnp.where(positions % 2 == core, 0, 2) + positions // 2
    order = order.astype(jnp.int32)
    attended, log_total = attend(projected, order, half_heads, head_dim)
    (w_out,) = place_pieces(
        [piece for piece, *_ in rest_pieces],
        placed(rest_pieces, rest_units, half_heads, 0, 0),
        [(half_heads, head_dim, width)],
        [log_total],
    )
    mlp_pieces, mlp_places = [], []
    for row, pieces in ((0, rest_pieces), (half_blocks, far_pieces)):
        for kind in range(2):
            mlp_pieces += [piece for piece, *_ in pieces]
            mlp_places += placed(pieces, (2 - kind) * half_blocks, half_blocks, kind, row)
    w_up, w_down = place_pieces(
        mlp_pieces, mlp_places, [(ff_blocks, head_dim, width)] * 2, [log_total]
    )
    w_out = w_out.reshape(-1, width)
    w_up = w_up.reshape(-1, width)
    w_down = w_down.reshape(-1, width)
    branch_far = dot(attended[:, half_rows:], w_out, 0, 0).astype(bf16)
    branch_got = swapped(branch_far, "ctx", 1)
    branch_own = dot(attended[:, :half_rows], w_out, 0, 0)
    middle = values_in + (branch_own + branch_got.astype(f32))
    normed_mid_b = (middle * inverse_rms(middle) * gains[1]).astype(bf16)
    hidden = dot(normed_mid_b, w_up, 1, 1)
    active_b = jax.nn.silu(hidden).astype(bf16)
    block_out = middle + dot(active_b, w_down, 1, 0)
    seq_length = 2 * half_rows
    row = jnp.arange(half_rows, dtype=jnp.int32)
    row_pos = (core + 2 * (row // block_rows)) * block_rows + row % block_rows
    valid = jnp.where(first_chip, valid_counts[0], valid_counts[1])
    counted = (row_pos >= seq_length - valid).astype(f32)
    count_term = jnp.sum(counted)

    out_grad = 2.0 * (block_out - targets_b.astype(f32)) * counted[:, None]
    out_grad_b = out_grad.astype(bf16)
    grad_active = dot(out_grad_b, w_down, 1, 1)
    sigma = jax.nn.sigmoid(hidden)
    grad_hidden_b = (grad_active * sigma * (1.0 + hidden * (1.0 - sigma))).astype(bf16)
    grad_normed_mid = dot(grad_hidden_b, w_up, 1, 0)
    inverse = inverse_rms(middle)
    scaled = grad_normed_mid * gains[1]
    grad_middle = out_grad + (
        inverse * scaled
        - middle * inverse**3 * jnp.mean(scaled * middle, axis=-1, keepdims=True)
    )
    grad_gain_two = jnp.sum(grad_normed_mid * middle * inverse, axis=0)
    grad_middle_own = grad_middle.astype(bf16)
    grad_middle_got = swapped(grad_middle_own, "ctx", 1)
    far_blocks = half_blocks * head_dim
    wide = slice(half_width + 256, half_width + lead)
    slim = slice(half_width, half_width + 256)
    block_grads = []
    for left, right in ((grad_hidden_b, normed_mid_b), (active_b, out_grad_b)):
        got = swapped(dot(left[:, far_blocks:], right, 0, 0).astype(bf16), "ctx", 1)
        total = dot(left[:, :far_blocks], right, 0, 0) + got.astype(f32)
        block_grads.append(total.astype(bf16).reshape(half_blocks, head_dim, width))
    block_grads = jnp.concatenate(block_grads)
    grad_middle_got, block_grads = lax.optimization_barrier((grad_middle_got, block_grads))
    grad_middle_b = jnp.concatenate([grad_middle_own, grad_middle_got])
    grad_attended = dot(w_out, grad_middle_b, 1, 1).astype(bf16)
    head_grads = dot(attended, grad_middle_b, 1, 0).astype(bf16)
    head_grads = head_grads.reshape(half_heads, head_dim, width)

    def early_columns(columns):
        return jnp.concatenate([head_grads[:, :, columns], block_grads[:, :, columns]])

    early_wide, early_slim = early_columns(wide), early_columns(slim)
    wide_got = swapped(early_wide, "ctx", 2)

    def last_columns(array):
        return jnp.concatenate(
            [array[..., lead:half_width], array[..., half_width + lead :]], axis=-1
        )

    early_last = jnp.concatenate([last_columns(head_grads), last_columns(block_grads)])
    grad_proj, grad_scale = attend_back(
        projected,
        grad_attended,
        log_total,
        multiplier[:, None],
        order,
        half_heads,
        head_dim,
        [early_wide, early_slim, early_last],
    )
    grad_proj = grad_proj.reshape(-1, grad_proj.shape[2])
    scale_term = (
        jnp.sum(grad_scale[:, :, 0], axis=0) / multiplier * base * jax.nn.sigmoid(query_scale)
    )

    low_order = jnp.stack([low_here, 1 - low_here])
    table_slots = (
        (2 * (jnp.arange(high_count) ^ high_here)[None, :, None] + low_order[:, None, None])
        * slot_count
        + core * half_slots
        + jnp.arange(half_slots)[None, None, :]
    ).reshape(-1)
    holds = table_slots[:, None] == slot_rows[None, :]
    unit_order = jnp.arange(unit_total, dtype=jnp.int32)
    slot_unit = jnp.sum(jnp.where(holds, unit_order[None, :] + 1, 0), axis=1) - 1
    kind = jnp.where(
        slot_unit < 4 * H, slot_unit // H, 4 + (slot_unit - 4 * H) // ff_blocks
    )
    kind_size = jnp.where(kind < 4, H, ff_blocks)
    within = jnp.where(kind < 4, slot_unit % H, (slot_unit - 4 * H) % ff_blocks)
    other_set = (within // (kind_size // 2) != core).astype(jnp.int32)
    rank = within % (kind_size // 2)
    grad_row = rank + jnp.where(
        kind <= 3, kind * half_heads, 4 * half_heads + (kind - 4) * half_blocks
    )
    empty = slot_unit < 0
    grad_from = jnp.where(empty, 2, other_set).astype(jnp.int32)
    grad_row = jnp.where(empty, 0, grad_row).astype(jnp.int32)
    grad_plan = copy_plan(grad_from, grad_row, 3)
    zero = jnp.zeros((1, head_dim, 256), bf16)

    def pick_table(own, got, offset, size, events=()):
        return copy_rows(
            [own, got, zero],
            [offset, offset, 0],
            size,
            grad_plan,
            [high_count * half_slots] * 2,
            events,
        )

    def table_sums(keep, got):
        sums = []
        for d in range(high_count):
            rows = slice(d * half_slots, (d + 1) * half_slots)
            sums.append((keep[rows].astype(f32) + got[rows].astype(f32)).astype(bf16))
        return sums

    def from_owners(tables):
        return [swapped(tables[d], "fsdp", 2 * d) for d in high_distances]

    def owner_sum(table, got):
        total = table.astype(f32)
        for part in got:
            total = total + part.astype(f32)
        return total.astype(bf16)

    def proj_grad(columns):
        return dot(grad_proj, columns, 1, 0).astype(bf16).reshape(-1, head_dim, columns.shape[1])

    def chip_sum(start, proj_got, early_got):
        near = slice(start, start + 256)
        parts = [
            (proj_grad(normed_b[:, near]), proj_got),
            (head_grads[:, :, near], early_got[:half_heads]),
            (block_grads[:, :, near], early_got[half_heads:]),
        ]
        return jnp.concatenate(
            [(own.astype(f32) + got.astype(f32)).astype(bf16) for own, got in parts]
        )

    proj_last = proj_grad(last_columns(normed_b))
    proj_last, wide_got = lax.optimization_barrier((proj_last, wide_got))
    total_last = jnp.concatenate([proj_last, early_last])
    wide_far = proj_grad(normed_b[:, wide])
    wide_proj = swapped(wide_far, "ctx", 2)
    keep_last, send_last = pick_table(
        total_last, swapped(total_last, "ctx", 1), 0, 256, [wide_far]
    )
    low_last = swapped(send_last, "fsdp", 1)
    keep_last, grad_proj = lax.optimization_barrier((keep_last, grad_proj))
    slim_far = jnp.concatenate([proj_grad(normed_b[:, slim]), early_slim])
    low_last, wide_proj, slim_far = lax.optimization_barrier((low_last, wide_proj, slim_far))
    slim_got = swapped(slim_far, "ctx", 2)
    total = chip_sum(256, wide_proj, wide_got)
    keep_three, send_three = pick_table(total, swapped(total, "ctx", 1), 0, 256)
    low_last, keep_three, grad_proj = lax.optimization_barrier((low_last, keep_three, grad_proj))
    low_three = swapped(send_three, "fsdp", 1)
    tables_last = table_sums(keep_last, low_last)
    high_last = from_owners(tables_last)
    low_three, high_last, slim_got = lax.optimization_barrier((low_three, high_last, slim_got))
    tables_three = table_sums(keep_three, low_three)
    high_three = from_owners(tables_three)
    total = chip_sum(0, slim_got[: 3 * half_heads], slim_got[3 * half_heads :])
    total_got = swapped(total, "ctx", 1)
    keep_two, send_two = pick_table(total, total_got, 128, 128, tables_three + high_last)
    low_two = swapped(send_two, "fsdp", 1)
    low_two, high_three = lax.optimization_barrier((low_two, high_three))
    tables_two = table_sums(keep_two, low_two)
    high_two = from_owners(tables_two)
    keep_one, send_one = pick_table(total, total_got, 0, 128, tables_two + high_three)

    normed_far = dot(grad_proj[:, half_rows:], w_qkv, 0, 0).astype(bf16)
    normed_got = swapped(normed_far, "ctx", 1)
    grad_normed_in = dot(grad_proj[:, :half_rows], w_qkv, 0, 0) + normed_got.astype(f32)
    inverse = inverse_rms(values_in)
    scaled = grad_normed_in * gains[0]
    input_grad = grad_middle + (
        inverse * scaled
        - values_in * inverse**3 * jnp.mean(scaled * values_in, axis=-1, keepdims=True)
    )
    grad_gain_one = jnp.sum(grad_normed_in * values_in * inverse, axis=0)

    gain_terms = columns_here(jnp.stack([grad_gain_one, grad_gain_two]))
    small = jnp.concatenate([gain_terms.reshape(-1), scale_term, count_term[None]])
    small = jnp.pad(small, (0, -small.shape[0] % 1024))
    keep_one, small = lax.optimization_barrier((keep_one, small))
    tables_one = table_sums(keep_one, swapped(send_one, "fsdp", 1))
    small = small + swapped(small, "fsdp", 1)
    tables_one, high_two, block_out, small = lax.optimization_barrier(
        (tables_one, high_two, block_out, small)
    )
    high_one = from_owners(tables_one)
    small_got = from_owners([small] * high_count)
    high_one, small_got = lax.optimization_barrier((high_one, small_got))
    small = summed((small + small_got[0]) + (small_got[1] + small_got[2]), "ctx")
    gain_sums = small[: 2 * width].reshape(2, width)
    scale_sums = small[2 * width : 2 * width + head_dim]
    count = small[2 * width + head_dim]

    owned_last = owner_sum(tables_last[0], high_last)
    owned_got = swapped(owned_last[:, :, tail:], "ctx", 2)
    owned = [
        owner_sum(tables_one[0], high_one),
        owner_sum(tables_two[0], high_two),
        owner_sum(tables_three[0], high_three),
        (owned_last[:, :, :tail].astype(f32) + owned_got.astype(f32)).astype(bf16),
    ]
    owned = jnp.concatenate(owned, axis=2).reshape(half_slots, head_dim, 2, column_count)
    kept = jnp.where(first_core, owned[:, :, 0], owned[:, :, 1])
    sent = swapped(jnp.where(first_core, owned[:, :, 1], owned[:, :, 0]), "ctx", 1)
    slot_sums = jnp.where(
        first_core, jnp.concatenate([kept, sent]), jnp.concatenate([sent, kept])
    ).astype(f32)
    new_master, new_first, new_second = adam_step(
        master, first_moment, second_moment, slot_sums / count, master_rate, decay_rate
    )
    new_gains, new_gain_first, new_gain_second = adam_step(
        norm_gains, gain_first, gain_second, gain_sums / count, gain_rate, 0.0
    )
    new_scale, new_scale_first, new_scale_second = adam_step(
        query_scale, scale_first, scale_second, scale_sums / count, scale_rate, 0.0
    )
    return (
        rows_home(block_out),
        rows_home(input_grad),
        new_master,
        new_first,
        new_second,
        new_gains,
        new_gain_first,
        new_gain_second,
        new_scale,
        new_scale_first,
        new_scale_second,
    )


def on_device(*arguments):
    paired = (
        lax.axis_size("ctx") == 4
        and lax.axis_size("fsdp") == 8
        and arguments[0].shape[0] == 2
    )
    return (paired_layer if paired else general_layer)(*arguments)


def solution(mesh):
    in_specs = (
        P("fsdp", "ctx", None),
        P("fsdp", "ctx", None),
        P("fsdp"),
        P(),
        P("fsdp", None, "ctx"),
        P("fsdp", None, "ctx"),
        P("fsdp", None, "ctx"),
        P(),
        P(),
        P(),
        P(),
        P(),
        P(),
    )
    out_specs = (
        P("fsdp", "ctx", None),
        P("fsdp", "ctx", None),
        P("fsdp", None, "ctx"),
        P("fsdp", None, "ctx"),
        P("fsdp", None, "ctx"),
        P(),
        P(),
        P(),
        P(),
        P(),
        P(),
    )
    return jax.shard_map(
        on_device, mesh=mesh, in_specs=in_specs, out_specs=out_specs, check_vma=False
    )
```

```python
import functools
import math

import jax
import jax.numpy as jnp
from jax import lax
from jax.experimental import pallas as pl
from jax.experimental.pallas import tpu as pltpu
from jax.sharding import PartitionSpec as P

H = 16
FF = 1280
STEP = 10


norm_eps = 1e-06
beta_first = 0.9
beta_second = 0.95
adam_eps = 1e-08
decay_rate = 0.1
master_rate = 0.05
gain_rate = 2.0
scale_rate = 2.0
score_base = 1.442695041
masked_score = -1e30


def from_behind(block, axis, distance):
    devices = range(lax.axis_size(axis))
    route = [(i - distance, i) for i in devices if i - distance in devices]
    return lax.ppermute(block, axis, route)


def shifted(array, axis, by):
    count = lax.axis_size(axis)
    return lax.ppermute(array, axis, [(i, (i + by) % count) for i in range(count)])


def unit_rows(owners, slot_count):
    unit_count = owners.shape[0]
    unit_order = jnp.arange(unit_count, dtype=jnp.int32)
    same_owner = owners[:, None] == owners[None, :]
    earlier = unit_order[None, :] < unit_order[:, None]
    slot_rank = jnp.sum((same_owner & earlier).astype(jnp.int32), axis=1)
    return owners * slot_count + slot_rank


def inverse_rms(values):
    return lax.rsqrt(jnp.mean(values * values, axis=-1, keepdims=True) + norm_eps)


def norm_back(values, gain, grad_normed):
    inverse = inverse_rms(values)
    scaled = grad_normed * gain
    grad_values = inverse * scaled - values * inverse**3 * jnp.mean(
        scaled * values, axis=-1, keepdims=True
    )
    grad_gain = jnp.sum(grad_normed * values * inverse, axis=(0, 1))
    return (grad_values, grad_gain)


def adam_step(values, moment_one, moment_two, gradient, step_rate, weight_decay):
    moment_one = beta_first * moment_one + (1.0 - beta_first) * gradient
    moment_two = beta_second * moment_two + (1.0 - beta_second) * gradient * gradient
    first_hat = moment_one / (1.0 - beta_first**STEP)
    second_hat = moment_two / (1.0 - beta_second**STEP)
    values = values - step_rate * (
        first_hat / (jnp.sqrt(second_hat) + adam_eps) + weight_decay * values
    )
    return (values, moment_one, moment_two)


def general_layer(
    inputs,
    targets,
    valid_counts,
    owners,
    master,
    first_moment,
    second_moment,
    norm_gains,
    gain_first,
    gain_second,
    query_scale,
    scale_first,
    scale_second,
):
    seq_local, block_rows, width = inputs.shape
    slot_count, head_dim, column_count = master.shape
    ff_blocks = FF // head_dim
    ctx_size = lax.axis_size("ctx")
    ctx_index = lax.axis_index("ctx")
    slot_rows = unit_rows(owners, slot_count)
    owner_table = lax.all_gather(master.astype(jnp.bfloat16), "fsdp", axis=0, tiled=True)
    picked = owner_table[slot_rows]
    weights = lax.all_gather(picked, "ctx", axis=2, tiled=True)
    w_qkv = weights[0 : 3 * H]
    w_out = weights[3 * H : 4 * H]
    w_up = weights[4 * H : 4 * H + ff_blocks]
    w_down = weights[4 * H + ff_blocks :]
    values_in = inputs.astype(jnp.float32)
    normed_b = (values_in * inverse_rms(values_in) * norm_gains[0]).astype(jnp.bfloat16)
    projected = jnp.einsum("sbd,hed->shbe", normed_b, w_qkv, preferred_element_type=jnp.float32)
    query_pre = projected[:, 0:H]
    multiplier = jax.nn.softplus(query_scale) * (score_base / math.sqrt(head_dim))
    query_b = (query_pre * multiplier).astype(jnp.bfloat16)
    key_b = projected[:, H : 2 * H].astype(jnp.bfloat16)
    value_b = projected[:, 2 * H : 3 * H].astype(jnp.bfloat16)
    query_rows = ctx_index * block_rows + jnp.arange(block_rows, dtype=jnp.int32)
    last_row = ctx_index * block_rows + block_rows - 1
    start_state = (
        jnp.full(query_pre.shape[:3], masked_score, jnp.float32),
        jnp.zeros(query_pre.shape[:3], jnp.float32),
        jnp.zeros(query_pre.shape, jnp.float32),
    )
    key_part = lax.all_gather(key_b, "ctx", axis=2, tiled=True)
    value_part = lax.all_gather(value_b, "ctx", axis=2, tiled=True)
    key_count = key_part.shape[2]

    def update(current):
        run_max, run_sum, accum = current
        key_rows = jnp.arange(key_count, dtype=jnp.int32)
        allowed = query_rows[:, None] >= key_rows[None, :]
        scores = jnp.einsum(
            "shqe,shke->shqk", query_b, key_part, preferred_element_type=jnp.float32
        )
        scores = jnp.where(allowed, scores, masked_score)
        new_max = jnp.maximum(run_max, jnp.max(scores, axis=-1))
        attn_probs = jnp.where(allowed, jnp.exp(scores - new_max[..., None]), 0.0)
        run_sum = jnp.sum(attn_probs, axis=-1)
        accum = jnp.einsum(
            "shqk,shke->shqe",
            attn_probs.astype(jnp.bfloat16),
            value_part,
            preferred_element_type=jnp.float32,
        )
        return (new_max, run_sum, accum)

    run_max, run_sum, accum = lax.cond(
        jnp.int32(0) <= last_row, update, lambda current: current, start_state
    )
    attended = accum / run_sum[..., None]
    log_total = run_max + jnp.log(run_sum)
    attended_b = attended.astype(jnp.bfloat16)
    branch = jnp.einsum("shbe,hed->sbd", attended_b, w_out, preferred_element_type=jnp.float32)
    middle = values_in + branch
    normed_mid_b = (middle * inverse_rms(middle) * norm_gains[1]).astype(jnp.bfloat16)
    hidden = jnp.einsum("sbd,fed->sbfe", normed_mid_b, w_up, preferred_element_type=jnp.float32)
    active_b = jax.nn.silu(hidden).astype(jnp.bfloat16)
    block_out = middle + jnp.einsum(
        "sbfe,fed->sbd", active_b, w_down, preferred_element_type=jnp.float32
    )
    seq_length = block_rows * ctx_size
    counted = (query_rows[None, :] >= (seq_length - valid_counts)[:, None]).astype(jnp.float32)
    count_term = jnp.sum(counted)
    out_grad = 2.0 * (block_out - targets.astype(jnp.float32)) * counted[..., None]
    out_grad_b = out_grad.astype(jnp.bfloat16)
    grad_down = jnp.einsum(
        "sbfe,sbd->fed", active_b, out_grad_b, preferred_element_type=jnp.float32
    )
    grad_active = jnp.einsum(
        "sbd,fed->sbfe", out_grad_b, w_down, preferred_element_type=jnp.float32
    )
    sigma = jax.nn.sigmoid(hidden)
    grad_hidden_b = (grad_active * sigma * (1.0 + hidden * (1.0 - sigma))).astype(jnp.bfloat16)
    grad_up = jnp.einsum(
        "sbfe,sbd->fed", grad_hidden_b, normed_mid_b, preferred_element_type=jnp.float32
    )
    grad_normed_mid = jnp.einsum(
        "sbfe,fed->sbd", grad_hidden_b, w_up, preferred_element_type=jnp.float32
    )
    grad_middle_norm, grad_gain_two = norm_back(middle, norm_gains[1], grad_normed_mid)
    grad_middle = out_grad + grad_middle_norm
    grad_middle_b = grad_middle.astype(jnp.bfloat16)
    grad_out = jnp.einsum(
        "shbe,sbd->hed", attended_b, grad_middle_b, preferred_element_type=jnp.float32
    )
    grad_attended_b = jnp.einsum(
        "sbd,hed->shbe", grad_middle_b, w_out, preferred_element_type=jnp.float32
    ).astype(jnp.bfloat16)
    delta = jnp.sum(grad_attended_b.astype(jnp.float32) * attended, axis=-1)

    def block_grads(source, key_cur, value_cur, partial_grads):
        grad_key, grad_value, grad_query = partial_grads
        key_rows = source * block_rows + jnp.arange(block_rows, dtype=jnp.int32)
        allowed = query_rows[:, None] >= key_rows[None, :]
        scores = jnp.einsum("shqe,shke->shqk", query_b, key_cur, preferred_element_type=jnp.float32)
        scores = jnp.where(allowed, scores, masked_score)
        attn_probs = jnp.exp(scores - log_total[..., None])
        grad_value = grad_value + jnp.einsum(
            "shqk,shqe->shke",
            attn_probs.astype(jnp.bfloat16),
            grad_attended_b,
            preferred_element_type=jnp.float32,
        )
        grad_probs = jnp.einsum(
            "shqe,shke->shqk", grad_attended_b, value_cur, preferred_element_type=jnp.float32
        )
        grad_scores_b = (attn_probs * (grad_probs - delta[..., None])).astype(jnp.bfloat16)
        grad_query = grad_query + jnp.einsum(
            "shqk,shke->shqe", grad_scores_b, key_cur, preferred_element_type=jnp.float32
        )
        grad_key = grad_key + jnp.einsum(
            "shqk,shqe->shke", grad_scores_b, query_b, preferred_element_type=jnp.float32
        )
        return (grad_key, grad_value, grad_query)

    zero_heads = jnp.zeros(query_pre.shape, jnp.float32)

    def back_turn(which_turn, current):
        key_cur, value_cur, grad_key, grad_value, grad_query = current
        source = (ctx_index - which_turn) % ctx_size
        grad_key, grad_value, grad_query = lax.cond(
            source <= ctx_index,
            lambda parts: block_grads(source, key_cur, value_cur, parts),
            lambda parts: parts,
            (grad_key, grad_value, grad_query),
        )
        key_cur, value_cur = from_behind((key_cur, value_cur), "ctx", 1)
        grad_key, grad_value = (
            shifted(grad_key.astype(jnp.bfloat16), "ctx", 1).astype(grad_key.dtype),
            shifted(grad_value.astype(jnp.bfloat16), "ctx", 1).astype(grad_value.dtype),
        )
        return (key_cur, value_cur, grad_key, grad_value, grad_query)

    back_state = (key_b, value_b, zero_heads, zero_heads, zero_heads)
    back_state = lax.fori_loop(0, ctx_size, back_turn, back_state)
    grad_key, grad_value, grad_query = (back_state[2], back_state[3], back_state[4])
    grad_proj_b = jnp.concatenate([grad_query * multiplier, grad_key, grad_value], axis=1).astype(
        jnp.bfloat16
    )
    grad_qkv = jnp.einsum(
        "shbe,sbd->hed", grad_proj_b, normed_b, preferred_element_type=jnp.float32
    )
    grad_normed_in = jnp.einsum(
        "shbe,hed->sbd", grad_proj_b, w_qkv, preferred_element_type=jnp.float32
    )
    grad_input_norm, grad_gain_one = norm_back(values_in, norm_gains[0], grad_normed_in)
    input_grad = grad_middle + grad_input_norm
    scale_term = (
        jnp.sum(grad_query * query_pre, axis=(0, 1, 2))
        * (score_base / math.sqrt(head_dim))
        * jax.nn.sigmoid(query_scale)
    )
    unit_grads = jnp.concatenate([grad_qkv, grad_out, grad_up, grad_down], axis=0)
    owner_total = lax.axis_size("fsdp") * slot_count
    table_grads = (
        jnp.zeros((owner_total, head_dim, width), jnp.float32).at[slot_rows].set(unit_grads)
    )
    owned = lax.psum_scatter(
        table_grads.astype(jnp.bfloat16), "fsdp", scatter_dimension=0, tiled=True
    )
    slot_sums = lax.psum_scatter(owned, "ctx", scatter_dimension=2, tiled=True).astype(jnp.float32)
    gain_sums, scale_sums, count = lax.psum(
        (jnp.stack([grad_gain_one, grad_gain_two]), scale_term, count_term), ("ctx", "fsdp")
    )
    new_master, new_first, new_second = adam_step(
        master, first_moment, second_moment, slot_sums / count, master_rate, decay_rate
    )
    new_gains, new_gain_first, new_gain_second = adam_step(
        norm_gains, gain_first, gain_second, gain_sums / count, gain_rate, 0.0
    )
    new_scale, new_scale_first, new_scale_second = adam_step(
        query_scale, scale_first, scale_second, scale_sums / count, scale_rate, 0.0
    )
    return (
        block_out,
        input_grad,
        new_master,
        new_first,
        new_second,
        new_gains,
        new_gain_first,
        new_gain_second,
        new_scale,
        new_scale_first,
        new_scale_second,
    )


def swapped(array, axis, distance):
    return lax.ppermute(
        array, axis, [(i, i ^ distance) for i in range(lax.axis_size(axis))]
    )


def summed(array, axis):
    size = lax.axis_size(axis)
    if size & (size - 1):
        return lax.psum(array, axis)
    distance = 1
    while distance < size:
        array = array + swapped(array, axis, distance)
        distance *= 2
    return array


def dot(left, right, left_dim, right_dim):
    return lax.dot_general(
        left,
        right,
        (((left_dim,), (right_dim,)), ((), ())),
        preferred_element_type=jnp.float32,
    )


def copy_rows_kernel(sizes, offsets, width, bound_ref, place_ref, row_ref, *refs):
    sources = refs[: len(offsets)]
    outs = refs[-2 - len(sizes) : -2]
    rows, sems = refs[-2:]
    for number, (source, offset) in enumerate(zip(sources, offsets)):

        @pl.loop(bound_ref[number], bound_ref[number + 1])
        def copy_row(i, source=source, offset=offset):
            pltpu.make_async_copy(
                source.at[row_ref[i], :, pl.ds(offset, width)],
                rows.at[place_ref[i]],
                sems.at[len(sizes)],
            ).start()

    pltpu.make_async_copy(rows, rows, sems.at[len(sizes)]).wait()
    copies, start = [], 0
    for place, (out, size) in enumerate(zip(outs, sizes)):
        copies.append(
            pltpu.make_async_copy(rows.at[pl.ds(start, size)], out, sems.at[place])
        )
        start += size
    for copy in copies:
        copy.start()
    for copy in copies:
        copy.wait()


def copy_plan(pick_from, pick_row, source_count):
    number = jnp.arange(pick_from.shape[0], dtype=jnp.int32)
    before = pick_from[None, :] < pick_from[:, None]
    same = (pick_from[None, :] == pick_from[:, None]) & (number[None, :] < number[:, None])
    rank = jnp.sum((before | same).astype(jnp.int32), axis=1)
    here = rank[None, :] == number[:, None]
    place = jnp.sum(jnp.where(here, number[None, :], 0), axis=1)
    row = jnp.sum(jnp.where(here, pick_row[None, :], 0), axis=1)
    bounds = jnp.sum(
        (pick_from[None, :] < jnp.arange(source_count + 1)[:, None]).astype(jnp.int32), axis=1
    )
    return (bounds.astype(jnp.int32), place.astype(jnp.int32), row.astype(jnp.int32))


def copy_rows(sources, offsets, width, plan, sizes, events=()):
    rows = sources[0].shape[1]
    total = sum(sizes)
    return pl.pallas_call(
        functools.partial(copy_rows_kernel, tuple(sizes), tuple(offsets), width),
        out_shape=[jax.ShapeDtypeStruct((size, rows, width), sources[0].dtype) for size in sizes],
        grid_spec=pltpu.PrefetchScalarGridSpec(
            num_scalar_prefetch=3,
            grid=(1,),
            in_specs=[pl.BlockSpec(memory_space=pl.ANY)] * (len(sources) + len(events)),
            out_specs=[pl.BlockSpec(memory_space=pl.ANY)] * len(sizes),
            scratch_shapes=[
                pltpu.VMEM((total, rows, width), sources[0].dtype),
                pltpu.SemaphoreType.DMA((len(sizes) + 1,)),
            ],
        ),
        compiler_params=pltpu.CompilerParams(vmem_limit_bytes=40 * 1024 * 1024),
        cost_estimate=pl.CostEstimate(flops=0, bytes_accessed=1024, transcendentals=0),
        name="copy_rows",
    )(*plan, *sources, *events)


def place_pieces_kernel(places, count_outs, *refs):
    pieces = refs[: len(places)]
    outs = refs[-1 - count_outs : -1]
    sems = refs[-1]
    copies = []
    for number, (piece, place) in enumerate(zip(pieces, places)):
        first, count, begin, size, column, out, row = place
        copies.append(
            pltpu.make_async_copy(
                piece.at[pl.ds(first, count), :, pl.ds(begin, size)],
                outs[out].at[pl.ds(row, count), :, pl.ds(column, size)],
                sems.at[number],
            )
        )
    for copy in copies:
        copy.start()
    for copy in copies:
        copy.wait()


def place_pieces(pieces, places, shapes, events=()):
    return pl.pallas_call(
        functools.partial(place_pieces_kernel, tuple(places), len(shapes)),
        out_shape=[jax.ShapeDtypeStruct(shape, pieces[0].dtype) for shape in shapes],
        in_specs=[pl.BlockSpec(memory_space=pl.ANY)] * (len(pieces) + len(events)),
        out_specs=[pl.BlockSpec(memory_space=pltpu.VMEM)] * len(shapes),
        scratch_shapes=[pltpu.SemaphoreType.DMA((len(pieces),))],
        compiler_params=pltpu.CompilerParams(vmem_limit_bytes=40 * 1024 * 1024),
        cost_estimate=pl.CostEstimate(flops=0, bytes_accessed=1024, transcendentals=0),
        name="place_pieces",
    )(*pieces, *events)


def attend_kernel(blocks, order_ref, q_ref, k_ref, v_ref, out_ref, log_ref, key_rows, value_cols):
    size = q_ref.shape[1] // blocks
    at = [pl.multiple_of(order_ref[i] * size, size) for i in range(blocks)]
    for i in range(blocks):
        key_rows[i * size : (i + 1) * size, :] = k_ref[:, pl.ds(at[i], size)].T
        value_cols[:, i * size : (i + 1) * size] = v_ref[:, pl.ds(at[i], size)]
    key_pos = lax.broadcasted_iota(jnp.int32, (size, size), 0)
    query_pos = lax.broadcasted_iota(jnp.int32, (size, size), 1)
    seen = key_pos <= query_pos
    for i in range(blocks):
        past = i * size
        query = q_ref[:, pl.ds(at[i], size)]
        near = jnp.where(
            seen, dot(key_rows[past : past + size, :], query, 1, 0), masked_score
        )
        top = jnp.max(near, axis=0, keepdims=True)
        if i:
            far = dot(key_rows[:past, :], query, 1, 0)
            top = jnp.maximum(top, jnp.max(far, axis=0, keepdims=True))
        near = jnp.exp(near - top)
        total = jnp.sum(near, axis=0, keepdims=True)
        value = dot(value_cols[:, past : past + size], near.astype(jnp.bfloat16), 1, 0)
        if i:
            far = jnp.exp(far - top)
            total = total + jnp.sum(far, axis=0, keepdims=True)
            value = value + dot(value_cols[:, :past], far.astype(jnp.bfloat16), 1, 0)
        out_ref[:, pl.ds(at[i], size)] = (value / total).astype(jnp.bfloat16)
        log_ref[0, :, pl.ds(at[i], size)] = top + jnp.log(total)


def attend(projected, order, heads, head_dim):
    tokens = projected.shape[1]
    blocks = order.shape[0]

    def part(first):
        return pl.BlockSpec((head_dim, tokens), lambda h, order, first=first: (first + h, 0))

    return pl.pallas_call(
        functools.partial(attend_kernel, blocks),
        out_shape=[
            jax.ShapeDtypeStruct((heads * head_dim, tokens), jnp.bfloat16),
            jax.ShapeDtypeStruct((heads, 1, tokens), jnp.float32),
        ],
        grid_spec=pltpu.PrefetchScalarGridSpec(
            num_scalar_prefetch=1,
            grid=(heads,),
            in_specs=[part(0), part(heads), part(2 * heads)],
            out_specs=[
                pl.BlockSpec((head_dim, tokens), lambda h, order: (h, 0)),
                pl.BlockSpec((1, 1, tokens), lambda h, order: (h, 0, 0)),
            ],
            scratch_shapes=[
                pltpu.VMEM((tokens, head_dim), jnp.bfloat16),
                pltpu.VMEM((head_dim, tokens), jnp.bfloat16),
            ],
        ),
        compiler_params=pltpu.CompilerParams(vmem_limit_bytes=40 * 1024 * 1024),
        cost_estimate=pl.CostEstimate(
            flops=heads * tokens * tokens * head_dim * 4,
            bytes_accessed=heads * head_dim * tokens * 8,
            transcendentals=heads * tokens * tokens,
        ),
        name="attend",
    )(order, projected, projected, projected)


def attend_back_kernel(
    blocks,
    order_ref,
    q_ref,
    k_ref,
    v_ref,
    grad_ref,
    log_ref,
    scale_ref,
    *refs,
):
    out_ref, term_ref, key_rows, key_cols, value_rows, key_sum, value_sum = refs[-7:]
    size = q_ref.shape[1] // blocks
    at = [pl.multiple_of(order_ref[i] * size, size) for i in range(blocks)]
    for i in range(blocks):
        here = slice(i * size, (i + 1) * size)
        key = k_ref[:, pl.ds(at[i], size)]
        key_rows[here, :] = key.T
        key_cols[:, here] = key
        value_rows[here, :] = v_ref[:, pl.ds(at[i], size)].T
    key_sum[...] = jnp.zeros_like(key_sum)
    value_sum[...] = jnp.zeros_like(value_sum)
    key_pos = lax.broadcasted_iota(jnp.int32, (size, size), 0)
    query_pos = lax.broadcasted_iota(jnp.int32, (size, size), 1)
    seen = key_pos <= query_pos
    term = jnp.zeros((q_ref.shape[0], 1), jnp.float32)
    for i in range(blocks):
        past = i * size
        query = q_ref[:, pl.ds(at[i], size)]
        grad = grad_ref[:, pl.ds(at[i], size)]
        log_total = log_ref[0, :, pl.ds(at[i], size)]
        parts = [(past, size)] + ([(0, past)] if i else [])
        probs, grads = [], []
        delta = jnp.zeros((1, size), jnp.float32)
        for first, count in parts:
            prob = jnp.exp(dot(key_rows[first : first + count, :], query, 1, 0) - log_total)
            if first == past:
                prob = jnp.where(seen, prob, 0.0)
            grad_prob = dot(value_rows[first : first + count, :], grad, 1, 0)
            delta = delta + jnp.sum(prob * grad_prob, axis=0, keepdims=True)
            probs.append(prob)
            grads.append(grad_prob)
        grad_query = jnp.zeros(query.shape, jnp.float32)
        for (first, count), prob, grad_prob in zip(parts, probs, grads):
            cols = slice(first, first + count)
            grad_score = (prob * (grad_prob - delta)).astype(jnp.bfloat16)
            value_sum[:, cols] += dot(grad, prob.astype(jnp.bfloat16), 1, 1)
            key_sum[:, cols] += dot(query, grad_score, 1, 1)
            grad_query = grad_query + dot(key_cols[:, cols], grad_score, 1, 0)
        term = term + jnp.sum(
            grad_query * query.astype(jnp.float32), axis=1, keepdims=True
        )
        out_ref[0, :, pl.ds(at[i], size)] = (grad_query * scale_ref[...]).astype(jnp.bfloat16)
    for i in range(blocks):
        here = slice(i * size, (i + 1) * size)
        out_ref[1, :, pl.ds(at[i], size)] = key_sum[:, here].astype(jnp.bfloat16)
        out_ref[2, :, pl.ds(at[i], size)] = value_sum[:, here].astype(jnp.bfloat16)
    term_ref[0] = term


def attend_back(
    projected, grad_attended, log_total, multiplier, order, heads, head_dim, events=()
):
    tokens = projected.shape[1]
    blocks = order.shape[0]

    def part(first):
        return pl.BlockSpec((head_dim, tokens), lambda h, order, first=first: (first + h, 0))

    return pl.pallas_call(
        functools.partial(attend_back_kernel, blocks),
        out_shape=[
            jax.ShapeDtypeStruct((3, heads * head_dim, tokens), jnp.bfloat16),
            jax.ShapeDtypeStruct((heads, head_dim, 1), jnp.float32),
        ],
        grid_spec=pltpu.PrefetchScalarGridSpec(
            num_scalar_prefetch=1,
            grid=(heads,),
            in_specs=[
                part(0),
                part(heads),
                part(2 * heads),
                part(0),
                pl.BlockSpec((1, 1, tokens), lambda h, order: (h, 0, 0)),
                pl.BlockSpec((head_dim, 1), lambda h, order: (0, 0)),
            ]
            + [pl.BlockSpec(memory_space=pl.ANY)] * len(events),
            out_specs=[
                pl.BlockSpec((3, head_dim, tokens), lambda h, order: (0, h, 0)),
                pl.BlockSpec((1, head_dim, 1), lambda h, order: (h, 0, 0)),
            ],
            scratch_shapes=[
                pltpu.VMEM((tokens, head_dim), jnp.bfloat16),
                pltpu.VMEM((head_dim, tokens), jnp.bfloat16),
                pltpu.VMEM((tokens, head_dim), jnp.bfloat16),
                pltpu.VMEM((head_dim, tokens), jnp.float32),
                pltpu.VMEM((head_dim, tokens), jnp.float32),
            ],
        ),
        compiler_params=pltpu.CompilerParams(vmem_limit_bytes=48 * 1024 * 1024),
        cost_estimate=pl.CostEstimate(
            flops=heads * tokens * tokens * head_dim * 10,
            bytes_accessed=heads * head_dim * tokens * 14,
            transcendentals=heads * tokens * tokens,
        ),
        name="attend_back",
    )(order, projected, projected, projected, grad_attended, log_total, multiplier, *events)


def paired_layer(
    inputs,
    targets,
    valid_counts,
    owners,
    master,
    first_moment,
    second_moment,
    norm_gains,
    gain_first,
    gain_second,
    query_scale,
    scale_first,
    scale_second,
):
    bf16 = jnp.bfloat16
    f32 = jnp.float32
    seq_local, block_rows, width = inputs.shape
    slot_count, head_dim, column_count = master.shape
    ff_blocks = FF // head_dim
    owner_count = lax.axis_size("fsdp")
    device = lax.axis_index("ctx")
    chip, core = device // 2, device % 2
    owner_here = lax.axis_index("fsdp")
    low_here = owner_here % 2
    high_here = owner_here // 2
    high_count = owner_count // 2
    high_distances = range(1, high_count)
    half_width = width // 2
    half_slots = slot_count // 2
    half_rows = seq_local * block_rows
    half_heads = H // 2
    half_blocks = ff_blocks // 2
    set_units = 4 * half_heads + 2 * half_blocks
    first_chip, first_core = chip == 0, core == 0

    def columns_here(array):
        return jnp.where(first_chip, array, jnp.roll(array, half_width, axis=-1))

    def sequence_rows(array):
        own = jnp.where(first_chip, array[0], array[1])
        got = swapped(jnp.where(first_chip, array[1], array[0]), "ctx", 2)
        return jnp.where(
            first_chip, jnp.concatenate([own, got]), jnp.concatenate([got, own])
        )

    def rows_home(array):
        array = columns_here(array)
        first, last = array[:block_rows], array[block_rows:]
        own = jnp.where(first_chip, first, last)
        got = swapped(jnp.where(first_chip, last, first).astype(bf16), "ctx", 2).astype(f32)
        return jnp.where(first_chip, jnp.stack([own, got]), jnp.stack([got, own]))

    slot_rows = unit_rows(owners, slot_count)
    unit_total = owners.shape[0]
    kind_sizes = [H, H, H, H, ff_blocks, ff_blocks]
    kind_starts = [sum(kind_sizes[:i]) for i in range(6)]

    def unit_list(kinds, which):
        return jnp.concatenate(
            [
                kind_starts[k] + which * (kind_sizes[k] // 2) + jnp.arange(kind_sizes[k] // 2)
                for k in kinds
            ]
        ).astype(jnp.int32)

    wanted = jnp.concatenate(
        [unit_list(range(6), core), unit_list((4, 5), 1 - core)]
    )
    wanted_rows = slot_rows[wanted]
    wanted_owner, wanted_slot = wanted_rows // slot_count, wanted_rows % slot_count
    weight_from = 2 * (wanted_slot // half_slots != core) + (wanted_owner % 2 != low_here)
    weight_from = weight_from.astype(jnp.int32)
    weight_row = ((wanted_owner // 2) ^ high_here) * half_slots + wanted_slot % half_slots
    weight_plan = copy_plan(weight_from, weight_row, 4)
    weight_sizes = [3 * half_heads, half_heads + 2 * half_blocks, 2 * half_blocks]

    chunks = [(0, 128), (128, 256)]
    lead = 384
    tail = half_width - lead
    shard = master.astype(bf16)
    own_half = jnp.where(first_core, shard[:half_slots], shard[half_slots:])
    got_half = swapped(jnp.where(first_core, shard[half_slots:], shard[:half_slots]), "ctx", 1)
    shard = jnp.where(
        first_core,
        jnp.concatenate([own_half, got_half], axis=2),
        jnp.concatenate([got_half, own_half], axis=2),
    )
    shard, inputs, targets = lax.optimization_barrier((shard, inputs, targets))
    values_b = columns_here(sequence_rows(inputs))
    targets_b = columns_here(sequence_rows(targets))
    half_tail = tail // 2
    shard_last = shard[:, :, lead:]
    last_got = swapped(shard_last, "ctx", 2)
    shards = [shard[:, :, start : start + size] for start, size in chunks]
    for start in (0, half_tail):
        part = slice(start, start + half_tail)
        shards.append(jnp.concatenate([shard_last[:, :, part], last_got[:, :, part]], axis=2))
    highs, lows, firsts = [], [], []
    for number, part in enumerate(shards):
        if number:
            part, gathered = lax.optimization_barrier((part, gathered))
            highs[-1] = gathered
        pieces = [part] + [swapped(part, "fsdp", 2 * d) for d in high_distances]
        firsts.append(pieces[1])
        gathered = jnp.concatenate(pieces)
        highs.append(gathered)
    own_units, rest_units, far_units = weight_sizes
    near_units = own_units + rest_units

    def pick_units(number, sizes, events):
        high, low = highs[number], lows[number]
        sources = [high, low, swapped(high, "ctx", 1), swapped(low, "ctx", 1)]
        return copy_rows(sources, [0] * 4, high.shape[2], weight_plan, sizes, events)

    lows.append(swapped(highs[0], "fsdp", 1))
    lows[0], highs[1] = lax.optimization_barrier((lows[0], highs[1]))
    near_one, far_one = pick_units(0, [near_units, far_units], [firsts[2]])
    got_one = swapped(near_one, "ctx", 2)
    highs[1], far_one = lax.optimization_barrier((highs[1], far_one))
    for number in range(1, 4):
        if number > 1:
            highs[number], lows[-1] = lax.optimization_barrier((highs[number], lows[-1]))
        lows.append(swapped(highs[number], "fsdp", 1))
    qkv_two, rest_two, far_two = pick_units(1, weight_sizes, [values_b, got_one])
    qkv_got = swapped(qkv_two, "ctx", 2)
    rest_two, qkv_got = lax.optimization_barrier((rest_two, qkv_got))
    rest_got = swapped(rest_two, "ctx", 2)
    last_one = pick_units(2, weight_sizes, [targets_b, qkv_got])
    last_two = pick_units(3, weight_sizes, [])

    def columns_of(owns, gots, lasts):
        pieces = []
        for start, last in zip((lead, lead + half_tail), lasts):
            pieces += [(last, 0, half_tail, start), (last, half_tail, half_tail, half_width + start)]
        for (start, size), own, got in zip(chunks, owns, gots):
            pieces += [(own, 0, size, start), (got, 0, size, half_width + start)]
        return pieces

    def placed(pieces, from_end, count, out, row):
        return [
            (piece.shape[0] - from_end if from_end else 0, count, *columns, out, row)
            for piece, *columns in pieces
        ]

    lasts = list(zip(last_one, last_two))
    qkv_pieces = columns_of([near_one, qkv_two], [got_one, qkv_got], lasts[0])
    rest_pieces = columns_of([near_one, rest_two], [got_one, rest_got], lasts[1])
    far_pieces = columns_of(
        [far_one, far_two], [swapped(got, "ctx", 1) for got in (got_one, rest_got)], lasts[2]
    )
    (w_qkv,) = place_pieces(
        [piece for piece, *_ in qkv_pieces],
        placed(qkv_pieces, 0, own_units, 0, 0),
        [(own_units, head_dim, width)],
    )
    w_qkv = w_qkv.reshape(-1, width)

    gains = columns_here(norm_gains)
    values_in = values_b.astype(f32)
    normed_own = (values_in * inverse_rms(values_in) * gains[0]).astype(bf16)
    normed_b = jnp.concatenate([normed_own, swapped(normed_own, "ctx", 1)])
    base = score_base / math.sqrt(head_dim)
    multiplier = jax.nn.softplus(query_scale) * base
    row_scale = jnp.concatenate(
        [jnp.tile(multiplier, half_heads), jnp.ones((2 * half_heads * head_dim,), f32)]
    )
    projected = (dot(w_qkv, normed_b, 1, 1) * row_scale[:, None]).astype(bf16)
    positions = jnp.arange(4, dtype=jnp.int32)
    order = jnp.where(positions % 2 == core, 0, 2) + positions // 2
    order = order.astype(jnp.int32)
    attended, log_total = attend(projected, order, half_heads, head_dim)
    (w_out,) = place_pieces(
        [piece for piece, *_ in rest_pieces],
        placed(rest_pieces, rest_units, half_heads, 0, 0),
        [(half_heads, head_dim, width)],
        [log_total],
    )
    mlp_pieces, mlp_places = [], []
    for row, pieces in ((0, rest_pieces), (half_blocks, far_pieces)):
        for kind in range(2):
            mlp_pieces += [piece for piece, *_ in pieces]
            mlp_places += placed(pieces, (2 - kind) * half_blocks, half_blocks, kind, row)
    w_up, w_down = place_pieces(
        mlp_pieces, mlp_places, [(ff_blocks, head_dim, width)] * 2, [log_total]
    )
    w_out = w_out.reshape(-1, width)
    w_up = w_up.reshape(-1, width)
    w_down = w_down.reshape(-1, width)
    branch_far = dot(attended[:, half_rows:], w_out, 0, 0).astype(bf16)
    branch_got = swapped(branch_far, "ctx", 1)
    branch_own = dot(attended[:, :half_rows], w_out, 0, 0)
    middle = values_in + (branch_own + branch_got.astype(f32))
    normed_mid_b = (middle * inverse_rms(middle) * gains[1]).astype(bf16)
    hidden = dot(normed_mid_b, w_up, 1, 1)
    active_b = jax.nn.silu(hidden).astype(bf16)
    block_out = middle + dot(active_b, w_down, 1, 0)
    seq_length = 2 * half_rows
    row = jnp.arange(half_rows, dtype=jnp.int32)
    row_pos = (core + 2 * (row // block_rows)) * block_rows + row % block_rows
    valid = jnp.where(first_chip, valid_counts[0], valid_counts[1])
    counted = (row_pos >= seq_length - valid).astype(f32)
    count_term = jnp.sum(counted)

    out_grad = 2.0 * (block_out - targets_b.astype(f32)) * counted[:, None]
    out_grad_b = out_grad.astype(bf16)
    grad_active = dot(out_grad_b, w_down, 1, 1)
    sigma = jax.nn.sigmoid(hidden)
    grad_hidden_b = (grad_active * sigma * (1.0 + hidden * (1.0 - sigma))).astype(bf16)
    grad_normed_mid = dot(grad_hidden_b, w_up, 1, 0)
    inverse = inverse_rms(middle)
    scaled = grad_normed_mid * gains[1]
    grad_middle = out_grad + (
        inverse * scaled
        - middle * inverse**3 * jnp.mean(scaled * middle, axis=-1, keepdims=True)
    )
    grad_gain_two = jnp.sum(grad_normed_mid * middle * inverse, axis=0)
    grad_middle_own = grad_middle.astype(bf16)
    grad_middle_got = swapped(grad_middle_own, "ctx", 1)
    far_blocks = half_blocks * head_dim
    wide = slice(half_width + 128, half_width + lead)
    slim = slice(half_width, half_width + 128)
    block_grads = []
    for left, right in ((grad_hidden_b, normed_mid_b), (active_b, out_grad_b)):
        got = swapped(dot(left[:, far_blocks:], right, 0, 0).astype(bf16), "ctx", 1)
        total = dot(left[:, :far_blocks], right, 0, 0) + got.astype(f32)
        block_grads.append(total.astype(bf16).reshape(half_blocks, head_dim, width))
    block_grads = jnp.concatenate(block_grads)
    grad_middle_got, block_grads = lax.optimization_barrier((grad_middle_got, block_grads))
    grad_middle_b = jnp.concatenate([grad_middle_own, grad_middle_got])
    grad_attended = dot(w_out, grad_middle_b, 1, 1).astype(bf16)
    head_grads = dot(attended, grad_middle_b, 1, 0).astype(bf16)
    head_grads = head_grads.reshape(half_heads, head_dim, width)

    def early_columns(columns):
        return jnp.concatenate([head_grads[:, :, columns], block_grads[:, :, columns]])

    early_wide, early_slim = early_columns(wide), early_columns(slim)
    wide_got = swapped(early_wide, "ctx", 2)

    def last_columns(array, number):
        start = lead + number * half_tail
        near, far = start, half_width + start
        return jnp.concatenate(
            [array[..., near : near + half_tail], array[..., far : far + half_tail]], axis=-1
        )

    early_last = [
        jnp.concatenate([last_columns(head_grads, number), last_columns(block_grads, number)])
        for number in range(2)
    ]
    grad_proj, grad_scale = attend_back(
        projected,
        grad_attended,
        log_total,
        multiplier[:, None],
        order,
        half_heads,
        head_dim,
        [early_wide, early_slim, *early_last],
    )
    grad_proj = grad_proj.reshape(-1, grad_proj.shape[2])
    scale_term = (
        jnp.sum(grad_scale[:, :, 0], axis=0) / multiplier * base * jax.nn.sigmoid(query_scale)
    )

    low_order = jnp.stack([low_here, 1 - low_here])
    table_slots = (
        (2 * (jnp.array([0, 2, 1, 3]) ^ high_here)[None, :, None] + low_order[:, None, None])
        * slot_count
        + core * half_slots
        + jnp.arange(half_slots)[None, None, :]
    ).reshape(-1)
    holds = table_slots[:, None] == slot_rows[None, :]
    unit_order = jnp.arange(unit_total, dtype=jnp.int32)
    slot_unit = jnp.sum(jnp.where(holds, unit_order[None, :] + 1, 0), axis=1) - 1
    kind = jnp.where(
        slot_unit < 4 * H, slot_unit // H, 4 + (slot_unit - 4 * H) // ff_blocks
    )
    kind_size = jnp.where(kind < 4, H, ff_blocks)
    within = jnp.where(kind < 4, slot_unit % H, (slot_unit - 4 * H) % ff_blocks)
    other_set = (within // (kind_size // 2) != core).astype(jnp.int32)
    rank = within % (kind_size // 2)
    grad_row = rank + jnp.where(
        kind <= 3, kind * half_heads, 4 * half_heads + (kind - 4) * half_blocks
    )
    empty = slot_unit < 0
    grad_from = jnp.where(empty, 2, other_set).astype(jnp.int32)
    grad_row = jnp.where(empty, 0, grad_row).astype(jnp.int32)
    grad_plan = copy_plan(grad_from, grad_row, 3)
    zero = jnp.zeros((1, head_dim, 256), bf16)

    def pick_table(own, got, offset, size, events=()):
        return copy_rows(
            [own, got, zero],
            [offset, offset, 0],
            size,
            grad_plan,
            [high_count * half_slots] * 2,
            events,
        )

    def added(own, got):
        return (own.astype(f32) + got.astype(f32)).astype(bf16)

    def table_sums(keep, got):
        half = 2 * half_slots
        return (added(keep[:half], got[:half]), added(keep[half:], got[half:]))

    def pair_sums(tables, got):
        own = tables[0]
        return (
            added(own[:half_slots], got[:half_slots]),
            added(own[half_slots:], got[half_slots:]),
        )

    def proj_grad(columns):
        return dot(grad_proj, columns, 1, 0).astype(bf16).reshape(-1, head_dim, columns.shape[1])

    def chip_sum(start, size, proj_got, early_got):
        near = slice(start, start + size)
        parts = [
            (proj_grad(normed_b[:, near]), proj_got),
            (head_grads[:, :, near], early_got[:half_heads]),
            (block_grads[:, :, near], early_got[half_heads:]),
        ]
        return jnp.concatenate(
            [(own.astype(f32) + got.astype(f32)).astype(bf16) for own, got in parts]
        )

    proj_last = proj_grad(last_columns(normed_b, 0))
    proj_last, wide_got = lax.optimization_barrier((proj_last, wide_got))
    total_last = jnp.concatenate([proj_last, early_last[0]])
    wide_far = proj_grad(normed_b[:, wide])
    wide_proj = swapped(wide_far, "ctx", 2)
    keep_last, send_last = pick_table(
        total_last, swapped(total_last, "ctx", 1), 0, 256, [wide_far]
    )
    low_last = swapped(send_last, "fsdp", 1)
    keep_last, grad_proj = lax.optimization_barrier((keep_last, grad_proj))
    normed_far = dot(grad_proj[:, half_rows:], w_qkv, 0, 0).astype(bf16)
    normed_got = swapped(normed_far, "ctx", 1)
    total_four = jnp.concatenate([proj_grad(last_columns(normed_b, 1)), early_last[1]])
    keep_four, send_four = pick_table(
        total_four, swapped(total_four, "ctx", 1), 0, 256, [low_last, normed_far]
    )
    low_four = swapped(send_four, "fsdp", 1)
    keep_four, grad_proj, wide_proj, low_last = lax.optimization_barrier(
        (keep_four, grad_proj, wide_proj, low_last)
    )
    tables_last = table_sums(keep_last, low_last)
    pair_last = swapped(tables_last[1], "fsdp", 2)
    slim_far = jnp.concatenate([proj_grad(normed_b[:, slim]), early_slim])
    slim_got = swapped(slim_far, "ctx", 2)
    total = chip_sum(128, 256, wide_proj, wide_got)
    keep_two, send_two = pick_table(
        total, swapped(total, "ctx", 1), 0, 256, [low_four, slim_far, tables_last[1]]
    )
    low_two = swapped(send_two, "fsdp", 1)
    keep_two, grad_proj, slim_got, low_four, pair_last, normed_got = lax.optimization_barrier(
        (keep_two, grad_proj, slim_got, low_four, pair_last, normed_got)
    )
    owned_last = pair_sums(tables_last, pair_last)
    owner_last = swapped(owned_last[1], "fsdp", 4)
    tables_four = table_sums(keep_four, low_four)
    pair_four = swapped(tables_four[1], "fsdp", 2)
    total = chip_sum(0, 128, slim_got[: 3 * half_heads], slim_got[3 * half_heads :])
    keep_one, send_one = pick_table(
        total, swapped(total, "ctx", 1), 0, 128, [low_two, owned_last[1], tables_four[1]]
    )

    grad_normed_in = dot(grad_proj[:, :half_rows], w_qkv, 0, 0) + normed_got.astype(f32)
    inverse = inverse_rms(values_in)
    scaled = grad_normed_in * gains[0]
    input_grad = grad_middle + (
        inverse * scaled
        - values_in * inverse**3 * jnp.mean(scaled * values_in, axis=-1, keepdims=True)
    )
    grad_gain_one = jnp.sum(grad_normed_in * values_in * inverse, axis=0)

    gain_terms = columns_here(jnp.stack([grad_gain_one, grad_gain_two]))
    small = jnp.concatenate([gain_terms.reshape(-1), scale_term, count_term[None]])
    small = jnp.pad(small, (0, -small.shape[0] % 1024))
    low_one = swapped(send_one, "fsdp", 1)
    keep_one, small, low_two, pair_four, owner_last = lax.optimization_barrier(
        (keep_one, small, low_two, pair_four, owner_last)
    )
    tables_two = table_sums(keep_two, low_two)
    pair_two = swapped(tables_two[1], "fsdp", 2)
    owned_four = pair_sums(tables_four, pair_four)
    owner_four = swapped(owned_four[1], "fsdp", 4)
    small = small + swapped(small, "fsdp", 1)
    low_one, pair_two, small, block_out, owner_four = lax.optimization_barrier(
        (low_one, pair_two, small, block_out, owner_four)
    )
    tables_one = table_sums(keep_one, low_one)
    pair_one = swapped(tables_one[1], "fsdp", 2)
    owned_two = pair_sums(tables_two, pair_two)
    owner_two = swapped(owned_two[1], "fsdp", 4)
    small = small + swapped(small, "fsdp", 2)
    pair_one, owner_two, small = lax.optimization_barrier((pair_one, owner_two, small))
    owned_one = pair_sums(tables_one, pair_one)
    owner_one = swapped(owned_one[1], "fsdp", 4)
    small_got = swapped(small, "fsdp", 4)
    owner_one, small_got = lax.optimization_barrier((owner_one, small_got))
    small = summed(small + small_got, "ctx")
    gain_sums = small[: 2 * width].reshape(2, width)
    scale_sums = small[2 * width : 2 * width + head_dim]
    count = small[2 * width + head_dim]

    owned_last = [added(owned_last[0], owner_last), added(owned_four[0], owner_four)]
    owned_got = swapped(
        jnp.concatenate([part[:, :, half_tail:] for part in owned_last], axis=2), "ctx", 2
    )
    owned_own = jnp.concatenate([part[:, :, :half_tail] for part in owned_last], axis=2)
    owned = [
        added(owned_one[0], owner_one),
        added(owned_two[0], owner_two),
        added(owned_own, owned_got),
    ]
    owned = jnp.concatenate(owned, axis=2).reshape(half_slots, head_dim, 2, column_count)
    kept = jnp.where(first_core, owned[:, :, 0], owned[:, :, 1])
    sent = swapped(jnp.where(first_core, owned[:, :, 1], owned[:, :, 0]), "ctx", 1)
    slot_sums = jnp.where(
        first_core, jnp.concatenate([kept, sent]), jnp.concatenate([sent, kept])
    ).astype(f32)
    new_master, new_first, new_second = adam_step(
        master, first_moment, second_moment, slot_sums / count, master_rate, decay_rate
    )
    new_gains, new_gain_first, new_gain_second = adam_step(
        norm_gains, gain_first, gain_second, gain_sums / count, gain_rate, 0.0
    )
    new_scale, new_scale_first, new_scale_second = adam_step(
        query_scale, scale_first, scale_second, scale_sums / count, scale_rate, 0.0
    )
    return (
        rows_home(block_out),
        rows_home(input_grad),
        new_master,
        new_first,
        new_second,
        new_gains,
        new_gain_first,
        new_gain_second,
        new_scale,
        new_scale_first,
        new_scale_second,
    )


def on_device(*arguments):
    paired = (
        lax.axis_size("ctx") == 4
        and lax.axis_size("fsdp") == 8
        and arguments[0].shape[0] == 2
    )
    return (paired_layer if paired else general_layer)(*arguments)


def solution(mesh):
    in_specs = (
        P("fsdp", "ctx", None),
        P("fsdp", "ctx", None),
        P("fsdp"),
        P(),
        P("fsdp", None, "ctx"),
        P("fsdp", None, "ctx"),
        P("fsdp", None, "ctx"),
        P(),
        P(),
        P(),
        P(),
        P(),
        P(),
    )
    out_specs = (
        P("fsdp", "ctx", None),
        P("fsdp", "ctx", None),
        P("fsdp", None, "ctx"),
        P("fsdp", None, "ctx"),
        P("fsdp", None, "ctx"),
        P(),
        P(),
        P(),
        P(),
        P(),
        P(),
    )
    return jax.shard_map(
        on_device, mesh=mesh, in_specs=in_specs, out_specs=out_specs, check_vma=False
    )
```

```python
import functools
import math

import jax
import jax.numpy as jnp
from jax import lax
from jax.experimental import pallas as pl
from jax.experimental.pallas import tpu as pltpu
from jax.sharding import PartitionSpec as P

H = 16
FF = 1280
STEP = 10


norm_eps = 1e-06
beta_first = 0.9
beta_second = 0.95
adam_eps = 1e-08
decay_rate = 0.1
master_rate = 0.05
gain_rate = 2.0
scale_rate = 2.0
score_base = 1.442695041
masked_score = -1e30


def from_behind(block, axis, distance):
    devices = range(lax.axis_size(axis))
    route = [(i - distance, i) for i in devices if i - distance in devices]
    return lax.ppermute(block, axis, route)


def shifted(array, axis, by):
    count = lax.axis_size(axis)
    return lax.ppermute(array, axis, [(i, (i + by) % count) for i in range(count)])


def unit_rows(owners, slot_count):
    unit_count = owners.shape[0]
    unit_order = jnp.arange(unit_count, dtype=jnp.int32)
    same_owner = owners[:, None] == owners[None, :]
    earlier = unit_order[None, :] < unit_order[:, None]
    slot_rank = jnp.sum((same_owner & earlier).astype(jnp.int32), axis=1)
    return owners * slot_count + slot_rank


def inverse_rms(values):
    return lax.rsqrt(jnp.mean(values * values, axis=-1, keepdims=True) + norm_eps)


def norm_back(values, gain, grad_normed):
    inverse = inverse_rms(values)
    scaled = grad_normed * gain
    grad_values = inverse * scaled - values * inverse**3 * jnp.mean(
        scaled * values, axis=-1, keepdims=True
    )
    grad_gain = jnp.sum(grad_normed * values * inverse, axis=(0, 1))
    return (grad_values, grad_gain)


def adam_step(values, moment_one, moment_two, gradient, step_rate, weight_decay):
    moment_one = beta_first * moment_one + (1.0 - beta_first) * gradient
    moment_two = beta_second * moment_two + (1.0 - beta_second) * gradient * gradient
    first_hat = moment_one / (1.0 - beta_first**STEP)
    second_hat = moment_two / (1.0 - beta_second**STEP)
    values = values - step_rate * (
        first_hat / (jnp.sqrt(second_hat) + adam_eps) + weight_decay * values
    )
    return (values, moment_one, moment_two)


def general_layer(
    inputs,
    targets,
    valid_counts,
    owners,
    master,
    first_moment,
    second_moment,
    norm_gains,
    gain_first,
    gain_second,
    query_scale,
    scale_first,
    scale_second,
):
    seq_local, block_rows, width = inputs.shape
    slot_count, head_dim, column_count = master.shape
    ff_blocks = FF // head_dim
    ctx_size = lax.axis_size("ctx")
    ctx_index = lax.axis_index("ctx")
    slot_rows = unit_rows(owners, slot_count)
    owner_table = lax.all_gather(master.astype(jnp.bfloat16), "fsdp", axis=0, tiled=True)
    picked = owner_table[slot_rows]
    weights = lax.all_gather(picked, "ctx", axis=2, tiled=True)
    w_qkv = weights[0 : 3 * H]
    w_out = weights[3 * H : 4 * H]
    w_up = weights[4 * H : 4 * H + ff_blocks]
    w_down = weights[4 * H + ff_blocks :]
    values_in = inputs.astype(jnp.float32)
    normed_b = (values_in * inverse_rms(values_in) * norm_gains[0]).astype(jnp.bfloat16)
    projected = jnp.einsum("sbd,hed->shbe", normed_b, w_qkv, preferred_element_type=jnp.float32)
    query_pre = projected[:, 0:H]
    multiplier = jax.nn.softplus(query_scale) * (score_base / math.sqrt(head_dim))
    query_b = (query_pre * multiplier).astype(jnp.bfloat16)
    key_b = projected[:, H : 2 * H].astype(jnp.bfloat16)
    value_b = projected[:, 2 * H : 3 * H].astype(jnp.bfloat16)
    query_rows = ctx_index * block_rows + jnp.arange(block_rows, dtype=jnp.int32)
    last_row = ctx_index * block_rows + block_rows - 1
    start_state = (
        jnp.full(query_pre.shape[:3], masked_score, jnp.float32),
        jnp.zeros(query_pre.shape[:3], jnp.float32),
        jnp.zeros(query_pre.shape, jnp.float32),
    )
    key_part = lax.all_gather(key_b, "ctx", axis=2, tiled=True)
    value_part = lax.all_gather(value_b, "ctx", axis=2, tiled=True)
    key_count = key_part.shape[2]

    def update(current):
        run_max, run_sum, accum = current
        key_rows = jnp.arange(key_count, dtype=jnp.int32)
        allowed = query_rows[:, None] >= key_rows[None, :]
        scores = jnp.einsum(
            "shqe,shke->shqk", query_b, key_part, preferred_element_type=jnp.float32
        )
        scores = jnp.where(allowed, scores, masked_score)
        new_max = jnp.maximum(run_max, jnp.max(scores, axis=-1))
        attn_probs = jnp.where(allowed, jnp.exp(scores - new_max[..., None]), 0.0)
        run_sum = jnp.sum(attn_probs, axis=-1)
        accum = jnp.einsum(
            "shqk,shke->shqe",
            attn_probs.astype(jnp.bfloat16),
            value_part,
            preferred_element_type=jnp.float32,
        )
        return (new_max, run_sum, accum)

    run_max, run_sum, accum = lax.cond(
        jnp.int32(0) <= last_row, update, lambda current: current, start_state
    )
    attended = accum / run_sum[..., None]
    log_total = run_max + jnp.log(run_sum)
    attended_b = attended.astype(jnp.bfloat16)
    branch = jnp.einsum("shbe,hed->sbd", attended_b, w_out, preferred_element_type=jnp.float32)
    middle = values_in + branch
    normed_mid_b = (middle * inverse_rms(middle) * norm_gains[1]).astype(jnp.bfloat16)
    hidden = jnp.einsum("sbd,fed->sbfe", normed_mid_b, w_up, preferred_element_type=jnp.float32)
    active_b = jax.nn.silu(hidden).astype(jnp.bfloat16)
    block_out = middle + jnp.einsum(
        "sbfe,fed->sbd", active_b, w_down, preferred_element_type=jnp.float32
    )
    seq_length = block_rows * ctx_size
    counted = (query_rows[None, :] >= (seq_length - valid_counts)[:, None]).astype(jnp.float32)
    count_term = jnp.sum(counted)
    out_grad = 2.0 * (block_out - targets.astype(jnp.float32)) * counted[..., None]
    out_grad_b = out_grad.astype(jnp.bfloat16)
    grad_down = jnp.einsum(
        "sbfe,sbd->fed", active_b, out_grad_b, preferred_element_type=jnp.float32
    )
    grad_active = jnp.einsum(
        "sbd,fed->sbfe", out_grad_b, w_down, preferred_element_type=jnp.float32
    )
    sigma = jax.nn.sigmoid(hidden)
    grad_hidden_b = (grad_active * sigma * (1.0 + hidden * (1.0 - sigma))).astype(jnp.bfloat16)
    grad_up = jnp.einsum(
        "sbfe,sbd->fed", grad_hidden_b, normed_mid_b, preferred_element_type=jnp.float32
    )
    grad_normed_mid = jnp.einsum(
        "sbfe,fed->sbd", grad_hidden_b, w_up, preferred_element_type=jnp.float32
    )
    grad_middle_norm, grad_gain_two = norm_back(middle, norm_gains[1], grad_normed_mid)
    grad_middle = out_grad + grad_middle_norm
    grad_middle_b = grad_middle.astype(jnp.bfloat16)
    grad_out = jnp.einsum(
        "shbe,sbd->hed", attended_b, grad_middle_b, preferred_element_type=jnp.float32
    )
    grad_attended_b = jnp.einsum(
        "sbd,hed->shbe", grad_middle_b, w_out, preferred_element_type=jnp.float32
    ).astype(jnp.bfloat16)
    delta = jnp.sum(grad_attended_b.astype(jnp.float32) * attended, axis=-1)

    def block_grads(source, key_cur, value_cur, partial_grads):
        grad_key, grad_value, grad_query = partial_grads
        key_rows = source * block_rows + jnp.arange(block_rows, dtype=jnp.int32)
        allowed = query_rows[:, None] >= key_rows[None, :]
        scores = jnp.einsum("shqe,shke->shqk", query_b, key_cur, preferred_element_type=jnp.float32)
        scores = jnp.where(allowed, scores, masked_score)
        attn_probs = jnp.exp(scores - log_total[..., None])
        grad_value = grad_value + jnp.einsum(
            "shqk,shqe->shke",
            attn_probs.astype(jnp.bfloat16),
            grad_attended_b,
            preferred_element_type=jnp.float32,
        )
        grad_probs = jnp.einsum(
            "shqe,shke->shqk", grad_attended_b, value_cur, preferred_element_type=jnp.float32
        )
        grad_scores_b = (attn_probs * (grad_probs - delta[..., None])).astype(jnp.bfloat16)
        grad_query = grad_query + jnp.einsum(
            "shqk,shke->shqe", grad_scores_b, key_cur, preferred_element_type=jnp.float32
        )
        grad_key = grad_key + jnp.einsum(
            "shqk,shqe->shke", grad_scores_b, query_b, preferred_element_type=jnp.float32
        )
        return (grad_key, grad_value, grad_query)

    zero_heads = jnp.zeros(query_pre.shape, jnp.float32)

    def back_turn(which_turn, current):
        key_cur, value_cur, grad_key, grad_value, grad_query = current
        source = (ctx_index - which_turn) % ctx_size
        grad_key, grad_value, grad_query = lax.cond(
            source <= ctx_index,
            lambda parts: block_grads(source, key_cur, value_cur, parts),
            lambda parts: parts,
            (grad_key, grad_value, grad_query),
        )
        key_cur, value_cur = from_behind((key_cur, value_cur), "ctx", 1)
        grad_key, grad_value = (
            shifted(grad_key.astype(jnp.bfloat16), "ctx", 1).astype(grad_key.dtype),
            shifted(grad_value.astype(jnp.bfloat16), "ctx", 1).astype(grad_value.dtype),
        )
        return (key_cur, value_cur, grad_key, grad_value, grad_query)

    back_state = (key_b, value_b, zero_heads, zero_heads, zero_heads)
    back_state = lax.fori_loop(0, ctx_size, back_turn, back_state)
    grad_key, grad_value, grad_query = (back_state[2], back_state[3], back_state[4])
    grad_proj_b = jnp.concatenate([grad_query * multiplier, grad_key, grad_value], axis=1).astype(
        jnp.bfloat16
    )
    grad_qkv = jnp.einsum(
        "shbe,sbd->hed", grad_proj_b, normed_b, preferred_element_type=jnp.float32
    )
    grad_normed_in = jnp.einsum(
        "shbe,hed->sbd", grad_proj_b, w_qkv, preferred_element_type=jnp.float32
    )
    grad_input_norm, grad_gain_one = norm_back(values_in, norm_gains[0], grad_normed_in)
    input_grad = grad_middle + grad_input_norm
    scale_term = (
        jnp.sum(grad_query * query_pre, axis=(0, 1, 2))
        * (score_base / math.sqrt(head_dim))
        * jax.nn.sigmoid(query_scale)
    )
    unit_grads = jnp.concatenate([grad_qkv, grad_out, grad_up, grad_down], axis=0)
    owner_total = lax.axis_size("fsdp") * slot_count
    table_grads = (
        jnp.zeros((owner_total, head_dim, width), jnp.float32).at[slot_rows].set(unit_grads)
    )
    owned = lax.psum_scatter(
        table_grads.astype(jnp.bfloat16), "fsdp", scatter_dimension=0, tiled=True
    )
    slot_sums = lax.psum_scatter(owned, "ctx", scatter_dimension=2, tiled=True).astype(jnp.float32)
    gain_sums, scale_sums, count = lax.psum(
        (jnp.stack([grad_gain_one, grad_gain_two]), scale_term, count_term), ("ctx", "fsdp")
    )
    new_master, new_first, new_second = adam_step(
        master, first_moment, second_moment, slot_sums / count, master_rate, decay_rate
    )
    new_gains, new_gain_first, new_gain_second = adam_step(
        norm_gains, gain_first, gain_second, gain_sums / count, gain_rate, 0.0
    )
    new_scale, new_scale_first, new_scale_second = adam_step(
        query_scale, scale_first, scale_second, scale_sums / count, scale_rate, 0.0
    )
    return (
        block_out,
        input_grad,
        new_master,
        new_first,
        new_second,
        new_gains,
        new_gain_first,
        new_gain_second,
        new_scale,
        new_scale_first,
        new_scale_second,
    )


def swapped(array, axis, distance):
    return lax.ppermute(
        array, axis, [(i, i ^ distance) for i in range(lax.axis_size(axis))]
    )


def summed(array, axis):
    size = lax.axis_size(axis)
    if size & (size - 1):
        return lax.psum(array, axis)
    distance = 1
    while distance < size:
        array = array + swapped(array, axis, distance)
        distance *= 2
    return array


def one_more(array):
    return swapped(array[0, :16, :128], "ctx", 1)


def dot(left, right, left_dim, right_dim):
    return lax.dot_general(
        left,
        right,
        (((left_dim,), (right_dim,)), ((), ())),
        preferred_element_type=jnp.float32,
    )


def copy_rows_kernel(sizes, offsets, width, bound_ref, place_ref, row_ref, *refs):
    sources = refs[: len(offsets)]
    outs = refs[-2 - len(sizes) : -2]
    rows, sems = refs[-2:]
    for number, (source, offset) in enumerate(zip(sources, offsets)):

        @pl.loop(bound_ref[number], bound_ref[number + 1])
        def copy_row(i, source=source, offset=offset):
            pltpu.make_async_copy(
                source.at[row_ref[i], :, pl.ds(offset, width)],
                rows.at[place_ref[i]],
                sems.at[len(sizes)],
            ).start()

    pltpu.make_async_copy(rows, rows, sems.at[len(sizes)]).wait()
    copies, start = [], 0
    for place, (out, size) in enumerate(zip(outs, sizes)):
        copies.append(
            pltpu.make_async_copy(rows.at[pl.ds(start, size)], out, sems.at[place])
        )
        start += size
    for copy in copies:
        copy.start()
    for copy in copies:
        copy.wait()


def copy_plan(pick_from, pick_row, source_count):
    number = jnp.arange(pick_from.shape[0], dtype=jnp.int32)
    before = pick_from[None, :] < pick_from[:, None]
    same = (pick_from[None, :] == pick_from[:, None]) & (number[None, :] < number[:, None])
    rank = jnp.sum((before | same).astype(jnp.int32), axis=1)
    here = rank[None, :] == number[:, None]
    place = jnp.sum(jnp.where(here, number[None, :], 0), axis=1)
    row = jnp.sum(jnp.where(here, pick_row[None, :], 0), axis=1)
    bounds = jnp.sum(
        (pick_from[None, :] < jnp.arange(source_count + 1)[:, None]).astype(jnp.int32), axis=1
    )
    return (bounds.astype(jnp.int32), place.astype(jnp.int32), row.astype(jnp.int32))


def copy_rows(sources, offsets, width, plan, sizes, events=()):
    rows = sources[0].shape[1]
    total = sum(sizes)
    return pl.pallas_call(
        functools.partial(copy_rows_kernel, tuple(sizes), tuple(offsets), width),
        out_shape=[jax.ShapeDtypeStruct((size, rows, width), sources[0].dtype) for size in sizes],
        grid_spec=pltpu.PrefetchScalarGridSpec(
            num_scalar_prefetch=3,
            grid=(1,),
            in_specs=[pl.BlockSpec(memory_space=pl.ANY)] * (len(sources) + len(events)),
            out_specs=[pl.BlockSpec(memory_space=pl.ANY)] * len(sizes),
            scratch_shapes=[
                pltpu.VMEM((total, rows, width), sources[0].dtype),
                pltpu.SemaphoreType.DMA((len(sizes) + 1,)),
            ],
        ),
        compiler_params=pltpu.CompilerParams(vmem_limit_bytes=40 * 1024 * 1024),
        cost_estimate=pl.CostEstimate(flops=0, bytes_accessed=1024, transcendentals=0),
        name="copy_rows",
    )(*plan, *sources, *events)


def place_pieces_kernel(places, count_outs, *refs):
    pieces = refs[: len(places)]
    outs = refs[-1 - count_outs : -1]
    sems = refs[-1]
    copies = []
    for number, (piece, place) in enumerate(zip(pieces, places)):
        first, count, begin, size, column, out, row = place
        copies.append(
            pltpu.make_async_copy(
                piece.at[pl.ds(first, count), :, pl.ds(begin, size)],
                outs[out].at[pl.ds(row, count), :, pl.ds(column, size)],
                sems.at[number],
            )
        )
    for copy in copies:
        copy.start()
    for copy in copies:
        copy.wait()


def place_pieces(pieces, places, shapes, events=()):
    return pl.pallas_call(
        functools.partial(place_pieces_kernel, tuple(places), len(shapes)),
        out_shape=[jax.ShapeDtypeStruct(shape, pieces[0].dtype) for shape in shapes],
        in_specs=[pl.BlockSpec(memory_space=pl.ANY)] * (len(pieces) + len(events)),
        out_specs=[pl.BlockSpec(memory_space=pltpu.VMEM)] * len(shapes),
        scratch_shapes=[pltpu.SemaphoreType.DMA((len(pieces),))],
        compiler_params=pltpu.CompilerParams(vmem_limit_bytes=40 * 1024 * 1024),
        cost_estimate=pl.CostEstimate(flops=0, bytes_accessed=1024, transcendentals=0),
        name="place_pieces",
    )(*pieces, *events)


def attend_kernel(blocks, order_ref, q_ref, k_ref, v_ref, out_ref, log_ref, key_rows, value_cols):
    size = q_ref.shape[1] // blocks
    at = [pl.multiple_of(order_ref[i] * size, size) for i in range(blocks)]
    for i in range(blocks):
        key_rows[i * size : (i + 1) * size, :] = k_ref[:, pl.ds(at[i], size)].T
        value_cols[:, i * size : (i + 1) * size] = v_ref[:, pl.ds(at[i], size)]
    key_pos = lax.broadcasted_iota(jnp.int32, (size, size), 0)
    query_pos = lax.broadcasted_iota(jnp.int32, (size, size), 1)
    seen = key_pos <= query_pos
    for i in range(blocks):
        past = i * size
        query = q_ref[:, pl.ds(at[i], size)]
        near = jnp.where(
            seen, dot(key_rows[past : past + size, :], query, 1, 0), masked_score
        )
        top = jnp.max(near, axis=0, keepdims=True)
        if i:
            far = dot(key_rows[:past, :], query, 1, 0)
            top = jnp.maximum(top, jnp.max(far, axis=0, keepdims=True))
        near = jnp.exp(near - top)
        total = jnp.sum(near, axis=0, keepdims=True)
        value = dot(value_cols[:, past : past + size], near.astype(jnp.bfloat16), 1, 0)
        if i:
            far = jnp.exp(far - top)
            total = total + jnp.sum(far, axis=0, keepdims=True)
            value = value + dot(value_cols[:, :past], far.astype(jnp.bfloat16), 1, 0)
        out_ref[:, pl.ds(at[i], size)] = (value / total).astype(jnp.bfloat16)
        log_ref[0, :, pl.ds(at[i], size)] = top + jnp.log(total)


def attend(projected, order, heads, head_dim):
    tokens = projected.shape[1]
    blocks = order.shape[0]

    def part(first):
        return pl.BlockSpec((head_dim, tokens), lambda h, order, first=first: (first + h, 0))

    return pl.pallas_call(
        functools.partial(attend_kernel, blocks),
        out_shape=[
            jax.ShapeDtypeStruct((heads * head_dim, tokens), jnp.bfloat16),
            jax.ShapeDtypeStruct((heads, 1, tokens), jnp.float32),
        ],
        grid_spec=pltpu.PrefetchScalarGridSpec(
            num_scalar_prefetch=1,
            grid=(heads,),
            in_specs=[part(0), part(heads), part(2 * heads)],
            out_specs=[
                pl.BlockSpec((head_dim, tokens), lambda h, order: (h, 0)),
                pl.BlockSpec((1, 1, tokens), lambda h, order: (h, 0, 0)),
            ],
            scratch_shapes=[
                pltpu.VMEM((tokens, head_dim), jnp.bfloat16),
                pltpu.VMEM((head_dim, tokens), jnp.bfloat16),
            ],
        ),
        compiler_params=pltpu.CompilerParams(vmem_limit_bytes=40 * 1024 * 1024),
        cost_estimate=pl.CostEstimate(
            flops=heads * tokens * tokens * head_dim * 4,
            bytes_accessed=heads * head_dim * tokens * 8,
            transcendentals=heads * tokens * tokens,
        ),
        name="attend",
    )(order, projected, projected, projected)


def attend_back_kernel(
    blocks,
    order_ref,
    q_ref,
    k_ref,
    v_ref,
    grad_ref,
    log_ref,
    scale_ref,
    *refs,
):
    out_ref, term_ref, key_rows, key_cols, value_rows, key_sum, value_sum = refs[-7:]
    size = q_ref.shape[1] // blocks
    at = [pl.multiple_of(order_ref[i] * size, size) for i in range(blocks)]
    for i in range(blocks):
        here = slice(i * size, (i + 1) * size)
        key = k_ref[:, pl.ds(at[i], size)]
        key_rows[here, :] = key.T
        key_cols[:, here] = key
        value_rows[here, :] = v_ref[:, pl.ds(at[i], size)].T
    key_sum[...] = jnp.zeros_like(key_sum)
    value_sum[...] = jnp.zeros_like(value_sum)
    key_pos = lax.broadcasted_iota(jnp.int32, (size, size), 0)
    query_pos = lax.broadcasted_iota(jnp.int32, (size, size), 1)
    seen = key_pos <= query_pos
    term = jnp.zeros((q_ref.shape[0], 1), jnp.float32)
    for i in range(blocks):
        past = i * size
        query = q_ref[:, pl.ds(at[i], size)]
        grad = grad_ref[:, pl.ds(at[i], size)]
        log_total = log_ref[0, :, pl.ds(at[i], size)]
        parts = [(past, size)] + ([(0, past)] if i else [])
        probs, grads = [], []
        delta = jnp.zeros((1, size), jnp.float32)
        for first, count in parts:
            prob = jnp.exp(dot(key_rows[first : first + count, :], query, 1, 0) - log_total)
            if first == past:
                prob = jnp.where(seen, prob, 0.0)
            grad_prob = dot(value_rows[first : first + count, :], grad, 1, 0)
            delta = delta + jnp.sum(prob * grad_prob, axis=0, keepdims=True)
            probs.append(prob)
            grads.append(grad_prob)
        grad_query = jnp.zeros(query.shape, jnp.float32)
        for (first, count), prob, grad_prob in zip(parts, probs, grads):
            cols = slice(first, first + count)
            grad_score = (prob * (grad_prob - delta)).astype(jnp.bfloat16)
            value_sum[:, cols] += dot(grad, prob.astype(jnp.bfloat16), 1, 1)
            key_sum[:, cols] += dot(query, grad_score, 1, 1)
            grad_query = grad_query + dot(key_cols[:, cols], grad_score, 1, 0)
        term = term + jnp.sum(
            grad_query * query.astype(jnp.float32), axis=1, keepdims=True
        )
        out_ref[0, :, pl.ds(at[i], size)] = (grad_query * scale_ref[...]).astype(jnp.bfloat16)
    for i in range(blocks):
        here = slice(i * size, (i + 1) * size)
        out_ref[1, :, pl.ds(at[i], size)] = key_sum[:, here].astype(jnp.bfloat16)
        out_ref[2, :, pl.ds(at[i], size)] = value_sum[:, here].astype(jnp.bfloat16)
    term_ref[0] = term


def attend_back(
    projected, grad_attended, log_total, multiplier, order, heads, head_dim, events=()
):
    tokens = projected.shape[1]
    blocks = order.shape[0]

    def part(first):
        return pl.BlockSpec((head_dim, tokens), lambda h, order, first=first: (first + h, 0))

    return pl.pallas_call(
        functools.partial(attend_back_kernel, blocks),
        out_shape=[
            jax.ShapeDtypeStruct((3, heads * head_dim, tokens), jnp.bfloat16),
            jax.ShapeDtypeStruct((heads, head_dim, 1), jnp.float32),
        ],
        grid_spec=pltpu.PrefetchScalarGridSpec(
            num_scalar_prefetch=1,
            grid=(heads,),
            in_specs=[
                part(0),
                part(heads),
                part(2 * heads),
                part(0),
                pl.BlockSpec((1, 1, tokens), lambda h, order: (h, 0, 0)),
                pl.BlockSpec((head_dim, 1), lambda h, order: (0, 0)),
            ]
            + [pl.BlockSpec(memory_space=pl.ANY)] * len(events),
            out_specs=[
                pl.BlockSpec((3, head_dim, tokens), lambda h, order: (0, h, 0)),
                pl.BlockSpec((1, head_dim, 1), lambda h, order: (h, 0, 0)),
            ],
            scratch_shapes=[
                pltpu.VMEM((tokens, head_dim), jnp.bfloat16),
                pltpu.VMEM((head_dim, tokens), jnp.bfloat16),
                pltpu.VMEM((tokens, head_dim), jnp.bfloat16),
                pltpu.VMEM((head_dim, tokens), jnp.float32),
                pltpu.VMEM((head_dim, tokens), jnp.float32),
            ],
        ),
        compiler_params=pltpu.CompilerParams(vmem_limit_bytes=48 * 1024 * 1024),
        cost_estimate=pl.CostEstimate(
            flops=heads * tokens * tokens * head_dim * 10,
            bytes_accessed=heads * head_dim * tokens * 14,
            transcendentals=heads * tokens * tokens,
        ),
        name="attend_back",
    )(order, projected, projected, projected, grad_attended, log_total, multiplier, *events)


def paired_layer(
    inputs,
    targets,
    valid_counts,
    owners,
    master,
    first_moment,
    second_moment,
    norm_gains,
    gain_first,
    gain_second,
    query_scale,
    scale_first,
    scale_second,
):
    bf16 = jnp.bfloat16
    f32 = jnp.float32
    seq_local, block_rows, width = inputs.shape
    slot_count, head_dim, column_count = master.shape
    ff_blocks = FF // head_dim
    owner_count = lax.axis_size("fsdp")
    device = lax.axis_index("ctx")
    chip, core = device // 2, device % 2
    owner_here = lax.axis_index("fsdp")
    low_here = owner_here % 2
    high_here = owner_here // 2
    high_count = owner_count // 2
    high_distances = range(1, high_count)
    half_width = width // 2
    half_slots = slot_count // 2
    half_rows = seq_local * block_rows
    half_heads = H // 2
    half_blocks = ff_blocks // 2
    set_units = 4 * half_heads + 2 * half_blocks
    first_chip, first_core = chip == 0, core == 0

    def columns_here(array):
        return jnp.where(first_chip, array, jnp.roll(array, half_width, axis=-1))

    def sequence_rows(array):
        own = jnp.where(first_chip, array[0], array[1])
        got = swapped(jnp.where(first_chip, array[1], array[0]), "ctx", 2)
        return jnp.where(
            first_chip, jnp.concatenate([own, got]), jnp.concatenate([got, own])
        )

    def rows_home(array):
        array = columns_here(array)
        first, last = array[:block_rows], array[block_rows:]
        own = jnp.where(first_chip, first, last)
        got = swapped(jnp.where(first_chip, last, first).astype(bf16), "ctx", 2).astype(f32)
        return jnp.where(first_chip, jnp.stack([own, got]), jnp.stack([got, own]))

    slot_rows = unit_rows(owners, slot_count)
    unit_total = owners.shape[0]
    kind_sizes = [H, H, H, H, ff_blocks, ff_blocks]
    kind_starts = [sum(kind_sizes[:i]) for i in range(6)]

    def unit_list(kinds, which):
        return jnp.concatenate(
            [
                kind_starts[k] + which * (kind_sizes[k] // 2) + jnp.arange(kind_sizes[k] // 2)
                for k in kinds
            ]
        ).astype(jnp.int32)

    wanted = jnp.concatenate(
        [unit_list(range(6), core), unit_list((4, 5), 1 - core)]
    )
    wanted_rows = slot_rows[wanted]
    wanted_owner, wanted_slot = wanted_rows // slot_count, wanted_rows % slot_count
    weight_from = 2 * (wanted_slot // half_slots != core) + (wanted_owner % 2 != low_here)
    weight_from = weight_from.astype(jnp.int32)
    weight_row = ((wanted_owner // 2) ^ high_here) * half_slots + wanted_slot % half_slots
    weight_plan = copy_plan(weight_from, weight_row, 4)
    weight_sizes = [3 * half_heads, half_heads + 2 * half_blocks, 2 * half_blocks]

    chunks = [(0, 128), (128, 128), (256, 256)]
    lead = 512
    tail = half_width - lead
    shard = master.astype(bf16)
    own_half = jnp.where(first_core, shard[:half_slots], shard[half_slots:])
    got_half = swapped(jnp.where(first_core, shard[half_slots:], shard[:half_slots]), "ctx", 1)
    shard = jnp.where(
        first_core,
        jnp.concatenate([own_half, got_half], axis=2),
        jnp.concatenate([got_half, own_half], axis=2),
    )
    shard, inputs, targets = lax.optimization_barrier((shard, inputs, targets))
    values_b = columns_here(sequence_rows(inputs))
    targets_b = columns_here(sequence_rows(targets))
    shard_last = shard[:, :, lead:]
    shards = [shard[:, :, start : start + size] for start, size in chunks]
    shards.append(jnp.concatenate([shard_last, swapped(shard_last, "ctx", 2)], axis=2))
    highs, lows, firsts = [], [], []
    for number, part in enumerate(shards):
        if number:
            part, gathered = lax.optimization_barrier((part, gathered))
            highs[-1] = gathered
        pieces = [part] + [swapped(part, "fsdp", 2 * d) for d in high_distances]
        firsts.append(pieces[1])
        gathered = jnp.concatenate(pieces)
        highs.append(gathered)
    own_units, rest_units, far_units = weight_sizes
    near_units = own_units + rest_units

    def pick_units(number, sizes, events):
        high, low = highs[number], lows[number]
        sources = [high, low, swapped(high, "ctx", 1), swapped(low, "ctx", 1)]
        return copy_rows(sources, [0] * 4, high.shape[2], weight_plan, sizes, events)

    lows.append(swapped(highs[0], "fsdp", 1))
    lows[0], highs[1] = lax.optimization_barrier((lows[0], highs[1]))
    near_one, far_one = pick_units(0, [near_units, far_units], [])
    got_one = swapped(near_one, "ctx", 2)
    highs[1], far_one = lax.optimization_barrier((highs[1], far_one))
    highs[2], firsts[2] = lax.optimization_barrier((highs[2], one_more(firsts[2])))
    for number in range(1, 4):
        if number == 3:
            near_two, far_two = pick_units(
                1, [near_units, far_units], [values_b, one_more(got_one)]
            )
            highs[3], far_two = lax.optimization_barrier((highs[3], far_two))
        if number > 1:
            highs[number], lows[-1] = lax.optimization_barrier((highs[number], lows[-1]))
        lows.append(swapped(highs[number], "fsdp", 1))
    got_two = swapped(near_two, "ctx", 2)
    qkv_three, rest_three, far_three = pick_units(2, weight_sizes, [targets_b, got_two])
    qkv_got = swapped(qkv_three, "ctx", 2)
    rest_three, qkv_got = lax.optimization_barrier((rest_three, qkv_got))
    rest_got = swapped(rest_three, "ctx", 2)
    qkv_last, rest_last, far_last = pick_units(3, weight_sizes, [one_more(qkv_got)])

    def columns_of(owns, gots, last):
        pieces = [(last, 0, tail, lead), (last, tail, tail, half_width + lead)]
        for (start, size), own, got in zip(chunks, owns, gots):
            pieces += [(own, 0, size, start), (got, 0, size, half_width + start)]
        return pieces

    def placed(pieces, from_end, count, out, row):
        return [
            (piece.shape[0] - from_end if from_end else 0, count, *columns, out, row)
            for piece, *columns in pieces
        ]

    qkv_pieces = columns_of(
        [near_one, near_two, qkv_three], [got_one, got_two, qkv_got], qkv_last
    )
    rest_pieces = columns_of(
        [near_one, near_two, rest_three], [got_one, got_two, rest_got], rest_last
    )
    far_pieces = columns_of(
        [far_one, far_two, far_three],
        [swapped(got, "ctx", 1) for got in (got_one, got_two, rest_got)],
        far_last,
    )
    (w_qkv,) = place_pieces(
        [piece for piece, *_ in qkv_pieces],
        placed(qkv_pieces, 0, own_units, 0, 0),
        [(own_units, head_dim, width)],
    )
    w_qkv = w_qkv.reshape(-1, width)

    gains = columns_here(norm_gains)
    values_in = values_b.astype(f32)
    normed_own = (values_in * inverse_rms(values_in) * gains[0]).astype(bf16)
    normed_b = jnp.concatenate([normed_own, swapped(normed_own, "ctx", 1)])
    base = score_base / math.sqrt(head_dim)
    multiplier = jax.nn.softplus(query_scale) * base
    row_scale = jnp.concatenate(
        [jnp.tile(multiplier, half_heads), jnp.ones((2 * half_heads * head_dim,), f32)]
    )
    projected = (dot(w_qkv, normed_b, 1, 1) * row_scale[:, None]).astype(bf16)
    positions = jnp.arange(4, dtype=jnp.int32)
    order = jnp.where(positions % 2 == core, 0, 2) + positions // 2
    order = order.astype(jnp.int32)
    attended, log_total = attend(projected, order, half_heads, head_dim)
    (w_out,) = place_pieces(
        [piece for piece, *_ in rest_pieces],
        placed(rest_pieces, rest_units, half_heads, 0, 0),
        [(half_heads, head_dim, width)],
        [log_total],
    )
    mlp_pieces, mlp_places = [], []
    for row, pieces in ((0, rest_pieces), (half_blocks, far_pieces)):
        for kind in range(2):
            mlp_pieces += [piece for piece, *_ in pieces]
            mlp_places += placed(pieces, (2 - kind) * half_blocks, half_blocks, kind, row)
    w_up, w_down = place_pieces(
        mlp_pieces, mlp_places, [(ff_blocks, head_dim, width)] * 2, [log_total]
    )
    w_out = w_out.reshape(-1, width)
    w_up = w_up.reshape(-1, width)
    w_down = w_down.reshape(-1, width)
    branch_far = dot(attended[:, half_rows:], w_out, 0, 0).astype(bf16)
    branch_got = swapped(branch_far, "ctx", 1)
    branch_own = dot(attended[:, :half_rows], w_out, 0, 0)
    middle = values_in + (branch_own + branch_got.astype(f32))
    normed_mid_b = (middle * inverse_rms(middle) * gains[1]).astype(bf16)
    hidden = dot(normed_mid_b, w_up, 1, 1)
    active_b = jax.nn.silu(hidden).astype(bf16)
    block_out = middle + dot(active_b, w_down, 1, 0)
    seq_length = 2 * half_rows
    row = jnp.arange(half_rows, dtype=jnp.int32)
    row_pos = (core + 2 * (row // block_rows)) * block_rows + row % block_rows
    valid = jnp.where(first_chip, valid_counts[0], valid_counts[1])
    counted = (row_pos >= seq_length - valid).astype(f32)
    count_term = jnp.sum(counted)

    out_grad = 2.0 * (block_out - targets_b.astype(f32)) * counted[:, None]
    out_grad_b = out_grad.astype(bf16)
    grad_active = dot(out_grad_b, w_down, 1, 1)
    sigma = jax.nn.sigmoid(hidden)
    grad_hidden_b = (grad_active * sigma * (1.0 + hidden * (1.0 - sigma))).astype(bf16)
    grad_normed_mid = dot(grad_hidden_b, w_up, 1, 0)
    inverse = inverse_rms(middle)
    scaled = grad_normed_mid * gains[1]
    grad_middle = out_grad + (
        inverse * scaled
        - middle * inverse**3 * jnp.mean(scaled * middle, axis=-1, keepdims=True)
    )
    grad_gain_two = jnp.sum(grad_normed_mid * middle * inverse, axis=0)
    grad_middle_own = grad_middle.astype(bf16)
    grad_middle_got = swapped(grad_middle_own, "ctx", 1)
    far_blocks = half_blocks * head_dim
    wide = slice(half_width + 256, half_width + lead)
    slim = slice(half_width, half_width + 256)
    block_grads = []
    for left, right in ((grad_hidden_b, normed_mid_b), (active_b, out_grad_b)):
        got = swapped(dot(left[:, far_blocks:], right, 0, 0).astype(bf16), "ctx", 1)
        total = dot(left[:, :far_blocks], right, 0, 0) + got.astype(f32)
        block_grads.append(total.astype(bf16).reshape(half_blocks, head_dim, width))
    block_grads = jnp.concatenate(block_grads)
    grad_middle_got, block_grads = lax.optimization_barrier((grad_middle_got, block_grads))
    grad_middle_b = jnp.concatenate([grad_middle_own, grad_middle_got])
    grad_attended = dot(w_out, grad_middle_b, 1, 1).astype(bf16)
    head_grads = dot(attended, grad_middle_b, 1, 0).astype(bf16)
    head_grads = head_grads.reshape(half_heads, head_dim, width)

    def early_columns(columns):
        return jnp.concatenate([head_grads[:, :, columns], block_grads[:, :, columns]])

    early_wide, early_slim = early_columns(wide), early_columns(slim)
    wide_got = swapped(early_wide, "ctx", 2)

    def last_columns(array):
        return jnp.concatenate(
            [array[..., lead:half_width], array[..., half_width + lead :]], axis=-1
        )

    early_last = jnp.concatenate([last_columns(head_grads), last_columns(block_grads)])
    grad_proj, grad_scale = attend_back(
        projected,
        grad_attended,
        log_total,
        multiplier[:, None],
        order,
        half_heads,
        head_dim,
        [early_wide, early_slim, early_last],
    )
    grad_proj = grad_proj.reshape(-1, grad_proj.shape[2])
    scale_term = (
        jnp.sum(grad_scale[:, :, 0], axis=0) / multiplier * base * jax.nn.sigmoid(query_scale)
    )

    low_order = jnp.stack([low_here, 1 - low_here])
    table_slots = (
        (2 * (jnp.array([0, 2, 1, 3]) ^ high_here)[None, :, None] + low_order[:, None, None])
        * slot_count
        + core * half_slots
        + jnp.arange(half_slots)[None, None, :]
    ).reshape(-1)
    holds = table_slots[:, None] == slot_rows[None, :]
    unit_order = jnp.arange(unit_total, dtype=jnp.int32)
    slot_unit = jnp.sum(jnp.where(holds, unit_order[None, :] + 1, 0), axis=1) - 1
    kind = jnp.where(
        slot_unit < 4 * H, slot_unit // H, 4 + (slot_unit - 4 * H) // ff_blocks
    )
    kind_size = jnp.where(kind < 4, H, ff_blocks)
    within = jnp.where(kind < 4, slot_unit % H, (slot_unit - 4 * H) % ff_blocks)
    other_set = (within // (kind_size // 2) != core).astype(jnp.int32)
    rank = within % (kind_size // 2)
    grad_row = rank + jnp.where(
        kind <= 3, kind * half_heads, 4 * half_heads + (kind - 4) * half_blocks
    )
    empty = slot_unit < 0
    grad_from = jnp.where(empty, 2, other_set).astype(jnp.int32)
    grad_row = jnp.where(empty, 0, grad_row).astype(jnp.int32)
    grad_plan = copy_plan(grad_from, grad_row, 3)
    zero = jnp.zeros((1, head_dim, 256), bf16)

    def pick_table(own, got, offset, size, events=()):
        return copy_rows(
            [own, got, zero],
            [offset, offset, 0],
            size,
            grad_plan,
            [high_count * half_slots] * 2,
            events,
        )

    def added(own, got):
        return (own.astype(f32) + got.astype(f32)).astype(bf16)

    def table_sums(keep, got):
        half = 2 * half_slots
        return (added(keep[:half], got[:half]), added(keep[half:], got[half:]))

    def pair_sums(tables, got):
        own = tables[0]
        return (
            added(own[:half_slots], got[:half_slots]),
            added(own[half_slots:], got[half_slots:]),
        )

    def proj_grad(columns):
        return dot(grad_proj, columns, 1, 0).astype(bf16).reshape(-1, head_dim, columns.shape[1])

    def chip_sum(start, proj_got, early_got):
        near = slice(start, start + 256)
        parts = [
            (proj_grad(normed_b[:, near]), proj_got),
            (head_grads[:, :, near], early_got[:half_heads]),
            (block_grads[:, :, near], early_got[half_heads:]),
        ]
        return jnp.concatenate(
            [(own.astype(f32) + got.astype(f32)).astype(bf16) for own, got in parts]
        )

    proj_last = proj_grad(last_columns(normed_b))
    early_slim, proj_last, wide_got = lax.optimization_barrier((early_slim, proj_last, wide_got))
    slim_got = swapped(early_slim, "ctx", 2)
    total_last = jnp.concatenate([proj_last, early_last])
    wide_far = proj_grad(normed_b[:, wide])
    wide_proj = swapped(wide_far, "ctx", 2)
    keep_last, send_last = pick_table(
        total_last, swapped(total_last, "ctx", 1), 0, 256, [wide_far]
    )
    low_last = swapped(send_last, "fsdp", 1)
    keep_last, grad_proj = lax.optimization_barrier((keep_last, grad_proj))
    slim_far = proj_grad(normed_b[:, slim])
    low_last, wide_proj, slim_far, slim_got = lax.optimization_barrier(
        (low_last, wide_proj, slim_far, slim_got)
    )
    slim_proj = swapped(slim_far, "ctx", 2)
    total = chip_sum(256, wide_proj, wide_got)
    keep_three, send_three = pick_table(total, swapped(total, "ctx", 1), 0, 256)
    low_three = swapped(send_three, "fsdp", 1)
    low_last, keep_three, grad_proj = lax.optimization_barrier((low_last, keep_three, grad_proj))
    tables_last = table_sums(keep_last, low_last)
    pair_last = swapped(tables_last[1], "fsdp", 2)
    normed_far = dot(grad_proj[:, half_rows:], w_qkv, 0, 0).astype(bf16)
    normed_got = swapped(normed_far, "ctx", 1)
    low_three, slim_proj = lax.optimization_barrier((low_three, slim_proj))
    total = chip_sum(0, slim_proj, slim_got)
    total_got = swapped(total, "ctx", 1)
    keep_two, send_two = pick_table(total, total_got, 128, 128, [tables_last[1], normed_far])
    low_two = swapped(send_two, "fsdp", 1)
    keep_two, grad_proj, normed_got, low_three, pair_last = lax.optimization_barrier(
        (keep_two, grad_proj, normed_got, low_three, pair_last)
    )
    owned_last = pair_sums(tables_last, pair_last)
    owner_last = swapped(owned_last[1], "fsdp", 4)
    tables_three = table_sums(keep_three, low_three)
    pair_three = swapped(tables_three[1], "fsdp", 2)
    keep_one, send_one = pick_table(
        total, total_got, 0, 128, [low_two, owned_last[1], tables_three[1]]
    )

    grad_normed_in = dot(grad_proj[:, :half_rows], w_qkv, 0, 0) + normed_got.astype(f32)
    inverse = inverse_rms(values_in)
    scaled = grad_normed_in * gains[0]
    input_grad = grad_middle + (
        inverse * scaled
        - values_in * inverse**3 * jnp.mean(scaled * values_in, axis=-1, keepdims=True)
    )
    grad_gain_one = jnp.sum(grad_normed_in * values_in * inverse, axis=0)

    gain_terms = columns_here(jnp.stack([grad_gain_one, grad_gain_two]))
    small = jnp.concatenate([gain_terms.reshape(-1), scale_term, count_term[None]])
    small = jnp.pad(small, (0, -small.shape[0] % 1024))
    low_one = swapped(send_one, "fsdp", 1)
    keep_one, small, low_two, pair_three, owner_last = lax.optimization_barrier(
        (keep_one, small, low_two, pair_three, owner_last)
    )
    tables_two = table_sums(keep_two, low_two)
    pair_two = swapped(tables_two[1], "fsdp", 2)
    owned_three = pair_sums(tables_three, pair_three)
    owner_three = swapped(owned_three[1], "fsdp", 4)
    small = small + swapped(small, "fsdp", 1)
    low_one, pair_two, small, block_out, owner_three = lax.optimization_barrier(
        (low_one, pair_two, small, block_out, owner_three)
    )
    tables_one = table_sums(keep_one, low_one)
    pair_one = swapped(tables_one[1], "fsdp", 2)
    owned_two = pair_sums(tables_two, pair_two)
    owner_two = swapped(owned_two[1], "fsdp", 4)
    small = small + swapped(small, "fsdp", 2)
    pair_one, owner_two, small = lax.optimization_barrier((pair_one, owner_two, small))
    owned_one = pair_sums(tables_one, pair_one)
    owner_one = swapped(owned_one[1], "fsdp", 4)
    small_got = swapped(small, "fsdp", 4)
    owner_one, small_got = lax.optimization_barrier((owner_one, small_got))
    small = summed(small + small_got, "ctx")
    gain_sums = small[: 2 * width].reshape(2, width)
    scale_sums = small[2 * width : 2 * width + head_dim]
    count = small[2 * width + head_dim]

    owned_last = added(owned_last[0], owner_last)
    owned_got = swapped(owned_last[:, :, tail:], "ctx", 2)
    owned = [
        added(owned_one[0], owner_one),
        added(owned_two[0], owner_two),
        added(owned_three[0], owner_three),
        added(owned_last[:, :, :tail], owned_got),
    ]
    owned = jnp.concatenate(owned, axis=2).reshape(half_slots, head_dim, 2, column_count)
    kept = jnp.where(first_core, owned[:, :, 0], owned[:, :, 1])
    sent = swapped(jnp.where(first_core, owned[:, :, 1], owned[:, :, 0]), "ctx", 1)
    slot_sums = jnp.where(
        first_core, jnp.concatenate([kept, sent]), jnp.concatenate([sent, kept])
    ).astype(f32)
    new_master, new_first, new_second = adam_step(
        master, first_moment, second_moment, slot_sums / count, master_rate, decay_rate
    )
    new_gains, new_gain_first, new_gain_second = adam_step(
        norm_gains, gain_first, gain_second, gain_sums / count, gain_rate, 0.0
    )
    new_scale, new_scale_first, new_scale_second = adam_step(
        query_scale, scale_first, scale_second, scale_sums / count, scale_rate, 0.0
    )
    return (
        rows_home(block_out),
        rows_home(input_grad),
        new_master,
        new_first,
        new_second,
        new_gains,
        new_gain_first,
        new_gain_second,
        new_scale,
        new_scale_first,
        new_scale_second,
    )


def on_device(*arguments):
    paired = (
        lax.axis_size("ctx") == 4
        and lax.axis_size("fsdp") == 8
        and arguments[0].shape[0] == 2
    )
    return (paired_layer if paired else general_layer)(*arguments)


def solution(mesh):
    in_specs = (
        P("fsdp", "ctx", None),
        P("fsdp", "ctx", None),
        P("fsdp"),
        P(),
        P("fsdp", None, "ctx"),
        P("fsdp", None, "ctx"),
        P("fsdp", None, "ctx"),
        P(),
        P(),
        P(),
        P(),
        P(),
        P(),
    )
    out_specs = (
        P("fsdp", "ctx", None),
        P("fsdp", "ctx", None),
        P("fsdp", None, "ctx"),
        P("fsdp", None, "ctx"),
        P("fsdp", None, "ctx"),
        P(),
        P(),
        P(),
        P(),
        P(),
        P(),
    )
    return jax.shard_map(
        on_device, mesh=mesh, in_specs=in_specs, out_specs=out_specs, check_vma=False
    )
```

```python
import functools
import math

import jax
import jax.numpy as jnp
from jax import lax
from jax.experimental import pallas as pl
from jax.experimental.pallas import tpu as pltpu
from jax.sharding import PartitionSpec as P

H = 16
FF = 1280
STEP = 10


norm_eps = 1e-06
beta_first = 0.9
beta_second = 0.95
adam_eps = 1e-08
decay_rate = 0.1
master_rate = 0.05
gain_rate = 2.0
scale_rate = 2.0
score_base = 1.442695041
masked_score = -1e30


def from_behind(block, axis, distance):
    devices = range(lax.axis_size(axis))
    route = [(i - distance, i) for i in devices if i - distance in devices]
    return lax.ppermute(block, axis, route)


def shifted(array, axis, by):
    count = lax.axis_size(axis)
    return lax.ppermute(array, axis, [(i, (i + by) % count) for i in range(count)])


def unit_rows(owners, slot_count):
    unit_count = owners.shape[0]
    unit_order = jnp.arange(unit_count, dtype=jnp.int32)
    same_owner = owners[:, None] == owners[None, :]
    earlier = unit_order[None, :] < unit_order[:, None]
    slot_rank = jnp.sum((same_owner & earlier).astype(jnp.int32), axis=1)
    return owners * slot_count + slot_rank


def inverse_rms(values):
    return lax.rsqrt(jnp.mean(values * values, axis=-1, keepdims=True) + norm_eps)


def norm_back(values, gain, grad_normed):
    inverse = inverse_rms(values)
    scaled = grad_normed * gain
    grad_values = inverse * scaled - values * inverse**3 * jnp.mean(
        scaled * values, axis=-1, keepdims=True
    )
    grad_gain = jnp.sum(grad_normed * values * inverse, axis=(0, 1))
    return (grad_values, grad_gain)


def adam_step(values, moment_one, moment_two, gradient, step_rate, weight_decay):
    moment_one = beta_first * moment_one + (1.0 - beta_first) * gradient
    moment_two = beta_second * moment_two + (1.0 - beta_second) * gradient * gradient
    first_hat = moment_one / (1.0 - beta_first**STEP)
    second_hat = moment_two / (1.0 - beta_second**STEP)
    values = values - step_rate * (
        first_hat / (jnp.sqrt(second_hat) + adam_eps) + weight_decay * values
    )
    return (values, moment_one, moment_two)


def general_layer(
    inputs,
    targets,
    valid_counts,
    owners,
    master,
    first_moment,
    second_moment,
    norm_gains,
    gain_first,
    gain_second,
    query_scale,
    scale_first,
    scale_second,
):
    seq_local, block_rows, width = inputs.shape
    slot_count, head_dim, column_count = master.shape
    ff_blocks = FF // head_dim
    ctx_size = lax.axis_size("ctx")
    ctx_index = lax.axis_index("ctx")
    slot_rows = unit_rows(owners, slot_count)
    owner_table = lax.all_gather(master.astype(jnp.bfloat16), "fsdp", axis=0, tiled=True)
    picked = owner_table[slot_rows]
    weights = lax.all_gather(picked, "ctx", axis=2, tiled=True)
    w_qkv = weights[0 : 3 * H]
    w_out = weights[3 * H : 4 * H]
    w_up = weights[4 * H : 4 * H + ff_blocks]
    w_down = weights[4 * H + ff_blocks :]
    values_in = inputs.astype(jnp.float32)
    normed_b = (values_in * inverse_rms(values_in) * norm_gains[0]).astype(jnp.bfloat16)
    projected = jnp.einsum("sbd,hed->shbe", normed_b, w_qkv, preferred_element_type=jnp.float32)
    query_pre = projected[:, 0:H]
    multiplier = jax.nn.softplus(query_scale) * (score_base / math.sqrt(head_dim))
    query_b = (query_pre * multiplier).astype(jnp.bfloat16)
    key_b = projected[:, H : 2 * H].astype(jnp.bfloat16)
    value_b = projected[:, 2 * H : 3 * H].astype(jnp.bfloat16)
    query_rows = ctx_index * block_rows + jnp.arange(block_rows, dtype=jnp.int32)
    last_row = ctx_index * block_rows + block_rows - 1
    start_state = (
        jnp.full(query_pre.shape[:3], masked_score, jnp.float32),
        jnp.zeros(query_pre.shape[:3], jnp.float32),
        jnp.zeros(query_pre.shape, jnp.float32),
    )
    key_part = lax.all_gather(key_b, "ctx", axis=2, tiled=True)
    value_part = lax.all_gather(value_b, "ctx", axis=2, tiled=True)
    key_count = key_part.shape[2]

    def update(current):
        run_max, run_sum, accum = current
        key_rows = jnp.arange(key_count, dtype=jnp.int32)
        allowed = query_rows[:, None] >= key_rows[None, :]
        scores = jnp.einsum(
            "shqe,shke->shqk", query_b, key_part, preferred_element_type=jnp.float32
        )
        scores = jnp.where(allowed, scores, masked_score)
        new_max = jnp.maximum(run_max, jnp.max(scores, axis=-1))
        attn_probs = jnp.where(allowed, jnp.exp(scores - new_max[..., None]), 0.0)
        run_sum = jnp.sum(attn_probs, axis=-1)
        accum = jnp.einsum(
            "shqk,shke->shqe",
            attn_probs.astype(jnp.bfloat16),
            value_part,
            preferred_element_type=jnp.float32,
        )
        return (new_max, run_sum, accum)

    run_max, run_sum, accum = lax.cond(
        jnp.int32(0) <= last_row, update, lambda current: current, start_state
    )
    attended = accum / run_sum[..., None]
    log_total = run_max + jnp.log(run_sum)
    attended_b = attended.astype(jnp.bfloat16)
    branch = jnp.einsum("shbe,hed->sbd", attended_b, w_out, preferred_element_type=jnp.float32)
    middle = values_in + branch
    normed_mid_b = (middle * inverse_rms(middle) * norm_gains[1]).astype(jnp.bfloat16)
    hidden = jnp.einsum("sbd,fed->sbfe", normed_mid_b, w_up, preferred_element_type=jnp.float32)
    active_b = jax.nn.silu(hidden).astype(jnp.bfloat16)
    block_out = middle + jnp.einsum(
        "sbfe,fed->sbd", active_b, w_down, preferred_element_type=jnp.float32
    )
    seq_length = block_rows * ctx_size
    counted = (query_rows[None, :] >= (seq_length - valid_counts)[:, None]).astype(jnp.float32)
    count_term = jnp.sum(counted)
    out_grad = 2.0 * (block_out - targets.astype(jnp.float32)) * counted[..., None]
    out_grad_b = out_grad.astype(jnp.bfloat16)
    grad_down = jnp.einsum(
        "sbfe,sbd->fed", active_b, out_grad_b, preferred_element_type=jnp.float32
    )
    grad_active = jnp.einsum(
        "sbd,fed->sbfe", out_grad_b, w_down, preferred_element_type=jnp.float32
    )
    sigma = jax.nn.sigmoid(hidden)
    grad_hidden_b = (grad_active * sigma * (1.0 + hidden * (1.0 - sigma))).astype(jnp.bfloat16)
    grad_up = jnp.einsum(
        "sbfe,sbd->fed", grad_hidden_b, normed_mid_b, preferred_element_type=jnp.float32
    )
    grad_normed_mid = jnp.einsum(
        "sbfe,fed->sbd", grad_hidden_b, w_up, preferred_element_type=jnp.float32
    )
    grad_middle_norm, grad_gain_two = norm_back(middle, norm_gains[1], grad_normed_mid)
    grad_middle = out_grad + grad_middle_norm
    grad_middle_b = grad_middle.astype(jnp.bfloat16)
    grad_out = jnp.einsum(
        "shbe,sbd->hed", attended_b, grad_middle_b, preferred_element_type=jnp.float32
    )
    grad_attended_b = jnp.einsum(
        "sbd,hed->shbe", grad_middle_b, w_out, preferred_element_type=jnp.float32
    ).astype(jnp.bfloat16)
    delta = jnp.sum(grad_attended_b.astype(jnp.float32) * attended, axis=-1)

    def block_grads(source, key_cur, value_cur, partial_grads):
        grad_key, grad_value, grad_query = partial_grads
        key_rows = source * block_rows + jnp.arange(block_rows, dtype=jnp.int32)
        allowed = query_rows[:, None] >= key_rows[None, :]
        scores = jnp.einsum("shqe,shke->shqk", query_b, key_cur, preferred_element_type=jnp.float32)
        scores = jnp.where(allowed, scores, masked_score)
        attn_probs = jnp.exp(scores - log_total[..., None])
        grad_value = grad_value + jnp.einsum(
            "shqk,shqe->shke",
            attn_probs.astype(jnp.bfloat16),
            grad_attended_b,
            preferred_element_type=jnp.float32,
        )
        grad_probs = jnp.einsum(
            "shqe,shke->shqk", grad_attended_b, value_cur, preferred_element_type=jnp.float32
        )
        grad_scores_b = (attn_probs * (grad_probs - delta[..., None])).astype(jnp.bfloat16)
        grad_query = grad_query + jnp.einsum(
            "shqk,shke->shqe", grad_scores_b, key_cur, preferred_element_type=jnp.float32
        )
        grad_key = grad_key + jnp.einsum(
            "shqk,shqe->shke", grad_scores_b, query_b, preferred_element_type=jnp.float32
        )
        return (grad_key, grad_value, grad_query)

    zero_heads = jnp.zeros(query_pre.shape, jnp.float32)

    def back_turn(which_turn, current):
        key_cur, value_cur, grad_key, grad_value, grad_query = current
        source = (ctx_index - which_turn) % ctx_size
        grad_key, grad_value, grad_query = lax.cond(
            source <= ctx_index,
            lambda parts: block_grads(source, key_cur, value_cur, parts),
            lambda parts: parts,
            (grad_key, grad_value, grad_query),
        )
        key_cur, value_cur = from_behind((key_cur, value_cur), "ctx", 1)
        grad_key, grad_value = (
            shifted(grad_key.astype(jnp.bfloat16), "ctx", 1).astype(grad_key.dtype),
            shifted(grad_value.astype(jnp.bfloat16), "ctx", 1).astype(grad_value.dtype),
        )
        return (key_cur, value_cur, grad_key, grad_value, grad_query)

    back_state = (key_b, value_b, zero_heads, zero_heads, zero_heads)
    back_state = lax.fori_loop(0, ctx_size, back_turn, back_state)
    grad_key, grad_value, grad_query = (back_state[2], back_state[3], back_state[4])
    grad_proj_b = jnp.concatenate([grad_query * multiplier, grad_key, grad_value], axis=1).astype(
        jnp.bfloat16
    )
    grad_qkv = jnp.einsum(
        "shbe,sbd->hed", grad_proj_b, normed_b, preferred_element_type=jnp.float32
    )
    grad_normed_in = jnp.einsum(
        "shbe,hed->sbd", grad_proj_b, w_qkv, preferred_element_type=jnp.float32
    )
    grad_input_norm, grad_gain_one = norm_back(values_in, norm_gains[0], grad_normed_in)
    input_grad = grad_middle + grad_input_norm
    scale_term = (
        jnp.sum(grad_query * query_pre, axis=(0, 1, 2))
        * (score_base / math.sqrt(head_dim))
        * jax.nn.sigmoid(query_scale)
    )
    unit_grads = jnp.concatenate([grad_qkv, grad_out, grad_up, grad_down], axis=0)
    owner_total = lax.axis_size("fsdp") * slot_count
    table_grads = (
        jnp.zeros((owner_total, head_dim, width), jnp.float32).at[slot_rows].set(unit_grads)
    )
    owned = lax.psum_scatter(
        table_grads.astype(jnp.bfloat16), "fsdp", scatter_dimension=0, tiled=True
    )
    slot_sums = lax.psum_scatter(owned, "ctx", scatter_dimension=2, tiled=True).astype(jnp.float32)
    gain_sums, scale_sums, count = lax.psum(
        (jnp.stack([grad_gain_one, grad_gain_two]), scale_term, count_term), ("ctx", "fsdp")
    )
    new_master, new_first, new_second = adam_step(
        master, first_moment, second_moment, slot_sums / count, master_rate, decay_rate
    )
    new_gains, new_gain_first, new_gain_second = adam_step(
        norm_gains, gain_first, gain_second, gain_sums / count, gain_rate, 0.0
    )
    new_scale, new_scale_first, new_scale_second = adam_step(
        query_scale, scale_first, scale_second, scale_sums / count, scale_rate, 0.0
    )
    return (
        block_out,
        input_grad,
        new_master,
        new_first,
        new_second,
        new_gains,
        new_gain_first,
        new_gain_second,
        new_scale,
        new_scale_first,
        new_scale_second,
    )


def swapped(array, axis, distance):
    return lax.ppermute(
        array, axis, [(i, i ^ distance) for i in range(lax.axis_size(axis))]
    )


def summed(array, axis):
    size = lax.axis_size(axis)
    if size & (size - 1):
        return lax.psum(array, axis)
    distance = 1
    while distance < size:
        array = array + swapped(array, axis, distance)
        distance *= 2
    return array


def dot(left, right, left_dim, right_dim):
    return lax.dot_general(
        left,
        right,
        (((left_dim,), (right_dim,)), ((), ())),
        preferred_element_type=jnp.float32,
    )


def copy_rows_kernel(sizes, offsets, width, bound_ref, place_ref, row_ref, *refs):
    sources = refs[: len(offsets)]
    outs = refs[-2 - len(sizes) : -2]
    rows, sems = refs[-2:]
    for number, (source, offset) in enumerate(zip(sources, offsets)):

        @pl.loop(bound_ref[number], bound_ref[number + 1])
        def copy_row(i, source=source, offset=offset):
            pltpu.make_async_copy(
                source.at[row_ref[i], :, pl.ds(offset, width)],
                rows.at[place_ref[i]],
                sems.at[len(sizes)],
            ).start()

    pltpu.make_async_copy(rows, rows, sems.at[len(sizes)]).wait()
    copies, start = [], 0
    for place, (out, size) in enumerate(zip(outs, sizes)):
        copies.append(
            pltpu.make_async_copy(rows.at[pl.ds(start, size)], out, sems.at[place])
        )
        start += size
    for copy in copies:
        copy.start()
    for copy in copies:
        copy.wait()


def copy_plan(pick_from, pick_row, source_count):
    number = jnp.arange(pick_from.shape[0], dtype=jnp.int32)
    before = pick_from[None, :] < pick_from[:, None]
    same = (pick_from[None, :] == pick_from[:, None]) & (number[None, :] < number[:, None])
    rank = jnp.sum((before | same).astype(jnp.int32), axis=1)
    here = rank[None, :] == number[:, None]
    place = jnp.sum(jnp.where(here, number[None, :], 0), axis=1)
    row = jnp.sum(jnp.where(here, pick_row[None, :], 0), axis=1)
    bounds = jnp.sum(
        (pick_from[None, :] < jnp.arange(source_count + 1)[:, None]).astype(jnp.int32), axis=1
    )
    return (bounds.astype(jnp.int32), place.astype(jnp.int32), row.astype(jnp.int32))


def copy_rows(sources, offsets, width, plan, sizes, events=()):
    rows = sources[0].shape[1]
    total = sum(sizes)
    return pl.pallas_call(
        functools.partial(copy_rows_kernel, tuple(sizes), tuple(offsets), width),
        out_shape=[jax.ShapeDtypeStruct((size, rows, width), sources[0].dtype) for size in sizes],
        grid_spec=pltpu.PrefetchScalarGridSpec(
            num_scalar_prefetch=3,
            grid=(1,),
            in_specs=[pl.BlockSpec(memory_space=pltpu.HBM)] * (len(sources) + len(events)),
            out_specs=[pl.BlockSpec(memory_space=pltpu.HBM)] * len(sizes),
            scratch_shapes=[
                pltpu.VMEM((total, rows, width), sources[0].dtype),
                pltpu.SemaphoreType.DMA((len(sizes) + 1,)),
            ],
        ),
        compiler_params=pltpu.CompilerParams(vmem_limit_bytes=40 * 1024 * 1024),
        cost_estimate=pl.CostEstimate(flops=0, bytes_accessed=1024, transcendentals=0),
        name="copy_rows",
    )(*plan, *sources, *events)


def place_pieces_kernel(places, count_outs, *refs):
    pieces = refs[: len(places)]
    outs = refs[-1 - count_outs : -1]
    sems = refs[-1]
    copies = []
    for number, (piece, place) in enumerate(zip(pieces, places)):
        first, count, begin, size, column, out, row = place
        copies.append(
            pltpu.make_async_copy(
                piece.at[pl.ds(first, count), :, pl.ds(begin, size)],
                outs[out].at[pl.ds(row, count), :, pl.ds(column, size)],
                sems.at[number],
            )
        )
    for copy in copies:
        copy.start()
    for copy in copies:
        copy.wait()


def place_pieces(pieces, places, shapes, events=()):
    return pl.pallas_call(
        functools.partial(place_pieces_kernel, tuple(places), len(shapes)),
        out_shape=[jax.ShapeDtypeStruct(shape, pieces[0].dtype) for shape in shapes],
        in_specs=[pl.BlockSpec(memory_space=pltpu.HBM)] * (len(pieces) + len(events)),
        out_specs=[pl.BlockSpec(memory_space=pltpu.VMEM)] * len(shapes),
        scratch_shapes=[pltpu.SemaphoreType.DMA((len(pieces),))],
        compiler_params=pltpu.CompilerParams(vmem_limit_bytes=40 * 1024 * 1024),
        cost_estimate=pl.CostEstimate(flops=0, bytes_accessed=1024, transcendentals=0),
        name="place_pieces",
    )(*pieces, *events)


def scores_of(blocks, key_rows, query, i):
    size = query.shape[1]
    parts = [(i * size, size)] + ([(0, i * size)] if i else [])
    return [dot(key_rows[first : first + count, :], query, 1, 0) for first, count in parts]


def attend_kernel(blocks, pair, order_ref, q_ref, k_ref, v_ref, out_ref, log_ref, *refs):
    key_rows, value_cols = refs[:pair], refs[pair:]
    head_dim = q_ref.shape[0] // pair
    size = q_ref.shape[1] // blocks
    at = [pl.multiple_of(order_ref[i] * size, size) for i in range(blocks)]
    heads = [slice(p * head_dim, (p + 1) * head_dim) for p in range(pair)]
    for i in range(blocks):
        here = slice(i * size, (i + 1) * size)
        for p in range(pair):
            key_rows[p][here, :] = k_ref[heads[p], pl.ds(at[i], size)].T
            value_cols[p][:, here] = v_ref[heads[p], pl.ds(at[i], size)]
    key_pos = lax.broadcasted_iota(jnp.int32, (size, size), 0)
    query_pos = lax.broadcasted_iota(jnp.int32, (size, size), 1)
    seen = key_pos <= query_pos

    def scores(i):
        return [
            scores_of(blocks, key_rows[p], q_ref[heads[p], pl.ds(at[i], size)], i)
            for p in range(pair)
        ]

    upcoming = scores(0)
    for i in range(blocks):
        current = upcoming
        if i + 1 < blocks:
            upcoming = scores(i + 1)
        past = i * size
        for p in range(pair):
            near, *far = current[p]
            near = jnp.where(seen, near, masked_score)
            top = jnp.max(near, axis=0, keepdims=True)
            for part in far:
                top = jnp.maximum(top, jnp.max(part, axis=0, keepdims=True))
            near = jnp.exp(near - top)
            total = jnp.sum(near, axis=0, keepdims=True)
            value = dot(
                value_cols[p][:, past : past + size], near.astype(jnp.bfloat16), 1, 0
            )
            for part in far:
                part = jnp.exp(part - top)
                total = total + jnp.sum(part, axis=0, keepdims=True)
                value = value + dot(value_cols[p][:, :past], part.astype(jnp.bfloat16), 1, 0)
            out_ref[heads[p], pl.ds(at[i], size)] = (value / total).astype(jnp.bfloat16)
            log_ref[p, :, pl.ds(at[i], size)] = top + jnp.log(total)


def attend(projected, order, heads, head_dim):
    tokens = projected.shape[1]
    blocks = order.shape[0]
    pair = 2
    rows = pair * head_dim

    def part(first):
        return pl.BlockSpec((rows, tokens), lambda h, order, first=first: (first // pair + h, 0))

    return pl.pallas_call(
        functools.partial(attend_kernel, blocks, pair),
        out_shape=[
            jax.ShapeDtypeStruct((heads * head_dim, tokens), jnp.bfloat16),
            jax.ShapeDtypeStruct((heads, 1, tokens), jnp.float32),
        ],
        grid_spec=pltpu.PrefetchScalarGridSpec(
            num_scalar_prefetch=1,
            grid=(heads // pair,),
            in_specs=[part(0), part(heads), part(2 * heads)],
            out_specs=[
                pl.BlockSpec((rows, tokens), lambda h, order: (h, 0)),
                pl.BlockSpec((pair, 1, tokens), lambda h, order: (h, 0, 0)),
            ],
            scratch_shapes=[pltpu.VMEM((tokens, head_dim), jnp.bfloat16)] * pair
            + [pltpu.VMEM((head_dim, tokens), jnp.bfloat16)] * pair,
        ),
        compiler_params=pltpu.CompilerParams(vmem_limit_bytes=48 * 1024 * 1024),
        cost_estimate=pl.CostEstimate(
            flops=heads * tokens * tokens * head_dim * 4,
            bytes_accessed=heads * head_dim * tokens * 8,
            transcendentals=heads * tokens * tokens,
        ),
        name="attend",
    )(order, projected, projected, projected)


def attend_back_kernel(
    blocks,
    pair,
    order_ref,
    q_ref,
    k_ref,
    v_ref,
    grad_ref,
    log_ref,
    scale_ref,
    *refs,
):
    scratch = refs[-5 * pair :]
    out_ref, term_ref = refs[-5 * pair - 2 : -5 * pair]
    key_rows, key_cols, value_rows, key_sum, value_sum = (
        scratch[n * pair : (n + 1) * pair] for n in range(5)
    )
    head_dim = q_ref.shape[0] // pair
    size = q_ref.shape[1] // blocks
    at = [pl.multiple_of(order_ref[i] * size, size) for i in range(blocks)]
    heads = [slice(p * head_dim, (p + 1) * head_dim) for p in range(pair)]
    for i in range(blocks):
        here = slice(i * size, (i + 1) * size)
        for p in range(pair):
            key = k_ref[heads[p], pl.ds(at[i], size)]
            key_rows[p][here, :] = key.T
            key_cols[p][:, here] = key
            value_rows[p][here, :] = v_ref[heads[p], pl.ds(at[i], size)].T
    for p in range(pair):
        key_sum[p][...] = jnp.zeros_like(key_sum[p])
        value_sum[p][...] = jnp.zeros_like(value_sum[p])
    key_pos = lax.broadcasted_iota(jnp.int32, (size, size), 0)
    query_pos = lax.broadcasted_iota(jnp.int32, (size, size), 1)
    seen = key_pos <= query_pos
    terms = [jnp.zeros((head_dim, 1), jnp.float32) for _ in range(pair)]

    def products(i):
        return [
            (
                scores_of(blocks, key_rows[p], q_ref[heads[p], pl.ds(at[i], size)], i),
                scores_of(blocks, value_rows[p], grad_ref[heads[p], pl.ds(at[i], size)], i),
            )
            for p in range(pair)
        ]

    upcoming = products(0)
    for i in range(blocks):
        current = upcoming
        if i + 1 < blocks:
            upcoming = products(i + 1)
        past = i * size
        spans = [slice(past, past + size)] + ([slice(0, past)] if i else [])
        for p in range(pair):
            query = q_ref[heads[p], pl.ds(at[i], size)]
            grad = grad_ref[heads[p], pl.ds(at[i], size)]
            log_total = log_ref[p, :, pl.ds(at[i], size)]
            scores, grads = current[p]
            probs = [jnp.exp(part - log_total) for part in scores]
            probs[0] = jnp.where(seen, probs[0], 0.0)
            delta = jnp.zeros((1, size), jnp.float32)
            for prob, grad_prob in zip(probs, grads):
                delta = delta + jnp.sum(prob * grad_prob, axis=0, keepdims=True)
            grad_query = jnp.zeros(query.shape, jnp.float32)
            for cols, prob, grad_prob in zip(spans, probs, grads):
                grad_score = (prob * (grad_prob - delta)).astype(jnp.bfloat16)
                value_sum[p][:, cols] += dot(grad, prob.astype(jnp.bfloat16), 1, 1)
                key_sum[p][:, cols] += dot(query, grad_score, 1, 1)
                grad_query = grad_query + dot(key_cols[p][:, cols], grad_score, 1, 0)
            terms[p] = terms[p] + jnp.sum(
                grad_query * query.astype(jnp.float32), axis=1, keepdims=True
            )
            out_ref[0, heads[p], pl.ds(at[i], size)] = (grad_query * scale_ref[...]).astype(
                jnp.bfloat16
            )
    for i in range(blocks):
        here = slice(i * size, (i + 1) * size)
        for p in range(pair):
            out_ref[1, heads[p], pl.ds(at[i], size)] = key_sum[p][:, here].astype(jnp.bfloat16)
            out_ref[2, heads[p], pl.ds(at[i], size)] = value_sum[p][:, here].astype(jnp.bfloat16)
    for p in range(pair):
        term_ref[p] = terms[p]


def attend_back(
    projected, grad_attended, log_total, multiplier, order, heads, head_dim, events=()
):
    tokens = projected.shape[1]
    blocks = order.shape[0]
    pair = 2
    rows = pair * head_dim

    def part(first):
        return pl.BlockSpec((rows, tokens), lambda h, order, first=first: (first // pair + h, 0))

    return pl.pallas_call(
        functools.partial(attend_back_kernel, blocks, pair),
        out_shape=[
            jax.ShapeDtypeStruct((3, heads * head_dim, tokens), jnp.bfloat16),
            jax.ShapeDtypeStruct((heads, head_dim, 1), jnp.float32),
        ],
        grid_spec=pltpu.PrefetchScalarGridSpec(
            num_scalar_prefetch=1,
            grid=(heads // pair,),
            in_specs=[
                part(0),
                part(heads),
                part(2 * heads),
                part(0),
                pl.BlockSpec((pair, 1, tokens), lambda h, order: (h, 0, 0)),
                pl.BlockSpec((head_dim, 1), lambda h, order: (0, 0)),
            ]
            + [pl.BlockSpec(memory_space=pltpu.HBM)] * len(events),
            out_specs=[
                pl.BlockSpec((3, rows, tokens), lambda h, order: (0, h, 0)),
                pl.BlockSpec((pair, head_dim, 1), lambda h, order: (h, 0, 0)),
            ],
            scratch_shapes=[pltpu.VMEM((tokens, head_dim), jnp.bfloat16)] * pair
            + [pltpu.VMEM((head_dim, tokens), jnp.bfloat16)] * pair
            + [pltpu.VMEM((tokens, head_dim), jnp.bfloat16)] * pair
            + [pltpu.VMEM((head_dim, tokens), jnp.float32)] * (2 * pair),
        ),
        compiler_params=pltpu.CompilerParams(vmem_limit_bytes=56 * 1024 * 1024),
        cost_estimate=pl.CostEstimate(
            flops=heads * tokens * tokens * head_dim * 10,
            bytes_accessed=heads * head_dim * tokens * 14,
            transcendentals=heads * tokens * tokens,
        ),
        name="attend_back",
    )(order, projected, projected, projected, grad_attended, log_total, multiplier, *events)


def paired_layer(
    inputs,
    targets,
    valid_counts,
    owners,
    master,
    first_moment,
    second_moment,
    norm_gains,
    gain_first,
    gain_second,
    query_scale,
    scale_first,
    scale_second,
):
    bf16 = jnp.bfloat16
    f32 = jnp.float32
    seq_local, block_rows, width = inputs.shape
    slot_count, head_dim, column_count = master.shape
    ff_blocks = FF // head_dim
    owner_count = lax.axis_size("fsdp")
    device = lax.axis_index("ctx")
    chip, core = device // 2, device % 2
    owner_here = lax.axis_index("fsdp")
    low_here = owner_here % 2
    high_here = owner_here // 2
    high_count = owner_count // 2
    high_distances = range(1, high_count)
    half_width = width // 2
    half_slots = slot_count // 2
    half_rows = seq_local * block_rows
    half_heads = H // 2
    half_blocks = ff_blocks // 2
    set_units = 4 * half_heads + 2 * half_blocks
    first_chip, first_core = chip == 0, core == 0

    def columns_here(array):
        return jnp.where(first_chip, array, jnp.roll(array, half_width, axis=-1))

    def sequence_rows(array):
        own = jnp.where(first_chip, array[0], array[1])
        got = swapped(jnp.where(first_chip, array[1], array[0]), "ctx", 2)
        return jnp.where(
            first_chip, jnp.concatenate([own, got]), jnp.concatenate([got, own])
        )

    def rows_apart(array):
        array = columns_here(array)
        first, last = array[:block_rows], array[block_rows:]
        other = jnp.where(first_chip, last, first).astype(bf16)
        return (jnp.where(first_chip, first, last), swapped(other, "ctx", 2))

    def rows_home(own, got):
        got = got.astype(f32)
        return jnp.where(first_chip, jnp.stack([own, got]), jnp.stack([got, own]))

    slot_rows = unit_rows(owners, slot_count)
    unit_total = owners.shape[0]
    kind_sizes = [H, H, H, H, ff_blocks, ff_blocks]
    kind_starts = [sum(kind_sizes[:i]) for i in range(6)]

    def unit_list(kinds, which):
        return jnp.concatenate(
            [
                kind_starts[k] + which * (kind_sizes[k] // 2) + jnp.arange(kind_sizes[k] // 2)
                for k in kinds
            ]
        ).astype(jnp.int32)

    wanted = jnp.concatenate(
        [unit_list(range(6), core), unit_list((4, 5), 1 - core)]
    )
    wanted_rows = slot_rows[wanted]
    wanted_owner, wanted_slot = wanted_rows // slot_count, wanted_rows % slot_count
    weight_from = 2 * (wanted_slot // half_slots != core) + (wanted_owner % 2 != low_here)
    weight_from = weight_from.astype(jnp.int32)
    weight_row = ((wanted_owner // 2) ^ high_here) * half_slots + wanted_slot % half_slots
    weight_plan = copy_plan(weight_from, weight_row, 4)
    weight_sizes = [3 * half_heads, half_heads + 2 * half_blocks, 2 * half_blocks]

    chunks = [(0, 128), (128, 128), (256, 256)]
    lead = 512
    tail = half_width - lead
    shard = master.astype(bf16)
    own_half = jnp.where(first_core, shard[:half_slots], shard[half_slots:])
    got_half = swapped(jnp.where(first_core, shard[half_slots:], shard[:half_slots]), "ctx", 1)
    shard = jnp.where(
        first_core,
        jnp.concatenate([own_half, got_half], axis=2),
        jnp.concatenate([got_half, own_half], axis=2),
    )
    shard, inputs, targets = lax.optimization_barrier((shard, inputs, targets))
    values_b = columns_here(sequence_rows(inputs))
    targets_b = columns_here(sequence_rows(targets))
    shard_last = shard[:, :, lead:]
    shards = [shard[:, :, start : start + size] for start, size in chunks]
    shards.append(jnp.concatenate([shard_last, swapped(shard_last, "ctx", 2)], axis=2))
    highs, lows, firsts = [], [], []
    for number, part in enumerate(shards):
        if number:
            part, gathered = lax.optimization_barrier((part, gathered))
            highs[-1] = gathered
        pieces = [part] + [swapped(part, "fsdp", 2 * d) for d in high_distances]
        firsts.append(pieces[1])
        gathered = jnp.concatenate(pieces)
        highs.append(gathered)
    own_units, rest_units, far_units = weight_sizes
    near_units = own_units + rest_units

    def pick_units(number, sizes, events):
        high, low = highs[number], lows[number]
        sources = [high, low, swapped(high, "ctx", 1), swapped(low, "ctx", 1)]
        return copy_rows(sources, [0] * 4, high.shape[2], weight_plan, sizes, events)

    lows.append(swapped(highs[0], "fsdp", 1))
    lows[0], highs[1] = lax.optimization_barrier((lows[0], highs[1]))
    near_one, far_one = pick_units(0, [near_units, far_units], [firsts[2]])
    got_one = swapped(near_one, "ctx", 2)
    highs[1], far_one = lax.optimization_barrier((highs[1], far_one))
    highs[3], got_one = lax.optimization_barrier((highs[3], got_one))
    for number in range(1, 4):
        if number == 3:
            near_two, far_two = pick_units(1, [near_units, far_units], [values_b, got_one])
            highs[3], far_two = lax.optimization_barrier((highs[3], far_two))
        if number > 1:
            highs[number], lows[-1] = lax.optimization_barrier((highs[number], lows[-1]))
        lows.append(swapped(highs[number], "fsdp", 1))
    got_two = swapped(near_two, "ctx", 2)
    qkv_three, rest_three, far_three = pick_units(2, weight_sizes, [targets_b, got_two])
    qkv_got = swapped(qkv_three, "ctx", 2)
    rest_three, qkv_got = lax.optimization_barrier((rest_three, qkv_got))
    rest_got = swapped(rest_three, "ctx", 2)
    qkv_last, rest_last, far_last = pick_units(3, weight_sizes, [qkv_got])

    def columns_of(owns, gots, last):
        pieces = [(last, 0, tail, lead), (last, tail, tail, half_width + lead)]
        for (start, size), own, got in zip(chunks, owns, gots):
            pieces += [(own, 0, size, start), (got, 0, size, half_width + start)]
        return pieces

    def placed(pieces, from_end, count, out, row):
        return [
            (piece.shape[0] - from_end if from_end else 0, count, *columns, out, row)
            for piece, *columns in pieces
        ]

    qkv_pieces = columns_of(
        [near_one, near_two, qkv_three], [got_one, got_two, qkv_got], qkv_last
    )
    rest_pieces = columns_of(
        [near_one, near_two, rest_three], [got_one, got_two, rest_got], rest_last
    )
    far_pieces = columns_of(
        [far_one, far_two, far_three],
        [swapped(got, "ctx", 1) for got in (got_one, got_two, rest_got)],
        far_last,
    )
    (w_qkv,) = place_pieces(
        [piece for piece, *_ in qkv_pieces],
        placed(qkv_pieces, 0, own_units, 0, 0),
        [(own_units, head_dim, width)],
    )
    w_qkv = w_qkv.reshape(-1, width)

    gains = columns_here(norm_gains)
    values_in = values_b.astype(f32)
    normed_own = (values_in * inverse_rms(values_in) * gains[0]).astype(bf16)
    normed_b = jnp.concatenate([normed_own, swapped(normed_own, "ctx", 1)])
    base = score_base / math.sqrt(head_dim)
    multiplier = jax.nn.softplus(query_scale) * base
    row_scale = jnp.concatenate(
        [jnp.tile(multiplier, half_heads), jnp.ones((2 * half_heads * head_dim,), f32)]
    )
    projected = (dot(w_qkv, normed_b, 1, 1) * row_scale[:, None]).astype(bf16)
    positions = jnp.arange(4, dtype=jnp.int32)
    order = jnp.where(positions % 2 == core, 0, 2) + positions // 2
    order = order.astype(jnp.int32)
    attended, log_total = attend(projected, order, half_heads, head_dim)
    (w_out,) = place_pieces(
        [piece for piece, *_ in rest_pieces],
        placed(rest_pieces, rest_units, half_heads, 0, 0),
        [(half_heads, head_dim, width)],
        [log_total],
    )
    mlp_pieces, mlp_places = [], []
    for row, pieces in ((0, rest_pieces), (half_blocks, far_pieces)):
        for kind in range(2):
            mlp_pieces += [piece for piece, *_ in pieces]
            mlp_places += placed(pieces, (2 - kind) * half_blocks, half_blocks, kind, row)
    w_up, w_down = place_pieces(
        mlp_pieces, mlp_places, [(ff_blocks, head_dim, width)] * 2, [log_total]
    )
    w_out = w_out.reshape(-1, width)
    w_up = w_up.reshape(-1, width)
    w_down = w_down.reshape(-1, width)
    branch_far = dot(attended[:, half_rows:], w_out, 0, 0).astype(bf16)
    branch_got = swapped(branch_far, "ctx", 1)
    branch_own = dot(attended[:, :half_rows], w_out, 0, 0)
    middle = values_in + (branch_own + branch_got.astype(f32))
    normed_mid_b = (middle * inverse_rms(middle) * gains[1]).astype(bf16)
    hidden = dot(normed_mid_b, w_up, 1, 1)
    active_b = jax.nn.silu(hidden).astype(bf16)
    block_out = middle + dot(active_b, w_down, 1, 0)
    seq_length = 2 * half_rows
    row = jnp.arange(half_rows, dtype=jnp.int32)
    row_pos = (core + 2 * (row // block_rows)) * block_rows + row % block_rows
    valid = jnp.where(first_chip, valid_counts[0], valid_counts[1])
    counted = (row_pos >= seq_length - valid).astype(f32)
    count_term = jnp.sum(counted)

    out_grad = 2.0 * (block_out - targets_b.astype(f32)) * counted[:, None]
    out_grad_b = out_grad.astype(bf16)
    grad_active = dot(out_grad_b, w_down, 1, 1)
    sigma = jax.nn.sigmoid(hidden)
    grad_hidden_b = (grad_active * sigma * (1.0 + hidden * (1.0 - sigma))).astype(bf16)
    grad_normed_mid = dot(grad_hidden_b, w_up, 1, 0)
    inverse = inverse_rms(middle)
    scaled = grad_normed_mid * gains[1]
    grad_middle = out_grad + (
        inverse * scaled
        - middle * inverse**3 * jnp.mean(scaled * middle, axis=-1, keepdims=True)
    )
    grad_gain_two = jnp.sum(grad_normed_mid * middle * inverse, axis=0)
    grad_middle_own = grad_middle.astype(bf16)
    grad_middle_got = swapped(grad_middle_own, "ctx", 1)
    far_blocks = half_blocks * head_dim
    wide = slice(half_width + 256, half_width + lead)
    slim = slice(half_width, half_width + 256)
    block_grads = []
    for left, right in ((grad_hidden_b, normed_mid_b), (active_b, out_grad_b)):
        got = swapped(dot(left[:, far_blocks:], right, 0, 0).astype(bf16), "ctx", 1)
        total = dot(left[:, :far_blocks], right, 0, 0) + got.astype(f32)
        block_grads.append(total.astype(bf16).reshape(half_blocks, head_dim, width))
    block_grads = jnp.concatenate(block_grads)
    block_own, block_got = rows_apart(block_out)
    grad_middle_got, block_grads, block_got = lax.optimization_barrier(
        (grad_middle_got, block_grads, block_got)
    )
    grad_middle_b = jnp.concatenate([grad_middle_own, grad_middle_got])
    grad_attended = dot(w_out, grad_middle_b, 1, 1).astype(bf16)
    head_grads = dot(attended, grad_middle_b, 1, 0).astype(bf16)
    head_grads = head_grads.reshape(half_heads, head_dim, width)

    def early_columns(columns):
        return jnp.concatenate([head_grads[:, :, columns], block_grads[:, :, columns]])

    early_wide, early_slim = early_columns(wide), early_columns(slim)
    wide_got = swapped(early_wide, "ctx", 2)

    def last_columns(array):
        return jnp.concatenate(
            [array[..., lead:half_width], array[..., half_width + lead :]], axis=-1
        )

    early_last = jnp.concatenate([last_columns(head_grads), last_columns(block_grads)])
    grad_proj, grad_scale = attend_back(
        projected,
        grad_attended,
        log_total,
        multiplier[:, None],
        order,
        half_heads,
        head_dim,
        [early_wide, early_slim, early_last],
    )
    grad_proj = grad_proj.reshape(-1, grad_proj.shape[2])
    scale_term = (
        jnp.sum(grad_scale[:, :, 0], axis=0) / multiplier * base * jax.nn.sigmoid(query_scale)
    )

    low_order = jnp.stack([low_here, 1 - low_here])
    table_slots = (
        (2 * (jnp.arange(high_count) ^ high_here)[None, :, None] + low_order[:, None, None])
        * slot_count
        + core * half_slots
        + jnp.arange(half_slots)[None, None, :]
    ).reshape(-1)
    holds = table_slots[:, None] == slot_rows[None, :]
    unit_order = jnp.arange(unit_total, dtype=jnp.int32)
    slot_unit = jnp.sum(jnp.where(holds, unit_order[None, :] + 1, 0), axis=1) - 1
    kind = jnp.where(
        slot_unit < 4 * H, slot_unit // H, 4 + (slot_unit - 4 * H) // ff_blocks
    )
    kind_size = jnp.where(kind < 4, H, ff_blocks)
    within = jnp.where(kind < 4, slot_unit % H, (slot_unit - 4 * H) % ff_blocks)
    other_set = (within // (kind_size // 2) != core).astype(jnp.int32)
    rank = within % (kind_size // 2)
    grad_row = rank + jnp.where(
        kind <= 3, kind * half_heads, 4 * half_heads + (kind - 4) * half_blocks
    )
    empty = slot_unit < 0
    grad_from = jnp.where(empty, 2, other_set).astype(jnp.int32)
    grad_row = jnp.where(empty, 0, grad_row).astype(jnp.int32)
    grad_plan = copy_plan(grad_from, grad_row, 3)
    zero = jnp.zeros((1, head_dim, 256), bf16)

    def pick_table(own, got, offset, size, events=()):
        return copy_rows(
            [own, got, zero],
            [offset, offset, 0],
            size,
            grad_plan,
            [high_count * half_slots] * 2,
            events,
        )

    def table_sums(keep, got):
        sums = []
        for d in range(high_count):
            rows = slice(d * half_slots, (d + 1) * half_slots)
            sums.append((keep[rows].astype(f32) + got[rows].astype(f32)).astype(bf16))
        return sums

    def from_owners(tables):
        return [swapped(tables[d], "fsdp", 2 * d) for d in high_distances]

    def owner_sum(table, got):
        total = table.astype(f32)
        for part in got:
            total = total + part.astype(f32)
        return total.astype(bf16)

    def proj_grad(columns):
        return dot(grad_proj, columns, 1, 0).astype(bf16).reshape(-1, head_dim, columns.shape[1])

    def chip_sum(start, proj_got, early_got):
        near = slice(start, start + 256)
        parts = [
            (proj_grad(normed_b[:, near]), proj_got),
            (head_grads[:, :, near], early_got[:half_heads]),
            (block_grads[:, :, near], early_got[half_heads:]),
        ]
        return jnp.concatenate(
            [(own.astype(f32) + got.astype(f32)).astype(bf16) for own, got in parts]
        )

    proj_last = proj_grad(last_columns(normed_b))
    proj_last, wide_got = lax.optimization_barrier((proj_last, wide_got))
    total_last = jnp.concatenate([proj_last, early_last])
    wide_far = proj_grad(normed_b[:, wide])
    wide_proj = swapped(wide_far, "ctx", 2)
    keep_last, send_last = pick_table(
        total_last, swapped(total_last, "ctx", 1), 0, 256, [wide_far]
    )
    low_last = swapped(send_last, "fsdp", 1)
    keep_last, grad_proj = lax.optimization_barrier((keep_last, grad_proj))
    slim_far = jnp.concatenate([proj_grad(normed_b[:, slim]), early_slim])
    low_last, wide_proj, slim_far = lax.optimization_barrier((low_last, wide_proj, slim_far))
    slim_got = swapped(slim_far, "ctx", 2)
    total = chip_sum(256, wide_proj, wide_got)
    keep_three, send_three = pick_table(total, swapped(total, "ctx", 1), 0, 256)
    low_last, keep_three, grad_proj = lax.optimization_barrier((low_last, keep_three, grad_proj))
    low_three = swapped(send_three, "fsdp", 1)
    tables_last = table_sums(keep_last, low_last)
    high_last = from_owners(tables_last)
    normed_far = dot(grad_proj[:, half_rows:], w_qkv, 0, 0).astype(bf16)
    low_three, high_last, slim_got, normed_far = lax.optimization_barrier(
        (low_three, high_last, slim_got, normed_far)
    )
    normed_got = swapped(normed_far, "ctx", 1)
    total = chip_sum(0, slim_got[: 3 * half_heads], slim_got[3 * half_heads :])
    total_got = swapped(total, "ctx", 1)
    keep_two, send_two = pick_table(
        total, total_got, 128, 128, [low_three]
    )
    low_two = swapped(send_two, "fsdp", 1)
    keep_two, low_three, normed_got, high_last = lax.optimization_barrier(
        (keep_two, low_three, normed_got, high_last)
    )
    tables_three = table_sums(keep_three, low_three)
    high_three = from_owners(tables_three)
    tables_two = table_sums(keep_two, low_two)
    keep_one, send_one = pick_table(total, total_got, 0, 128, tables_two)
    tables_two, high_three = lax.optimization_barrier((tables_two, high_three))
    high_two = from_owners(tables_two)

    grad_normed_in = dot(grad_proj[:, :half_rows], w_qkv, 0, 0) + normed_got.astype(f32)
    inverse = inverse_rms(values_in)
    scaled = grad_normed_in * gains[0]
    input_grad = grad_middle + (
        inverse * scaled
        - values_in * inverse**3 * jnp.mean(scaled * values_in, axis=-1, keepdims=True)
    )
    grad_gain_one = jnp.sum(grad_normed_in * values_in * inverse, axis=0)

    gain_terms = columns_here(jnp.stack([grad_gain_one, grad_gain_two]))
    small = jnp.concatenate([gain_terms.reshape(-1), scale_term, count_term[None]])
    small = jnp.pad(small, (0, -small.shape[0] % 1024))
    keep_one, small = lax.optimization_barrier((keep_one, small))
    tables_one = table_sums(keep_one, swapped(send_one, "fsdp", 1))
    small = small + swapped(small, "fsdp", 1)
    tables_one, high_two, small, input_grad = lax.optimization_barrier(
        (tables_one, high_two, small, input_grad)
    )
    high_one = from_owners(tables_one)
    small_got = from_owners([small] * high_count)
    high_one, small_got = lax.optimization_barrier((high_one, small_got))
    small = summed((small + small_got[0]) + (small_got[1] + small_got[2]), "ctx")
    gain_sums = small[: 2 * width].reshape(2, width)
    scale_sums = small[2 * width : 2 * width + head_dim]
    count = small[2 * width + head_dim]

    owned_last = owner_sum(tables_last[0], high_last)
    owned_got = swapped(owned_last[:, :, tail:], "ctx", 2)
    owned = [
        owner_sum(tables_one[0], high_one),
        owner_sum(tables_two[0], high_two),
        owner_sum(tables_three[0], high_three),
        (owned_last[:, :, :tail].astype(f32) + owned_got.astype(f32)).astype(bf16),
    ]
    owned = jnp.concatenate(owned, axis=2).reshape(half_slots, head_dim, 2, column_count)
    kept = jnp.where(first_core, owned[:, :, 0], owned[:, :, 1])
    sent = swapped(jnp.where(first_core, owned[:, :, 1], owned[:, :, 0]), "ctx", 1)
    slot_sums = jnp.where(
        first_core, jnp.concatenate([kept, sent]), jnp.concatenate([sent, kept])
    ).astype(f32)
    new_master, new_first, new_second = adam_step(
        master, first_moment, second_moment, slot_sums / count, master_rate, decay_rate
    )
    new_gains, new_gain_first, new_gain_second = adam_step(
        norm_gains, gain_first, gain_second, gain_sums / count, gain_rate, 0.0
    )
    new_scale, new_scale_first, new_scale_second = adam_step(
        query_scale, scale_first, scale_second, scale_sums / count, scale_rate, 0.0
    )
    return (
        rows_home(block_own, block_got),
        rows_home(*rows_apart(input_grad)),
        new_master,
        new_first,
        new_second,
        new_gains,
        new_gain_first,
        new_gain_second,
        new_scale,
        new_scale_first,
        new_scale_second,
    )


def on_device(*arguments):
    paired = (
        lax.axis_size("ctx") == 4
        and lax.axis_size("fsdp") == 8
        and arguments[0].shape[0] == 2
    )
    return (paired_layer if paired else general_layer)(*arguments)


def solution(mesh):
    in_specs = (
        P("fsdp", "ctx", None),
        P("fsdp", "ctx", None),
        P("fsdp"),
        P(),
        P("fsdp", None, "ctx"),
        P("fsdp", None, "ctx"),
        P("fsdp", None, "ctx"),
        P(),
        P(),
        P(),
        P(),
        P(),
        P(),
    )
    out_specs = (
        P("fsdp", "ctx", None),
        P("fsdp", "ctx", None),
        P("fsdp", None, "ctx"),
        P("fsdp", None, "ctx"),
        P("fsdp", None, "ctx"),
        P(),
        P(),
        P(),
        P(),
        P(),
        P(),
    )
    return jax.shard_map(
        on_device, mesh=mesh, in_specs=in_specs, out_specs=out_specs, check_vma=False
    )
```

```python
import functools
import math

import jax
import jax.numpy as jnp
from jax import lax
from jax.experimental import pallas as pl
from jax.experimental.pallas import tpu as pltpu
from jax.sharding import PartitionSpec as P

H = 16
FF = 1280
STEP = 10


norm_eps = 1e-06
beta_first = 0.9
beta_second = 0.95
adam_eps = 1e-08
decay_rate = 0.1
master_rate = 0.05
gain_rate = 2.0
scale_rate = 2.0
score_base = 1.442695041
masked_score = -1e30


def from_behind(block, axis, distance):
    devices = range(lax.axis_size(axis))
    route = [(i - distance, i) for i in devices if i - distance in devices]
    return lax.ppermute(block, axis, route)


def shifted(array, axis, by):
    count = lax.axis_size(axis)
    return lax.ppermute(array, axis, [(i, (i + by) % count) for i in range(count)])


def unit_rows(owners, slot_count):
    unit_count = owners.shape[0]
    unit_order = jnp.arange(unit_count, dtype=jnp.int32)
    same_owner = owners[:, None] == owners[None, :]
    earlier = unit_order[None, :] < unit_order[:, None]
    slot_rank = jnp.sum((same_owner & earlier).astype(jnp.int32), axis=1)
    return owners * slot_count + slot_rank


def inverse_rms(values):
    return lax.rsqrt(jnp.mean(values * values, axis=-1, keepdims=True) + norm_eps)


def norm_back(values, gain, grad_normed):
    inverse = inverse_rms(values)
    scaled = grad_normed * gain
    grad_values = inverse * scaled - values * inverse**3 * jnp.mean(
        scaled * values, axis=-1, keepdims=True
    )
    grad_gain = jnp.sum(grad_normed * values * inverse, axis=(0, 1))
    return (grad_values, grad_gain)


def adam_step(values, moment_one, moment_two, gradient, step_rate, weight_decay):
    moment_one = beta_first * moment_one + (1.0 - beta_first) * gradient
    moment_two = beta_second * moment_two + (1.0 - beta_second) * gradient * gradient
    first_hat = moment_one / (1.0 - beta_first**STEP)
    second_hat = moment_two / (1.0 - beta_second**STEP)
    values = values - step_rate * (
        first_hat / (jnp.sqrt(second_hat) + adam_eps) + weight_decay * values
    )
    return (values, moment_one, moment_two)


def general_layer(
    inputs,
    targets,
    valid_counts,
    owners,
    master,
    first_moment,
    second_moment,
    norm_gains,
    gain_first,
    gain_second,
    query_scale,
    scale_first,
    scale_second,
):
    seq_local, block_rows, width = inputs.shape
    slot_count, head_dim, column_count = master.shape
    ff_blocks = FF // head_dim
    ctx_size = lax.axis_size("ctx")
    ctx_index = lax.axis_index("ctx")
    slot_rows = unit_rows(owners, slot_count)
    owner_table = lax.all_gather(master.astype(jnp.bfloat16), "fsdp", axis=0, tiled=True)
    picked = owner_table[slot_rows]
    weights = lax.all_gather(picked, "ctx", axis=2, tiled=True)
    w_qkv = weights[0 : 3 * H]
    w_out = weights[3 * H : 4 * H]
    w_up = weights[4 * H : 4 * H + ff_blocks]
    w_down = weights[4 * H + ff_blocks :]
    values_in = inputs.astype(jnp.float32)
    normed_b = (values_in * inverse_rms(values_in) * norm_gains[0]).astype(jnp.bfloat16)
    projected = jnp.einsum("sbd,hed->shbe", normed_b, w_qkv, preferred_element_type=jnp.float32)
    query_pre = projected[:, 0:H]
    multiplier = jax.nn.softplus(query_scale) * (score_base / math.sqrt(head_dim))
    query_b = (query_pre * multiplier).astype(jnp.bfloat16)
    key_b = projected[:, H : 2 * H].astype(jnp.bfloat16)
    value_b = projected[:, 2 * H : 3 * H].astype(jnp.bfloat16)
    query_rows = ctx_index * block_rows + jnp.arange(block_rows, dtype=jnp.int32)
    last_row = ctx_index * block_rows + block_rows - 1
    start_state = (
        jnp.full(query_pre.shape[:3], masked_score, jnp.float32),
        jnp.zeros(query_pre.shape[:3], jnp.float32),
        jnp.zeros(query_pre.shape, jnp.float32),
    )
    key_part = lax.all_gather(key_b, "ctx", axis=2, tiled=True)
    value_part = lax.all_gather(value_b, "ctx", axis=2, tiled=True)
    key_count = key_part.shape[2]

    def update(current):
        run_max, run_sum, accum = current
        key_rows = jnp.arange(key_count, dtype=jnp.int32)
        allowed = query_rows[:, None] >= key_rows[None, :]
        scores = jnp.einsum(
            "shqe,shke->shqk", query_b, key_part, preferred_element_type=jnp.float32
        )
        scores = jnp.where(allowed, scores, masked_score)
        new_max = jnp.maximum(run_max, jnp.max(scores, axis=-1))
        attn_probs = jnp.where(allowed, jnp.exp(scores - new_max[..., None]), 0.0)
        run_sum = jnp.sum(attn_probs, axis=-1)
        accum = jnp.einsum(
            "shqk,shke->shqe",
            attn_probs.astype(jnp.bfloat16),
            value_part,
            preferred_element_type=jnp.float32,
        )
        return (new_max, run_sum, accum)

    run_max, run_sum, accum = lax.cond(
        jnp.int32(0) <= last_row, update, lambda current: current, start_state
    )
    attended = accum / run_sum[..., None]
    log_total = run_max + jnp.log(run_sum)
    attended_b = attended.astype(jnp.bfloat16)
    branch = jnp.einsum("shbe,hed->sbd", attended_b, w_out, preferred_element_type=jnp.float32)
    middle = values_in + branch
    normed_mid_b = (middle * inverse_rms(middle) * norm_gains[1]).astype(jnp.bfloat16)
    hidden = jnp.einsum("sbd,fed->sbfe", normed_mid_b, w_up, preferred_element_type=jnp.float32)
    active_b = jax.nn.silu(hidden).astype(jnp.bfloat16)
    block_out = middle + jnp.einsum(
        "sbfe,fed->sbd", active_b, w_down, preferred_element_type=jnp.float32
    )
    seq_length = block_rows * ctx_size
    counted = (query_rows[None, :] >= (seq_length - valid_counts)[:, None]).astype(jnp.float32)
    count_term = jnp.sum(counted)
    out_grad = 2.0 * (block_out - targets.astype(jnp.float32)) * counted[..., None]
    out_grad_b = out_grad.astype(jnp.bfloat16)
    grad_down = jnp.einsum(
        "sbfe,sbd->fed", active_b, out_grad_b, preferred_element_type=jnp.float32
    )
    grad_active = jnp.einsum(
        "sbd,fed->sbfe", out_grad_b, w_down, preferred_element_type=jnp.float32
    )
    sigma = jax.nn.sigmoid(hidden)
    grad_hidden_b = (grad_active * sigma * (1.0 + hidden * (1.0 - sigma))).astype(jnp.bfloat16)
    grad_up = jnp.einsum(
        "sbfe,sbd->fed", grad_hidden_b, normed_mid_b, preferred_element_type=jnp.float32
    )
    grad_normed_mid = jnp.einsum(
        "sbfe,fed->sbd", grad_hidden_b, w_up, preferred_element_type=jnp.float32
    )
    grad_middle_norm, grad_gain_two = norm_back(middle, norm_gains[1], grad_normed_mid)
    grad_middle = out_grad + grad_middle_norm
    grad_middle_b = grad_middle.astype(jnp.bfloat16)
    grad_out = jnp.einsum(
        "shbe,sbd->hed", attended_b, grad_middle_b, preferred_element_type=jnp.float32
    )
    grad_attended_b = jnp.einsum(
        "sbd,hed->shbe", grad_middle_b, w_out, preferred_element_type=jnp.float32
    ).astype(jnp.bfloat16)
    delta = jnp.sum(grad_attended_b.astype(jnp.float32) * attended, axis=-1)

    def block_grads(source, key_cur, value_cur, partial_grads):
        grad_key, grad_value, grad_query = partial_grads
        key_rows = source * block_rows + jnp.arange(block_rows, dtype=jnp.int32)
        allowed = query_rows[:, None] >= key_rows[None, :]
        scores = jnp.einsum("shqe,shke->shqk", query_b, key_cur, preferred_element_type=jnp.float32)
        scores = jnp.where(allowed, scores, masked_score)
        attn_probs = jnp.exp(scores - log_total[..., None])
        grad_value = grad_value + jnp.einsum(
            "shqk,shqe->shke",
            attn_probs.astype(jnp.bfloat16),
            grad_attended_b,
            preferred_element_type=jnp.float32,
        )
        grad_probs = jnp.einsum(
            "shqe,shke->shqk", grad_attended_b, value_cur, preferred_element_type=jnp.float32
        )
        grad_scores_b = (attn_probs * (grad_probs - delta[..., None])).astype(jnp.bfloat16)
        grad_query = grad_query + jnp.einsum(
            "shqk,shke->shqe", grad_scores_b, key_cur, preferred_element_type=jnp.float32
        )
        grad_key = grad_key + jnp.einsum(
            "shqk,shqe->shke", grad_scores_b, query_b, preferred_element_type=jnp.float32
        )
        return (grad_key, grad_value, grad_query)

    zero_heads = jnp.zeros(query_pre.shape, jnp.float32)

    def back_turn(which_turn, current):
        key_cur, value_cur, grad_key, grad_value, grad_query = current
        source = (ctx_index - which_turn) % ctx_size
        grad_key, grad_value, grad_query = lax.cond(
            source <= ctx_index,
            lambda parts: block_grads(source, key_cur, value_cur, parts),
            lambda parts: parts,
            (grad_key, grad_value, grad_query),
        )
        key_cur, value_cur = from_behind((key_cur, value_cur), "ctx", 1)
        grad_key, grad_value = (
            shifted(grad_key.astype(jnp.bfloat16), "ctx", 1).astype(grad_key.dtype),
            shifted(grad_value.astype(jnp.bfloat16), "ctx", 1).astype(grad_value.dtype),
        )
        return (key_cur, value_cur, grad_key, grad_value, grad_query)

    back_state = (key_b, value_b, zero_heads, zero_heads, zero_heads)
    back_state = lax.fori_loop(0, ctx_size, back_turn, back_state)
    grad_key, grad_value, grad_query = (back_state[2], back_state[3], back_state[4])
    grad_proj_b = jnp.concatenate([grad_query * multiplier, grad_key, grad_value], axis=1).astype(
        jnp.bfloat16
    )
    grad_qkv = jnp.einsum(
        "shbe,sbd->hed", grad_proj_b, normed_b, preferred_element_type=jnp.float32
    )
    grad_normed_in = jnp.einsum(
        "shbe,hed->sbd", grad_proj_b, w_qkv, preferred_element_type=jnp.float32
    )
    grad_input_norm, grad_gain_one = norm_back(values_in, norm_gains[0], grad_normed_in)
    input_grad = grad_middle + grad_input_norm
    scale_term = (
        jnp.sum(grad_query * query_pre, axis=(0, 1, 2))
        * (score_base / math.sqrt(head_dim))
        * jax.nn.sigmoid(query_scale)
    )
    unit_grads = jnp.concatenate([grad_qkv, grad_out, grad_up, grad_down], axis=0)
    owner_total = lax.axis_size("fsdp") * slot_count
    table_grads = (
        jnp.zeros((owner_total, head_dim, width), jnp.float32).at[slot_rows].set(unit_grads)
    )
    owned = lax.psum_scatter(
        table_grads.astype(jnp.bfloat16), "fsdp", scatter_dimension=0, tiled=True
    )
    slot_sums = lax.psum_scatter(owned, "ctx", scatter_dimension=2, tiled=True).astype(jnp.float32)
    gain_sums, scale_sums, count = lax.psum(
        (jnp.stack([grad_gain_one, grad_gain_two]), scale_term, count_term), ("ctx", "fsdp")
    )
    new_master, new_first, new_second = adam_step(
        master, first_moment, second_moment, slot_sums / count, master_rate, decay_rate
    )
    new_gains, new_gain_first, new_gain_second = adam_step(
        norm_gains, gain_first, gain_second, gain_sums / count, gain_rate, 0.0
    )
    new_scale, new_scale_first, new_scale_second = adam_step(
        query_scale, scale_first, scale_second, scale_sums / count, scale_rate, 0.0
    )
    return (
        block_out,
        input_grad,
        new_master,
        new_first,
        new_second,
        new_gains,
        new_gain_first,
        new_gain_second,
        new_scale,
        new_scale_first,
        new_scale_second,
    )


def swapped(array, axis, distance):
    return lax.ppermute(
        array, axis, [(i, i ^ distance) for i in range(lax.axis_size(axis))]
    )


def summed(array, axis):
    size = lax.axis_size(axis)
    if size & (size - 1):
        return lax.psum(array, axis)
    distance = 1
    while distance < size:
        array = array + swapped(array, axis, distance)
        distance *= 2
    return array


def dot(left, right, left_dim, right_dim):
    return lax.dot_general(
        left,
        right,
        (((left_dim,), (right_dim,)), ((), ())),
        preferred_element_type=jnp.float32,
    )


def copy_rows_kernel(sizes, offsets, width, bound_ref, place_ref, row_ref, *refs):
    sources = refs[: len(offsets)]
    outs = refs[-2 - len(sizes) : -2]
    rows, sems = refs[-2:]
    for number, (source, offset) in enumerate(zip(sources, offsets)):

        @pl.loop(bound_ref[number], bound_ref[number + 1])
        def copy_row(i, source=source, offset=offset):
            pltpu.make_async_copy(
                source.at[row_ref[i], :, pl.ds(offset, width)],
                rows.at[place_ref[i]],
                sems.at[len(sizes)],
            ).start()

    pltpu.make_async_copy(rows, rows, sems.at[len(sizes)]).wait()
    copies, start = [], 0
    for place, (out, size) in enumerate(zip(outs, sizes)):
        copies.append(
            pltpu.make_async_copy(rows.at[pl.ds(start, size)], out, sems.at[place])
        )
        start += size
    for copy in copies:
        copy.start()
    for copy in copies:
        copy.wait()


def copy_plan(pick_from, pick_row, source_count):
    number = jnp.arange(pick_from.shape[0], dtype=jnp.int32)
    before = pick_from[None, :] < pick_from[:, None]
    same = (pick_from[None, :] == pick_from[:, None]) & (number[None, :] < number[:, None])
    rank = jnp.sum((before | same).astype(jnp.int32), axis=1)
    here = rank[None, :] == number[:, None]
    place = jnp.sum(jnp.where(here, number[None, :], 0), axis=1)
    row = jnp.sum(jnp.where(here, pick_row[None, :], 0), axis=1)
    bounds = jnp.sum(
        (pick_from[None, :] < jnp.arange(source_count + 1)[:, None]).astype(jnp.int32), axis=1
    )
    return (bounds.astype(jnp.int32), place.astype(jnp.int32), row.astype(jnp.int32))


def copy_rows(sources, offsets, width, plan, sizes, events=()):
    rows = sources[0].shape[1]
    total = sum(sizes)
    return pl.pallas_call(
        functools.partial(copy_rows_kernel, tuple(sizes), tuple(offsets), width),
        out_shape=[jax.ShapeDtypeStruct((size, rows, width), sources[0].dtype) for size in sizes],
        grid_spec=pltpu.PrefetchScalarGridSpec(
            num_scalar_prefetch=3,
            grid=(1,),
            in_specs=[pl.BlockSpec(memory_space=pltpu.HBM)] * (len(sources) + len(events)),
            out_specs=[pl.BlockSpec(memory_space=pltpu.HBM)] * len(sizes),
            scratch_shapes=[
                pltpu.VMEM((total, rows, width), sources[0].dtype),
                pltpu.SemaphoreType.DMA((len(sizes) + 1,)),
            ],
        ),
        compiler_params=pltpu.CompilerParams(vmem_limit_bytes=40 * 1024 * 1024),
        cost_estimate=pl.CostEstimate(flops=0, bytes_accessed=1024, transcendentals=0),
        name="copy_rows",
    )(*plan, *sources, *events)


def place_pieces_kernel(places, count_outs, *refs):
    pieces = refs[: len(places)]
    outs = refs[-1 - count_outs : -1]
    sems = refs[-1]
    copies = []
    for number, (piece, place) in enumerate(zip(pieces, places)):
        first, count, begin, size, column, out, row = place
        copies.append(
            pltpu.make_async_copy(
                piece.at[pl.ds(first, count), :, pl.ds(begin, size)],
                outs[out].at[pl.ds(row, count), :, pl.ds(column, size)],
                sems.at[number],
            )
        )
    for copy in copies:
        copy.start()
    for copy in copies:
        copy.wait()


def place_pieces(pieces, places, shapes, events=()):
    return pl.pallas_call(
        functools.partial(place_pieces_kernel, tuple(places), len(shapes)),
        out_shape=[jax.ShapeDtypeStruct(shape, pieces[0].dtype) for shape in shapes],
        in_specs=[pl.BlockSpec(memory_space=pltpu.HBM)] * (len(pieces) + len(events)),
        out_specs=[pl.BlockSpec(memory_space=pltpu.VMEM)] * len(shapes),
        scratch_shapes=[pltpu.SemaphoreType.DMA((len(pieces),))],
        compiler_params=pltpu.CompilerParams(vmem_limit_bytes=40 * 1024 * 1024),
        cost_estimate=pl.CostEstimate(flops=0, bytes_accessed=1024, transcendentals=0),
        name="place_pieces",
    )(*pieces, *events)


def scores_of(blocks, key_rows, query, i):
    size = query.shape[1]
    parts = [(i * size, size)] + ([(0, i * size)] if i else [])
    return [dot(key_rows[first : first + count, :], query, 1, 0) for first, count in parts]


def attend_kernel(blocks, pair, order_ref, q_ref, k_ref, v_ref, out_ref, log_ref, *refs):
    key_rows, value_cols = refs[:pair], refs[pair:]
    head_dim = q_ref.shape[0] // pair
    size = q_ref.shape[1] // blocks
    at = [pl.multiple_of(order_ref[i] * size, size) for i in range(blocks)]
    heads = [slice(p * head_dim, (p + 1) * head_dim) for p in range(pair)]
    for i in range(blocks):
        here = slice(i * size, (i + 1) * size)
        for p in range(pair):
            key_rows[p][here, :] = k_ref[heads[p], pl.ds(at[i], size)].T
            value_cols[p][:, here] = v_ref[heads[p], pl.ds(at[i], size)]
    key_pos = lax.broadcasted_iota(jnp.int32, (size, size), 0)
    query_pos = lax.broadcasted_iota(jnp.int32, (size, size), 1)
    seen = key_pos <= query_pos

    def scores(i):
        return [
            scores_of(blocks, key_rows[p], q_ref[heads[p], pl.ds(at[i], size)], i)
            for p in range(pair)
        ]

    upcoming = scores(0)
    for i in range(blocks):
        current = upcoming
        if i + 1 < blocks:
            upcoming = scores(i + 1)
        past = i * size
        for p in range(pair):
            near, *far = current[p]
            near = jnp.where(seen, near, masked_score)
            top = jnp.max(near, axis=0, keepdims=True)
            for part in far:
                top = jnp.maximum(top, jnp.max(part, axis=0, keepdims=True))
            near = jnp.exp(near - top)
            total = jnp.sum(near, axis=0, keepdims=True)
            value = dot(
                value_cols[p][:, past : past + size], near.astype(jnp.bfloat16), 1, 0
            )
            for part in far:
                part = jnp.exp(part - top)
                total = total + jnp.sum(part, axis=0, keepdims=True)
                value = value + dot(value_cols[p][:, :past], part.astype(jnp.bfloat16), 1, 0)
            out_ref[heads[p], pl.ds(at[i], size)] = (value / total).astype(jnp.bfloat16)
            log_ref[p, :, pl.ds(at[i], size)] = top + jnp.log(total)


def attend(projected, order, heads, head_dim):
    tokens = projected.shape[1]
    blocks = order.shape[0]
    pair = 4
    rows = pair * head_dim

    def part(first):
        return pl.BlockSpec((rows, tokens), lambda h, order, first=first: (first // pair + h, 0))

    return pl.pallas_call(
        functools.partial(attend_kernel, blocks, pair),
        out_shape=[
            jax.ShapeDtypeStruct((heads * head_dim, tokens), jnp.bfloat16),
            jax.ShapeDtypeStruct((heads, 1, tokens), jnp.float32),
        ],
        grid_spec=pltpu.PrefetchScalarGridSpec(
            num_scalar_prefetch=1,
            grid=(heads // pair,),
            in_specs=[part(0), part(heads), part(2 * heads)],
            out_specs=[
                pl.BlockSpec((rows, tokens), lambda h, order: (h, 0)),
                pl.BlockSpec((pair, 1, tokens), lambda h, order: (h, 0, 0)),
            ],
            scratch_shapes=[pltpu.VMEM((tokens, head_dim), jnp.bfloat16)] * pair
            + [pltpu.VMEM((head_dim, tokens), jnp.bfloat16)] * pair,
        ),
        compiler_params=pltpu.CompilerParams(vmem_limit_bytes=48 * 1024 * 1024),
        cost_estimate=pl.CostEstimate(
            flops=heads * tokens * tokens * head_dim * 4,
            bytes_accessed=heads * head_dim * tokens * 8,
            transcendentals=heads * tokens * tokens,
        ),
        name="attend",
    )(order, projected, projected, projected)


def attend_back_kernel(
    blocks,
    pair,
    order_ref,
    q_ref,
    k_ref,
    v_ref,
    grad_ref,
    log_ref,
    scale_ref,
    *refs,
):
    scratch = refs[-5 * pair :]
    out_ref, term_ref = refs[-5 * pair - 2 : -5 * pair]
    key_rows, key_cols, value_rows, key_sum, value_sum = (
        scratch[n * pair : (n + 1) * pair] for n in range(5)
    )
    head_dim = q_ref.shape[0] // pair
    size = q_ref.shape[1] // blocks
    at = [pl.multiple_of(order_ref[i] * size, size) for i in range(blocks)]
    heads = [slice(p * head_dim, (p + 1) * head_dim) for p in range(pair)]
    for i in range(blocks):
        here = slice(i * size, (i + 1) * size)
        for p in range(pair):
            key = k_ref[heads[p], pl.ds(at[i], size)]
            key_rows[p][here, :] = key.T
            key_cols[p][:, here] = key
            value_rows[p][here, :] = v_ref[heads[p], pl.ds(at[i], size)].T
    for p in range(pair):
        key_sum[p][...] = jnp.zeros_like(key_sum[p])
        value_sum[p][...] = jnp.zeros_like(value_sum[p])
    key_pos = lax.broadcasted_iota(jnp.int32, (size, size), 0)
    query_pos = lax.broadcasted_iota(jnp.int32, (size, size), 1)
    seen = key_pos <= query_pos
    terms = [jnp.zeros((head_dim, 1), jnp.float32) for _ in range(pair)]

    def products(i):
        return [
            (
                scores_of(blocks, key_rows[p], q_ref[heads[p], pl.ds(at[i], size)], i),
                scores_of(blocks, value_rows[p], grad_ref[heads[p], pl.ds(at[i], size)], i),
            )
            for p in range(pair)
        ]

    upcoming = products(0)
    for i in range(blocks):
        current = upcoming
        if i + 1 < blocks:
            upcoming = products(i + 1)
        past = i * size
        spans = [slice(past, past + size)] + ([slice(0, past)] if i else [])
        for p in range(pair):
            query = q_ref[heads[p], pl.ds(at[i], size)]
            grad = grad_ref[heads[p], pl.ds(at[i], size)]
            log_total = log_ref[p, :, pl.ds(at[i], size)]
            scores, grads = current[p]
            probs = [jnp.exp(part - log_total) for part in scores]
            probs[0] = jnp.where(seen, probs[0], 0.0)
            delta = jnp.zeros((1, size), jnp.float32)
            for prob, grad_prob in zip(probs, grads):
                delta = delta + jnp.sum(prob * grad_prob, axis=0, keepdims=True)
            grad_query = jnp.zeros(query.shape, jnp.float32)
            for cols, prob, grad_prob in zip(spans, probs, grads):
                grad_score = (prob * (grad_prob - delta)).astype(jnp.bfloat16)
                value_sum[p][:, cols] += dot(grad, prob.astype(jnp.bfloat16), 1, 1)
                key_sum[p][:, cols] += dot(query, grad_score, 1, 1)
                grad_query = grad_query + dot(key_cols[p][:, cols], grad_score, 1, 0)
            terms[p] = terms[p] + jnp.sum(
                grad_query * query.astype(jnp.float32), axis=1, keepdims=True
            )
            out_ref[0, heads[p], pl.ds(at[i], size)] = (grad_query * scale_ref[...]).astype(
                jnp.bfloat16
            )
    for i in range(blocks):
        here = slice(i * size, (i + 1) * size)
        for p in range(pair):
            out_ref[1, heads[p], pl.ds(at[i], size)] = key_sum[p][:, here].astype(jnp.bfloat16)
            out_ref[2, heads[p], pl.ds(at[i], size)] = value_sum[p][:, here].astype(jnp.bfloat16)
    for p in range(pair):
        term_ref[p] = terms[p]


def attend_back(
    projected, grad_attended, log_total, multiplier, order, heads, head_dim, events=()
):
    tokens = projected.shape[1]
    blocks = order.shape[0]
    pair = 4
    rows = pair * head_dim

    def part(first):
        return pl.BlockSpec((rows, tokens), lambda h, order, first=first: (first // pair + h, 0))

    return pl.pallas_call(
        functools.partial(attend_back_kernel, blocks, pair),
        out_shape=[
            jax.ShapeDtypeStruct((3, heads * head_dim, tokens), jnp.bfloat16),
            jax.ShapeDtypeStruct((heads, head_dim, 1), jnp.float32),
        ],
        grid_spec=pltpu.PrefetchScalarGridSpec(
            num_scalar_prefetch=1,
            grid=(heads // pair,),
            in_specs=[
                part(0),
                part(heads),
                part(2 * heads),
                part(0),
                pl.BlockSpec((pair, 1, tokens), lambda h, order: (h, 0, 0)),
                pl.BlockSpec((head_dim, 1), lambda h, order: (0, 0)),
            ]
            + [pl.BlockSpec(memory_space=pltpu.HBM)] * len(events),
            out_specs=[
                pl.BlockSpec((3, rows, tokens), lambda h, order: (0, h, 0)),
                pl.BlockSpec((pair, head_dim, 1), lambda h, order: (h, 0, 0)),
            ],
            scratch_shapes=[pltpu.VMEM((tokens, head_dim), jnp.bfloat16)] * pair
            + [pltpu.VMEM((head_dim, tokens), jnp.bfloat16)] * pair
            + [pltpu.VMEM((tokens, head_dim), jnp.bfloat16)] * pair
            + [pltpu.VMEM((head_dim, tokens), jnp.float32)] * (2 * pair),
        ),
        compiler_params=pltpu.CompilerParams(vmem_limit_bytes=56 * 1024 * 1024),
        cost_estimate=pl.CostEstimate(
            flops=heads * tokens * tokens * head_dim * 10,
            bytes_accessed=heads * head_dim * tokens * 14,
            transcendentals=heads * tokens * tokens,
        ),
        name="attend_back",
    )(order, projected, projected, projected, grad_attended, log_total, multiplier, *events)


def paired_layer(
    inputs,
    targets,
    valid_counts,
    owners,
    master,
    first_moment,
    second_moment,
    norm_gains,
    gain_first,
    gain_second,
    query_scale,
    scale_first,
    scale_second,
):
    bf16 = jnp.bfloat16
    f32 = jnp.float32
    seq_local, block_rows, width = inputs.shape
    slot_count, head_dim, column_count = master.shape
    ff_blocks = FF // head_dim
    owner_count = lax.axis_size("fsdp")
    device = lax.axis_index("ctx")
    chip, core = device // 2, device % 2
    owner_here = lax.axis_index("fsdp")
    low_here = owner_here % 2
    high_here = owner_here // 2
    high_count = owner_count // 2
    high_distances = range(1, high_count)
    half_width = width // 2
    half_slots = slot_count // 2
    half_rows = seq_local * block_rows
    half_heads = H // 2
    half_blocks = ff_blocks // 2
    set_units = 4 * half_heads + 2 * half_blocks
    first_chip, first_core = chip == 0, core == 0

    def columns_here(array):
        return jnp.where(first_chip, array, jnp.roll(array, half_width, axis=-1))

    def sequence_rows(array):
        own = jnp.where(first_chip, array[0], array[1])
        got = swapped(jnp.where(first_chip, array[1], array[0]), "ctx", 2)
        return jnp.where(
            first_chip, jnp.concatenate([own, got]), jnp.concatenate([got, own])
        )

    def rows_apart(array):
        array = columns_here(array)
        first, last = array[:block_rows], array[block_rows:]
        other = jnp.where(first_chip, last, first).astype(bf16)
        return (jnp.where(first_chip, first, last), swapped(other, "ctx", 2))

    def rows_home(own, got):
        got = got.astype(f32)
        return jnp.where(first_chip, jnp.stack([own, got]), jnp.stack([got, own]))

    slot_rows = unit_rows(owners, slot_count)
    unit_total = owners.shape[0]
    kind_sizes = [H, H, H, H, ff_blocks, ff_blocks]
    kind_starts = [sum(kind_sizes[:i]) for i in range(6)]

    def unit_list(kinds, which):
        return jnp.concatenate(
            [
                kind_starts[k] + which * (kind_sizes[k] // 2) + jnp.arange(kind_sizes[k] // 2)
                for k in kinds
            ]
        ).astype(jnp.int32)

    wanted = jnp.concatenate(
        [unit_list(range(6), core), unit_list((4, 5), 1 - core)]
    )
    wanted_rows = slot_rows[wanted]
    wanted_owner, wanted_slot = wanted_rows // slot_count, wanted_rows % slot_count
    weight_from = 2 * (wanted_slot // half_slots != core) + (wanted_owner % 2 != low_here)
    weight_from = weight_from.astype(jnp.int32)
    weight_row = ((wanted_owner // 2) ^ high_here) * half_slots + wanted_slot % half_slots
    weight_plan = copy_plan(weight_from, weight_row, 4)
    weight_sizes = [3 * half_heads, half_heads + 2 * half_blocks, 2 * half_blocks]

    chunks = [(0, 128), (128, 128), (256, 256)]
    lead = 512
    tail = half_width - lead
    shard = master.astype(bf16)
    own_half = jnp.where(first_core, shard[:half_slots], shard[half_slots:])
    got_half = swapped(jnp.where(first_core, shard[half_slots:], shard[:half_slots]), "ctx", 1)
    shard = jnp.where(
        first_core,
        jnp.concatenate([own_half, got_half], axis=2),
        jnp.concatenate([got_half, own_half], axis=2),
    )
    shard, inputs, targets = lax.optimization_barrier((shard, inputs, targets))
    values_b = columns_here(sequence_rows(inputs))
    targets_b = columns_here(sequence_rows(targets))
    shard_last = shard[:, :, lead:]
    shards = [shard[:, :, start : start + size] for start, size in chunks]
    shards.append(jnp.concatenate([shard_last, swapped(shard_last, "ctx", 2)], axis=2))
    highs, lows, firsts = [], [], []
    for number, part in enumerate(shards):
        if number:
            part, gathered = lax.optimization_barrier((part, gathered))
            highs[-1] = gathered
        pieces = [part] + [swapped(part, "fsdp", 2 * d) for d in high_distances]
        firsts.append(pieces[1])
        gathered = jnp.concatenate(pieces)
        highs.append(gathered)
    own_units, rest_units, far_units = weight_sizes
    near_units = own_units + rest_units

    def pick_units(number, sizes, events):
        high, low = highs[number], lows[number]
        sources = [high, low, swapped(high, "ctx", 1), swapped(low, "ctx", 1)]
        return copy_rows(sources, [0] * 4, high.shape[2], weight_plan, sizes, events)

    lows.append(swapped(highs[0], "fsdp", 1))
    lows[0], highs[1] = lax.optimization_barrier((lows[0], highs[1]))
    near_one, far_one = pick_units(0, [near_units, far_units], [firsts[2]])
    got_one = swapped(near_one, "ctx", 2)
    highs[1], far_one = lax.optimization_barrier((highs[1], far_one))
    highs[3], got_one = lax.optimization_barrier((highs[3], got_one))
    for number in range(1, 4):
        if number == 3:
            near_two, far_two = pick_units(1, [near_units, far_units], [values_b, got_one])
            highs[3], far_two = lax.optimization_barrier((highs[3], far_two))
        if number > 1:
            highs[number], lows[-1] = lax.optimization_barrier((highs[number], lows[-1]))
        lows.append(swapped(highs[number], "fsdp", 1))
    got_two = swapped(near_two, "ctx", 2)
    qkv_three, rest_three, far_three = pick_units(2, weight_sizes, [targets_b, got_two])
    qkv_got = swapped(qkv_three, "ctx", 2)
    rest_three, qkv_got = lax.optimization_barrier((rest_three, qkv_got))
    rest_got = swapped(rest_three, "ctx", 2)
    qkv_last, rest_last, far_last = pick_units(3, weight_sizes, [qkv_got])

    def columns_of(owns, gots, last):
        pieces = [(last, 0, tail, lead), (last, tail, tail, half_width + lead)]
        for (start, size), own, got in zip(chunks, owns, gots):
            pieces += [(own, 0, size, start), (got, 0, size, half_width + start)]
        return pieces

    def placed(pieces, from_end, count, out, row):
        return [
            (piece.shape[0] - from_end if from_end else 0, count, *columns, out, row)
            for piece, *columns in pieces
        ]

    qkv_pieces = columns_of(
        [near_one, near_two, qkv_three], [got_one, got_two, qkv_got], qkv_last
    )
    rest_pieces = columns_of(
        [near_one, near_two, rest_three], [got_one, got_two, rest_got], rest_last
    )
    far_pieces = columns_of(
        [far_one, far_two, far_three],
        [swapped(got, "ctx", 1) for got in (got_one, got_two, rest_got)],
        far_last,
    )
    (w_qkv,) = place_pieces(
        [piece for piece, *_ in qkv_pieces],
        placed(qkv_pieces, 0, own_units, 0, 0),
        [(own_units, head_dim, width)],
    )
    w_qkv = w_qkv.reshape(-1, width)

    gains = columns_here(norm_gains)
    values_in = values_b.astype(f32)
    normed_own = (values_in * inverse_rms(values_in) * gains[0]).astype(bf16)
    normed_b = jnp.concatenate([normed_own, swapped(normed_own, "ctx", 1)])
    base = score_base / math.sqrt(head_dim)
    multiplier = jax.nn.softplus(query_scale) * base
    row_scale = jnp.concatenate(
        [jnp.tile(multiplier, half_heads), jnp.ones((2 * half_heads * head_dim,), f32)]
    )
    projected = (dot(w_qkv, normed_b, 1, 1) * row_scale[:, None]).astype(bf16)
    positions = jnp.arange(4, dtype=jnp.int32)
    order = jnp.where(positions % 2 == core, 0, 2) + positions // 2
    order = order.astype(jnp.int32)
    attended, log_total = attend(projected, order, half_heads, head_dim)
    (w_out,) = place_pieces(
        [piece for piece, *_ in rest_pieces],
        placed(rest_pieces, rest_units, half_heads, 0, 0),
        [(half_heads, head_dim, width)],
        [log_total],
    )
    mlp_pieces, mlp_places = [], []
    for row, pieces in ((0, rest_pieces), (half_blocks, far_pieces)):
        for kind in range(2):
            mlp_pieces += [piece for piece, *_ in pieces]
            mlp_places += placed(pieces, (2 - kind) * half_blocks, half_blocks, kind, row)
    w_up, w_down = place_pieces(
        mlp_pieces, mlp_places, [(ff_blocks, head_dim, width)] * 2, [log_total]
    )
    w_out = w_out.reshape(-1, width)
    w_up = w_up.reshape(-1, width)
    w_down = w_down.reshape(-1, width)
    branch_far = dot(attended[:, half_rows:], w_out, 0, 0).astype(bf16)
    branch_got = swapped(branch_far, "ctx", 1)
    branch_own = dot(attended[:, :half_rows], w_out, 0, 0)
    middle = values_in + (branch_own + branch_got.astype(f32))
    normed_mid_b = (middle * inverse_rms(middle) * gains[1]).astype(bf16)
    hidden = dot(normed_mid_b, w_up, 1, 1)
    active_b = jax.nn.silu(hidden).astype(bf16)
    block_out = middle + dot(active_b, w_down, 1, 0)
    seq_length = 2 * half_rows
    row = jnp.arange(half_rows, dtype=jnp.int32)
    row_pos = (core + 2 * (row // block_rows)) * block_rows + row % block_rows
    valid = jnp.where(first_chip, valid_counts[0], valid_counts[1])
    counted = (row_pos >= seq_length - valid).astype(f32)
    count_term = jnp.sum(counted)

    (apart,) = lax.optimization_barrier((block_out,))
    block_own, block_got = rows_apart(apart)

    out_grad = 2.0 * (block_out - targets_b.astype(f32)) * counted[:, None]
    out_grad_b = out_grad.astype(bf16)
    grad_active = dot(out_grad_b, w_down, 1, 1)
    sigma = jax.nn.sigmoid(hidden)
    grad_hidden_b = (grad_active * sigma * (1.0 + hidden * (1.0 - sigma))).astype(bf16)
    grad_normed_mid = dot(grad_hidden_b, w_up, 1, 0)
    inverse = inverse_rms(middle)
    scaled = grad_normed_mid * gains[1]
    grad_middle = out_grad + (
        inverse * scaled
        - middle * inverse**3 * jnp.mean(scaled * middle, axis=-1, keepdims=True)
    )
    grad_gain_two = jnp.sum(grad_normed_mid * middle * inverse, axis=0)
    grad_middle_own = grad_middle.astype(bf16)
    grad_middle_got = swapped(grad_middle_own, "ctx", 1)
    far_blocks = half_blocks * head_dim
    wide = slice(half_width + 256, half_width + lead)
    slim = slice(half_width, half_width + 256)
    block_grads = []
    for left, right in ((grad_hidden_b, normed_mid_b), (active_b, out_grad_b)):
        got = swapped(dot(left[:, far_blocks:], right, 0, 0).astype(bf16), "ctx", 1)
        total = dot(left[:, :far_blocks], right, 0, 0) + got.astype(f32)
        block_grads.append(total.astype(bf16).reshape(half_blocks, head_dim, width))
    block_grads = jnp.concatenate(block_grads)
    grad_middle_got, block_grads = lax.optimization_barrier((grad_middle_got, block_grads))
    grad_middle_b = jnp.concatenate([grad_middle_own, grad_middle_got])
    grad_attended = dot(w_out, grad_middle_b, 1, 1).astype(bf16)
    head_grads = dot(attended, grad_middle_b, 1, 0).astype(bf16)
    head_grads = head_grads.reshape(half_heads, head_dim, width)

    def early_columns(columns):
        return jnp.concatenate([head_grads[:, :, columns], block_grads[:, :, columns]])

    early_wide, early_slim = early_columns(wide), early_columns(slim)
    wide_got = swapped(early_wide, "ctx", 2)

    def last_columns(array):
        return jnp.concatenate(
            [array[..., lead:half_width], array[..., half_width + lead :]], axis=-1
        )

    early_last = jnp.concatenate([last_columns(head_grads), last_columns(block_grads)])
    grad_proj, grad_scale = attend_back(
        projected,
        grad_attended,
        log_total,
        multiplier[:, None],
        order,
        half_heads,
        head_dim,
        [early_wide, early_slim, early_last, block_got],
    )
    grad_proj = grad_proj.reshape(-1, grad_proj.shape[2])
    scale_term = (
        jnp.sum(grad_scale[:, :, 0], axis=0) / multiplier * base * jax.nn.sigmoid(query_scale)
    )

    low_order = jnp.stack([low_here, 1 - low_here])
    table_slots = (
        (2 * (jnp.arange(high_count) ^ high_here)[None, :, None] + low_order[:, None, None])
        * slot_count
        + core * half_slots
        + jnp.arange(half_slots)[None, None, :]
    ).reshape(-1)
    holds = table_slots[:, None] == slot_rows[None, :]
    unit_order = jnp.arange(unit_total, dtype=jnp.int32)
    slot_unit = jnp.sum(jnp.where(holds, unit_order[None, :] + 1, 0), axis=1) - 1
    kind = jnp.where(
        slot_unit < 4 * H, slot_unit // H, 4 + (slot_unit - 4 * H) // ff_blocks
    )
    kind_size = jnp.where(kind < 4, H, ff_blocks)
    within = jnp.where(kind < 4, slot_unit % H, (slot_unit - 4 * H) % ff_blocks)
    other_set = (within // (kind_size // 2) != core).astype(jnp.int32)
    rank = within % (kind_size // 2)
    grad_row = rank + jnp.where(
        kind <= 3, kind * half_heads, 4 * half_heads + (kind - 4) * half_blocks
    )
    empty = slot_unit < 0
    grad_from = jnp.where(empty, 2, other_set).astype(jnp.int32)
    grad_row = jnp.where(empty, 0, grad_row).astype(jnp.int32)
    grad_plan = copy_plan(grad_from, grad_row, 3)
    zero = jnp.zeros((1, head_dim, 256), bf16)

    def pick_table(own, got, offset, size, events=()):
        return copy_rows(
            [own, got, zero],
            [offset, offset, 0],
            size,
            grad_plan,
            [high_count * half_slots] * 2,
            events,
        )

    def table_sums(keep, got):
        sums = []
        for d in range(high_count):
            rows = slice(d * half_slots, (d + 1) * half_slots)
            sums.append((keep[rows].astype(f32) + got[rows].astype(f32)).astype(bf16))
        return sums

    def from_owners(tables):
        return [swapped(tables[d], "fsdp", 2 * d) for d in high_distances]

    def owner_sum(table, got):
        total = table.astype(f32)
        for part in got:
            total = total + part.astype(f32)
        return total.astype(bf16)

    def proj_grad(columns):
        return dot(grad_proj, columns, 1, 0).astype(bf16).reshape(-1, head_dim, columns.shape[1])

    def chip_sum(start, proj_got, early_got):
        near = slice(start, start + 256)
        parts = [
            (proj_grad(normed_b[:, near]), proj_got),
            (head_grads[:, :, near], early_got[:half_heads]),
            (block_grads[:, :, near], early_got[half_heads:]),
        ]
        return jnp.concatenate(
            [(own.astype(f32) + got.astype(f32)).astype(bf16) for own, got in parts]
        )

    proj_last = proj_grad(last_columns(normed_b))
    proj_last, wide_got = lax.optimization_barrier((proj_last, wide_got))
    total_last = jnp.concatenate([proj_last, early_last])
    wide_far = proj_grad(normed_b[:, wide])
    wide_proj = swapped(wide_far, "ctx", 2)
    keep_last, send_last = pick_table(
        total_last, swapped(total_last, "ctx", 1), 0, 256, [wide_far]
    )
    low_last = swapped(send_last, "fsdp", 1)
    keep_last, grad_proj = lax.optimization_barrier((keep_last, grad_proj))
    slim_far = jnp.concatenate([proj_grad(normed_b[:, slim]), early_slim])
    normed_far = dot(grad_proj[:, half_rows:], w_qkv, 0, 0).astype(bf16)
    normed_got = swapped(normed_far, "ctx", 1)
    low_last, wide_proj, slim_far, normed_got = lax.optimization_barrier(
        (low_last, wide_proj, slim_far, normed_got)
    )
    slim_got = swapped(slim_far, "ctx", 2)
    total = chip_sum(256, wide_proj, wide_got)
    keep_three, send_three = pick_table(total, swapped(total, "ctx", 1), 0, 256)
    low_last, keep_three, grad_proj = lax.optimization_barrier((low_last, keep_three, grad_proj))
    low_three = swapped(send_three, "fsdp", 1)
    tables_last = table_sums(keep_last, low_last)
    high_last = from_owners(tables_last)
    grad_normed_in = dot(grad_proj[:, :half_rows], w_qkv, 0, 0) + normed_got.astype(f32)
    inverse = inverse_rms(values_in)
    scaled = grad_normed_in * gains[0]
    input_grad = grad_middle + (
        inverse * scaled
        - values_in * inverse**3 * jnp.mean(scaled * values_in, axis=-1, keepdims=True)
    )
    grad_gain_one = jnp.sum(grad_normed_in * values_in * inverse, axis=0)
    low_three, high_last, slim_got, input_grad = lax.optimization_barrier(
        (low_three, high_last, slim_got, input_grad)
    )
    total = chip_sum(0, slim_got[: 3 * half_heads], slim_got[3 * half_heads :])
    total_got = swapped(total, "ctx", 1)
    keep_two, send_two = pick_table(
        total, total_got, 128, 128, [low_three]
    )
    low_two = swapped(send_two, "fsdp", 1)
    keep_two, low_three, high_last = lax.optimization_barrier((keep_two, low_three, high_last))
    tables_three = table_sums(keep_three, low_three)
    high_three = from_owners(tables_three)
    tables_two = table_sums(keep_two, low_two)
    keep_one, send_one = pick_table(total, total_got, 0, 128, tables_two)
    tables_two, high_three = lax.optimization_barrier((tables_two, high_three))
    high_two = from_owners(tables_two)

    gain_terms = columns_here(jnp.stack([grad_gain_one, grad_gain_two]))
    small = jnp.concatenate([gain_terms.reshape(-1), scale_term, count_term[None]])
    small = jnp.pad(small, (0, -small.shape[0] % 1024))
    keep_one, small = lax.optimization_barrier((keep_one, small))
    tables_one = table_sums(keep_one, swapped(send_one, "fsdp", 1))
    small = small + swapped(small, "fsdp", 1)
    tables_one, high_two, small, input_grad = lax.optimization_barrier(
        (tables_one, high_two, small, input_grad)
    )
    high_one = from_owners(tables_one)
    small_got = from_owners([small] * high_count)
    high_one, small_got = lax.optimization_barrier((high_one, small_got))
    small = summed((small + small_got[0]) + (small_got[1] + small_got[2]), "ctx")
    gain_sums = small[: 2 * width].reshape(2, width)
    scale_sums = small[2 * width : 2 * width + head_dim]
    count = small[2 * width + head_dim]

    owned_last = owner_sum(tables_last[0], high_last)
    owned_got = swapped(owned_last[:, :, tail:], "ctx", 2)
    owned = [
        owner_sum(tables_one[0], high_one),
        owner_sum(tables_two[0], high_two),
        owner_sum(tables_three[0], high_three),
        (owned_last[:, :, :tail].astype(f32) + owned_got.astype(f32)).astype(bf16),
    ]
    owned = jnp.concatenate(owned, axis=2).reshape(half_slots, head_dim, 2, column_count)
    kept = jnp.where(first_core, owned[:, :, 0], owned[:, :, 1])
    sent = swapped(jnp.where(first_core, owned[:, :, 1], owned[:, :, 0]), "ctx", 1)
    slot_sums = jnp.where(
        first_core, jnp.concatenate([kept, sent]), jnp.concatenate([sent, kept])
    ).astype(f32)
    new_master, new_first, new_second = adam_step(
        master, first_moment, second_moment, slot_sums / count, master_rate, decay_rate
    )
    new_gains, new_gain_first, new_gain_second = adam_step(
        norm_gains, gain_first, gain_second, gain_sums / count, gain_rate, 0.0
    )
    new_scale, new_scale_first, new_scale_second = adam_step(
        query_scale, scale_first, scale_second, scale_sums / count, scale_rate, 0.0
    )
    return (
        rows_home(block_own, block_got),
        rows_home(*rows_apart(input_grad)),
        new_master,
        new_first,
        new_second,
        new_gains,
        new_gain_first,
        new_gain_second,
        new_scale,
        new_scale_first,
        new_scale_second,
    )


def on_device(*arguments):
    paired = (
        lax.axis_size("ctx") == 4
        and lax.axis_size("fsdp") == 8
        and arguments[0].shape[0] == 2
    )
    return (paired_layer if paired else general_layer)(*arguments)


def solution(mesh):
    in_specs = (
        P("fsdp", "ctx", None),
        P("fsdp", "ctx", None),
        P("fsdp"),
        P(),
        P("fsdp", None, "ctx"),
        P("fsdp", None, "ctx"),
        P("fsdp", None, "ctx"),
        P(),
        P(),
        P(),
        P(),
        P(),
        P(),
    )
    out_specs = (
        P("fsdp", "ctx", None),
        P("fsdp", "ctx", None),
        P("fsdp", None, "ctx"),
        P("fsdp", None, "ctx"),
        P("fsdp", None, "ctx"),
        P(),
        P(),
        P(),
        P(),
        P(),
        P(),
    )
    return jax.shard_map(
        on_device, mesh=mesh, in_specs=in_specs, out_specs=out_specs, check_vma=False
    )
```

```python
import functools
import math

import jax
import jax.numpy as jnp
from jax import lax
from jax.experimental import pallas as pl
from jax.experimental.pallas import tpu as pltpu
from jax.sharding import PartitionSpec as P

H = 16
FF = 1280
STEP = 10


norm_eps = 1e-06
beta_first = 0.9
beta_second = 0.95
adam_eps = 1e-08
decay_rate = 0.1
master_rate = 0.05
gain_rate = 2.0
scale_rate = 2.0
score_base = 1.442695041
masked_score = -1e30


def from_behind(block, axis, distance):
    devices = range(lax.axis_size(axis))
    route = [(i - distance, i) for i in devices if i - distance in devices]
    return lax.ppermute(block, axis, route)


def shifted(array, axis, by):
    count = lax.axis_size(axis)
    return lax.ppermute(array, axis, [(i, (i + by) % count) for i in range(count)])


def unit_rows(owners, slot_count):
    unit_count = owners.shape[0]
    unit_order = jnp.arange(unit_count, dtype=jnp.int32)
    same_owner = owners[:, None] == owners[None, :]
    earlier = unit_order[None, :] < unit_order[:, None]
    slot_rank = jnp.sum((same_owner & earlier).astype(jnp.int32), axis=1)
    return owners * slot_count + slot_rank


def inverse_rms(values):
    return lax.rsqrt(jnp.mean(values * values, axis=-1, keepdims=True) + norm_eps)


def norm_back(values, gain, grad_normed):
    inverse = inverse_rms(values)
    scaled = grad_normed * gain
    grad_values = inverse * scaled - values * inverse**3 * jnp.mean(
        scaled * values, axis=-1, keepdims=True
    )
    grad_gain = jnp.sum(grad_normed * values * inverse, axis=(0, 1))
    return (grad_values, grad_gain)


def adam_step(values, moment_one, moment_two, gradient, step_rate, weight_decay):
    moment_one = beta_first * moment_one + (1.0 - beta_first) * gradient
    moment_two = beta_second * moment_two + (1.0 - beta_second) * gradient * gradient
    first_hat = moment_one / (1.0 - beta_first**STEP)
    second_hat = moment_two / (1.0 - beta_second**STEP)
    values = values - step_rate * (
        first_hat / (jnp.sqrt(second_hat) + adam_eps) + weight_decay * values
    )
    return (values, moment_one, moment_two)


def general_layer(
    inputs,
    targets,
    valid_counts,
    owners,
    master,
    first_moment,
    second_moment,
    norm_gains,
    gain_first,
    gain_second,
    query_scale,
    scale_first,
    scale_second,
):
    seq_local, block_rows, width = inputs.shape
    slot_count, head_dim, column_count = master.shape
    ff_blocks = FF // head_dim
    ctx_size = lax.axis_size("ctx")
    ctx_index = lax.axis_index("ctx")
    slot_rows = unit_rows(owners, slot_count)
    owner_table = lax.all_gather(master.astype(jnp.bfloat16), "fsdp", axis=0, tiled=True)
    picked = owner_table[slot_rows]
    weights = lax.all_gather(picked, "ctx", axis=2, tiled=True)
    w_qkv = weights[0 : 3 * H]
    w_out = weights[3 * H : 4 * H]
    w_up = weights[4 * H : 4 * H + ff_blocks]
    w_down = weights[4 * H + ff_blocks :]
    values_in = inputs.astype(jnp.float32)
    normed_b = (values_in * inverse_rms(values_in) * norm_gains[0]).astype(jnp.bfloat16)
    projected = jnp.einsum("sbd,hed->shbe", normed_b, w_qkv, preferred_element_type=jnp.float32)
    query_pre = projected[:, 0:H]
    multiplier = jax.nn.softplus(query_scale) * (score_base / math.sqrt(head_dim))
    query_b = (query_pre * multiplier).astype(jnp.bfloat16)
    key_b = projected[:, H : 2 * H].astype(jnp.bfloat16)
    value_b = projected[:, 2 * H : 3 * H].astype(jnp.bfloat16)
    query_rows = ctx_index * block_rows + jnp.arange(block_rows, dtype=jnp.int32)
    last_row = ctx_index * block_rows + block_rows - 1
    start_state = (
        jnp.full(query_pre.shape[:3], masked_score, jnp.float32),
        jnp.zeros(query_pre.shape[:3], jnp.float32),
        jnp.zeros(query_pre.shape, jnp.float32),
    )
    key_part = lax.all_gather(key_b, "ctx", axis=2, tiled=True)
    value_part = lax.all_gather(value_b, "ctx", axis=2, tiled=True)
    key_count = key_part.shape[2]

    def update(current):
        run_max, run_sum, accum = current
        key_rows = jnp.arange(key_count, dtype=jnp.int32)
        allowed = query_rows[:, None] >= key_rows[None, :]
        scores = jnp.einsum(
            "shqe,shke->shqk", query_b, key_part, preferred_element_type=jnp.float32
        )
        scores = jnp.where(allowed, scores, masked_score)
        new_max = jnp.maximum(run_max, jnp.max(scores, axis=-1))
        attn_probs = jnp.where(allowed, jnp.exp(scores - new_max[..., None]), 0.0)
        run_sum = jnp.sum(attn_probs, axis=-1)
        accum = jnp.einsum(
            "shqk,shke->shqe",
            attn_probs.astype(jnp.bfloat16),
            value_part,
            preferred_element_type=jnp.float32,
        )
        return (new_max, run_sum, accum)

    run_max, run_sum, accum = lax.cond(
        jnp.int32(0) <= last_row, update, lambda current: current, start_state
    )
    attended = accum / run_sum[..., None]
    log_total = run_max + jnp.log(run_sum)
    attended_b = attended.astype(jnp.bfloat16)
    branch = jnp.einsum("shbe,hed->sbd", attended_b, w_out, preferred_element_type=jnp.float32)
    middle = values_in + branch
    normed_mid_b = (middle * inverse_rms(middle) * norm_gains[1]).astype(jnp.bfloat16)
    hidden = jnp.einsum("sbd,fed->sbfe", normed_mid_b, w_up, preferred_element_type=jnp.float32)
    active_b = jax.nn.silu(hidden).astype(jnp.bfloat16)
    block_out = middle + jnp.einsum(
        "sbfe,fed->sbd", active_b, w_down, preferred_element_type=jnp.float32
    )
    seq_length = block_rows * ctx_size
    counted = (query_rows[None, :] >= (seq_length - valid_counts)[:, None]).astype(jnp.float32)
    count_term = jnp.sum(counted)
    out_grad = 2.0 * (block_out - targets.astype(jnp.float32)) * counted[..., None]
    out_grad_b = out_grad.astype(jnp.bfloat16)
    grad_down = jnp.einsum(
        "sbfe,sbd->fed", active_b, out_grad_b, preferred_element_type=jnp.float32
    )
    grad_active = jnp.einsum(
        "sbd,fed->sbfe", out_grad_b, w_down, preferred_element_type=jnp.float32
    )
    sigma = jax.nn.sigmoid(hidden)
    grad_hidden_b = (grad_active * sigma * (1.0 + hidden * (1.0 - sigma))).astype(jnp.bfloat16)
    grad_up = jnp.einsum(
        "sbfe,sbd->fed", grad_hidden_b, normed_mid_b, preferred_element_type=jnp.float32
    )
    grad_normed_mid = jnp.einsum(
        "sbfe,fed->sbd", grad_hidden_b, w_up, preferred_element_type=jnp.float32
    )
    grad_middle_norm, grad_gain_two = norm_back(middle, norm_gains[1], grad_normed_mid)
    grad_middle = out_grad + grad_middle_norm
    grad_middle_b = grad_middle.astype(jnp.bfloat16)
    grad_out = jnp.einsum(
        "shbe,sbd->hed", attended_b, grad_middle_b, preferred_element_type=jnp.float32
    )
    grad_attended_b = jnp.einsum(
        "sbd,hed->shbe", grad_middle_b, w_out, preferred_element_type=jnp.float32
    ).astype(jnp.bfloat16)
    delta = jnp.sum(grad_attended_b.astype(jnp.float32) * attended, axis=-1)

    def block_grads(source, key_cur, value_cur, partial_grads):
        grad_key, grad_value, grad_query = partial_grads
        key_rows = source * block_rows + jnp.arange(block_rows, dtype=jnp.int32)
        allowed = query_rows[:, None] >= key_rows[None, :]
        scores = jnp.einsum("shqe,shke->shqk", query_b, key_cur, preferred_element_type=jnp.float32)
        scores = jnp.where(allowed, scores, masked_score)
        attn_probs = jnp.exp(scores - log_total[..., None])
        grad_value = grad_value + jnp.einsum(
            "shqk,shqe->shke",
            attn_probs.astype(jnp.bfloat16),
            grad_attended_b,
            preferred_element_type=jnp.float32,
        )
        grad_probs = jnp.einsum(
            "shqe,shke->shqk", grad_attended_b, value_cur, preferred_element_type=jnp.float32
        )
        grad_scores_b = (attn_probs * (grad_probs - delta[..., None])).astype(jnp.bfloat16)
        grad_query = grad_query + jnp.einsum(
            "shqk,shke->shqe", grad_scores_b, key_cur, preferred_element_type=jnp.float32
        )
        grad_key = grad_key + jnp.einsum(
            "shqk,shqe->shke", grad_scores_b, query_b, preferred_element_type=jnp.float32
        )
        return (grad_key, grad_value, grad_query)

    zero_heads = jnp.zeros(query_pre.shape, jnp.float32)

    def back_turn(which_turn, current):
        key_cur, value_cur, grad_key, grad_value, grad_query = current
        source = (ctx_index - which_turn) % ctx_size
        grad_key, grad_value, grad_query = lax.cond(
            source <= ctx_index,
            lambda parts: block_grads(source, key_cur, value_cur, parts),
            lambda parts: parts,
            (grad_key, grad_value, grad_query),
        )
        key_cur, value_cur = from_behind((key_cur, value_cur), "ctx", 1)
        grad_key, grad_value = (
            shifted(grad_key.astype(jnp.bfloat16), "ctx", 1).astype(grad_key.dtype),
            shifted(grad_value.astype(jnp.bfloat16), "ctx", 1).astype(grad_value.dtype),
        )
        return (key_cur, value_cur, grad_key, grad_value, grad_query)

    back_state = (key_b, value_b, zero_heads, zero_heads, zero_heads)
    back_state = lax.fori_loop(0, ctx_size, back_turn, back_state)
    grad_key, grad_value, grad_query = (back_state[2], back_state[3], back_state[4])
    grad_proj_b = jnp.concatenate([grad_query * multiplier, grad_key, grad_value], axis=1).astype(
        jnp.bfloat16
    )
    grad_qkv = jnp.einsum(
        "shbe,sbd->hed", grad_proj_b, normed_b, preferred_element_type=jnp.float32
    )
    grad_normed_in = jnp.einsum(
        "shbe,hed->sbd", grad_proj_b, w_qkv, preferred_element_type=jnp.float32
    )
    grad_input_norm, grad_gain_one = norm_back(values_in, norm_gains[0], grad_normed_in)
    input_grad = grad_middle + grad_input_norm
    scale_term = (
        jnp.sum(grad_query * query_pre, axis=(0, 1, 2))
        * (score_base / math.sqrt(head_dim))
        * jax.nn.sigmoid(query_scale)
    )
    unit_grads = jnp.concatenate([grad_qkv, grad_out, grad_up, grad_down], axis=0)
    owner_total = lax.axis_size("fsdp") * slot_count
    table_grads = (
        jnp.zeros((owner_total, head_dim, width), jnp.float32).at[slot_rows].set(unit_grads)
    )
    owned = lax.psum_scatter(
        table_grads.astype(jnp.bfloat16), "fsdp", scatter_dimension=0, tiled=True
    )
    slot_sums = lax.psum_scatter(owned, "ctx", scatter_dimension=2, tiled=True).astype(jnp.float32)
    gain_sums, scale_sums, count = lax.psum(
        (jnp.stack([grad_gain_one, grad_gain_two]), scale_term, count_term), ("ctx", "fsdp")
    )
    new_master, new_first, new_second = adam_step(
        master, first_moment, second_moment, slot_sums / count, master_rate, decay_rate
    )
    new_gains, new_gain_first, new_gain_second = adam_step(
        norm_gains, gain_first, gain_second, gain_sums / count, gain_rate, 0.0
    )
    new_scale, new_scale_first, new_scale_second = adam_step(
        query_scale, scale_first, scale_second, scale_sums / count, scale_rate, 0.0
    )
    return (
        block_out,
        input_grad,
        new_master,
        new_first,
        new_second,
        new_gains,
        new_gain_first,
        new_gain_second,
        new_scale,
        new_scale_first,
        new_scale_second,
    )


def swapped(array, axis, distance):
    return lax.ppermute(
        array, axis, [(i, i ^ distance) for i in range(lax.axis_size(axis))]
    )


def summed(array, axis):
    size = lax.axis_size(axis)
    if size & (size - 1):
        return lax.psum(array, axis)
    distance = 1
    while distance < size:
        array = array + swapped(array, axis, distance)
        distance *= 2
    return array


def dot(left, right, left_dim, right_dim):
    return lax.dot_general(
        left,
        right,
        (((left_dim,), (right_dim,)), ((), ())),
        preferred_element_type=jnp.float32,
    )


def copy_rows_kernel(sizes, offsets, width, bound_ref, place_ref, row_ref, *refs):
    sources = refs[: len(offsets)]
    outs = refs[-2 - len(sizes) : -2]
    rows, sems = refs[-2:]
    for number, (source, offset) in enumerate(zip(sources, offsets)):

        @pl.loop(bound_ref[number], bound_ref[number + 1])
        def copy_row(i, source=source, offset=offset):
            pltpu.make_async_copy(
                source.at[row_ref[i], :, pl.ds(offset, width)],
                rows.at[place_ref[i]],
                sems.at[len(sizes)],
            ).start()

    pltpu.make_async_copy(rows, rows, sems.at[len(sizes)]).wait()
    copies, start = [], 0
    for place, (out, size) in enumerate(zip(outs, sizes)):
        copies.append(
            pltpu.make_async_copy(rows.at[pl.ds(start, size)], out, sems.at[place])
        )
        start += size
    for copy in copies:
        copy.start()
    for copy in copies:
        copy.wait()


def copy_plan(pick_from, pick_row, source_count):
    number = jnp.arange(pick_from.shape[0], dtype=jnp.int32)
    before = pick_from[None, :] < pick_from[:, None]
    same = (pick_from[None, :] == pick_from[:, None]) & (number[None, :] < number[:, None])
    rank = jnp.sum((before | same).astype(jnp.int32), axis=1)
    here = rank[None, :] == number[:, None]
    place = jnp.sum(jnp.where(here, number[None, :], 0), axis=1)
    row = jnp.sum(jnp.where(here, pick_row[None, :], 0), axis=1)
    bounds = jnp.sum(
        (pick_from[None, :] < jnp.arange(source_count + 1)[:, None]).astype(jnp.int32), axis=1
    )
    return (bounds.astype(jnp.int32), place.astype(jnp.int32), row.astype(jnp.int32))


def copy_rows(sources, offsets, width, plan, sizes, events=()):
    rows = sources[0].shape[1]
    total = sum(sizes)
    return pl.pallas_call(
        functools.partial(copy_rows_kernel, tuple(sizes), tuple(offsets), width),
        out_shape=[jax.ShapeDtypeStruct((size, rows, width), sources[0].dtype) for size in sizes],
        grid_spec=pltpu.PrefetchScalarGridSpec(
            num_scalar_prefetch=3,
            grid=(1,),
            in_specs=[pl.BlockSpec(memory_space=pltpu.HBM)] * (len(sources) + len(events)),
            out_specs=[pl.BlockSpec(memory_space=pltpu.HBM)] * len(sizes),
            scratch_shapes=[
                pltpu.VMEM((total, rows, width), sources[0].dtype),
                pltpu.SemaphoreType.DMA((len(sizes) + 1,)),
            ],
        ),
        compiler_params=pltpu.CompilerParams(vmem_limit_bytes=40 * 1024 * 1024),
        cost_estimate=pl.CostEstimate(flops=0, bytes_accessed=1024, transcendentals=0),
        name="copy_rows",
    )(*plan, *sources, *events)


def place_pieces_kernel(places, count_outs, *refs):
    pieces = refs[: len(places)]
    outs = refs[-1 - count_outs : -1]
    sems = refs[-1]
    copies = []
    for number, (piece, place) in enumerate(zip(pieces, places)):
        first, count, begin, size, column, out, row = place
        copies.append(
            pltpu.make_async_copy(
                piece.at[pl.ds(first, count), :, pl.ds(begin, size)],
                outs[out].at[pl.ds(row, count), :, pl.ds(column, size)],
                sems.at[number],
            )
        )
    for copy in copies:
        copy.start()
    for copy in copies:
        copy.wait()


def place_pieces(pieces, places, shapes, events=()):
    return pl.pallas_call(
        functools.partial(place_pieces_kernel, tuple(places), len(shapes)),
        out_shape=[jax.ShapeDtypeStruct(shape, pieces[0].dtype) for shape in shapes],
        in_specs=[pl.BlockSpec(memory_space=pltpu.HBM)] * (len(pieces) + len(events)),
        out_specs=[pl.BlockSpec(memory_space=pltpu.VMEM)] * len(shapes),
        scratch_shapes=[pltpu.SemaphoreType.DMA((len(pieces),))],
        compiler_params=pltpu.CompilerParams(vmem_limit_bytes=40 * 1024 * 1024),
        cost_estimate=pl.CostEstimate(flops=0, bytes_accessed=1024, transcendentals=0),
        name="place_pieces",
    )(*pieces, *events)


def scores_of(blocks, key_rows, query, i):
    size = query.shape[1]
    parts = [(i * size, size)] + ([(0, i * size)] if i else [])
    return [dot(key_rows[first : first + count, :], query, 1, 0) for first, count in parts]


def attend_kernel(blocks, pair, order_ref, q_ref, k_ref, v_ref, out_ref, log_ref, *refs):
    key_rows, value_cols = refs[:pair], refs[pair:]
    head_dim = q_ref.shape[0] // pair
    size = q_ref.shape[1] // blocks
    at = [pl.multiple_of(order_ref[i] * size, size) for i in range(blocks)]
    heads = [slice(p * head_dim, (p + 1) * head_dim) for p in range(pair)]
    for i in range(blocks):
        here = slice(i * size, (i + 1) * size)
        for p in range(pair):
            key_rows[p][here, :] = k_ref[heads[p], pl.ds(at[i], size)].T
            value_cols[p][:, here] = v_ref[heads[p], pl.ds(at[i], size)]
    key_pos = lax.broadcasted_iota(jnp.int32, (size, size), 0)
    query_pos = lax.broadcasted_iota(jnp.int32, (size, size), 1)
    seen = key_pos <= query_pos

    def scores(i):
        return [
            scores_of(blocks, key_rows[p], q_ref[heads[p], pl.ds(at[i], size)], i)
            for p in range(pair)
        ]

    upcoming = scores(0)
    for i in range(blocks):
        current = upcoming
        if i + 1 < blocks:
            upcoming = scores(i + 1)
        past = i * size
        for p in range(pair):
            near, *far = current[p]
            near = jnp.where(seen, near, masked_score)
            top = jnp.max(near, axis=0, keepdims=True)
            for part in far:
                top = jnp.maximum(top, jnp.max(part, axis=0, keepdims=True))
            near = jnp.exp(near - top)
            total = jnp.sum(near, axis=0, keepdims=True)
            value = dot(
                value_cols[p][:, past : past + size], near.astype(jnp.bfloat16), 1, 0
            )
            for part in far:
                part = jnp.exp(part - top)
                total = total + jnp.sum(part, axis=0, keepdims=True)
                value = value + dot(value_cols[p][:, :past], part.astype(jnp.bfloat16), 1, 0)
            out_ref[heads[p], pl.ds(at[i], size)] = (value / total).astype(jnp.bfloat16)
            log_ref[p, :, pl.ds(at[i], size)] = top + jnp.log(total)


def attend(projected, order, heads, head_dim):
    tokens = projected.shape[1]
    blocks = order.shape[0]
    pair = 4
    rows = pair * head_dim

    def part(first):
        return pl.BlockSpec((rows, tokens), lambda h, order, first=first: (first // pair + h, 0))

    return pl.pallas_call(
        functools.partial(attend_kernel, blocks, pair),
        out_shape=[
            jax.ShapeDtypeStruct((heads * head_dim, tokens), jnp.bfloat16),
            jax.ShapeDtypeStruct((heads, 1, tokens), jnp.float32),
        ],
        grid_spec=pltpu.PrefetchScalarGridSpec(
            num_scalar_prefetch=1,
            grid=(heads // pair,),
            in_specs=[part(0), part(heads), part(2 * heads)],
            out_specs=[
                pl.BlockSpec((rows, tokens), lambda h, order: (h, 0)),
                pl.BlockSpec((pair, 1, tokens), lambda h, order: (h, 0, 0)),
            ],
            scratch_shapes=[pltpu.VMEM((tokens, head_dim), jnp.bfloat16)] * pair
            + [pltpu.VMEM((head_dim, tokens), jnp.bfloat16)] * pair,
        ),
        compiler_params=pltpu.CompilerParams(vmem_limit_bytes=48 * 1024 * 1024),
        cost_estimate=pl.CostEstimate(
            flops=heads * tokens * tokens * head_dim * 4,
            bytes_accessed=heads * head_dim * tokens * 8,
            transcendentals=heads * tokens * tokens,
        ),
        name="attend",
    )(order, projected, projected, projected)


def attend_back_kernel(
    blocks,
    pair,
    order_ref,
    q_ref,
    k_ref,
    v_ref,
    grad_ref,
    log_ref,
    scale_ref,
    *refs,
):
    scratch = refs[-5 * pair :]
    out_ref, term_ref = refs[-5 * pair - 2 : -5 * pair]
    key_rows, key_cols, value_rows, key_sum, value_sum = (
        scratch[n * pair : (n + 1) * pair] for n in range(5)
    )
    head_dim = q_ref.shape[0] // pair
    size = q_ref.shape[1] // blocks
    at = [pl.multiple_of(order_ref[i] * size, size) for i in range(blocks)]
    heads = [slice(p * head_dim, (p + 1) * head_dim) for p in range(pair)]
    for i in range(blocks):
        here = slice(i * size, (i + 1) * size)
        for p in range(pair):
            key = k_ref[heads[p], pl.ds(at[i], size)]
            key_rows[p][here, :] = key.T
            key_cols[p][:, here] = key
            value_rows[p][here, :] = v_ref[heads[p], pl.ds(at[i], size)].T
    for p in range(pair):
        key_sum[p][...] = jnp.zeros_like(key_sum[p])
        value_sum[p][...] = jnp.zeros_like(value_sum[p])
    key_pos = lax.broadcasted_iota(jnp.int32, (size, size), 0)
    query_pos = lax.broadcasted_iota(jnp.int32, (size, size), 1)
    seen = key_pos <= query_pos
    terms = [jnp.zeros((head_dim, 1), jnp.float32) for _ in range(pair)]

    def products(i):
        return [
            (
                scores_of(blocks, key_rows[p], q_ref[heads[p], pl.ds(at[i], size)], i),
                scores_of(blocks, value_rows[p], grad_ref[heads[p], pl.ds(at[i], size)], i),
            )
            for p in range(pair)
        ]

    upcoming = products(0)
    for i in range(blocks):
        current = upcoming
        if i + 1 < blocks:
            upcoming = products(i + 1)
        past = i * size
        spans = [slice(past, past + size)] + ([slice(0, past)] if i else [])
        for p in range(pair):
            query = q_ref[heads[p], pl.ds(at[i], size)]
            grad = grad_ref[heads[p], pl.ds(at[i], size)]
            log_total = log_ref[p, :, pl.ds(at[i], size)]
            scores, grads = current[p]
            probs = [jnp.exp(part - log_total) for part in scores]
            probs[0] = jnp.where(seen, probs[0], 0.0)
            delta = jnp.zeros((1, size), jnp.float32)
            for prob, grad_prob in zip(probs, grads):
                delta = delta + jnp.sum(prob * grad_prob, axis=0, keepdims=True)
            grad_query = jnp.zeros(query.shape, jnp.float32)
            for cols, prob, grad_prob in zip(spans, probs, grads):
                grad_score = (prob * (grad_prob - delta)).astype(jnp.bfloat16)
                value_sum[p][:, cols] += dot(grad, prob.astype(jnp.bfloat16), 1, 1)
                key_sum[p][:, cols] += dot(query, grad_score, 1, 1)
                grad_query = grad_query + dot(key_cols[p][:, cols], grad_score, 1, 0)
            terms[p] = terms[p] + jnp.sum(
                grad_query * query.astype(jnp.float32), axis=1, keepdims=True
            )
            out_ref[0, heads[p], pl.ds(at[i], size)] = (grad_query * scale_ref[...]).astype(
                jnp.bfloat16
            )
    for i in range(blocks):
        here = slice(i * size, (i + 1) * size)
        for p in range(pair):
            out_ref[1, heads[p], pl.ds(at[i], size)] = key_sum[p][:, here].astype(jnp.bfloat16)
            out_ref[2, heads[p], pl.ds(at[i], size)] = value_sum[p][:, here].astype(jnp.bfloat16)
    for p in range(pair):
        term_ref[p] = terms[p]


def attend_back(
    projected, grad_attended, log_total, multiplier, order, heads, head_dim, events=()
):
    tokens = projected.shape[1]
    blocks = order.shape[0]
    pair = 4
    rows = pair * head_dim

    def part(first):
        return pl.BlockSpec((rows, tokens), lambda h, order, first=first: (first // pair + h, 0))

    return pl.pallas_call(
        functools.partial(attend_back_kernel, blocks, pair),
        out_shape=[
            jax.ShapeDtypeStruct((3, heads * head_dim, tokens), jnp.bfloat16),
            jax.ShapeDtypeStruct((heads, head_dim, 1), jnp.float32),
        ],
        grid_spec=pltpu.PrefetchScalarGridSpec(
            num_scalar_prefetch=1,
            grid=(heads // pair,),
            in_specs=[
                part(0),
                part(heads),
                part(2 * heads),
                part(0),
                pl.BlockSpec((pair, 1, tokens), lambda h, order: (h, 0, 0)),
                pl.BlockSpec((head_dim, 1), lambda h, order: (0, 0)),
            ]
            + [pl.BlockSpec(memory_space=pltpu.HBM)] * len(events),
            out_specs=[
                pl.BlockSpec((3, rows, tokens), lambda h, order: (0, h, 0)),
                pl.BlockSpec((pair, head_dim, 1), lambda h, order: (h, 0, 0)),
            ],
            scratch_shapes=[pltpu.VMEM((tokens, head_dim), jnp.bfloat16)] * pair
            + [pltpu.VMEM((head_dim, tokens), jnp.bfloat16)] * pair
            + [pltpu.VMEM((tokens, head_dim), jnp.bfloat16)] * pair
            + [pltpu.VMEM((head_dim, tokens), jnp.float32)] * (2 * pair),
        ),
        compiler_params=pltpu.CompilerParams(vmem_limit_bytes=56 * 1024 * 1024),
        cost_estimate=pl.CostEstimate(
            flops=heads * tokens * tokens * head_dim * 10,
            bytes_accessed=heads * head_dim * tokens * 14,
            transcendentals=heads * tokens * tokens,
        ),
        name="attend_back",
    )(order, projected, projected, projected, grad_attended, log_total, multiplier, *events)


def paired_layer(
    inputs,
    targets,
    valid_counts,
    owners,
    master,
    first_moment,
    second_moment,
    norm_gains,
    gain_first,
    gain_second,
    query_scale,
    scale_first,
    scale_second,
):
    bf16 = jnp.bfloat16
    f32 = jnp.float32
    seq_local, block_rows, width = inputs.shape
    slot_count, head_dim, column_count = master.shape
    ff_blocks = FF // head_dim
    owner_count = lax.axis_size("fsdp")
    device = lax.axis_index("ctx")
    chip, core = device // 2, device % 2
    owner_here = lax.axis_index("fsdp")
    low_here = owner_here % 2
    high_here = owner_here // 2
    high_count = owner_count // 2
    high_distances = range(1, high_count)
    half_width = width // 2
    half_slots = slot_count // 2
    half_rows = seq_local * block_rows
    half_heads = H // 2
    half_blocks = ff_blocks // 2
    set_units = 4 * half_heads + 2 * half_blocks
    first_chip, first_core = chip == 0, core == 0

    def columns_here(array):
        return jnp.where(first_chip, array, jnp.roll(array, half_width, axis=-1))

    def sequence_rows(array):
        own = jnp.where(first_chip, array[0], array[1])
        got = swapped(jnp.where(first_chip, array[1], array[0]), "ctx", 2)
        return jnp.where(
            first_chip, jnp.concatenate([own, got]), jnp.concatenate([got, own])
        )

    def rows_apart(array):
        array = columns_here(array)
        first, last = array[:block_rows], array[block_rows:]
        other = jnp.where(first_chip, last, first).astype(bf16)
        return (jnp.where(first_chip, first, last), swapped(other, "ctx", 2))

    def rows_home(own, got):
        got = got.astype(f32)
        return jnp.where(first_chip, jnp.stack([own, got]), jnp.stack([got, own]))

    slot_rows = unit_rows(owners, slot_count)
    unit_total = owners.shape[0]
    kind_sizes = [H, H, H, H, ff_blocks, ff_blocks]
    kind_starts = [sum(kind_sizes[:i]) for i in range(6)]

    def unit_list(kinds, which):
        return jnp.concatenate(
            [
                kind_starts[k] + which * (kind_sizes[k] // 2) + jnp.arange(kind_sizes[k] // 2)
                for k in kinds
            ]
        ).astype(jnp.int32)

    wanted = jnp.concatenate(
        [unit_list(range(6), core), unit_list((4, 5), 1 - core)]
    )
    wanted_rows = slot_rows[wanted]
    wanted_owner, wanted_slot = wanted_rows // slot_count, wanted_rows % slot_count
    weight_from = 2 * (wanted_slot // half_slots != core) + (wanted_owner % 2 != low_here)
    weight_from = weight_from.astype(jnp.int32)
    weight_row = ((wanted_owner // 2) ^ high_here) * half_slots + wanted_slot % half_slots
    weight_plan = copy_plan(weight_from, weight_row, 4)
    weight_sizes = [3 * half_heads, half_heads + 2 * half_blocks, 2 * half_blocks]

    chunks = [(0, 256), (256, 256)]
    lead = 512
    tail = half_width - lead
    shard = master.astype(bf16)
    own_half = jnp.where(first_core, shard[:half_slots], shard[half_slots:])
    got_half = swapped(jnp.where(first_core, shard[half_slots:], shard[:half_slots]), "ctx", 1)
    shard = jnp.where(
        first_core,
        jnp.concatenate([own_half, got_half], axis=2),
        jnp.concatenate([got_half, own_half], axis=2),
    )
    shard, inputs, targets = lax.optimization_barrier((shard, inputs, targets))
    values_b = columns_here(sequence_rows(inputs))
    targets_b = columns_here(sequence_rows(targets))
    shard_last = shard[:, :, lead:]
    shards = [shard[:, :, start : start + size] for start, size in chunks]
    shards.append(jnp.concatenate([shard_last, swapped(shard_last, "ctx", 2)], axis=2))
    highs = []
    for number, part in enumerate(shards):
        if number:
            part, highs[-1] = lax.optimization_barrier((part, highs[-1]))
        highs.append(
            jnp.concatenate([part] + [swapped(part, "fsdp", 2 * d) for d in high_distances])
        )
    lows = [swapped(high, "fsdp", 1) for high in highs]
    own_units, rest_units, far_units = weight_sizes
    near_units = own_units + rest_units

    def pick_units(number, sizes, events):
        high, low = highs[number], lows[number]
        sources = [high, low, swapped(high, "ctx", 1), swapped(low, "ctx", 1)]
        return copy_rows(sources, [0] * 4, high.shape[2], weight_plan, sizes, events)

    lows[0], highs[1] = lax.optimization_barrier((lows[0], highs[1]))
    near_one, far_one = pick_units(
        0, [near_units, far_units], [shards[2], values_b, targets_b]
    )
    got_one = swapped(near_one, "ctx", 2)
    lows[1], far_one, highs[2] = lax.optimization_barrier((lows[1], far_one, highs[2]))
    qkv_two, rest_two, far_two = pick_units(1, weight_sizes, [got_one])
    qkv_got = swapped(qkv_two, "ctx", 2)
    rest_two, qkv_got = lax.optimization_barrier((rest_two, qkv_got))
    rest_got = swapped(rest_two, "ctx", 2)
    lows[2], far_two, got_one = lax.optimization_barrier((lows[2], far_two, got_one))
    qkv_last, rest_last, far_last = pick_units(2, weight_sizes, [])

    def columns_of(owns, gots, last):
        pieces = [(last, 0, tail, lead), (last, tail, tail, half_width + lead)]
        for (start, size), own, got in zip(chunks, owns, gots):
            pieces += [(own, 0, size, start), (got, 0, size, half_width + start)]
        return pieces

    def placed(pieces, from_end, count, out, row):
        return [
            (piece.shape[0] - from_end if from_end else 0, count, *columns, out, row)
            for piece, *columns in pieces
        ]

    qkv_pieces = columns_of([near_one, qkv_two], [got_one, qkv_got], qkv_last)
    rest_pieces = columns_of([near_one, rest_two], [got_one, rest_got], rest_last)
    far_pieces = columns_of(
        [far_one, far_two], [swapped(got, "ctx", 1) for got in (got_one, rest_got)], far_last
    )
    (w_qkv,) = place_pieces(
        [piece for piece, *_ in qkv_pieces],
        placed(qkv_pieces, 0, own_units, 0, 0),
        [(own_units, head_dim, width)],
    )
    w_qkv = w_qkv.reshape(-1, width)

    gains = columns_here(norm_gains)
    values_in = values_b.astype(f32)
    normed_own = (values_in * inverse_rms(values_in) * gains[0]).astype(bf16)
    normed_b = jnp.concatenate([normed_own, swapped(normed_own, "ctx", 1)])
    base = score_base / math.sqrt(head_dim)
    multiplier = jax.nn.softplus(query_scale) * base
    row_scale = jnp.concatenate(
        [jnp.tile(multiplier, half_heads), jnp.ones((2 * half_heads * head_dim,), f32)]
    )
    projected = (dot(w_qkv, normed_b, 1, 1) * row_scale[:, None]).astype(bf16)
    positions = jnp.arange(4, dtype=jnp.int32)
    order = jnp.where(positions % 2 == core, 0, 2) + positions // 2
    order = order.astype(jnp.int32)
    attended, log_total = attend(projected, order, half_heads, head_dim)
    (w_out,) = place_pieces(
        [piece for piece, *_ in rest_pieces],
        placed(rest_pieces, rest_units, half_heads, 0, 0),
        [(half_heads, head_dim, width)],
        [log_total],
    )
    mlp_pieces, mlp_places = [], []
    for row, pieces in ((0, rest_pieces), (half_blocks, far_pieces)):
        for kind in range(2):
            mlp_pieces += [piece for piece, *_ in pieces]
            mlp_places += placed(pieces, (2 - kind) * half_blocks, half_blocks, kind, row)
    w_up, w_down = place_pieces(
        mlp_pieces, mlp_places, [(ff_blocks, head_dim, width)] * 2, [log_total]
    )
    w_out = w_out.reshape(-1, width)
    w_up = w_up.reshape(-1, width)
    w_down = w_down.reshape(-1, width)
    branch_far = dot(attended[:, half_rows:], w_out, 0, 0).astype(bf16)
    branch_got = swapped(branch_far, "ctx", 1)
    branch_own = dot(attended[:, :half_rows], w_out, 0, 0)
    middle = values_in + (branch_own + branch_got.astype(f32))
    normed_mid_b = (middle * inverse_rms(middle) * gains[1]).astype(bf16)
    hidden = dot(normed_mid_b, w_up, 1, 1)
    active_b = jax.nn.silu(hidden).astype(bf16)
    block_out = middle + dot(active_b, w_down, 1, 0)
    seq_length = 2 * half_rows
    row = jnp.arange(half_rows, dtype=jnp.int32)
    row_pos = (core + 2 * (row // block_rows)) * block_rows + row % block_rows
    valid = jnp.where(first_chip, valid_counts[0], valid_counts[1])
    counted = (row_pos >= seq_length - valid).astype(f32)
    count_term = jnp.sum(counted)

    (apart,) = lax.optimization_barrier((block_out,))
    block_own, block_got = rows_apart(apart)

    out_grad = 2.0 * (block_out - targets_b.astype(f32)) * counted[:, None]
    out_grad_b = out_grad.astype(bf16)
    grad_active = dot(out_grad_b, w_down, 1, 1)
    sigma = jax.nn.sigmoid(hidden)
    grad_hidden_b = (grad_active * sigma * (1.0 + hidden * (1.0 - sigma))).astype(bf16)
    grad_normed_mid = dot(grad_hidden_b, w_up, 1, 0)
    inverse = inverse_rms(middle)
    scaled = grad_normed_mid * gains[1]
    grad_middle = out_grad + (
        inverse * scaled
        - middle * inverse**3 * jnp.mean(scaled * middle, axis=-1, keepdims=True)
    )
    grad_gain_two = jnp.sum(grad_normed_mid * middle * inverse, axis=0)
    grad_middle_own = grad_middle.astype(bf16)
    grad_middle_got = swapped(grad_middle_own, "ctx", 1)
    far_blocks = half_blocks * head_dim
    wide = slice(half_width + 256, half_width + lead)
    slim = slice(half_width, half_width + 256)
    block_grads = []
    for left, right in ((grad_hidden_b, normed_mid_b), (active_b, out_grad_b)):
        got = swapped(dot(left[:, far_blocks:], right, 0, 0).astype(bf16), "ctx", 1)
        total = dot(left[:, :far_blocks], right, 0, 0) + got.astype(f32)
        block_grads.append(total.astype(bf16).reshape(half_blocks, head_dim, width))
    block_grads = jnp.concatenate(block_grads)
    grad_middle_got, block_grads = lax.optimization_barrier((grad_middle_got, block_grads))
    grad_middle_b = jnp.concatenate([grad_middle_own, grad_middle_got])
    grad_attended = dot(w_out, grad_middle_b, 1, 1).astype(bf16)
    head_grads = dot(attended, grad_middle_b, 1, 0).astype(bf16)
    head_grads = head_grads.reshape(half_heads, head_dim, width)

    def early_columns(columns):
        return jnp.concatenate([head_grads[:, :, columns], block_grads[:, :, columns]])

    early_wide, early_slim = early_columns(wide), early_columns(slim)
    wide_got = swapped(early_wide, "ctx", 2)

    def last_columns(array):
        return jnp.concatenate(
            [array[..., lead:half_width], array[..., half_width + lead :]], axis=-1
        )

    early_last = jnp.concatenate([last_columns(head_grads), last_columns(block_grads)])
    grad_proj, grad_scale = attend_back(
        projected,
        grad_attended,
        log_total,
        multiplier[:, None],
        order,
        half_heads,
        head_dim,
        [early_wide, early_slim, early_last, block_got],
    )
    grad_proj = grad_proj.reshape(-1, grad_proj.shape[2])
    scale_term = (
        jnp.sum(grad_scale[:, :, 0], axis=0) / multiplier * base * jax.nn.sigmoid(query_scale)
    )

    low_order = jnp.stack([low_here, 1 - low_here])
    table_slots = (
        (2 * (jnp.arange(high_count) ^ high_here)[None, :, None] + low_order[:, None, None])
        * slot_count
        + core * half_slots
        + jnp.arange(half_slots)[None, None, :]
    ).reshape(-1)
    holds = table_slots[:, None] == slot_rows[None, :]
    unit_order = jnp.arange(unit_total, dtype=jnp.int32)
    slot_unit = jnp.sum(jnp.where(holds, unit_order[None, :] + 1, 0), axis=1) - 1
    kind = jnp.where(
        slot_unit < 4 * H, slot_unit // H, 4 + (slot_unit - 4 * H) // ff_blocks
    )
    kind_size = jnp.where(kind < 4, H, ff_blocks)
    within = jnp.where(kind < 4, slot_unit % H, (slot_unit - 4 * H) % ff_blocks)
    other_set = (within // (kind_size // 2) != core).astype(jnp.int32)
    rank = within % (kind_size // 2)
    grad_row = rank + jnp.where(
        kind <= 3, kind * half_heads, 4 * half_heads + (kind - 4) * half_blocks
    )
    empty = slot_unit < 0
    grad_from = jnp.where(empty, 2, other_set).astype(jnp.int32)
    grad_row = jnp.where(empty, 0, grad_row).astype(jnp.int32)
    grad_plan = copy_plan(grad_from, grad_row, 3)
    zero = jnp.zeros((1, head_dim, 256), bf16)

    def pick_table(own, got, offset, size, events=()):
        return copy_rows(
            [own, got, zero],
            [offset, offset, 0],
            size,
            grad_plan,
            [high_count * half_slots] * 2,
            events,
        )

    def table_sums(keep, got):
        sums = []
        for d in range(high_count):
            rows = slice(d * half_slots, (d + 1) * half_slots)
            sums.append((keep[rows].astype(f32) + got[rows].astype(f32)).astype(bf16))
        return sums

    def from_owners(tables):
        return [swapped(tables[d], "fsdp", 2 * d) for d in high_distances]

    def owner_sum(table, got):
        total = table.astype(f32)
        for part in got:
            total = total + part.astype(f32)
        return total.astype(bf16)

    def proj_grad(columns):
        return dot(grad_proj, columns, 1, 0).astype(bf16).reshape(-1, head_dim, columns.shape[1])

    def chip_sum(start, proj_got, early_got):
        near = slice(start, start + 256)
        parts = [
            (proj_grad(normed_b[:, near]), proj_got),
            (head_grads[:, :, near], early_got[:half_heads]),
            (block_grads[:, :, near], early_got[half_heads:]),
        ]
        return jnp.concatenate(
            [(own.astype(f32) + got.astype(f32)).astype(bf16) for own, got in parts]
        )

    proj_last = proj_grad(last_columns(normed_b))
    proj_last, wide_got = lax.optimization_barrier((proj_last, wide_got))
    total_last = jnp.concatenate([proj_last, early_last])
    wide_far = proj_grad(normed_b[:, wide])
    wide_proj = swapped(wide_far, "ctx", 2)
    keep_last, send_last = pick_table(
        total_last, swapped(total_last, "ctx", 1), 0, 256, [wide_far]
    )
    low_last = swapped(send_last, "fsdp", 1)
    keep_last, grad_proj = lax.optimization_barrier((keep_last, grad_proj))
    slim_far = jnp.concatenate([proj_grad(normed_b[:, slim]), early_slim])
    normed_far = dot(grad_proj[:, half_rows:], w_qkv, 0, 0).astype(bf16)
    normed_got = swapped(normed_far, "ctx", 1)
    low_last, wide_proj, slim_far, normed_got = lax.optimization_barrier(
        (low_last, wide_proj, slim_far, normed_got)
    )
    slim_got = swapped(slim_far, "ctx", 2)
    total = chip_sum(256, wide_proj, wide_got)
    keep_three, send_three = pick_table(total, swapped(total, "ctx", 1), 0, 256)
    low_last, keep_three, grad_proj = lax.optimization_barrier((low_last, keep_three, grad_proj))
    low_three = swapped(send_three, "fsdp", 1)
    tables_last = table_sums(keep_last, low_last)
    high_last = from_owners(tables_last)
    grad_normed_in = dot(grad_proj[:, :half_rows], w_qkv, 0, 0) + normed_got.astype(f32)
    inverse = inverse_rms(values_in)
    scaled = grad_normed_in * gains[0]
    input_grad = grad_middle + (
        inverse * scaled
        - values_in * inverse**3 * jnp.mean(scaled * values_in, axis=-1, keepdims=True)
    )
    grad_gain_one = jnp.sum(grad_normed_in * values_in * inverse, axis=0)
    low_three, high_last, slim_got, input_grad = lax.optimization_barrier(
        (low_three, high_last, slim_got, input_grad)
    )
    total = chip_sum(0, slim_got[: 3 * half_heads], slim_got[3 * half_heads :])
    keep_one, send_one = pick_table(total, swapped(total, "ctx", 1), 0, 256, [low_three])
    keep_one, low_three = lax.optimization_barrier((keep_one, low_three))
    tables_three = table_sums(keep_three, low_three)
    high_three = from_owners(tables_three)

    gain_terms = columns_here(jnp.stack([grad_gain_one, grad_gain_two]))
    small = jnp.concatenate([gain_terms.reshape(-1), scale_term, count_term[None]])
    small = jnp.pad(small, (0, -small.shape[0] % 1024))
    keep_one, small = lax.optimization_barrier((keep_one, small))
    tables_one = table_sums(keep_one, swapped(send_one, "fsdp", 1))
    small = small + swapped(small, "fsdp", 1)
    tables_one, high_three, high_last, small, input_grad = lax.optimization_barrier(
        (tables_one, high_three, high_last, small, input_grad)
    )
    high_one = from_owners(tables_one)
    small_got = from_owners([small] * high_count)
    high_one, small_got = lax.optimization_barrier((high_one, small_got))
    small = summed((small + small_got[0]) + (small_got[1] + small_got[2]), "ctx")
    gain_sums = small[: 2 * width].reshape(2, width)
    scale_sums = small[2 * width : 2 * width + head_dim]
    count = small[2 * width + head_dim]

    owned_last = owner_sum(tables_last[0], high_last)
    owned_got = swapped(owned_last[:, :, tail:], "ctx", 2)
    owned = [
        owner_sum(tables_one[0], high_one),
        owner_sum(tables_three[0], high_three),
        (owned_last[:, :, :tail].astype(f32) + owned_got.astype(f32)).astype(bf16),
    ]
    owned = jnp.concatenate(owned, axis=2).reshape(half_slots, head_dim, 2, column_count)
    kept = jnp.where(first_core, owned[:, :, 0], owned[:, :, 1])
    sent = swapped(jnp.where(first_core, owned[:, :, 1], owned[:, :, 0]), "ctx", 1)
    slot_sums = jnp.where(
        first_core, jnp.concatenate([kept, sent]), jnp.concatenate([sent, kept])
    ).astype(f32)
    new_master, new_first, new_second = adam_step(
        master, first_moment, second_moment, slot_sums / count, master_rate, decay_rate
    )
    new_gains, new_gain_first, new_gain_second = adam_step(
        norm_gains, gain_first, gain_second, gain_sums / count, gain_rate, 0.0
    )
    new_scale, new_scale_first, new_scale_second = adam_step(
        query_scale, scale_first, scale_second, scale_sums / count, scale_rate, 0.0
    )
    return (
        rows_home(block_own, block_got),
        rows_home(*rows_apart(input_grad)),
        new_master,
        new_first,
        new_second,
        new_gains,
        new_gain_first,
        new_gain_second,
        new_scale,
        new_scale_first,
        new_scale_second,
    )


def on_device(*arguments):
    paired = (
        lax.axis_size("ctx") == 4
        and lax.axis_size("fsdp") == 8
        and arguments[0].shape[0] == 2
    )
    return (paired_layer if paired else general_layer)(*arguments)


def solution(mesh):
    in_specs = (
        P("fsdp", "ctx", None),
        P("fsdp", "ctx", None),
        P("fsdp"),
        P(),
        P("fsdp", None, "ctx"),
        P("fsdp", None, "ctx"),
        P("fsdp", None, "ctx"),
        P(),
        P(),
        P(),
        P(),
        P(),
        P(),
    )
    out_specs = (
        P("fsdp", "ctx", None),
        P("fsdp", "ctx", None),
        P("fsdp", None, "ctx"),
        P("fsdp", None, "ctx"),
        P("fsdp", None, "ctx"),
        P(),
        P(),
        P(),
        P(),
        P(),
        P(),
    )
    return jax.shard_map(
        on_device, mesh=mesh, in_specs=in_specs, out_specs=out_specs, check_vma=False
    )
```

```python
import functools
import math

import jax
import jax.numpy as jnp
from jax import lax
from jax.experimental import pallas as pl
from jax.experimental.pallas import tpu as pltpu
from jax.sharding import PartitionSpec as P

H = 16
FF = 1280
STEP = 10


norm_eps = 1e-06
beta_first = 0.9
beta_second = 0.95
adam_eps = 1e-08
decay_rate = 0.1
master_rate = 0.05
gain_rate = 2.0
scale_rate = 2.0
score_base = 1.442695041
masked_score = -1e30


def from_behind(block, axis, distance):
    devices = range(lax.axis_size(axis))
    route = [(i - distance, i) for i in devices if i - distance in devices]
    return lax.ppermute(block, axis, route)


def shifted(array, axis, by):
    count = lax.axis_size(axis)
    return lax.ppermute(array, axis, [(i, (i + by) % count) for i in range(count)])


def unit_rows(owners, slot_count):
    unit_count = owners.shape[0]
    unit_order = jnp.arange(unit_count, dtype=jnp.int32)
    same_owner = owners[:, None] == owners[None, :]
    earlier = unit_order[None, :] < unit_order[:, None]
    slot_rank = jnp.sum((same_owner & earlier).astype(jnp.int32), axis=1)
    return owners * slot_count + slot_rank


def inverse_rms(values):
    return lax.rsqrt(jnp.mean(values * values, axis=-1, keepdims=True) + norm_eps)


def norm_back(values, gain, grad_normed):
    inverse = inverse_rms(values)
    scaled = grad_normed * gain
    grad_values = inverse * scaled - values * inverse**3 * jnp.mean(
        scaled * values, axis=-1, keepdims=True
    )
    grad_gain = jnp.sum(grad_normed * values * inverse, axis=(0, 1))
    return (grad_values, grad_gain)


def adam_step(values, moment_one, moment_two, gradient, step_rate, weight_decay):
    moment_one = beta_first * moment_one + (1.0 - beta_first) * gradient
    moment_two = beta_second * moment_two + (1.0 - beta_second) * gradient * gradient
    first_hat = moment_one / (1.0 - beta_first**STEP)
    second_hat = moment_two / (1.0 - beta_second**STEP)
    values = values - step_rate * (
        first_hat / (jnp.sqrt(second_hat) + adam_eps) + weight_decay * values
    )
    return (values, moment_one, moment_two)


def general_layer(
    inputs,
    targets,
    valid_counts,
    owners,
    master,
    first_moment,
    second_moment,
    norm_gains,
    gain_first,
    gain_second,
    query_scale,
    scale_first,
    scale_second,
):
    seq_local, block_rows, width = inputs.shape
    slot_count, head_dim, column_count = master.shape
    ff_blocks = FF // head_dim
    ctx_size = lax.axis_size("ctx")
    ctx_index = lax.axis_index("ctx")
    slot_rows = unit_rows(owners, slot_count)
    owner_table = lax.all_gather(master.astype(jnp.bfloat16), "fsdp", axis=0, tiled=True)
    picked = owner_table[slot_rows]
    weights = lax.all_gather(picked, "ctx", axis=2, tiled=True)
    w_qkv = weights[0 : 3 * H]
    w_out = weights[3 * H : 4 * H]
    w_up = weights[4 * H : 4 * H + ff_blocks]
    w_down = weights[4 * H + ff_blocks :]
    values_in = inputs.astype(jnp.float32)
    normed_b = (values_in * inverse_rms(values_in) * norm_gains[0]).astype(jnp.bfloat16)
    projected = jnp.einsum("sbd,hed->shbe", normed_b, w_qkv, preferred_element_type=jnp.float32)
    query_pre = projected[:, 0:H]
    multiplier = jax.nn.softplus(query_scale) * (score_base / math.sqrt(head_dim))
    query_b = (query_pre * multiplier).astype(jnp.bfloat16)
    key_b = projected[:, H : 2 * H].astype(jnp.bfloat16)
    value_b = projected[:, 2 * H : 3 * H].astype(jnp.bfloat16)
    query_rows = ctx_index * block_rows + jnp.arange(block_rows, dtype=jnp.int32)
    last_row = ctx_index * block_rows + block_rows - 1
    start_state = (
        jnp.full(query_pre.shape[:3], masked_score, jnp.float32),
        jnp.zeros(query_pre.shape[:3], jnp.float32),
        jnp.zeros(query_pre.shape, jnp.float32),
    )
    key_part = lax.all_gather(key_b, "ctx", axis=2, tiled=True)
    value_part = lax.all_gather(value_b, "ctx", axis=2, tiled=True)
    key_count = key_part.shape[2]

    def update(current):
        run_max, run_sum, accum = current
        key_rows = jnp.arange(key_count, dtype=jnp.int32)
        allowed = query_rows[:, None] >= key_rows[None, :]
        scores = jnp.einsum(
            "shqe,shke->shqk", query_b, key_part, preferred_element_type=jnp.float32
        )
        scores = jnp.where(allowed, scores, masked_score)
        new_max = jnp.maximum(run_max, jnp.max(scores, axis=-1))
        attn_probs = jnp.where(allowed, jnp.exp(scores - new_max[..., None]), 0.0)
        run_sum = jnp.sum(attn_probs, axis=-1)
        accum = jnp.einsum(
            "shqk,shke->shqe",
            attn_probs.astype(jnp.bfloat16),
            value_part,
            preferred_element_type=jnp.float32,
        )
        return (new_max, run_sum, accum)

    run_max, run_sum, accum = lax.cond(
        jnp.int32(0) <= last_row, update, lambda current: current, start_state
    )
    attended = accum / run_sum[..., None]
    log_total = run_max + jnp.log(run_sum)
    attended_b = attended.astype(jnp.bfloat16)
    branch = jnp.einsum("shbe,hed->sbd", attended_b, w_out, preferred_element_type=jnp.float32)
    middle = values_in + branch
    normed_mid_b = (middle * inverse_rms(middle) * norm_gains[1]).astype(jnp.bfloat16)
    hidden = jnp.einsum("sbd,fed->sbfe", normed_mid_b, w_up, preferred_element_type=jnp.float32)
    active_b = jax.nn.silu(hidden).astype(jnp.bfloat16)
    block_out = middle + jnp.einsum(
        "sbfe,fed->sbd", active_b, w_down, preferred_element_type=jnp.float32
    )
    seq_length = block_rows * ctx_size
    counted = (query_rows[None, :] >= (seq_length - valid_counts)[:, None]).astype(jnp.float32)
    count_term = jnp.sum(counted)
    out_grad = 2.0 * (block_out - targets.astype(jnp.float32)) * counted[..., None]
    out_grad_b = out_grad.astype(jnp.bfloat16)
    grad_down = jnp.einsum(
        "sbfe,sbd->fed", active_b, out_grad_b, preferred_element_type=jnp.float32
    )
    grad_active = jnp.einsum(
        "sbd,fed->sbfe", out_grad_b, w_down, preferred_element_type=jnp.float32
    )
    sigma = jax.nn.sigmoid(hidden)
    grad_hidden_b = (grad_active * sigma * (1.0 + hidden * (1.0 - sigma))).astype(jnp.bfloat16)
    grad_up = jnp.einsum(
        "sbfe,sbd->fed", grad_hidden_b, normed_mid_b, preferred_element_type=jnp.float32
    )
    grad_normed_mid = jnp.einsum(
        "sbfe,fed->sbd", grad_hidden_b, w_up, preferred_element_type=jnp.float32
    )
    grad_middle_norm, grad_gain_two = norm_back(middle, norm_gains[1], grad_normed_mid)
    grad_middle = out_grad + grad_middle_norm
    grad_middle_b = grad_middle.astype(jnp.bfloat16)
    grad_out = jnp.einsum(
        "shbe,sbd->hed", attended_b, grad_middle_b, preferred_element_type=jnp.float32
    )
    grad_attended_b = jnp.einsum(
        "sbd,hed->shbe", grad_middle_b, w_out, preferred_element_type=jnp.float32
    ).astype(jnp.bfloat16)
    delta = jnp.sum(grad_attended_b.astype(jnp.float32) * attended, axis=-1)

    def block_grads(source, key_cur, value_cur, partial_grads):
        grad_key, grad_value, grad_query = partial_grads
        key_rows = source * block_rows + jnp.arange(block_rows, dtype=jnp.int32)
        allowed = query_rows[:, None] >= key_rows[None, :]
        scores = jnp.einsum("shqe,shke->shqk", query_b, key_cur, preferred_element_type=jnp.float32)
        scores = jnp.where(allowed, scores, masked_score)
        attn_probs = jnp.exp(scores - log_total[..., None])
        grad_value = grad_value + jnp.einsum(
            "shqk,shqe->shke",
            attn_probs.astype(jnp.bfloat16),
            grad_attended_b,
            preferred_element_type=jnp.float32,
        )
        grad_probs = jnp.einsum(
            "shqe,shke->shqk", grad_attended_b, value_cur, preferred_element_type=jnp.float32
        )
        grad_scores_b = (attn_probs * (grad_probs - delta[..., None])).astype(jnp.bfloat16)
        grad_query = grad_query + jnp.einsum(
            "shqk,shke->shqe", grad_scores_b, key_cur, preferred_element_type=jnp.float32
        )
        grad_key = grad_key + jnp.einsum(
            "shqk,shqe->shke", grad_scores_b, query_b, preferred_element_type=jnp.float32
        )
        return (grad_key, grad_value, grad_query)

    zero_heads = jnp.zeros(query_pre.shape, jnp.float32)

    def back_turn(which_turn, current):
        key_cur, value_cur, grad_key, grad_value, grad_query = current
        source = (ctx_index - which_turn) % ctx_size
        grad_key, grad_value, grad_query = lax.cond(
            source <= ctx_index,
            lambda parts: block_grads(source, key_cur, value_cur, parts),
            lambda parts: parts,
            (grad_key, grad_value, grad_query),
        )
        key_cur, value_cur = from_behind((key_cur, value_cur), "ctx", 1)
        grad_key, grad_value = (
            shifted(grad_key.astype(jnp.bfloat16), "ctx", 1).astype(grad_key.dtype),
            shifted(grad_value.astype(jnp.bfloat16), "ctx", 1).astype(grad_value.dtype),
        )
        return (key_cur, value_cur, grad_key, grad_value, grad_query)

    back_state = (key_b, value_b, zero_heads, zero_heads, zero_heads)
    back_state = lax.fori_loop(0, ctx_size, back_turn, back_state)
    grad_key, grad_value, grad_query = (back_state[2], back_state[3], back_state[4])
    grad_proj_b = jnp.concatenate([grad_query * multiplier, grad_key, grad_value], axis=1).astype(
        jnp.bfloat16
    )
    grad_qkv = jnp.einsum(
        "shbe,sbd->hed", grad_proj_b, normed_b, preferred_element_type=jnp.float32
    )
    grad_normed_in = jnp.einsum(
        "shbe,hed->sbd", grad_proj_b, w_qkv, preferred_element_type=jnp.float32
    )
    grad_input_norm, grad_gain_one = norm_back(values_in, norm_gains[0], grad_normed_in)
    input_grad = grad_middle + grad_input_norm
    scale_term = (
        jnp.sum(grad_query * query_pre, axis=(0, 1, 2))
        * (score_base / math.sqrt(head_dim))
        * jax.nn.sigmoid(query_scale)
    )
    unit_grads = jnp.concatenate([grad_qkv, grad_out, grad_up, grad_down], axis=0)
    owner_total = lax.axis_size("fsdp") * slot_count
    table_grads = (
        jnp.zeros((owner_total, head_dim, width), jnp.float32).at[slot_rows].set(unit_grads)
    )
    owned = lax.psum_scatter(
        table_grads.astype(jnp.bfloat16), "fsdp", scatter_dimension=0, tiled=True
    )
    slot_sums = lax.psum_scatter(owned, "ctx", scatter_dimension=2, tiled=True).astype(jnp.float32)
    gain_sums, scale_sums, count = lax.psum(
        (jnp.stack([grad_gain_one, grad_gain_two]), scale_term, count_term), ("ctx", "fsdp")
    )
    new_master, new_first, new_second = adam_step(
        master, first_moment, second_moment, slot_sums / count, master_rate, decay_rate
    )
    new_gains, new_gain_first, new_gain_second = adam_step(
        norm_gains, gain_first, gain_second, gain_sums / count, gain_rate, 0.0
    )
    new_scale, new_scale_first, new_scale_second = adam_step(
        query_scale, scale_first, scale_second, scale_sums / count, scale_rate, 0.0
    )
    return (
        block_out,
        input_grad,
        new_master,
        new_first,
        new_second,
        new_gains,
        new_gain_first,
        new_gain_second,
        new_scale,
        new_scale_first,
        new_scale_second,
    )


def swapped(array, axis, distance):
    return lax.ppermute(
        array, axis, [(i, i ^ distance) for i in range(lax.axis_size(axis))]
    )


def summed(array, axis):
    size = lax.axis_size(axis)
    if size & (size - 1):
        return lax.psum(array, axis)
    distance = 1
    while distance < size:
        array = array + swapped(array, axis, distance)
        distance *= 2
    return array


def dot(left, right, left_dim, right_dim):
    return lax.dot_general(
        left,
        right,
        (((left_dim,), (right_dim,)), ((), ())),
        preferred_element_type=jnp.float32,
    )


def copy_rows_kernel(sizes, offsets, width, bound_ref, place_ref, row_ref, *refs):
    sources = refs[: len(offsets)]
    outs = refs[-2 - len(sizes) : -2]
    rows, sems = refs[-2:]
    for number, (source, offset) in enumerate(zip(sources, offsets)):

        @pl.loop(bound_ref[number], bound_ref[number + 1])
        def copy_row(i, source=source, offset=offset):
            pltpu.make_async_copy(
                source.at[row_ref[i], :, pl.ds(offset, width)],
                rows.at[place_ref[i]],
                sems.at[len(sizes)],
            ).start()

    pltpu.make_async_copy(rows, rows, sems.at[len(sizes)]).wait()
    copies, start = [], 0
    for place, (out, size) in enumerate(zip(outs, sizes)):
        copies.append(
            pltpu.make_async_copy(rows.at[pl.ds(start, size)], out, sems.at[place])
        )
        start += size
    for copy in copies:
        copy.start()
    for copy in copies:
        copy.wait()


def copy_plan(pick_from, pick_row, source_count):
    number = jnp.arange(pick_from.shape[0], dtype=jnp.int32)
    before = pick_from[None, :] < pick_from[:, None]
    same = (pick_from[None, :] == pick_from[:, None]) & (number[None, :] < number[:, None])
    rank = jnp.sum((before | same).astype(jnp.int32), axis=1)
    here = rank[None, :] == number[:, None]
    place = jnp.sum(jnp.where(here, number[None, :], 0), axis=1)
    row = jnp.sum(jnp.where(here, pick_row[None, :], 0), axis=1)
    bounds = jnp.sum(
        (pick_from[None, :] < jnp.arange(source_count + 1)[:, None]).astype(jnp.int32), axis=1
    )
    return (bounds.astype(jnp.int32), place.astype(jnp.int32), row.astype(jnp.int32))


def copy_rows(sources, offsets, width, plan, sizes, events=()):
    rows = sources[0].shape[1]
    total = sum(sizes)
    return pl.pallas_call(
        functools.partial(copy_rows_kernel, tuple(sizes), tuple(offsets), width),
        out_shape=[jax.ShapeDtypeStruct((size, rows, width), sources[0].dtype) for size in sizes],
        grid_spec=pltpu.PrefetchScalarGridSpec(
            num_scalar_prefetch=3,
            grid=(1,),
            in_specs=[pl.BlockSpec(memory_space=pltpu.HBM)] * (len(sources) + len(events)),
            out_specs=[pl.BlockSpec(memory_space=pltpu.HBM)] * len(sizes),
            scratch_shapes=[
                pltpu.VMEM((total, rows, width), sources[0].dtype),
                pltpu.SemaphoreType.DMA((len(sizes) + 1,)),
            ],
        ),
        compiler_params=pltpu.CompilerParams(vmem_limit_bytes=40 * 1024 * 1024),
        cost_estimate=pl.CostEstimate(flops=0, bytes_accessed=1024, transcendentals=0),
        name="copy_rows",
    )(*plan, *sources, *events)


def place_pieces_kernel(places, count_outs, *refs):
    pieces = refs[: len(places)]
    outs = refs[-1 - count_outs : -1]
    sems = refs[-1]
    copies = []
    for number, (piece, place) in enumerate(zip(pieces, places)):
        first, count, begin, size, column, out, row = place
        copies.append(
            pltpu.make_async_copy(
                piece.at[pl.ds(first, count), :, pl.ds(begin, size)],
                outs[out].at[pl.ds(row, count), :, pl.ds(column, size)],
                sems.at[number],
            )
        )
    for copy in copies:
        copy.start()
    for copy in copies:
        copy.wait()


def place_pieces(pieces, places, shapes, events=()):
    return pl.pallas_call(
        functools.partial(place_pieces_kernel, tuple(places), len(shapes)),
        out_shape=[jax.ShapeDtypeStruct(shape, pieces[0].dtype) for shape in shapes],
        in_specs=[pl.BlockSpec(memory_space=pltpu.HBM)] * (len(pieces) + len(events)),
        out_specs=[pl.BlockSpec(memory_space=pltpu.VMEM)] * len(shapes),
        scratch_shapes=[pltpu.SemaphoreType.DMA((len(pieces),))],
        compiler_params=pltpu.CompilerParams(vmem_limit_bytes=40 * 1024 * 1024),
        cost_estimate=pl.CostEstimate(flops=0, bytes_accessed=1024, transcendentals=0),
        name="place_pieces",
    )(*pieces, *events)


def scores_of(blocks, key_rows, query, i):
    size = query.shape[1]
    parts = [(i * size, size)] + ([(0, i * size)] if i else [])
    return [dot(key_rows[first : first + count, :], query, 1, 0) for first, count in parts]


def attend_kernel(blocks, pair, order_ref, q_ref, k_ref, v_ref, out_ref, log_ref, *refs):
    key_rows, value_cols = refs[:pair], refs[pair:]
    head_dim = q_ref.shape[0] // pair
    size = q_ref.shape[1] // blocks
    at = [pl.multiple_of(order_ref[i] * size, size) for i in range(blocks)]
    heads = [slice(p * head_dim, (p + 1) * head_dim) for p in range(pair)]
    for i in range(blocks):
        here = slice(i * size, (i + 1) * size)
        for p in range(pair):
            key_rows[p][here, :] = k_ref[heads[p], pl.ds(at[i], size)].T
            value_cols[p][:, here] = v_ref[heads[p], pl.ds(at[i], size)]
    key_pos = lax.broadcasted_iota(jnp.int32, (size, size), 0)
    query_pos = lax.broadcasted_iota(jnp.int32, (size, size), 1)
    seen = key_pos <= query_pos

    def scores(i):
        return [
            scores_of(blocks, key_rows[p], q_ref[heads[p], pl.ds(at[i], size)], i)
            for p in range(pair)
        ]

    upcoming = scores(0)
    for i in range(blocks):
        current = upcoming
        if i + 1 < blocks:
            upcoming = scores(i + 1)
        past = i * size
        for p in range(pair):
            near, *far = current[p]
            near = jnp.where(seen, near, masked_score)
            top = jnp.max(near, axis=0, keepdims=True)
            for part in far:
                top = jnp.maximum(top, jnp.max(part, axis=0, keepdims=True))
            near = jnp.exp(near - top)
            total = jnp.sum(near, axis=0, keepdims=True)
            value = dot(
                value_cols[p][:, past : past + size], near.astype(jnp.bfloat16), 1, 0
            )
            for part in far:
                part = jnp.exp(part - top)
                total = total + jnp.sum(part, axis=0, keepdims=True)
                value = value + dot(value_cols[p][:, :past], part.astype(jnp.bfloat16), 1, 0)
            out_ref[heads[p], pl.ds(at[i], size)] = (value / total).astype(jnp.bfloat16)
            log_ref[p, :, pl.ds(at[i], size)] = top + jnp.log(total)


def attend(projected, order, heads, head_dim):
    tokens = projected.shape[1]
    blocks = order.shape[0]
    pair = 4
    rows = pair * head_dim

    def part(first):
        return pl.BlockSpec((rows, tokens), lambda h, order, first=first: (first // pair + h, 0))

    return pl.pallas_call(
        functools.partial(attend_kernel, blocks, pair),
        out_shape=[
            jax.ShapeDtypeStruct((heads * head_dim, tokens), jnp.bfloat16),
            jax.ShapeDtypeStruct((heads, 1, tokens), jnp.float32),
        ],
        grid_spec=pltpu.PrefetchScalarGridSpec(
            num_scalar_prefetch=1,
            grid=(heads // pair,),
            in_specs=[part(0), part(heads), part(2 * heads)],
            out_specs=[
                pl.BlockSpec((rows, tokens), lambda h, order: (h, 0)),
                pl.BlockSpec((pair, 1, tokens), lambda h, order: (h, 0, 0)),
            ],
            scratch_shapes=[pltpu.VMEM((tokens, head_dim), jnp.bfloat16)] * pair
            + [pltpu.VMEM((head_dim, tokens), jnp.bfloat16)] * pair,
        ),
        compiler_params=pltpu.CompilerParams(vmem_limit_bytes=48 * 1024 * 1024),
        cost_estimate=pl.CostEstimate(
            flops=heads * tokens * tokens * head_dim * 4,
            bytes_accessed=heads * head_dim * tokens * 8,
            transcendentals=heads * tokens * tokens,
        ),
        name="attend",
    )(order, projected, projected, projected)


def attend_back_kernel(
    blocks,
    pair,
    order_ref,
    q_ref,
    k_ref,
    v_ref,
    grad_ref,
    log_ref,
    scale_ref,
    *refs,
):
    scratch = refs[-5 * pair :]
    out_ref, term_ref = refs[-5 * pair - 2 : -5 * pair]
    key_rows, key_cols, value_rows, key_sum, value_sum = (
        scratch[n * pair : (n + 1) * pair] for n in range(5)
    )
    head_dim = q_ref.shape[0] // pair
    size = q_ref.shape[1] // blocks
    at = [pl.multiple_of(order_ref[i] * size, size) for i in range(blocks)]
    heads = [slice(p * head_dim, (p + 1) * head_dim) for p in range(pair)]
    for i in range(blocks):
        here = slice(i * size, (i + 1) * size)
        for p in range(pair):
            key = k_ref[heads[p], pl.ds(at[i], size)]
            key_rows[p][here, :] = key.T
            key_cols[p][:, here] = key
            value_rows[p][here, :] = v_ref[heads[p], pl.ds(at[i], size)].T
    for p in range(pair):
        key_sum[p][...] = jnp.zeros_like(key_sum[p])
        value_sum[p][...] = jnp.zeros_like(value_sum[p])
    key_pos = lax.broadcasted_iota(jnp.int32, (size, size), 0)
    query_pos = lax.broadcasted_iota(jnp.int32, (size, size), 1)
    seen = key_pos <= query_pos
    terms = [jnp.zeros((head_dim, 1), jnp.float32) for _ in range(pair)]

    def products(i):
        return [
            (
                scores_of(blocks, key_rows[p], q_ref[heads[p], pl.ds(at[i], size)], i),
                scores_of(blocks, value_rows[p], grad_ref[heads[p], pl.ds(at[i], size)], i),
            )
            for p in range(pair)
        ]

    upcoming = products(0)
    for i in range(blocks):
        current = upcoming
        if i + 1 < blocks:
            upcoming = products(i + 1)
        past = i * size
        spans = [slice(past, past + size)] + ([slice(0, past)] if i else [])
        for p in range(pair):
            query = q_ref[heads[p], pl.ds(at[i], size)]
            grad = grad_ref[heads[p], pl.ds(at[i], size)]
            log_total = log_ref[p, :, pl.ds(at[i], size)]
            scores, grads = current[p]
            probs = [jnp.exp(part - log_total) for part in scores]
            probs[0] = jnp.where(seen, probs[0], 0.0)
            delta = jnp.zeros((1, size), jnp.float32)
            for prob, grad_prob in zip(probs, grads):
                delta = delta + jnp.sum(prob * grad_prob, axis=0, keepdims=True)
            grad_query = jnp.zeros(query.shape, jnp.float32)
            for cols, prob, grad_prob in zip(spans, probs, grads):
                grad_score = (prob * (grad_prob - delta)).astype(jnp.bfloat16)
                value_sum[p][:, cols] += dot(grad, prob.astype(jnp.bfloat16), 1, 1)
                key_sum[p][:, cols] += dot(query, grad_score, 1, 1)
                grad_query = grad_query + dot(key_cols[p][:, cols], grad_score, 1, 0)
            terms[p] = terms[p] + jnp.sum(
                grad_query * query.astype(jnp.float32), axis=1, keepdims=True
            )
            out_ref[0, heads[p], pl.ds(at[i], size)] = (grad_query * scale_ref[...]).astype(
                jnp.bfloat16
            )
    for i in range(blocks):
        here = slice(i * size, (i + 1) * size)
        for p in range(pair):
            out_ref[1, heads[p], pl.ds(at[i], size)] = key_sum[p][:, here].astype(jnp.bfloat16)
            out_ref[2, heads[p], pl.ds(at[i], size)] = value_sum[p][:, here].astype(jnp.bfloat16)
    for p in range(pair):
        term_ref[p] = terms[p]


def attend_back(
    projected, grad_attended, log_total, multiplier, order, heads, head_dim, events=()
):
    tokens = projected.shape[1]
    blocks = order.shape[0]
    pair = 4
    rows = pair * head_dim

    def part(first):
        return pl.BlockSpec((rows, tokens), lambda h, order, first=first: (first // pair + h, 0))

    return pl.pallas_call(
        functools.partial(attend_back_kernel, blocks, pair),
        out_shape=[
            jax.ShapeDtypeStruct((3, heads * head_dim, tokens), jnp.bfloat16),
            jax.ShapeDtypeStruct((heads, head_dim, 1), jnp.float32),
        ],
        grid_spec=pltpu.PrefetchScalarGridSpec(
            num_scalar_prefetch=1,
            grid=(heads // pair,),
            in_specs=[
                part(0),
                part(heads),
                part(2 * heads),
                part(0),
                pl.BlockSpec((pair, 1, tokens), lambda h, order: (h, 0, 0)),
                pl.BlockSpec((head_dim, 1), lambda h, order: (0, 0)),
            ]
            + [pl.BlockSpec(memory_space=pltpu.HBM)] * len(events),
            out_specs=[
                pl.BlockSpec((3, rows, tokens), lambda h, order: (0, h, 0)),
                pl.BlockSpec((pair, head_dim, 1), lambda h, order: (h, 0, 0)),
            ],
            scratch_shapes=[pltpu.VMEM((tokens, head_dim), jnp.bfloat16)] * pair
            + [pltpu.VMEM((head_dim, tokens), jnp.bfloat16)] * pair
            + [pltpu.VMEM((tokens, head_dim), jnp.bfloat16)] * pair
            + [pltpu.VMEM((head_dim, tokens), jnp.float32)] * (2 * pair),
        ),
        compiler_params=pltpu.CompilerParams(vmem_limit_bytes=56 * 1024 * 1024),
        cost_estimate=pl.CostEstimate(
            flops=heads * tokens * tokens * head_dim * 10,
            bytes_accessed=heads * head_dim * tokens * 14,
            transcendentals=heads * tokens * tokens,
        ),
        name="attend_back",
    )(order, projected, projected, projected, grad_attended, log_total, multiplier, *events)


def paired_layer(
    inputs,
    targets,
    valid_counts,
    owners,
    master,
    first_moment,
    second_moment,
    norm_gains,
    gain_first,
    gain_second,
    query_scale,
    scale_first,
    scale_second,
):
    bf16 = jnp.bfloat16
    f32 = jnp.float32
    seq_local, block_rows, width = inputs.shape
    slot_count, head_dim, column_count = master.shape
    ff_blocks = FF // head_dim
    owner_count = lax.axis_size("fsdp")
    device = lax.axis_index("ctx")
    chip, core = device // 2, device % 2
    owner_here = lax.axis_index("fsdp")
    low_here = owner_here % 2
    high_here = owner_here // 2
    high_count = owner_count // 2
    high_distances = range(1, high_count)
    half_width = width // 2
    half_slots = slot_count // 2
    half_rows = seq_local * block_rows
    half_heads = H // 2
    half_blocks = ff_blocks // 2
    set_units = 4 * half_heads + 2 * half_blocks
    first_chip, first_core = chip == 0, core == 0

    def columns_here(array):
        return jnp.where(first_chip, array, jnp.roll(array, half_width, axis=-1))

    def sequence_rows(array):
        own = jnp.where(first_chip, array[0], array[1])
        got = swapped(jnp.where(first_chip, array[1], array[0]), "ctx", 2)
        return jnp.where(
            first_chip, jnp.concatenate([own, got]), jnp.concatenate([got, own])
        )

    def rows_apart(array):
        array = columns_here(array)
        first, last = array[:block_rows], array[block_rows:]
        other = jnp.where(first_chip, last, first).astype(bf16)
        return (jnp.where(first_chip, first, last), swapped(other, "ctx", 2))

    def rows_home(own, got):
        got = got.astype(f32)
        return jnp.where(first_chip, jnp.stack([own, got]), jnp.stack([got, own]))

    slot_rows = unit_rows(owners, slot_count)
    unit_total = owners.shape[0]
    kind_sizes = [H, H, H, H, ff_blocks, ff_blocks]
    kind_starts = [sum(kind_sizes[:i]) for i in range(6)]

    def unit_list(kinds, which):
        return jnp.concatenate(
            [
                kind_starts[k] + which * (kind_sizes[k] // 2) + jnp.arange(kind_sizes[k] // 2)
                for k in kinds
            ]
        ).astype(jnp.int32)

    wanted = jnp.concatenate(
        [unit_list(range(6), core), unit_list((4, 5), 1 - core)]
    )
    wanted_rows = slot_rows[wanted]
    wanted_owner, wanted_slot = wanted_rows // slot_count, wanted_rows % slot_count
    weight_from = 2 * (wanted_slot // half_slots != core) + (wanted_owner % 2 != low_here)
    weight_from = weight_from.astype(jnp.int32)
    weight_row = ((wanted_owner // 2) ^ high_here) * half_slots + wanted_slot % half_slots
    weight_plan = copy_plan(weight_from, weight_row, 4)
    weight_sizes = [3 * half_heads, half_heads + 2 * half_blocks, 2 * half_blocks]

    chunks = [(0, 256), (256, 256)]
    lead = 512
    tail = half_width - lead
    shard = master.astype(bf16)
    own_half = jnp.where(first_core, shard[:half_slots], shard[half_slots:])
    got_half = swapped(jnp.where(first_core, shard[half_slots:], shard[:half_slots]), "ctx", 1)
    shard = jnp.where(
        first_core,
        jnp.concatenate([own_half, got_half], axis=2),
        jnp.concatenate([got_half, own_half], axis=2),
    )
    shard, inputs, targets = lax.optimization_barrier((shard, inputs, targets))
    values_b = columns_here(sequence_rows(inputs))
    targets_b = columns_here(sequence_rows(targets))
    shard_last = shard[:, :, lead:]
    shards = [shard[:, :, start : start + size] for start, size in chunks]
    shards.append(jnp.concatenate([shard_last, swapped(shard_last, "ctx", 2)], axis=2))
    highs = []
    for number, part in enumerate(shards):
        if number:
            part, highs[-1] = lax.optimization_barrier((part, highs[-1]))
        highs.append(
            jnp.concatenate([part] + [swapped(part, "fsdp", 2 * d) for d in high_distances])
        )
    lows = [swapped(high, "fsdp", 1) for high in highs]
    own_units, rest_units, far_units = weight_sizes
    near_units = own_units + rest_units

    def pick_units(number, sizes, events):
        high, low = highs[number], lows[number]
        sources = [high, low, swapped(high, "ctx", 1), swapped(low, "ctx", 1)]
        return copy_rows(sources, [0] * 4, high.shape[2], weight_plan, sizes, events)

    lows[0], highs[1] = lax.optimization_barrier((lows[0], highs[1]))
    near_one, far_one = pick_units(
        0, [near_units, far_units], [shards[2], values_b, targets_b]
    )
    got_one = swapped(near_one, "ctx", 2)
    lows[1], far_one, highs[2] = lax.optimization_barrier((lows[1], far_one, highs[2]))
    qkv_two, rest_two, far_two = pick_units(1, weight_sizes, [got_one])
    qkv_got = swapped(qkv_two, "ctx", 2)
    rest_two, qkv_got = lax.optimization_barrier((rest_two, qkv_got))
    rest_got = swapped(rest_two, "ctx", 2)
    lows[2], far_two, got_one = lax.optimization_barrier((lows[2], far_two, got_one))
    qkv_last, rest_last, far_last = pick_units(2, weight_sizes, [])

    def columns_of(owns, gots, last):
        pieces = [(last, 0, tail, lead), (last, tail, tail, half_width + lead)]
        for (start, size), own, got in zip(chunks, owns, gots):
            pieces += [(own, 0, size, start), (got, 0, size, half_width + start)]
        return pieces

    def placed(pieces, from_end, count, out, row):
        return [
            (piece.shape[0] - from_end if from_end else 0, count, *columns, out, row)
            for piece, *columns in pieces
        ]

    qkv_pieces = columns_of([near_one, qkv_two], [got_one, qkv_got], qkv_last)
    rest_pieces = columns_of([near_one, rest_two], [got_one, rest_got], rest_last)
    far_pieces = columns_of(
        [far_one, far_two], [swapped(got, "ctx", 1) for got in (got_one, rest_got)], far_last
    )
    (w_qkv,) = place_pieces(
        [piece for piece, *_ in qkv_pieces],
        placed(qkv_pieces, 0, own_units, 0, 0),
        [(own_units, head_dim, width)],
    )
    w_qkv = w_qkv.reshape(-1, width)

    gains = columns_here(norm_gains)
    values_in = values_b.astype(f32)
    normed_own = (values_in * inverse_rms(values_in) * gains[0]).astype(bf16)
    normed_b = jnp.concatenate([normed_own, swapped(normed_own, "ctx", 1)])
    base = score_base / math.sqrt(head_dim)
    multiplier = jax.nn.softplus(query_scale) * base
    row_scale = jnp.concatenate(
        [jnp.tile(multiplier, half_heads), jnp.ones((2 * half_heads * head_dim,), f32)]
    )
    projected = (dot(w_qkv, normed_b, 1, 1) * row_scale[:, None]).astype(bf16)
    positions = jnp.arange(4, dtype=jnp.int32)
    order = jnp.where(positions % 2 == core, 0, 2) + positions // 2
    order = order.astype(jnp.int32)
    attended, log_total = attend(projected, order, half_heads, head_dim)
    count = summed(jnp.sum(valid_counts)[None], "fsdp")
    (w_out,) = place_pieces(
        [piece for piece, *_ in rest_pieces],
        placed(rest_pieces, rest_units, half_heads, 0, 0),
        [(half_heads, head_dim, width)],
        [log_total, count],
    )
    mlp_pieces, mlp_places = [], []
    for row, pieces in ((0, rest_pieces), (half_blocks, far_pieces)):
        for kind in range(2):
            mlp_pieces += [piece for piece, *_ in pieces]
            mlp_places += placed(pieces, (2 - kind) * half_blocks, half_blocks, kind, row)
    w_up, w_down = place_pieces(
        mlp_pieces, mlp_places, [(ff_blocks, head_dim, width)] * 2, [log_total]
    )
    w_out = w_out.reshape(-1, width)
    w_up = w_up.reshape(-1, width)
    w_down = w_down.reshape(-1, width)
    branch_far = dot(attended[:, half_rows:], w_out, 0, 0).astype(bf16)
    branch_got = swapped(branch_far, "ctx", 1)
    branch_own = dot(attended[:, :half_rows], w_out, 0, 0)
    middle = values_in + (branch_own + branch_got.astype(f32))
    normed_mid_b = (middle * inverse_rms(middle) * gains[1]).astype(bf16)
    hidden = dot(normed_mid_b, w_up, 1, 1)
    active_b = jax.nn.silu(hidden).astype(bf16)
    block_out = middle + dot(active_b, w_down, 1, 0)
    seq_length = 2 * half_rows
    row = jnp.arange(half_rows, dtype=jnp.int32)
    row_pos = (core + 2 * (row // block_rows)) * block_rows + row % block_rows
    valid = jnp.where(first_chip, valid_counts[0], valid_counts[1])
    counted = (row_pos >= seq_length - valid).astype(f32)

    (apart,) = lax.optimization_barrier((block_out,))
    block_own, block_got = rows_apart(apart)

    out_grad = 2.0 * (block_out - targets_b.astype(f32)) * counted[:, None]
    out_grad_b = out_grad.astype(bf16)
    grad_active = dot(out_grad_b, w_down, 1, 1)
    sigma = jax.nn.sigmoid(hidden)
    grad_hidden_b = (grad_active * sigma * (1.0 + hidden * (1.0 - sigma))).astype(bf16)
    grad_normed_mid = dot(grad_hidden_b, w_up, 1, 0)
    inverse = inverse_rms(middle)
    scaled = grad_normed_mid * gains[1]
    grad_middle = out_grad + (
        inverse * scaled
        - middle * inverse**3 * jnp.mean(scaled * middle, axis=-1, keepdims=True)
    )
    grad_gain_two = jnp.sum(grad_normed_mid * middle * inverse, axis=0)
    grad_middle_own = grad_middle.astype(bf16)
    grad_middle_got = swapped(grad_middle_own, "ctx", 1)
    far_blocks = half_blocks * head_dim
    wide = slice(half_width + 256, half_width + lead)
    slim = slice(half_width, half_width + 256)
    block_grads = []
    for left, right in ((grad_hidden_b, normed_mid_b), (active_b, out_grad_b)):
        got = swapped(dot(left[:, far_blocks:], right, 0, 0).astype(bf16), "ctx", 1)
        total = dot(left[:, :far_blocks], right, 0, 0) + got.astype(f32)
        block_grads.append(total.astype(bf16).reshape(half_blocks, head_dim, width))
    block_grads = jnp.concatenate(block_grads)
    grad_middle_got, block_grads = lax.optimization_barrier((grad_middle_got, block_grads))
    grad_middle_b = jnp.concatenate([grad_middle_own, grad_middle_got])
    grad_attended = dot(w_out, grad_middle_b, 1, 1).astype(bf16)
    head_grads = dot(attended, grad_middle_b, 1, 0).astype(bf16)
    head_grads = head_grads.reshape(half_heads, head_dim, width)

    def early_columns(columns):
        return jnp.concatenate([head_grads[:, :, columns], block_grads[:, :, columns]])

    early_wide, early_slim = early_columns(wide), early_columns(slim)
    wide_got = swapped(early_wide, "ctx", 2)

    def last_columns(array):
        return jnp.concatenate(
            [array[..., lead:half_width], array[..., half_width + lead :]], axis=-1
        )

    early_last = jnp.concatenate([last_columns(head_grads), last_columns(block_grads)])
    grad_proj, grad_scale = attend_back(
        projected,
        grad_attended,
        log_total,
        multiplier[:, None],
        order,
        half_heads,
        head_dim,
        [early_wide, early_slim, early_last, block_got],
    )
    grad_proj = grad_proj.reshape(-1, grad_proj.shape[2])
    scale_term = (
        jnp.sum(grad_scale[:, :, 0], axis=0) / multiplier * base * jax.nn.sigmoid(query_scale)
    )

    low_order = jnp.stack([low_here, 1 - low_here])
    table_slots = (
        (2 * (jnp.arange(high_count) ^ high_here)[None, :, None] + low_order[:, None, None])
        * slot_count
        + core * half_slots
        + jnp.arange(half_slots)[None, None, :]
    ).reshape(-1)
    holds = table_slots[:, None] == slot_rows[None, :]
    unit_order = jnp.arange(unit_total, dtype=jnp.int32)
    slot_unit = jnp.sum(jnp.where(holds, unit_order[None, :] + 1, 0), axis=1) - 1
    kind = jnp.where(
        slot_unit < 4 * H, slot_unit // H, 4 + (slot_unit - 4 * H) // ff_blocks
    )
    kind_size = jnp.where(kind < 4, H, ff_blocks)
    within = jnp.where(kind < 4, slot_unit % H, (slot_unit - 4 * H) % ff_blocks)
    other_set = (within // (kind_size // 2) != core).astype(jnp.int32)
    rank = within % (kind_size // 2)
    grad_row = rank + jnp.where(
        kind <= 3, kind * half_heads, 4 * half_heads + (kind - 4) * half_blocks
    )
    empty = slot_unit < 0
    grad_from = jnp.where(empty, 2, other_set).astype(jnp.int32)
    grad_row = jnp.where(empty, 0, grad_row).astype(jnp.int32)
    grad_plan = copy_plan(grad_from, grad_row, 3)
    zero = jnp.zeros((1, head_dim, 256), bf16)

    def pick_table(own, got, offset, size, events=()):
        return copy_rows(
            [own, got, zero],
            [offset, offset, 0],
            size,
            grad_plan,
            [high_count * half_slots] * 2,
            events,
        )

    def table_sums(keep, got):
        sums = []
        for d in range(high_count):
            rows = slice(d * half_slots, (d + 1) * half_slots)
            sums.append((keep[rows].astype(f32) + got[rows].astype(f32)).astype(bf16))
        return sums

    def from_owners(tables):
        return [swapped(tables[d], "fsdp", 2 * d) for d in high_distances]

    def owner_sum(table, got):
        total = table.astype(f32)
        for part in got:
            total = total + part.astype(f32)
        return total.astype(bf16)

    def proj_grad(columns):
        return dot(grad_proj, columns, 1, 0).astype(bf16).reshape(-1, head_dim, columns.shape[1])

    def chip_sum(start, proj_got, early_got):
        near = slice(start, start + 256)
        parts = [
            (proj_grad(normed_b[:, near]), proj_got),
            (head_grads[:, :, near], early_got[:half_heads]),
            (block_grads[:, :, near], early_got[half_heads:]),
        ]
        return jnp.concatenate(
            [(own.astype(f32) + got.astype(f32)).astype(bf16) for own, got in parts]
        )

    proj_last = proj_grad(last_columns(normed_b))
    proj_last, wide_got = lax.optimization_barrier((proj_last, wide_got))
    total_last = jnp.concatenate([proj_last, early_last])
    wide_far = proj_grad(normed_b[:, wide])
    wide_proj = swapped(wide_far, "ctx", 2)
    keep_last, send_last = pick_table(
        total_last, swapped(total_last, "ctx", 1), 0, 256, [wide_far]
    )
    low_last = swapped(send_last, "fsdp", 1)
    keep_last, grad_proj = lax.optimization_barrier((keep_last, grad_proj))
    slim_far = jnp.concatenate([proj_grad(normed_b[:, slim]), early_slim])
    normed_far = dot(grad_proj[:, half_rows:], w_qkv, 0, 0).astype(bf16)
    low_last, wide_proj, slim_far, normed_far = lax.optimization_barrier(
        (low_last, wide_proj, slim_far, normed_far)
    )
    normed_got = swapped(normed_far, "ctx", 1)
    slim_got = swapped(slim_far, "ctx", 2)
    total = chip_sum(256, wide_proj, wide_got)
    keep_three, send_three = pick_table(total, swapped(total, "ctx", 1), 0, 256, [normed_got])
    low_last, keep_three, grad_proj = lax.optimization_barrier((low_last, keep_three, grad_proj))
    low_three = swapped(send_three, "fsdp", 1)
    tables_last = table_sums(keep_last, low_last)
    high_last = from_owners(tables_last)
    grad_normed_in = dot(grad_proj[:, :half_rows], w_qkv, 0, 0) + normed_got.astype(f32)
    inverse = inverse_rms(values_in)
    scaled = grad_normed_in * gains[0]
    input_grad = grad_middle + (
        inverse * scaled
        - values_in * inverse**3 * jnp.mean(scaled * values_in, axis=-1, keepdims=True)
    )
    grad_gain_one = jnp.sum(grad_normed_in * values_in * inverse, axis=0)
    low_three, high_last, slim_got, input_grad = lax.optimization_barrier(
        (low_three, high_last, slim_got, input_grad)
    )
    total = chip_sum(0, slim_got[: 3 * half_heads], slim_got[3 * half_heads :])
    keep_one, send_one = pick_table(total, swapped(total, "ctx", 1), 0, 256, [low_three])
    keep_one, low_three = lax.optimization_barrier((keep_one, low_three))
    tables_three = table_sums(keep_three, low_three)
    high_three = from_owners(tables_three)

    gain_terms = columns_here(jnp.stack([grad_gain_one, grad_gain_two]))
    small = jnp.concatenate([gain_terms.reshape(-1), scale_term])
    small = jnp.pad(small, (0, -small.shape[0] % 1024))
    keep_one, small = lax.optimization_barrier((keep_one, small))
    tables_one = table_sums(keep_one, swapped(send_one, "fsdp", 1))
    small = small + swapped(small, "fsdp", 1)
    tables_one, high_three, high_last, small, input_grad = lax.optimization_barrier(
        (tables_one, high_three, high_last, small, input_grad)
    )
    high_one = from_owners(tables_one)
    small = small + swapped(small, "fsdp", 2)
    owned_last = owner_sum(tables_last[0], high_last)
    owned_got = swapped(owned_last[:, :, tail:], "ctx", 2)
    input_own, input_got = rows_apart(input_grad)
    high_one, small, input_got, owned_got = lax.optimization_barrier(
        (high_one, small, input_got, owned_got)
    )
    small = summed(small + swapped(small, "fsdp", 4), "ctx")
    gain_sums = small[: 2 * width].reshape(2, width)
    scale_sums = small[2 * width : 2 * width + head_dim]

    count = count[0].astype(f32)
    owned = [
        owner_sum(tables_one[0], high_one),
        owner_sum(tables_three[0], high_three),
        (owned_last[:, :, :tail].astype(f32) + owned_got.astype(f32)).astype(bf16),
    ]
    owned = jnp.concatenate(owned, axis=2).reshape(half_slots, head_dim, 2, column_count)
    kept = jnp.where(first_core, owned[:, :, 0], owned[:, :, 1])
    sent = swapped(jnp.where(first_core, owned[:, :, 1], owned[:, :, 0]), "ctx", 1)
    slot_sums = jnp.where(
        first_core, jnp.concatenate([kept, sent]), jnp.concatenate([sent, kept])
    ).astype(f32)
    new_master, new_first, new_second = adam_step(
        master, first_moment, second_moment, slot_sums / count, master_rate, decay_rate
    )
    new_gains, new_gain_first, new_gain_second = adam_step(
        norm_gains, gain_first, gain_second, gain_sums / count, gain_rate, 0.0
    )
    new_scale, new_scale_first, new_scale_second = adam_step(
        query_scale, scale_first, scale_second, scale_sums / count, scale_rate, 0.0
    )
    return (
        rows_home(block_own, block_got),
        rows_home(input_own, input_got),
        new_master,
        new_first,
        new_second,
        new_gains,
        new_gain_first,
        new_gain_second,
        new_scale,
        new_scale_first,
        new_scale_second,
    )


def on_device(*arguments):
    paired = (
        lax.axis_size("ctx") == 4
        and lax.axis_size("fsdp") == 8
        and arguments[0].shape[0] == 2
    )
    return (paired_layer if paired else general_layer)(*arguments)


def solution(mesh):
    in_specs = (
        P("fsdp", "ctx", None),
        P("fsdp", "ctx", None),
        P("fsdp"),
        P(),
        P("fsdp", None, "ctx"),
        P("fsdp", None, "ctx"),
        P("fsdp", None, "ctx"),
        P(),
        P(),
        P(),
        P(),
        P(),
        P(),
    )
    out_specs = (
        P("fsdp", "ctx", None),
        P("fsdp", "ctx", None),
        P("fsdp", None, "ctx"),
        P("fsdp", None, "ctx"),
        P("fsdp", None, "ctx"),
        P(),
        P(),
        P(),
        P(),
        P(),
        P(),
    )
    return jax.shard_map(
        on_device, mesh=mesh, in_specs=in_specs, out_specs=out_specs, check_vma=False
    )
```

```python
import functools
import math

import jax
import jax.numpy as jnp
from jax import lax
from jax.experimental import pallas as pl
from jax.experimental.pallas import tpu as pltpu
from jax.sharding import PartitionSpec as P

H = 16
FF = 1280
STEP = 10


norm_eps = 1e-06
beta_first = 0.9
beta_second = 0.95
adam_eps = 1e-08
decay_rate = 0.1
master_rate = 0.05
gain_rate = 2.0
scale_rate = 2.0
score_base = 1.442695041
masked_score = -1e30


def from_behind(block, axis, distance):
    devices = range(lax.axis_size(axis))
    route = [(i - distance, i) for i in devices if i - distance in devices]
    return lax.ppermute(block, axis, route)


def shifted(array, axis, by):
    count = lax.axis_size(axis)
    return lax.ppermute(array, axis, [(i, (i + by) % count) for i in range(count)])


def unit_rows(owners, slot_count):
    unit_count = owners.shape[0]
    unit_order = jnp.arange(unit_count, dtype=jnp.int32)
    same_owner = owners[:, None] == owners[None, :]
    earlier = unit_order[None, :] < unit_order[:, None]
    slot_rank = jnp.sum((same_owner & earlier).astype(jnp.int32), axis=1)
    return owners * slot_count + slot_rank


def inverse_rms(values):
    return lax.rsqrt(jnp.mean(values * values, axis=-1, keepdims=True) + norm_eps)


def norm_back(values, gain, grad_normed):
    inverse = inverse_rms(values)
    scaled = grad_normed * gain
    grad_values = inverse * scaled - values * inverse**3 * jnp.mean(
        scaled * values, axis=-1, keepdims=True
    )
    grad_gain = jnp.sum(grad_normed * values * inverse, axis=(0, 1))
    return (grad_values, grad_gain)


def adam_step(values, moment_one, moment_two, gradient, step_rate, weight_decay):
    moment_one = beta_first * moment_one + (1.0 - beta_first) * gradient
    moment_two = beta_second * moment_two + (1.0 - beta_second) * gradient * gradient
    first_hat = moment_one / (1.0 - beta_first**STEP)
    second_hat = moment_two / (1.0 - beta_second**STEP)
    values = values - step_rate * (
        first_hat / (jnp.sqrt(second_hat) + adam_eps) + weight_decay * values
    )
    return (values, moment_one, moment_two)


def general_layer(
    inputs,
    targets,
    valid_counts,
    owners,
    master,
    first_moment,
    second_moment,
    norm_gains,
    gain_first,
    gain_second,
    query_scale,
    scale_first,
    scale_second,
):
    seq_local, block_rows, width = inputs.shape
    slot_count, head_dim, column_count = master.shape
    ff_blocks = FF // head_dim
    ctx_size = lax.axis_size("ctx")
    ctx_index = lax.axis_index("ctx")
    slot_rows = unit_rows(owners, slot_count)
    owner_table = lax.all_gather(master.astype(jnp.bfloat16), "fsdp", axis=0, tiled=True)
    picked = owner_table[slot_rows]
    weights = lax.all_gather(picked, "ctx", axis=2, tiled=True)
    w_qkv = weights[0 : 3 * H]
    w_out = weights[3 * H : 4 * H]
    w_up = weights[4 * H : 4 * H + ff_blocks]
    w_down = weights[4 * H + ff_blocks :]
    values_in = inputs.astype(jnp.float32)
    normed_b = (values_in * inverse_rms(values_in) * norm_gains[0]).astype(jnp.bfloat16)
    projected = jnp.einsum("sbd,hed->shbe", normed_b, w_qkv, preferred_element_type=jnp.float32)
    query_pre = projected[:, 0:H]
    multiplier = jax.nn.softplus(query_scale) * (score_base / math.sqrt(head_dim))
    query_b = (query_pre * multiplier).astype(jnp.bfloat16)
    key_b = projected[:, H : 2 * H].astype(jnp.bfloat16)
    value_b = projected[:, 2 * H : 3 * H].astype(jnp.bfloat16)
    query_rows = ctx_index * block_rows + jnp.arange(block_rows, dtype=jnp.int32)
    last_row = ctx_index * block_rows + block_rows - 1
    start_state = (
        jnp.full(query_pre.shape[:3], masked_score, jnp.float32),
        jnp.zeros(query_pre.shape[:3], jnp.float32),
        jnp.zeros(query_pre.shape, jnp.float32),
    )
    key_part = lax.all_gather(key_b, "ctx", axis=2, tiled=True)
    value_part = lax.all_gather(value_b, "ctx", axis=2, tiled=True)
    key_count = key_part.shape[2]

    def update(current):
        run_max, run_sum, accum = current
        key_rows = jnp.arange(key_count, dtype=jnp.int32)
        allowed = query_rows[:, None] >= key_rows[None, :]
        scores = jnp.einsum(
            "shqe,shke->shqk", query_b, key_part, preferred_element_type=jnp.float32
        )
        scores = jnp.where(allowed, scores, masked_score)
        new_max = jnp.maximum(run_max, jnp.max(scores, axis=-1))
        attn_probs = jnp.where(allowed, jnp.exp(scores - new_max[..., None]), 0.0)
        run_sum = jnp.sum(attn_probs, axis=-1)
        accum = jnp.einsum(
            "shqk,shke->shqe",
            attn_probs.astype(jnp.bfloat16),
            value_part,
            preferred_element_type=jnp.float32,
        )
        return (new_max, run_sum, accum)

    run_max, run_sum, accum = lax.cond(
        jnp.int32(0) <= last_row, update, lambda current: current, start_state
    )
    attended = accum / run_sum[..., None]
    log_total = run_max + jnp.log(run_sum)
    attended_b = attended.astype(jnp.bfloat16)
    branch = jnp.einsum("shbe,hed->sbd", attended_b, w_out, preferred_element_type=jnp.float32)
    middle = values_in + branch
    normed_mid_b = (middle * inverse_rms(middle) * norm_gains[1]).astype(jnp.bfloat16)
    hidden = jnp.einsum("sbd,fed->sbfe", normed_mid_b, w_up, preferred_element_type=jnp.float32)
    active_b = jax.nn.silu(hidden).astype(jnp.bfloat16)
    block_out = middle + jnp.einsum(
        "sbfe,fed->sbd", active_b, w_down, preferred_element_type=jnp.float32
    )
    seq_length = block_rows * ctx_size
    counted = (query_rows[None, :] >= (seq_length - valid_counts)[:, None]).astype(jnp.float32)
    count_term = jnp.sum(counted)
    out_grad = 2.0 * (block_out - targets.astype(jnp.float32)) * counted[..., None]
    out_grad_b = out_grad.astype(jnp.bfloat16)
    grad_down = jnp.einsum(
        "sbfe,sbd->fed", active_b, out_grad_b, preferred_element_type=jnp.float32
    )
    grad_active = jnp.einsum(
        "sbd,fed->sbfe", out_grad_b, w_down, preferred_element_type=jnp.float32
    )
    sigma = jax.nn.sigmoid(hidden)
    grad_hidden_b = (grad_active * sigma * (1.0 + hidden * (1.0 - sigma))).astype(jnp.bfloat16)
    grad_up = jnp.einsum(
        "sbfe,sbd->fed", grad_hidden_b, normed_mid_b, preferred_element_type=jnp.float32
    )
    grad_normed_mid = jnp.einsum(
        "sbfe,fed->sbd", grad_hidden_b, w_up, preferred_element_type=jnp.float32
    )
    grad_middle_norm, grad_gain_two = norm_back(middle, norm_gains[1], grad_normed_mid)
    grad_middle = out_grad + grad_middle_norm
    grad_middle_b = grad_middle.astype(jnp.bfloat16)
    grad_out = jnp.einsum(
        "shbe,sbd->hed", attended_b, grad_middle_b, preferred_element_type=jnp.float32
    )
    grad_attended_b = jnp.einsum(
        "sbd,hed->shbe", grad_middle_b, w_out, preferred_element_type=jnp.float32
    ).astype(jnp.bfloat16)
    delta = jnp.sum(grad_attended_b.astype(jnp.float32) * attended, axis=-1)

    def block_grads(source, key_cur, value_cur, partial_grads):
        grad_key, grad_value, grad_query = partial_grads
        key_rows = source * block_rows + jnp.arange(block_rows, dtype=jnp.int32)
        allowed = query_rows[:, None] >= key_rows[None, :]
        scores = jnp.einsum("shqe,shke->shqk", query_b, key_cur, preferred_element_type=jnp.float32)
        scores = jnp.where(allowed, scores, masked_score)
        attn_probs = jnp.exp(scores - log_total[..., None])
        grad_value = grad_value + jnp.einsum(
            "shqk,shqe->shke",
            attn_probs.astype(jnp.bfloat16),
            grad_attended_b,
            preferred_element_type=jnp.float32,
        )
        grad_probs = jnp.einsum(
            "shqe,shke->shqk", grad_attended_b, value_cur, preferred_element_type=jnp.float32
        )
        grad_scores_b = (attn_probs * (grad_probs - delta[..., None])).astype(jnp.bfloat16)
        grad_query = grad_query + jnp.einsum(
            "shqk,shke->shqe", grad_scores_b, key_cur, preferred_element_type=jnp.float32
        )
        grad_key = grad_key + jnp.einsum(
            "shqk,shqe->shke", grad_scores_b, query_b, preferred_element_type=jnp.float32
        )
        return (grad_key, grad_value, grad_query)

    zero_heads = jnp.zeros(query_pre.shape, jnp.float32)

    def back_turn(which_turn, current):
        key_cur, value_cur, grad_key, grad_value, grad_query = current
        source = (ctx_index - which_turn) % ctx_size
        grad_key, grad_value, grad_query = lax.cond(
            source <= ctx_index,
            lambda parts: block_grads(source, key_cur, value_cur, parts),
            lambda parts: parts,
            (grad_key, grad_value, grad_query),
        )
        key_cur, value_cur = from_behind((key_cur, value_cur), "ctx", 1)
        grad_key, grad_value = (
            shifted(grad_key.astype(jnp.bfloat16), "ctx", 1).astype(grad_key.dtype),
            shifted(grad_value.astype(jnp.bfloat16), "ctx", 1).astype(grad_value.dtype),
        )
        return (key_cur, value_cur, grad_key, grad_value, grad_query)

    back_state = (key_b, value_b, zero_heads, zero_heads, zero_heads)
    back_state = lax.fori_loop(0, ctx_size, back_turn, back_state)
    grad_key, grad_value, grad_query = (back_state[2], back_state[3], back_state[4])
    grad_proj_b = jnp.concatenate([grad_query * multiplier, grad_key, grad_value], axis=1).astype(
        jnp.bfloat16
    )
    grad_qkv = jnp.einsum(
        "shbe,sbd->hed", grad_proj_b, normed_b, preferred_element_type=jnp.float32
    )
    grad_normed_in = jnp.einsum(
        "shbe,hed->sbd", grad_proj_b, w_qkv, preferred_element_type=jnp.float32
    )
    grad_input_norm, grad_gain_one = norm_back(values_in, norm_gains[0], grad_normed_in)
    input_grad = grad_middle + grad_input_norm
    scale_term = (
        jnp.sum(grad_query * query_pre, axis=(0, 1, 2))
        * (score_base / math.sqrt(head_dim))
        * jax.nn.sigmoid(query_scale)
    )
    unit_grads = jnp.concatenate([grad_qkv, grad_out, grad_up, grad_down], axis=0)
    owner_total = lax.axis_size("fsdp") * slot_count
    table_grads = (
        jnp.zeros((owner_total, head_dim, width), jnp.float32).at[slot_rows].set(unit_grads)
    )
    owned = lax.psum_scatter(
        table_grads.astype(jnp.bfloat16), "fsdp", scatter_dimension=0, tiled=True
    )
    slot_sums = lax.psum_scatter(owned, "ctx", scatter_dimension=2, tiled=True).astype(jnp.float32)
    gain_sums, scale_sums, count = lax.psum(
        (jnp.stack([grad_gain_one, grad_gain_two]), scale_term, count_term), ("ctx", "fsdp")
    )
    new_master, new_first, new_second = adam_step(
        master, first_moment, second_moment, slot_sums / count, master_rate, decay_rate
    )
    new_gains, new_gain_first, new_gain_second = adam_step(
        norm_gains, gain_first, gain_second, gain_sums / count, gain_rate, 0.0
    )
    new_scale, new_scale_first, new_scale_second = adam_step(
        query_scale, scale_first, scale_second, scale_sums / count, scale_rate, 0.0
    )
    return (
        block_out,
        input_grad,
        new_master,
        new_first,
        new_second,
        new_gains,
        new_gain_first,
        new_gain_second,
        new_scale,
        new_scale_first,
        new_scale_second,
    )


def swapped(array, axis, distance):
    return lax.ppermute(
        array, axis, [(i, i ^ distance) for i in range(lax.axis_size(axis))]
    )


def summed(array, axis):
    size = lax.axis_size(axis)
    if size & (size - 1):
        return lax.psum(array, axis)
    distance = 1
    while distance < size:
        array = array + swapped(array, axis, distance)
        distance *= 2
    return array


def dot(left, right, left_dim, right_dim):
    return lax.dot_general(
        left,
        right,
        (((left_dim,), (right_dim,)), ((), ())),
        preferred_element_type=jnp.float32,
    )


def copy_rows_kernel(sizes, offsets, width, bound_ref, place_ref, row_ref, *refs):
    sources = refs[: len(offsets)]
    outs = refs[-2 - len(sizes) : -2]
    rows, sems = refs[-2:]
    for number, (source, offset) in enumerate(zip(sources, offsets)):

        @pl.loop(bound_ref[number], bound_ref[number + 1])
        def copy_row(i, source=source, offset=offset):
            pltpu.make_async_copy(
                source.at[row_ref[i], :, pl.ds(offset, width)],
                rows.at[place_ref[i]],
                sems.at[len(sizes)],
            ).start()

    pltpu.make_async_copy(rows, rows, sems.at[len(sizes)]).wait()
    copies, start = [], 0
    for place, (out, size) in enumerate(zip(outs, sizes)):
        copies.append(
            pltpu.make_async_copy(rows.at[pl.ds(start, size)], out, sems.at[place])
        )
        start += size
    for copy in copies:
        copy.start()
    for copy in copies:
        copy.wait()


def copy_plan(pick_from, pick_row, source_count):
    number = jnp.arange(pick_from.shape[0], dtype=jnp.int32)
    before = pick_from[None, :] < pick_from[:, None]
    same = (pick_from[None, :] == pick_from[:, None]) & (number[None, :] < number[:, None])
    rank = jnp.sum((before | same).astype(jnp.int32), axis=1)
    here = rank[None, :] == number[:, None]
    place = jnp.sum(jnp.where(here, number[None, :], 0), axis=1)
    row = jnp.sum(jnp.where(here, pick_row[None, :], 0), axis=1)
    bounds = jnp.sum(
        (pick_from[None, :] < jnp.arange(source_count + 1)[:, None]).astype(jnp.int32), axis=1
    )
    return (bounds.astype(jnp.int32), place.astype(jnp.int32), row.astype(jnp.int32))


def copy_rows(sources, offsets, width, plan, sizes, events=()):
    rows = sources[0].shape[1]
    total = sum(sizes)
    return pl.pallas_call(
        functools.partial(copy_rows_kernel, tuple(sizes), tuple(offsets), width),
        out_shape=[jax.ShapeDtypeStruct((size, rows, width), sources[0].dtype) for size in sizes],
        grid_spec=pltpu.PrefetchScalarGridSpec(
            num_scalar_prefetch=3,
            grid=(1,),
            in_specs=[pl.BlockSpec(memory_space=pltpu.HBM)] * (len(sources) + len(events)),
            out_specs=[pl.BlockSpec(memory_space=pltpu.HBM)] * len(sizes),
            scratch_shapes=[
                pltpu.VMEM((total, rows, width), sources[0].dtype),
                pltpu.SemaphoreType.DMA((len(sizes) + 1,)),
            ],
        ),
        compiler_params=pltpu.CompilerParams(vmem_limit_bytes=40 * 1024 * 1024),
        cost_estimate=pl.CostEstimate(flops=0, bytes_accessed=1024, transcendentals=0),
        name="copy_rows",
    )(*plan, *sources, *events)


def place_pieces_kernel(places, count_outs, *refs):
    pieces = refs[: len(places)]
    outs = refs[-1 - count_outs : -1]
    sems = refs[-1]
    copies = []
    for number, (piece, place) in enumerate(zip(pieces, places)):
        first, count, begin, size, column, out, row = place
        copies.append(
            pltpu.make_async_copy(
                piece.at[pl.ds(first, count), :, pl.ds(begin, size)],
                outs[out].at[pl.ds(row, count), :, pl.ds(column, size)],
                sems.at[number],
            )
        )
    for copy in copies:
        copy.start()
    for copy in copies:
        copy.wait()


def place_pieces(pieces, places, shapes, events=()):
    return pl.pallas_call(
        functools.partial(place_pieces_kernel, tuple(places), len(shapes)),
        out_shape=[jax.ShapeDtypeStruct(shape, pieces[0].dtype) for shape in shapes],
        in_specs=[pl.BlockSpec(memory_space=pltpu.HBM)] * (len(pieces) + len(events)),
        out_specs=[pl.BlockSpec(memory_space=pltpu.VMEM)] * len(shapes),
        scratch_shapes=[pltpu.SemaphoreType.DMA((len(pieces),))],
        compiler_params=pltpu.CompilerParams(vmem_limit_bytes=40 * 1024 * 1024),
        cost_estimate=pl.CostEstimate(flops=0, bytes_accessed=1024, transcendentals=0),
        name="place_pieces",
    )(*pieces, *events)


def scores_of(blocks, key_rows, query, i):
    size = query.shape[1]
    parts = [(i * size, size)] + ([(0, i * size)] if i else [])
    return [dot(key_rows[first : first + count, :], query, 1, 0) for first, count in parts]


def attend_kernel(blocks, pair, order_ref, q_ref, k_ref, v_ref, out_ref, log_ref, *refs):
    key_rows, value_cols = refs[:pair], refs[pair:]
    head_dim = q_ref.shape[0] // pair
    size = q_ref.shape[1] // blocks
    at = [pl.multiple_of(order_ref[i] * size, size) for i in range(blocks)]
    heads = [slice(p * head_dim, (p + 1) * head_dim) for p in range(pair)]
    for i in range(blocks):
        here = slice(i * size, (i + 1) * size)
        for p in range(pair):
            key_rows[p][here, :] = k_ref[heads[p], pl.ds(at[i], size)].T
            value_cols[p][:, here] = v_ref[heads[p], pl.ds(at[i], size)]
    key_pos = lax.broadcasted_iota(jnp.int32, (size, size), 0)
    query_pos = lax.broadcasted_iota(jnp.int32, (size, size), 1)
    seen = key_pos <= query_pos

    def scores(i):
        return [
            scores_of(blocks, key_rows[p], q_ref[heads[p], pl.ds(at[i], size)], i)
            for p in range(pair)
        ]

    upcoming = scores(0)
    for i in range(blocks):
        current = upcoming
        if i + 1 < blocks:
            upcoming = scores(i + 1)
        past = i * size
        for p in range(pair):
            near, *far = current[p]
            near = jnp.where(seen, near, masked_score)
            top = jnp.max(near, axis=0, keepdims=True)
            for part in far:
                top = jnp.maximum(top, jnp.max(part, axis=0, keepdims=True))
            near = jnp.exp(near - top)
            total = jnp.sum(near, axis=0, keepdims=True)
            value = dot(
                value_cols[p][:, past : past + size], near.astype(jnp.bfloat16), 1, 0
            )
            for part in far:
                part = jnp.exp(part - top)
                total = total + jnp.sum(part, axis=0, keepdims=True)
                value = value + dot(value_cols[p][:, :past], part.astype(jnp.bfloat16), 1, 0)
            out_ref[heads[p], pl.ds(at[i], size)] = (value / total).astype(jnp.bfloat16)
            log_ref[p, :, pl.ds(at[i], size)] = top + jnp.log(total)


def attend(projected, order, heads, head_dim):
    tokens = projected.shape[1]
    blocks = order.shape[0]
    pair = 4
    rows = pair * head_dim

    def part(first):
        return pl.BlockSpec((rows, tokens), lambda h, order, first=first: (first // pair + h, 0))

    return pl.pallas_call(
        functools.partial(attend_kernel, blocks, pair),
        out_shape=[
            jax.ShapeDtypeStruct((heads * head_dim, tokens), jnp.bfloat16),
            jax.ShapeDtypeStruct((heads, 1, tokens), jnp.float32),
        ],
        grid_spec=pltpu.PrefetchScalarGridSpec(
            num_scalar_prefetch=1,
            grid=(heads // pair,),
            in_specs=[part(0), part(heads), part(2 * heads)],
            out_specs=[
                pl.BlockSpec((rows, tokens), lambda h, order: (h, 0)),
                pl.BlockSpec((pair, 1, tokens), lambda h, order: (h, 0, 0)),
            ],
            scratch_shapes=[pltpu.VMEM((tokens, head_dim), jnp.bfloat16)] * pair
            + [pltpu.VMEM((head_dim, tokens), jnp.bfloat16)] * pair,
        ),
        compiler_params=pltpu.CompilerParams(vmem_limit_bytes=48 * 1024 * 1024),
        cost_estimate=pl.CostEstimate(
            flops=heads * tokens * tokens * head_dim * 4,
            bytes_accessed=heads * head_dim * tokens * 8,
            transcendentals=heads * tokens * tokens,
        ),
        name="attend",
    )(order, projected, projected, projected)


def attend_back_kernel(
    blocks,
    pair,
    order_ref,
    q_ref,
    k_ref,
    v_ref,
    grad_ref,
    log_ref,
    scale_ref,
    *refs,
):
    scratch = refs[-5 * pair :]
    out_ref, term_ref = refs[-5 * pair - 2 : -5 * pair]
    key_rows, key_cols, value_rows, key_sum, value_sum = (
        scratch[n * pair : (n + 1) * pair] for n in range(5)
    )
    head_dim = q_ref.shape[0] // pair
    size = q_ref.shape[1] // blocks
    at = [pl.multiple_of(order_ref[i] * size, size) for i in range(blocks)]
    heads = [slice(p * head_dim, (p + 1) * head_dim) for p in range(pair)]
    for i in range(blocks):
        here = slice(i * size, (i + 1) * size)
        for p in range(pair):
            key = k_ref[heads[p], pl.ds(at[i], size)]
            key_rows[p][here, :] = key.T
            key_cols[p][:, here] = key
            value_rows[p][here, :] = v_ref[heads[p], pl.ds(at[i], size)].T
    for p in range(pair):
        key_sum[p][...] = jnp.zeros_like(key_sum[p])
        value_sum[p][...] = jnp.zeros_like(value_sum[p])
    key_pos = lax.broadcasted_iota(jnp.int32, (size, size), 0)
    query_pos = lax.broadcasted_iota(jnp.int32, (size, size), 1)
    seen = key_pos <= query_pos
    terms = [jnp.zeros((head_dim, 1), jnp.float32) for _ in range(pair)]

    def products(i):
        return [
            (
                scores_of(blocks, key_rows[p], q_ref[heads[p], pl.ds(at[i], size)], i),
                scores_of(blocks, value_rows[p], grad_ref[heads[p], pl.ds(at[i], size)], i),
            )
            for p in range(pair)
        ]

    upcoming = products(0)
    for i in range(blocks):
        current = upcoming
        if i + 1 < blocks:
            upcoming = products(i + 1)
        past = i * size
        spans = [slice(past, past + size)] + ([slice(0, past)] if i else [])
        for p in range(pair):
            query = q_ref[heads[p], pl.ds(at[i], size)]
            grad = grad_ref[heads[p], pl.ds(at[i], size)]
            log_total = log_ref[p, :, pl.ds(at[i], size)]
            scores, grads = current[p]
            probs = [jnp.exp(part - log_total) for part in scores]
            probs[0] = jnp.where(seen, probs[0], 0.0)
            delta = jnp.zeros((1, size), jnp.float32)
            for prob, grad_prob in zip(probs, grads):
                delta = delta + jnp.sum(prob * grad_prob, axis=0, keepdims=True)
            grad_query = jnp.zeros(query.shape, jnp.float32)
            for cols, prob, grad_prob in zip(spans, probs, grads):
                grad_score = (prob * (grad_prob - delta)).astype(jnp.bfloat16)
                value_sum[p][:, cols] += dot(grad, prob.astype(jnp.bfloat16), 1, 1)
                key_sum[p][:, cols] += dot(query, grad_score, 1, 1)
                grad_query = grad_query + dot(key_cols[p][:, cols], grad_score, 1, 0)
            terms[p] = terms[p] + jnp.sum(
                grad_query * query.astype(jnp.float32), axis=1, keepdims=True
            )
            out_ref[0, heads[p], pl.ds(at[i], size)] = (grad_query * scale_ref[...]).astype(
                jnp.bfloat16
            )
    for i in range(blocks):
        here = slice(i * size, (i + 1) * size)
        for p in range(pair):
            out_ref[1, heads[p], pl.ds(at[i], size)] = key_sum[p][:, here].astype(jnp.bfloat16)
            out_ref[2, heads[p], pl.ds(at[i], size)] = value_sum[p][:, here].astype(jnp.bfloat16)
    for p in range(pair):
        term_ref[p] = terms[p]


def attend_back(
    projected, grad_attended, log_total, multiplier, order, heads, head_dim, events=()
):
    tokens = projected.shape[1]
    blocks = order.shape[0]
    pair = 2
    rows = pair * head_dim

    def part(first):
        return pl.BlockSpec((rows, tokens), lambda h, order, first=first: (first // pair + h, 0))

    return pl.pallas_call(
        functools.partial(attend_back_kernel, blocks, pair),
        out_shape=[
            jax.ShapeDtypeStruct((3, heads * head_dim, tokens), jnp.bfloat16),
            jax.ShapeDtypeStruct((heads, head_dim, 1), jnp.float32),
        ],
        grid_spec=pltpu.PrefetchScalarGridSpec(
            num_scalar_prefetch=1,
            grid=(heads // pair,),
            in_specs=[
                part(0),
                part(heads),
                part(2 * heads),
                part(0),
                pl.BlockSpec((pair, 1, tokens), lambda h, order: (h, 0, 0)),
                pl.BlockSpec((head_dim, 1), lambda h, order: (0, 0)),
            ]
            + [pl.BlockSpec(memory_space=pltpu.HBM)] * len(events),
            out_specs=[
                pl.BlockSpec((3, rows, tokens), lambda h, order: (0, h, 0)),
                pl.BlockSpec((pair, head_dim, 1), lambda h, order: (h, 0, 0)),
            ],
            scratch_shapes=[pltpu.VMEM((tokens, head_dim), jnp.bfloat16)] * pair
            + [pltpu.VMEM((head_dim, tokens), jnp.bfloat16)] * pair
            + [pltpu.VMEM((tokens, head_dim), jnp.bfloat16)] * pair
            + [pltpu.VMEM((head_dim, tokens), jnp.float32)] * (2 * pair),
        ),
        compiler_params=pltpu.CompilerParams(vmem_limit_bytes=56 * 1024 * 1024),
        cost_estimate=pl.CostEstimate(
            flops=heads * tokens * tokens * head_dim * 10,
            bytes_accessed=heads * head_dim * tokens * 14,
            transcendentals=heads * tokens * tokens,
        ),
        name="attend_back",
    )(order, projected, projected, projected, grad_attended, log_total, multiplier, *events)


def paired_layer(
    inputs,
    targets,
    valid_counts,
    owners,
    master,
    first_moment,
    second_moment,
    norm_gains,
    gain_first,
    gain_second,
    query_scale,
    scale_first,
    scale_second,
):
    bf16 = jnp.bfloat16
    f32 = jnp.float32
    seq_local, block_rows, width = inputs.shape
    slot_count, head_dim, column_count = master.shape
    ff_blocks = FF // head_dim
    owner_count = lax.axis_size("fsdp")
    device = lax.axis_index("ctx")
    chip, core = device // 2, device % 2
    owner_here = lax.axis_index("fsdp")
    low_here = owner_here % 2
    high_here = owner_here // 2
    high_count = owner_count // 2
    high_distances = range(1, high_count)
    half_width = width // 2
    half_slots = slot_count // 2
    half_rows = seq_local * block_rows
    half_heads = H // 2
    half_blocks = ff_blocks // 2
    set_units = 4 * half_heads + 2 * half_blocks
    first_chip, first_core = chip == 0, core == 0

    def columns_here(array):
        return jnp.where(first_chip, array, jnp.roll(array, half_width, axis=-1))

    def sequence_rows(array):
        own = jnp.where(first_chip, array[0], array[1])
        got = swapped(jnp.where(first_chip, array[1], array[0]), "ctx", 2)
        return jnp.where(
            first_chip, jnp.concatenate([own, got]), jnp.concatenate([got, own])
        )

    def rows_apart(array):
        array = columns_here(array)
        first, last = array[:block_rows], array[block_rows:]
        other = jnp.where(first_chip, last, first).astype(bf16)
        return (jnp.where(first_chip, first, last), swapped(other, "ctx", 2))

    def rows_home(own, got):
        got = got.astype(f32)
        return jnp.where(first_chip, jnp.stack([own, got]), jnp.stack([got, own]))

    slot_rows = unit_rows(owners, slot_count)
    unit_total = owners.shape[0]
    kind_sizes = [H, H, H, H, ff_blocks, ff_blocks]
    kind_starts = [sum(kind_sizes[:i]) for i in range(6)]

    def unit_list(kinds, which):
        return jnp.concatenate(
            [
                kind_starts[k] + which * (kind_sizes[k] // 2) + jnp.arange(kind_sizes[k] // 2)
                for k in kinds
            ]
        ).astype(jnp.int32)

    wanted = jnp.concatenate(
        [unit_list(range(6), core), unit_list((4, 5), 1 - core)]
    )
    wanted_rows = slot_rows[wanted]
    wanted_owner, wanted_slot = wanted_rows // slot_count, wanted_rows % slot_count
    weight_from = 2 * (wanted_slot // half_slots != core) + (wanted_owner % 2 != low_here)
    weight_from = weight_from.astype(jnp.int32)
    weight_row = ((wanted_owner // 2) ^ high_here) * half_slots + wanted_slot % half_slots
    weight_plan = copy_plan(weight_from, weight_row, 4)
    weight_sizes = [3 * half_heads, half_heads + 2 * half_blocks, 2 * half_blocks]

    chunks = [(0, 256), (256, 256)]
    lead = 512
    tail = half_width - lead
    shard = master.astype(bf16)
    own_half = jnp.where(first_core, shard[:half_slots], shard[half_slots:])
    got_half = swapped(jnp.where(first_core, shard[half_slots:], shard[:half_slots]), "ctx", 1)
    shard = jnp.where(
        first_core,
        jnp.concatenate([own_half, got_half], axis=2),
        jnp.concatenate([got_half, own_half], axis=2),
    )
    shard, inputs, targets = lax.optimization_barrier((shard, inputs, targets))
    values_b = columns_here(sequence_rows(inputs))
    targets_b = columns_here(sequence_rows(targets))
    shard_last = shard[:, :, lead:]
    shards = [shard[:, :, start : start + size] for start, size in chunks]
    shards.append(jnp.concatenate([shard_last, swapped(shard_last, "ctx", 2)], axis=2))
    highs = []
    for number, part in enumerate(shards):
        if number:
            part, highs[-1] = lax.optimization_barrier((part, highs[-1]))
        highs.append(
            jnp.concatenate([part] + [swapped(part, "fsdp", 2 * d) for d in high_distances])
        )
    lows = [swapped(high, "fsdp", 1) for high in highs]
    own_units, rest_units, far_units = weight_sizes
    near_units = own_units + rest_units

    def pick_units(number, sizes, events):
        high, low = highs[number], lows[number]
        sources = [high, low, swapped(high, "ctx", 1), swapped(low, "ctx", 1)]
        return copy_rows(sources, [0] * 4, high.shape[2], weight_plan, sizes, events)

    lows[0], highs[1] = lax.optimization_barrier((lows[0], highs[1]))
    near_one, far_one = pick_units(
        0, [near_units, far_units], [shards[2], values_b, targets_b]
    )
    got_one = swapped(near_one, "ctx", 2)
    lows[1], far_one, highs[2] = lax.optimization_barrier((lows[1], far_one, highs[2]))
    qkv_two, rest_two, far_two = pick_units(1, weight_sizes, [got_one])
    qkv_got = swapped(qkv_two, "ctx", 2)
    rest_two, qkv_got = lax.optimization_barrier((rest_two, qkv_got))
    rest_got = swapped(rest_two, "ctx", 2)
    lows[2], far_two, got_one = lax.optimization_barrier((lows[2], far_two, got_one))
    qkv_last, rest_last, far_last = pick_units(2, weight_sizes, [])

    def columns_of(owns, gots, last):
        pieces = [(last, 0, tail, lead), (last, tail, tail, half_width + lead)]
        for (start, size), own, got in zip(chunks, owns, gots):
            pieces += [(own, 0, size, start), (got, 0, size, half_width + start)]
        return pieces

    def placed(pieces, from_end, count, out, row):
        return [
            (piece.shape[0] - from_end if from_end else 0, count, *columns, out, row)
            for piece, *columns in pieces
        ]

    qkv_pieces = columns_of([near_one, qkv_two], [got_one, qkv_got], qkv_last)
    rest_pieces = columns_of([near_one, rest_two], [got_one, rest_got], rest_last)
    far_pieces = columns_of(
        [far_one, far_two], [swapped(got, "ctx", 1) for got in (got_one, rest_got)], far_last
    )
    (w_qkv,) = place_pieces(
        [piece for piece, *_ in qkv_pieces],
        placed(qkv_pieces, 0, own_units, 0, 0),
        [(own_units, head_dim, width)],
    )
    w_qkv = w_qkv.reshape(-1, width)

    gains = columns_here(norm_gains)
    values_in = values_b.astype(f32)
    normed_own = (values_in * inverse_rms(values_in) * gains[0]).astype(bf16)
    normed_b = jnp.concatenate([normed_own, swapped(normed_own, "ctx", 1)])
    base = score_base / math.sqrt(head_dim)
    multiplier = jax.nn.softplus(query_scale) * base
    row_scale = jnp.concatenate(
        [jnp.tile(multiplier, half_heads), jnp.ones((2 * half_heads * head_dim,), f32)]
    )
    projected = (dot(w_qkv, normed_b, 1, 1) * row_scale[:, None]).astype(bf16)
    positions = jnp.arange(4, dtype=jnp.int32)
    order = jnp.where(positions % 2 == core, 0, 2) + positions // 2
    order = order.astype(jnp.int32)
    attended, log_total = attend(projected, order, half_heads, head_dim)
    count = summed(jnp.sum(valid_counts)[None], "fsdp")
    (w_out,) = place_pieces(
        [piece for piece, *_ in rest_pieces],
        placed(rest_pieces, rest_units, half_heads, 0, 0),
        [(half_heads, head_dim, width)],
        [log_total, count],
    )
    mlp_pieces, mlp_places = [], []
    for row, pieces in ((0, rest_pieces), (half_blocks, far_pieces)):
        for kind in range(2):
            mlp_pieces += [piece for piece, *_ in pieces]
            mlp_places += placed(pieces, (2 - kind) * half_blocks, half_blocks, kind, row)
    w_up, w_down = place_pieces(
        mlp_pieces, mlp_places, [(ff_blocks, head_dim, width)] * 2, [log_total]
    )
    w_out = w_out.reshape(-1, width)
    w_up = w_up.reshape(-1, width)
    w_down = w_down.reshape(-1, width)
    branch_far = dot(attended[:, half_rows:], w_out, 0, 0).astype(bf16)
    branch_got = swapped(branch_far, "ctx", 1)
    branch_own = dot(attended[:, :half_rows], w_out, 0, 0)
    middle = values_in + (branch_own + branch_got.astype(f32))
    normed_mid_b = (middle * inverse_rms(middle) * gains[1]).astype(bf16)
    hidden = dot(normed_mid_b, w_up, 1, 1)
    active_b = jax.nn.silu(hidden).astype(bf16)
    block_out = middle + dot(active_b, w_down, 1, 0)
    seq_length = 2 * half_rows
    row = jnp.arange(half_rows, dtype=jnp.int32)
    row_pos = (core + 2 * (row // block_rows)) * block_rows + row % block_rows
    valid = jnp.where(first_chip, valid_counts[0], valid_counts[1])
    counted = (row_pos >= seq_length - valid).astype(f32)

    (apart,) = lax.optimization_barrier((block_out,))
    block_own, block_got = rows_apart(apart)

    out_grad = 2.0 * (block_out - targets_b.astype(f32)) * counted[:, None]
    out_grad_b = out_grad.astype(bf16)
    grad_active = dot(out_grad_b, w_down, 1, 1)
    sigma = jax.nn.sigmoid(hidden)
    grad_hidden_b = (grad_active * sigma * (1.0 + hidden * (1.0 - sigma))).astype(bf16)
    grad_normed_mid = dot(grad_hidden_b, w_up, 1, 0)
    inverse = inverse_rms(middle)
    scaled = grad_normed_mid * gains[1]
    grad_middle = out_grad + (
        inverse * scaled
        - middle * inverse**3 * jnp.mean(scaled * middle, axis=-1, keepdims=True)
    )
    grad_gain_two = jnp.sum(grad_normed_mid * middle * inverse, axis=0)
    grad_middle_own = grad_middle.astype(bf16)
    grad_middle_got = swapped(grad_middle_own, "ctx", 1)
    far_blocks = half_blocks * head_dim
    wide = slice(half_width + 256, half_width + lead)
    slim = slice(half_width, half_width + 256)
    block_grads = []
    for left, right in ((grad_hidden_b, normed_mid_b), (active_b, out_grad_b)):
        got = swapped(dot(left[:, far_blocks:], right, 0, 0).astype(bf16), "ctx", 1)
        total = dot(left[:, :far_blocks], right, 0, 0) + got.astype(f32)
        block_grads.append(total.astype(bf16).reshape(half_blocks, head_dim, width))
    block_grads = jnp.concatenate(block_grads)
    grad_middle_got, block_grads = lax.optimization_barrier((grad_middle_got, block_grads))
    grad_middle_b = jnp.concatenate([grad_middle_own, grad_middle_got])
    grad_attended = dot(w_out, grad_middle_b, 1, 1).astype(bf16)
    head_grads = dot(attended, grad_middle_b, 1, 0).astype(bf16)
    head_grads = head_grads.reshape(half_heads, head_dim, width)

    def early_columns(columns):
        return jnp.concatenate([head_grads[:, :, columns], block_grads[:, :, columns]])

    early_wide, early_slim = early_columns(wide), early_columns(slim)
    wide_got = swapped(early_wide, "ctx", 2)

    def last_columns(array):
        return jnp.concatenate(
            [array[..., lead:half_width], array[..., half_width + lead :]], axis=-1
        )

    early_last = jnp.concatenate([last_columns(head_grads), last_columns(block_grads)])
    grad_proj, grad_scale = attend_back(
        projected,
        grad_attended,
        log_total,
        multiplier[:, None],
        order,
        half_heads,
        head_dim,
        [early_wide, early_slim, early_last, block_got],
    )
    grad_proj = grad_proj.reshape(-1, grad_proj.shape[2])
    scale_term = (
        jnp.sum(grad_scale[:, :, 0], axis=0) / multiplier * base * jax.nn.sigmoid(query_scale)
    )

    low_order = jnp.stack([low_here, 1 - low_here])
    table_slots = (
        (2 * (jnp.arange(high_count) ^ high_here)[None, :, None] + low_order[:, None, None])
        * slot_count
        + core * half_slots
        + jnp.arange(half_slots)[None, None, :]
    ).reshape(-1)
    holds = table_slots[:, None] == slot_rows[None, :]
    unit_order = jnp.arange(unit_total, dtype=jnp.int32)
    slot_unit = jnp.sum(jnp.where(holds, unit_order[None, :] + 1, 0), axis=1) - 1
    kind = jnp.where(
        slot_unit < 4 * H, slot_unit // H, 4 + (slot_unit - 4 * H) // ff_blocks
    )
    kind_size = jnp.where(kind < 4, H, ff_blocks)
    within = jnp.where(kind < 4, slot_unit % H, (slot_unit - 4 * H) % ff_blocks)
    other_set = (within // (kind_size // 2) != core).astype(jnp.int32)
    rank = within % (kind_size // 2)
    grad_row = rank + jnp.where(
        kind <= 3, kind * half_heads, 4 * half_heads + (kind - 4) * half_blocks
    )
    empty = slot_unit < 0
    grad_from = jnp.where(empty, 2, other_set).astype(jnp.int32)
    grad_row = jnp.where(empty, 0, grad_row).astype(jnp.int32)
    grad_plan = copy_plan(grad_from, grad_row, 3)
    zero = jnp.zeros((1, head_dim, 256), bf16)

    def pick_table(own, got, offset, size, events=()):
        return copy_rows(
            [own, got, zero],
            [offset, offset, 0],
            size,
            grad_plan,
            [high_count * half_slots] * 2,
            events,
        )

    def table_sums(keep, got):
        sums = []
        for d in range(high_count):
            rows = slice(d * half_slots, (d + 1) * half_slots)
            sums.append((keep[rows].astype(f32) + got[rows].astype(f32)).astype(bf16))
        return sums

    def from_owners(tables):
        return [swapped(tables[d], "fsdp", 2 * d) for d in high_distances]

    def owner_sum(table, got):
        total = table.astype(f32)
        for part in got:
            total = total + part.astype(f32)
        return total.astype(bf16)

    def proj_grad(columns):
        return dot(grad_proj, columns, 1, 0).astype(bf16).reshape(-1, head_dim, columns.shape[1])

    def chip_sum(start, proj_got, early_got):
        near = slice(start, start + 256)
        parts = [
            (proj_grad(normed_b[:, near]), proj_got),
            (head_grads[:, :, near], early_got[:half_heads]),
            (block_grads[:, :, near], early_got[half_heads:]),
        ]
        return jnp.concatenate(
            [(own.astype(f32) + got.astype(f32)).astype(bf16) for own, got in parts]
        )

    proj_last = proj_grad(last_columns(normed_b))
    proj_last, wide_got = lax.optimization_barrier((proj_last, wide_got))
    total_last = jnp.concatenate([proj_last, early_last])
    wide_far = proj_grad(normed_b[:, wide])
    wide_proj = swapped(wide_far, "ctx", 2)
    keep_last, send_last = pick_table(
        total_last, swapped(total_last, "ctx", 1), 0, 256, [wide_far]
    )
    low_last = swapped(send_last, "fsdp", 1)
    keep_last, grad_proj = lax.optimization_barrier((keep_last, grad_proj))
    slim_far = jnp.concatenate([proj_grad(normed_b[:, slim]), early_slim])
    normed_far = dot(grad_proj[:, half_rows:], w_qkv, 0, 0).astype(bf16)
    slim_far, wide_proj = lax.optimization_barrier((slim_far, wide_proj))
    low_last, wide_proj, normed_far = lax.optimization_barrier((low_last, wide_proj, normed_far))
    normed_got = swapped(normed_far, "ctx", 1)
    slim_got = swapped(slim_far, "ctx", 2)
    total = chip_sum(256, wide_proj, wide_got)
    keep_three, send_three = pick_table(total, swapped(total, "ctx", 1), 0, 256, [normed_got])
    low_last, keep_three, grad_proj = lax.optimization_barrier((low_last, keep_three, grad_proj))
    low_three = swapped(send_three, "fsdp", 1)
    tables_last = table_sums(keep_last, low_last)
    high_last = from_owners(tables_last)
    grad_normed_in = dot(grad_proj[:, :half_rows], w_qkv, 0, 0) + normed_got.astype(f32)
    inverse = inverse_rms(values_in)
    scaled = grad_normed_in * gains[0]
    input_grad = grad_middle + (
        inverse * scaled
        - values_in * inverse**3 * jnp.mean(scaled * values_in, axis=-1, keepdims=True)
    )
    grad_gain_one = jnp.sum(grad_normed_in * values_in * inverse, axis=0)
    low_three, high_last, slim_got, input_grad = lax.optimization_barrier(
        (low_three, high_last, slim_got, input_grad)
    )
    total = chip_sum(0, slim_got[: 3 * half_heads], slim_got[3 * half_heads :])
    keep_one, send_one = pick_table(total, swapped(total, "ctx", 1), 0, 256, [low_three])
    keep_one, low_three = lax.optimization_barrier((keep_one, low_three))
    tables_three = table_sums(keep_three, low_three)
    high_three = from_owners(tables_three)

    gain_terms = columns_here(jnp.stack([grad_gain_one, grad_gain_two]))
    small = jnp.concatenate([gain_terms.reshape(-1), scale_term])
    small = jnp.pad(small, (0, -small.shape[0] % 1024))
    keep_one, small = lax.optimization_barrier((keep_one, small))
    tables_one = table_sums(keep_one, swapped(send_one, "fsdp", 1))
    small = summed(small, "ctx")
    input_own, input_got = rows_apart(input_grad)
    tables_one, high_three, high_last, small, input_got = lax.optimization_barrier(
        (tables_one, high_three, high_last, small, input_got)
    )
    high_one = from_owners(tables_one)
    small = small + swapped(small, "fsdp", 1)
    owned_last = owner_sum(tables_last[0], high_last)
    owned_got = swapped(owned_last[:, :, tail:], "ctx", 2)
    high_one, small, owned_got = lax.optimization_barrier((high_one, small, owned_got))

    owned = [
        owner_sum(tables_one[0], high_one),
        owner_sum(tables_three[0], high_three),
        (owned_last[:, :, :tail].astype(f32) + owned_got.astype(f32)).astype(bf16),
    ]
    owned = jnp.concatenate(owned, axis=2).reshape(half_slots, head_dim, 2, column_count)
    kept = jnp.where(first_core, owned[:, :, 0], owned[:, :, 1])
    sent = swapped(jnp.where(first_core, owned[:, :, 1], owned[:, :, 0]), "ctx", 1)
    sent, small = lax.optimization_barrier((sent, small))
    small = small + swapped(small, "fsdp", 2)
    small = small + swapped(small, "fsdp", 4)
    gain_sums = small[: 2 * width].reshape(2, width)
    scale_sums = small[2 * width : 2 * width + head_dim]

    count = count[0].astype(f32)
    slot_sums = jnp.where(
        first_core, jnp.concatenate([kept, sent]), jnp.concatenate([sent, kept])
    ).astype(f32)
    new_master, new_first, new_second = adam_step(
        master, first_moment, second_moment, slot_sums / count, master_rate, decay_rate
    )
    new_gains, new_gain_first, new_gain_second = adam_step(
        norm_gains, gain_first, gain_second, gain_sums / count, gain_rate, 0.0
    )
    new_scale, new_scale_first, new_scale_second = adam_step(
        query_scale, scale_first, scale_second, scale_sums / count, scale_rate, 0.0
    )
    return (
        rows_home(block_own, block_got),
        rows_home(input_own, input_got),
        new_master,
        new_first,
        new_second,
        new_gains,
        new_gain_first,
        new_gain_second,
        new_scale,
        new_scale_first,
        new_scale_second,
    )


def on_device(*arguments):
    paired = (
        lax.axis_size("ctx") == 4
        and lax.axis_size("fsdp") == 8
        and arguments[0].shape[0] == 2
    )
    return (paired_layer if paired else general_layer)(*arguments)


def solution(mesh):
    in_specs = (
        P("fsdp", "ctx", None),
        P("fsdp", "ctx", None),
        P("fsdp"),
        P(),
        P("fsdp", None, "ctx"),
        P("fsdp", None, "ctx"),
        P("fsdp", None, "ctx"),
        P(),
        P(),
        P(),
        P(),
        P(),
        P(),
    )
    out_specs = (
        P("fsdp", "ctx", None),
        P("fsdp", "ctx", None),
        P("fsdp", None, "ctx"),
        P("fsdp", None, "ctx"),
        P("fsdp", None, "ctx"),
        P(),
        P(),
        P(),
        P(),
        P(),
        P(),
    )
    return jax.shard_map(
        on_device, mesh=mesh, in_specs=in_specs, out_specs=out_specs, check_vma=False
    )
```

```python
import functools
import math

import jax
import jax.numpy as jnp
from jax import lax
from jax.experimental import pallas as pl
from jax.experimental.pallas import tpu as pltpu
from jax.sharding import PartitionSpec as P

H = 16
FF = 1280
STEP = 10


norm_eps = 1e-06
beta_first = 0.9
beta_second = 0.95
adam_eps = 1e-08
decay_rate = 0.1
master_rate = 0.05
gain_rate = 2.0
scale_rate = 2.0
score_base = 1.442695041
masked_score = -1e30


def from_behind(block, axis, distance):
    devices = range(lax.axis_size(axis))
    route = [(i - distance, i) for i in devices if i - distance in devices]
    return lax.ppermute(block, axis, route)


def shifted(array, axis, by):
    count = lax.axis_size(axis)
    return lax.ppermute(array, axis, [(i, (i + by) % count) for i in range(count)])


def unit_rows(owners, slot_count):
    unit_count = owners.shape[0]
    unit_order = jnp.arange(unit_count, dtype=jnp.int32)
    same_owner = owners[:, None] == owners[None, :]
    earlier = unit_order[None, :] < unit_order[:, None]
    slot_rank = jnp.sum((same_owner & earlier).astype(jnp.int32), axis=1)
    return owners * slot_count + slot_rank


def inverse_rms(values):
    return lax.rsqrt(jnp.mean(values * values, axis=-1, keepdims=True) + norm_eps)


def norm_back(values, gain, grad_normed):
    inverse = inverse_rms(values)
    scaled = grad_normed * gain
    grad_values = inverse * scaled - values * inverse**3 * jnp.mean(
        scaled * values, axis=-1, keepdims=True
    )
    grad_gain = jnp.sum(grad_normed * values * inverse, axis=(0, 1))
    return (grad_values, grad_gain)


def adam_step(values, moment_one, moment_two, gradient, step_rate, weight_decay):
    moment_one = beta_first * moment_one + (1.0 - beta_first) * gradient
    moment_two = beta_second * moment_two + (1.0 - beta_second) * gradient * gradient
    first_hat = moment_one / (1.0 - beta_first**STEP)
    second_hat = moment_two / (1.0 - beta_second**STEP)
    values = values - step_rate * (
        first_hat / (jnp.sqrt(second_hat) + adam_eps) + weight_decay * values
    )
    return (values, moment_one, moment_two)


def general_layer(
    inputs,
    targets,
    valid_counts,
    owners,
    master,
    first_moment,
    second_moment,
    norm_gains,
    gain_first,
    gain_second,
    query_scale,
    scale_first,
    scale_second,
):
    seq_local, block_rows, width = inputs.shape
    slot_count, head_dim, column_count = master.shape
    ff_blocks = FF // head_dim
    ctx_size = lax.axis_size("ctx")
    ctx_index = lax.axis_index("ctx")
    slot_rows = unit_rows(owners, slot_count)
    owner_table = lax.all_gather(master.astype(jnp.bfloat16), "fsdp", axis=0, tiled=True)
    picked = owner_table[slot_rows]
    weights = lax.all_gather(picked, "ctx", axis=2, tiled=True)
    w_qkv = weights[0 : 3 * H]
    w_out = weights[3 * H : 4 * H]
    w_up = weights[4 * H : 4 * H + ff_blocks]
    w_down = weights[4 * H + ff_blocks :]
    values_in = inputs.astype(jnp.float32)
    normed_b = (values_in * inverse_rms(values_in) * norm_gains[0]).astype(jnp.bfloat16)
    projected = jnp.einsum("sbd,hed->shbe", normed_b, w_qkv, preferred_element_type=jnp.float32)
    query_pre = projected[:, 0:H]
    multiplier = jax.nn.softplus(query_scale) * (score_base / math.sqrt(head_dim))
    query_b = (query_pre * multiplier).astype(jnp.bfloat16)
    key_b = projected[:, H : 2 * H].astype(jnp.bfloat16)
    value_b = projected[:, 2 * H : 3 * H].astype(jnp.bfloat16)
    query_rows = ctx_index * block_rows + jnp.arange(block_rows, dtype=jnp.int32)
    last_row = ctx_index * block_rows + block_rows - 1
    start_state = (
        jnp.full(query_pre.shape[:3], masked_score, jnp.float32),
        jnp.zeros(query_pre.shape[:3], jnp.float32),
        jnp.zeros(query_pre.shape, jnp.float32),
    )
    key_part = lax.all_gather(key_b, "ctx", axis=2, tiled=True)
    value_part = lax.all_gather(value_b, "ctx", axis=2, tiled=True)
    key_count = key_part.shape[2]

    def update(current):
        run_max, run_sum, accum = current
        key_rows = jnp.arange(key_count, dtype=jnp.int32)
        allowed = query_rows[:, None] >= key_rows[None, :]
        scores = jnp.einsum(
            "shqe,shke->shqk", query_b, key_part, preferred_element_type=jnp.float32
        )
        scores = jnp.where(allowed, scores, masked_score)
        new_max = jnp.maximum(run_max, jnp.max(scores, axis=-1))
        attn_probs = jnp.where(allowed, jnp.exp(scores - new_max[..., None]), 0.0)
        run_sum = jnp.sum(attn_probs, axis=-1)
        accum = jnp.einsum(
            "shqk,shke->shqe",
            attn_probs.astype(jnp.bfloat16),
            value_part,
            preferred_element_type=jnp.float32,
        )
        return (new_max, run_sum, accum)

    run_max, run_sum, accum = lax.cond(
        jnp.int32(0) <= last_row, update, lambda current: current, start_state
    )
    attended = accum / run_sum[..., None]
    log_total = run_max + jnp.log(run_sum)
    attended_b = attended.astype(jnp.bfloat16)
    branch = jnp.einsum("shbe,hed->sbd", attended_b, w_out, preferred_element_type=jnp.float32)
    middle = values_in + branch
    normed_mid_b = (middle * inverse_rms(middle) * norm_gains[1]).astype(jnp.bfloat16)
    hidden = jnp.einsum("sbd,fed->sbfe", normed_mid_b, w_up, preferred_element_type=jnp.float32)
    active_b = jax.nn.silu(hidden).astype(jnp.bfloat16)
    block_out = middle + jnp.einsum(
        "sbfe,fed->sbd", active_b, w_down, preferred_element_type=jnp.float32
    )
    seq_length = block_rows * ctx_size
    counted = (query_rows[None, :] >= (seq_length - valid_counts)[:, None]).astype(jnp.float32)
    count_term = jnp.sum(counted)
    out_grad = 2.0 * (block_out - targets.astype(jnp.float32)) * counted[..., None]
    out_grad_b = out_grad.astype(jnp.bfloat16)
    grad_down = jnp.einsum(
        "sbfe,sbd->fed", active_b, out_grad_b, preferred_element_type=jnp.float32
    )
    grad_active = jnp.einsum(
        "sbd,fed->sbfe", out_grad_b, w_down, preferred_element_type=jnp.float32
    )
    sigma = jax.nn.sigmoid(hidden)
    grad_hidden_b = (grad_active * sigma * (1.0 + hidden * (1.0 - sigma))).astype(jnp.bfloat16)
    grad_up = jnp.einsum(
        "sbfe,sbd->fed", grad_hidden_b, normed_mid_b, preferred_element_type=jnp.float32
    )
    grad_normed_mid = jnp.einsum(
        "sbfe,fed->sbd", grad_hidden_b, w_up, preferred_element_type=jnp.float32
    )
    grad_middle_norm, grad_gain_two = norm_back(middle, norm_gains[1], grad_normed_mid)
    grad_middle = out_grad + grad_middle_norm
    grad_middle_b = grad_middle.astype(jnp.bfloat16)
    grad_out = jnp.einsum(
        "shbe,sbd->hed", attended_b, grad_middle_b, preferred_element_type=jnp.float32
    )
    grad_attended_b = jnp.einsum(
        "sbd,hed->shbe", grad_middle_b, w_out, preferred_element_type=jnp.float32
    ).astype(jnp.bfloat16)
    delta = jnp.sum(grad_attended_b.astype(jnp.float32) * attended, axis=-1)

    def block_grads(source, key_cur, value_cur, partial_grads):
        grad_key, grad_value, grad_query = partial_grads
        key_rows = source * block_rows + jnp.arange(block_rows, dtype=jnp.int32)
        allowed = query_rows[:, None] >= key_rows[None, :]
        scores = jnp.einsum("shqe,shke->shqk", query_b, key_cur, preferred_element_type=jnp.float32)
        scores = jnp.where(allowed, scores, masked_score)
        attn_probs = jnp.exp(scores - log_total[..., None])
        grad_value = grad_value + jnp.einsum(
            "shqk,shqe->shke",
            attn_probs.astype(jnp.bfloat16),
            grad_attended_b,
            preferred_element_type=jnp.float32,
        )
        grad_probs = jnp.einsum(
            "shqe,shke->shqk", grad_attended_b, value_cur, preferred_element_type=jnp.float32
        )
        grad_scores_b = (attn_probs * (grad_probs - delta[..., None])).astype(jnp.bfloat16)
        grad_query = grad_query + jnp.einsum(
            "shqk,shke->shqe", grad_scores_b, key_cur, preferred_element_type=jnp.float32
        )
        grad_key = grad_key + jnp.einsum(
            "shqk,shqe->shke", grad_scores_b, query_b, preferred_element_type=jnp.float32
        )
        return (grad_key, grad_value, grad_query)

    zero_heads = jnp.zeros(query_pre.shape, jnp.float32)

    def back_turn(which_turn, current):
        key_cur, value_cur, grad_key, grad_value, grad_query = current
        source = (ctx_index - which_turn) % ctx_size
        grad_key, grad_value, grad_query = lax.cond(
            source <= ctx_index,
            lambda parts: block_grads(source, key_cur, value_cur, parts),
            lambda parts: parts,
            (grad_key, grad_value, grad_query),
        )
        key_cur, value_cur = from_behind((key_cur, value_cur), "ctx", 1)
        grad_key, grad_value = (
            shifted(grad_key.astype(jnp.bfloat16), "ctx", 1).astype(grad_key.dtype),
            shifted(grad_value.astype(jnp.bfloat16), "ctx", 1).astype(grad_value.dtype),
        )
        return (key_cur, value_cur, grad_key, grad_value, grad_query)

    back_state = (key_b, value_b, zero_heads, zero_heads, zero_heads)
    back_state = lax.fori_loop(0, ctx_size, back_turn, back_state)
    grad_key, grad_value, grad_query = (back_state[2], back_state[3], back_state[4])
    grad_proj_b = jnp.concatenate([grad_query * multiplier, grad_key, grad_value], axis=1).astype(
        jnp.bfloat16
    )
    grad_qkv = jnp.einsum(
        "shbe,sbd->hed", grad_proj_b, normed_b, preferred_element_type=jnp.float32
    )
    grad_normed_in = jnp.einsum(
        "shbe,hed->sbd", grad_proj_b, w_qkv, preferred_element_type=jnp.float32
    )
    grad_input_norm, grad_gain_one = norm_back(values_in, norm_gains[0], grad_normed_in)
    input_grad = grad_middle + grad_input_norm
    scale_term = (
        jnp.sum(grad_query * query_pre, axis=(0, 1, 2))
        * (score_base / math.sqrt(head_dim))
        * jax.nn.sigmoid(query_scale)
    )
    unit_grads = jnp.concatenate([grad_qkv, grad_out, grad_up, grad_down], axis=0)
    owner_total = lax.axis_size("fsdp") * slot_count
    table_grads = (
        jnp.zeros((owner_total, head_dim, width), jnp.float32).at[slot_rows].set(unit_grads)
    )
    owned = lax.psum_scatter(
        table_grads.astype(jnp.bfloat16), "fsdp", scatter_dimension=0, tiled=True
    )
    slot_sums = lax.psum_scatter(owned, "ctx", scatter_dimension=2, tiled=True).astype(jnp.float32)
    gain_sums, scale_sums, count = lax.psum(
        (jnp.stack([grad_gain_one, grad_gain_two]), scale_term, count_term), ("ctx", "fsdp")
    )
    new_master, new_first, new_second = adam_step(
        master, first_moment, second_moment, slot_sums / count, master_rate, decay_rate
    )
    new_gains, new_gain_first, new_gain_second = adam_step(
        norm_gains, gain_first, gain_second, gain_sums / count, gain_rate, 0.0
    )
    new_scale, new_scale_first, new_scale_second = adam_step(
        query_scale, scale_first, scale_second, scale_sums / count, scale_rate, 0.0
    )
    return (
        block_out,
        input_grad,
        new_master,
        new_first,
        new_second,
        new_gains,
        new_gain_first,
        new_gain_second,
        new_scale,
        new_scale_first,
        new_scale_second,
    )


def swapped(array, axis, distance):
    return lax.ppermute(
        array, axis, [(i, i ^ distance) for i in range(lax.axis_size(axis))]
    )


def summed(array, axis):
    size = lax.axis_size(axis)
    if size & (size - 1):
        return lax.psum(array, axis)
    distance = 1
    while distance < size:
        array = array + swapped(array, axis, distance)
        distance *= 2
    return array


def dot(left, right, left_dim, right_dim):
    return lax.dot_general(
        left,
        right,
        (((left_dim,), (right_dim,)), ((), ())),
        preferred_element_type=jnp.float32,
    )


def copy_rows_kernel(sizes, offsets, width, bound_ref, place_ref, row_ref, *refs):
    sources = refs[: len(offsets)]
    outs = refs[-2 - len(sizes) : -2]
    rows, sems = refs[-2:]
    for number, (source, offset) in enumerate(zip(sources, offsets)):

        @pl.loop(bound_ref[number], bound_ref[number + 1])
        def copy_row(i, source=source, offset=offset):
            pltpu.make_async_copy(
                source.at[row_ref[i], :, pl.ds(offset, width)],
                rows.at[place_ref[i]],
                sems.at[len(sizes)],
            ).start()

    pltpu.make_async_copy(rows, rows, sems.at[len(sizes)]).wait()
    copies, start = [], 0
    for place, (out, size) in enumerate(zip(outs, sizes)):
        copies.append(
            pltpu.make_async_copy(rows.at[pl.ds(start, size)], out, sems.at[place])
        )
        start += size
    for copy in copies:
        copy.start()
    for copy in copies:
        copy.wait()


def copy_plan(pick_from, pick_row, source_count):
    number = jnp.arange(pick_from.shape[0], dtype=jnp.int32)
    before = pick_from[None, :] < pick_from[:, None]
    same = (pick_from[None, :] == pick_from[:, None]) & (number[None, :] < number[:, None])
    rank = jnp.sum((before | same).astype(jnp.int32), axis=1)
    here = rank[None, :] == number[:, None]
    place = jnp.sum(jnp.where(here, number[None, :], 0), axis=1)
    row = jnp.sum(jnp.where(here, pick_row[None, :], 0), axis=1)
    bounds = jnp.sum(
        (pick_from[None, :] < jnp.arange(source_count + 1)[:, None]).astype(jnp.int32), axis=1
    )
    return (bounds.astype(jnp.int32), place.astype(jnp.int32), row.astype(jnp.int32))


def copy_rows(sources, offsets, width, plan, sizes, events=()):
    rows = sources[0].shape[1]
    total = sum(sizes)
    return pl.pallas_call(
        functools.partial(copy_rows_kernel, tuple(sizes), tuple(offsets), width),
        out_shape=[jax.ShapeDtypeStruct((size, rows, width), sources[0].dtype) for size in sizes],
        grid_spec=pltpu.PrefetchScalarGridSpec(
            num_scalar_prefetch=3,
            grid=(1,),
            in_specs=[pl.BlockSpec(memory_space=pltpu.HBM)] * (len(sources) + len(events)),
            out_specs=[pl.BlockSpec(memory_space=pltpu.HBM)] * len(sizes),
            scratch_shapes=[
                pltpu.VMEM((total, rows, width), sources[0].dtype),
                pltpu.SemaphoreType.DMA((len(sizes) + 1,)),
            ],
        ),
        compiler_params=pltpu.CompilerParams(vmem_limit_bytes=40 * 1024 * 1024),
        cost_estimate=pl.CostEstimate(flops=0, bytes_accessed=1024, transcendentals=0),
        name="copy_rows",
    )(*plan, *sources, *events)


def place_pieces_kernel(places, count_outs, *refs):
    pieces = refs[: len(places)]
    outs = refs[-1 - count_outs : -1]
    sems = refs[-1]
    copies = []
    for number, (piece, place) in enumerate(zip(pieces, places)):
        first, count, begin, size, column, out, row = place
        copies.append(
            pltpu.make_async_copy(
                piece.at[pl.ds(first, count), :, pl.ds(begin, size)],
                outs[out].at[pl.ds(row, count), :, pl.ds(column, size)],
                sems.at[number],
            )
        )
    for copy in copies:
        copy.start()
    for copy in copies:
        copy.wait()


def place_pieces(pieces, places, shapes, events=()):
    return pl.pallas_call(
        functools.partial(place_pieces_kernel, tuple(places), len(shapes)),
        out_shape=[jax.ShapeDtypeStruct(shape, pieces[0].dtype) for shape in shapes],
        in_specs=[pl.BlockSpec(memory_space=pltpu.HBM)] * (len(pieces) + len(events)),
        out_specs=[pl.BlockSpec(memory_space=pltpu.VMEM)] * len(shapes),
        scratch_shapes=[pltpu.SemaphoreType.DMA((len(pieces),))],
        compiler_params=pltpu.CompilerParams(vmem_limit_bytes=40 * 1024 * 1024),
        cost_estimate=pl.CostEstimate(flops=0, bytes_accessed=1024, transcendentals=0),
        name="place_pieces",
    )(*pieces, *events)


def scores_of(blocks, key_rows, query, i):
    size = query.shape[1]
    parts = [(i * size, size)] + ([(0, i * size)] if i else [])
    return [dot(key_rows[first : first + count, :], query, 1, 0) for first, count in parts]


def attend_kernel(blocks, pair, order_ref, q_ref, k_ref, v_ref, out_ref, log_ref, *refs):
    key_rows, value_cols = refs[:pair], refs[pair:]
    head_dim = q_ref.shape[0] // pair
    size = q_ref.shape[1] // blocks
    at = [pl.multiple_of(order_ref[i] * size, size) for i in range(blocks)]
    heads = [slice(p * head_dim, (p + 1) * head_dim) for p in range(pair)]
    for i in range(blocks):
        here = slice(i * size, (i + 1) * size)
        for p in range(pair):
            key_rows[p][here, :] = k_ref[heads[p], pl.ds(at[i], size)].T
            value_cols[p][:, here] = v_ref[heads[p], pl.ds(at[i], size)]
    key_pos = lax.broadcasted_iota(jnp.int32, (size, size), 0)
    query_pos = lax.broadcasted_iota(jnp.int32, (size, size), 1)
    seen = key_pos <= query_pos

    def scores(i):
        return [
            scores_of(blocks, key_rows[p], q_ref[heads[p], pl.ds(at[i], size)], i)
            for p in range(pair)
        ]

    upcoming = scores(0)
    for i in range(blocks):
        current = upcoming
        if i + 1 < blocks:
            upcoming = scores(i + 1)
        past = i * size
        for p in range(pair):
            near, *far = current[p]
            near = jnp.where(seen, near, masked_score)
            top = jnp.max(near, axis=0, keepdims=True)
            for part in far:
                top = jnp.maximum(top, jnp.max(part, axis=0, keepdims=True))
            near = jnp.exp(near - top)
            total = jnp.sum(near, axis=0, keepdims=True)
            value = dot(
                value_cols[p][:, past : past + size], near.astype(jnp.bfloat16), 1, 0
            )
            for part in far:
                part = jnp.exp(part - top)
                total = total + jnp.sum(part, axis=0, keepdims=True)
                value = value + dot(value_cols[p][:, :past], part.astype(jnp.bfloat16), 1, 0)
            out_ref[heads[p], pl.ds(at[i], size)] = (value / total).astype(jnp.bfloat16)
            log_ref[p, :, pl.ds(at[i], size)] = top + jnp.log(total)


def attend(projected, order, heads, head_dim):
    tokens = projected.shape[1]
    blocks = order.shape[0]
    pair = 4
    rows = pair * head_dim

    def part(first):
        return pl.BlockSpec((rows, tokens), lambda h, order, first=first: (first // pair + h, 0))

    return pl.pallas_call(
        functools.partial(attend_kernel, blocks, pair),
        out_shape=[
            jax.ShapeDtypeStruct((heads * head_dim, tokens), jnp.bfloat16),
            jax.ShapeDtypeStruct((heads, 1, tokens), jnp.float32),
        ],
        grid_spec=pltpu.PrefetchScalarGridSpec(
            num_scalar_prefetch=1,
            grid=(heads // pair,),
            in_specs=[part(0), part(heads), part(2 * heads)],
            out_specs=[
                pl.BlockSpec((rows, tokens), lambda h, order: (h, 0)),
                pl.BlockSpec((pair, 1, tokens), lambda h, order: (h, 0, 0)),
            ],
            scratch_shapes=[pltpu.VMEM((tokens, head_dim), jnp.bfloat16)] * pair
            + [pltpu.VMEM((head_dim, tokens), jnp.bfloat16)] * pair,
        ),
        compiler_params=pltpu.CompilerParams(vmem_limit_bytes=48 * 1024 * 1024),
        cost_estimate=pl.CostEstimate(
            flops=heads * tokens * tokens * head_dim * 4,
            bytes_accessed=heads * head_dim * tokens * 8,
            transcendentals=heads * tokens * tokens,
        ),
        name="attend",
    )(order, projected, projected, projected)


def attend_back_kernel(
    blocks,
    pair,
    order_ref,
    q_ref,
    k_ref,
    v_ref,
    grad_ref,
    log_ref,
    scale_ref,
    *refs,
):
    scratch = refs[-5 * pair :]
    out_ref, term_ref = refs[-5 * pair - 2 : -5 * pair]
    key_rows, key_cols, value_rows, key_sum, value_sum = (
        scratch[n * pair : (n + 1) * pair] for n in range(5)
    )
    head_dim = q_ref.shape[0] // pair
    size = q_ref.shape[1] // blocks
    at = [pl.multiple_of(order_ref[i] * size, size) for i in range(blocks)]
    heads = [slice(p * head_dim, (p + 1) * head_dim) for p in range(pair)]
    for i in range(blocks):
        here = slice(i * size, (i + 1) * size)
        for p in range(pair):
            key = k_ref[heads[p], pl.ds(at[i], size)]
            key_rows[p][here, :] = key.T
            key_cols[p][:, here] = key
            value_rows[p][here, :] = v_ref[heads[p], pl.ds(at[i], size)].T
    for p in range(pair):
        key_sum[p][...] = jnp.zeros_like(key_sum[p])
        value_sum[p][...] = jnp.zeros_like(value_sum[p])
    key_pos = lax.broadcasted_iota(jnp.int32, (size, size), 0)
    query_pos = lax.broadcasted_iota(jnp.int32, (size, size), 1)
    seen = key_pos <= query_pos
    terms = [jnp.zeros((head_dim, 1), jnp.float32) for _ in range(pair)]

    def products(i):
        return [
            (
                scores_of(blocks, key_rows[p], q_ref[heads[p], pl.ds(at[i], size)], i),
                scores_of(blocks, value_rows[p], grad_ref[heads[p], pl.ds(at[i], size)], i),
            )
            for p in range(pair)
        ]

    upcoming = products(0)
    for i in range(blocks):
        current = upcoming
        if i + 1 < blocks:
            upcoming = products(i + 1)
        past = i * size
        spans = [slice(past, past + size)] + ([slice(0, past)] if i else [])
        for p in range(pair):
            query = q_ref[heads[p], pl.ds(at[i], size)]
            grad = grad_ref[heads[p], pl.ds(at[i], size)]
            log_total = log_ref[p, :, pl.ds(at[i], size)]
            scores, grads = current[p]
            probs = [jnp.exp(part - log_total) for part in scores]
            probs[0] = jnp.where(seen, probs[0], 0.0)
            delta = jnp.zeros((1, size), jnp.float32)
            for prob, grad_prob in zip(probs, grads):
                delta = delta + jnp.sum(prob * grad_prob, axis=0, keepdims=True)
            grad_query = jnp.zeros(query.shape, jnp.float32)
            for cols, prob, grad_prob in zip(spans, probs, grads):
                grad_score = (prob * (grad_prob - delta)).astype(jnp.bfloat16)
                value_sum[p][:, cols] += dot(grad, prob.astype(jnp.bfloat16), 1, 1)
                key_sum[p][:, cols] += dot(query, grad_score, 1, 1)
                grad_query = grad_query + dot(key_cols[p][:, cols], grad_score, 1, 0)
            terms[p] = terms[p] + jnp.sum(
                grad_query * query.astype(jnp.float32), axis=1, keepdims=True
            )
            out_ref[0, heads[p], pl.ds(at[i], size)] = (grad_query * scale_ref[...]).astype(
                jnp.bfloat16
            )
    for i in range(blocks):
        here = slice(i * size, (i + 1) * size)
        for p in range(pair):
            out_ref[1, heads[p], pl.ds(at[i], size)] = key_sum[p][:, here].astype(jnp.bfloat16)
            out_ref[2, heads[p], pl.ds(at[i], size)] = value_sum[p][:, here].astype(jnp.bfloat16)
    for p in range(pair):
        term_ref[p] = terms[p]


def attend_back(
    projected, grad_attended, log_total, multiplier, order, heads, head_dim, events=()
):
    tokens = projected.shape[1]
    blocks = order.shape[0]
    pair = 2
    rows = pair * head_dim

    def part(first):
        return pl.BlockSpec((rows, tokens), lambda h, order, first=first: (first // pair + h, 0))

    return pl.pallas_call(
        functools.partial(attend_back_kernel, blocks, pair),
        out_shape=[
            jax.ShapeDtypeStruct((3, heads * head_dim, tokens), jnp.bfloat16),
            jax.ShapeDtypeStruct((heads, head_dim, 1), jnp.float32),
        ],
        grid_spec=pltpu.PrefetchScalarGridSpec(
            num_scalar_prefetch=1,
            grid=(heads // pair,),
            in_specs=[
                part(0),
                part(heads),
                part(2 * heads),
                part(0),
                pl.BlockSpec((pair, 1, tokens), lambda h, order: (h, 0, 0)),
                pl.BlockSpec((head_dim, 1), lambda h, order: (0, 0)),
            ]
            + [pl.BlockSpec(memory_space=pltpu.HBM)] * len(events),
            out_specs=[
                pl.BlockSpec((3, rows, tokens), lambda h, order: (0, h, 0)),
                pl.BlockSpec((pair, head_dim, 1), lambda h, order: (h, 0, 0)),
            ],
            scratch_shapes=[pltpu.VMEM((tokens, head_dim), jnp.bfloat16)] * pair
            + [pltpu.VMEM((head_dim, tokens), jnp.bfloat16)] * pair
            + [pltpu.VMEM((tokens, head_dim), jnp.bfloat16)] * pair
            + [pltpu.VMEM((head_dim, tokens), jnp.float32)] * (2 * pair),
        ),
        compiler_params=pltpu.CompilerParams(vmem_limit_bytes=56 * 1024 * 1024),
        cost_estimate=pl.CostEstimate(
            flops=heads * tokens * tokens * head_dim * 10,
            bytes_accessed=heads * head_dim * tokens * 14,
            transcendentals=heads * tokens * tokens,
        ),
        name="attend_back",
    )(order, projected, projected, projected, grad_attended, log_total, multiplier, *events)


def paired_layer(
    inputs,
    targets,
    valid_counts,
    owners,
    master,
    first_moment,
    second_moment,
    norm_gains,
    gain_first,
    gain_second,
    query_scale,
    scale_first,
    scale_second,
):
    bf16 = jnp.bfloat16
    f32 = jnp.float32
    seq_local, block_rows, width = inputs.shape
    slot_count, head_dim, column_count = master.shape
    ff_blocks = FF // head_dim
    owner_count = lax.axis_size("fsdp")
    device = lax.axis_index("ctx")
    chip, core = device // 2, device % 2
    owner_here = lax.axis_index("fsdp")
    low_here = owner_here % 2
    high_here = owner_here // 2
    high_count = owner_count // 2
    high_distances = range(1, high_count)
    half_width = width // 2
    half_slots = slot_count // 2
    half_rows = seq_local * block_rows
    half_heads = H // 2
    half_blocks = ff_blocks // 2
    set_units = 4 * half_heads + 2 * half_blocks
    first_chip, first_core = chip == 0, core == 0

    def columns_here(array):
        return jnp.where(first_chip, array, jnp.roll(array, half_width, axis=-1))

    def sequence_rows(array):
        own = jnp.where(first_chip, array[0], array[1])
        got = swapped(jnp.where(first_chip, array[1], array[0]), "ctx", 2)
        return jnp.where(
            first_chip, jnp.concatenate([own, got]), jnp.concatenate([got, own])
        )

    def rows_apart(array):
        array = columns_here(array)
        first, last = array[:block_rows], array[block_rows:]
        other = jnp.where(first_chip, last, first).astype(bf16)
        return (jnp.where(first_chip, first, last), swapped(other, "ctx", 2))

    def rows_home(own, got):
        got = got.astype(f32)
        return jnp.where(first_chip, jnp.stack([own, got]), jnp.stack([got, own]))

    slot_rows = unit_rows(owners, slot_count)
    unit_total = owners.shape[0]
    kind_sizes = [H, H, H, H, ff_blocks, ff_blocks]
    kind_starts = [sum(kind_sizes[:i]) for i in range(6)]

    def unit_list(kinds, which):
        return jnp.concatenate(
            [
                kind_starts[k] + which * (kind_sizes[k] // 2) + jnp.arange(kind_sizes[k] // 2)
                for k in kinds
            ]
        ).astype(jnp.int32)

    wanted = jnp.concatenate(
        [unit_list(range(6), core), unit_list((4, 5), 1 - core)]
    )
    wanted_rows = slot_rows[wanted]
    wanted_owner, wanted_slot = wanted_rows // slot_count, wanted_rows % slot_count
    weight_from = 2 * (wanted_slot // half_slots != core) + (wanted_owner % 2 != low_here)
    weight_from = weight_from.astype(jnp.int32)
    weight_row = ((wanted_owner // 2) ^ high_here) * half_slots + wanted_slot % half_slots
    weight_plan = copy_plan(weight_from, weight_row, 4)
    weight_sizes = [3 * half_heads, half_heads + 2 * half_blocks, 2 * half_blocks]

    chunks = [(0, 256), (256, 256)]
    lead = 512
    tail = half_width - lead
    shard = master.astype(bf16)
    own_half = jnp.where(first_core, shard[:half_slots], shard[half_slots:])
    got_half = swapped(jnp.where(first_core, shard[half_slots:], shard[:half_slots]), "ctx", 1)
    shard = jnp.where(
        first_core,
        jnp.concatenate([own_half, got_half], axis=2),
        jnp.concatenate([got_half, own_half], axis=2),
    )
    shard, inputs, targets = lax.optimization_barrier((shard, inputs, targets))
    values_b = columns_here(sequence_rows(inputs))
    targets_b = columns_here(sequence_rows(targets))
    shard_last = shard[:, :, lead:]
    shards = [shard[:, :, start : start + size] for start, size in chunks]
    shards.append(jnp.concatenate([shard_last, swapped(shard_last, "ctx", 2)], axis=2))
    highs = []
    for number, part in enumerate(shards):
        if number:
            part, highs[-1] = lax.optimization_barrier((part, highs[-1]))
        highs.append(
            jnp.concatenate([part] + [swapped(part, "fsdp", 2 * d) for d in high_distances])
        )
    lows = [swapped(high, "fsdp", 1) for high in highs]
    own_units, rest_units, far_units = weight_sizes
    near_units = own_units + rest_units

    def pick_units(number, sizes, events):
        high, low = highs[number], lows[number]
        sources = [high, low, swapped(high, "ctx", 1), swapped(low, "ctx", 1)]
        return copy_rows(sources, [0] * 4, high.shape[2], weight_plan, sizes, events)

    lows[0], highs[1] = lax.optimization_barrier((lows[0], highs[1]))
    near_one, far_one = pick_units(
        0, [near_units, far_units], [shards[2], values_b, targets_b]
    )
    got_one = swapped(near_one, "ctx", 2)
    lows[1], far_one, highs[2] = lax.optimization_barrier((lows[1], far_one, highs[2]))
    qkv_two, rest_two, far_two = pick_units(1, weight_sizes, [got_one])
    qkv_got = swapped(qkv_two, "ctx", 2)
    rest_two, qkv_got = lax.optimization_barrier((rest_two, qkv_got))
    rest_got = swapped(rest_two, "ctx", 2)
    lows[2], far_two, got_one = lax.optimization_barrier((lows[2], far_two, got_one))
    qkv_last, rest_last, far_last = pick_units(2, weight_sizes, [])

    def columns_of(owns, gots, last):
        pieces = [(last, 0, tail, lead), (last, tail, tail, half_width + lead)]
        for (start, size), own, got in zip(chunks, owns, gots):
            pieces += [(own, 0, size, start), (got, 0, size, half_width + start)]
        return pieces

    def placed(pieces, from_end, count, out, row):
        return [
            (piece.shape[0] - from_end if from_end else 0, count, *columns, out, row)
            for piece, *columns in pieces
        ]

    qkv_pieces = columns_of([near_one, qkv_two], [got_one, qkv_got], qkv_last)
    rest_pieces = columns_of([near_one, rest_two], [got_one, rest_got], rest_last)
    far_pieces = columns_of(
        [far_one, far_two], [swapped(got, "ctx", 1) for got in (got_one, rest_got)], far_last
    )
    (w_qkv,) = place_pieces(
        [piece for piece, *_ in qkv_pieces],
        placed(qkv_pieces, 0, own_units, 0, 0),
        [(own_units, head_dim, width)],
    )
    w_qkv = w_qkv.reshape(-1, width)

    gains = columns_here(norm_gains)
    values_in = values_b.astype(f32)
    normed_own = (values_in * inverse_rms(values_in) * gains[0]).astype(bf16)
    normed_b = jnp.concatenate([normed_own, swapped(normed_own, "ctx", 1)])
    base = score_base / math.sqrt(head_dim)
    multiplier = jax.nn.softplus(query_scale) * base
    row_scale = jnp.concatenate(
        [jnp.tile(multiplier, half_heads), jnp.ones((2 * half_heads * head_dim,), f32)]
    )
    projected = (dot(w_qkv, normed_b, 1, 1) * row_scale[:, None]).astype(bf16)
    positions = jnp.arange(4, dtype=jnp.int32)
    order = jnp.where(positions % 2 == core, 0, 2) + positions // 2
    order = order.astype(jnp.int32)
    attended, log_total = attend(projected, order, half_heads, head_dim)
    count = summed(jnp.sum(valid_counts)[None], "fsdp")
    (w_out,) = place_pieces(
        [piece for piece, *_ in rest_pieces],
        placed(rest_pieces, rest_units, half_heads, 0, 0),
        [(half_heads, head_dim, width)],
        [log_total, count],
    )
    mlp_pieces, mlp_places = [], []
    for row, pieces in ((0, rest_pieces), (half_blocks, far_pieces)):
        for kind in range(2):
            mlp_pieces += [piece for piece, *_ in pieces]
            mlp_places += placed(pieces, (2 - kind) * half_blocks, half_blocks, kind, row)
    w_up, w_down = place_pieces(
        mlp_pieces, mlp_places, [(ff_blocks, head_dim, width)] * 2, [log_total]
    )
    w_out = w_out.reshape(-1, width)
    w_up = w_up.reshape(-1, width)
    w_down = w_down.reshape(-1, width)
    branch_far = dot(attended[:, half_rows:], w_out, 0, 0).astype(bf16)
    branch_got = swapped(branch_far, "ctx", 1)
    branch_own = dot(attended[:, :half_rows], w_out, 0, 0)
    middle = values_in + (branch_own + branch_got.astype(f32))
    normed_mid_b = (middle * inverse_rms(middle) * gains[1]).astype(bf16)
    hidden = dot(normed_mid_b, w_up, 1, 1)
    active_b = jax.nn.silu(hidden).astype(bf16)
    block_out = middle + dot(active_b, w_down, 1, 0)
    seq_length = 2 * half_rows
    row = jnp.arange(half_rows, dtype=jnp.int32)
    row_pos = (core + 2 * (row // block_rows)) * block_rows + row % block_rows
    valid = jnp.where(first_chip, valid_counts[0], valid_counts[1])
    counted = (row_pos >= seq_length - valid).astype(f32)

    (apart,) = lax.optimization_barrier((block_out,))
    block_own, block_got = rows_apart(apart)

    out_grad = 2.0 * (block_out - targets_b.astype(f32)) * counted[:, None]
    out_grad_b = out_grad.astype(bf16)
    grad_active = dot(out_grad_b, w_down, 1, 1)
    sigma = jax.nn.sigmoid(hidden)
    grad_hidden_b = (grad_active * sigma * (1.0 + hidden * (1.0 - sigma))).astype(bf16)
    grad_normed_mid = dot(grad_hidden_b, w_up, 1, 0)
    inverse = inverse_rms(middle)
    scaled = grad_normed_mid * gains[1]
    grad_middle = out_grad + (
        inverse * scaled
        - middle * inverse**3 * jnp.mean(scaled * middle, axis=-1, keepdims=True)
    )
    grad_gain_two = jnp.sum(grad_normed_mid * middle * inverse, axis=0)
    grad_middle_own = grad_middle.astype(bf16)
    grad_middle_got = swapped(grad_middle_own, "ctx", 1)
    far_blocks = half_blocks * head_dim
    wide = slice(half_width + 256, half_width + lead)
    slim = slice(half_width, half_width + 256)
    block_grads = []
    for left, right in ((grad_hidden_b, normed_mid_b), (active_b, out_grad_b)):
        got = swapped(dot(left[:, far_blocks:], right, 0, 0).astype(bf16), "ctx", 1)
        total = dot(left[:, :far_blocks], right, 0, 0) + got.astype(f32)
        block_grads.append(total.astype(bf16).reshape(half_blocks, head_dim, width))
    block_grads = jnp.concatenate(block_grads)
    grad_middle_got, block_grads = lax.optimization_barrier((grad_middle_got, block_grads))
    grad_middle_b = jnp.concatenate([grad_middle_own, grad_middle_got])
    grad_attended = dot(w_out, grad_middle_b, 1, 1).astype(bf16)
    head_grads = dot(attended, grad_middle_b, 1, 0).astype(bf16)
    head_grads = head_grads.reshape(half_heads, head_dim, width)

    def early_columns(columns):
        return jnp.concatenate([head_grads[:, :, columns], block_grads[:, :, columns]])

    early_wide, early_slim = early_columns(wide), early_columns(slim)
    wide_got = swapped(early_wide, "ctx", 2)

    def last_columns(array):
        return jnp.concatenate(
            [array[..., lead:half_width], array[..., half_width + lead :]], axis=-1
        )

    early_last = jnp.concatenate([last_columns(head_grads), last_columns(block_grads)])
    grad_proj, grad_scale = attend_back(
        projected,
        grad_attended,
        log_total,
        multiplier[:, None],
        order,
        half_heads,
        head_dim,
        [early_wide, early_slim, early_last, block_got],
    )
    grad_proj = grad_proj.reshape(-1, grad_proj.shape[2])
    scale_term = (
        jnp.sum(grad_scale[:, :, 0], axis=0) / multiplier * base * jax.nn.sigmoid(query_scale)
    )

    low_order = jnp.stack([low_here, 1 - low_here])
    table_slots = (
        (2 * (jnp.arange(high_count) ^ high_here)[None, :, None] + low_order[:, None, None])
        * slot_count
        + core * half_slots
        + jnp.arange(half_slots)[None, None, :]
    ).reshape(-1)
    holds = table_slots[:, None] == slot_rows[None, :]
    unit_order = jnp.arange(unit_total, dtype=jnp.int32)
    slot_unit = jnp.sum(jnp.where(holds, unit_order[None, :] + 1, 0), axis=1) - 1
    kind = jnp.where(
        slot_unit < 4 * H, slot_unit // H, 4 + (slot_unit - 4 * H) // ff_blocks
    )
    kind_size = jnp.where(kind < 4, H, ff_blocks)
    within = jnp.where(kind < 4, slot_unit % H, (slot_unit - 4 * H) % ff_blocks)
    other_set = (within // (kind_size // 2) != core).astype(jnp.int32)
    rank = within % (kind_size // 2)
    early = (kind >= 3).astype(jnp.int32)
    grad_row = rank + jnp.where(
        kind <= 3, kind % 3 * half_heads, half_heads + (kind - 4) * half_blocks
    )
    empty = slot_unit < 0
    grad_from = jnp.where(empty, 4, 2 * early + other_set).astype(jnp.int32)
    grad_row = jnp.where(empty, 0, grad_row).astype(jnp.int32)
    grad_plan = copy_plan(grad_from, grad_row, 5)
    zero = jnp.zeros((1, head_dim, 256), bf16)

    def pick_table(parts, events=()):
        sources = [side for part in parts for side in (part, swapped(part, "ctx", 1))]
        return copy_rows(
            [*sources, zero], [0] * 5, 256, grad_plan, [high_count * half_slots] * 2, events
        )

    def table_sums(keep, got):
        sums = []
        for d in range(high_count):
            rows = slice(d * half_slots, (d + 1) * half_slots)
            sums.append((keep[rows].astype(f32) + got[rows].astype(f32)).astype(bf16))
        return sums

    def from_owners(tables):
        return [swapped(tables[d], "fsdp", 2 * d) for d in high_distances]

    def owner_sum(table, got):
        total = table.astype(f32)
        for part in got:
            total = total + part.astype(f32)
        return total.astype(bf16)

    def proj_grad(columns):
        return dot(grad_proj, columns, 1, 0).astype(bf16).reshape(-1, head_dim, columns.shape[1])

    def chip_sums(start, proj_got, early_got):
        near = slice(start, start + 256)

        def added(own, got):
            return (own.astype(f32) + got.astype(f32)).astype(bf16)

        early = [
            added(head_grads[:, :, near], early_got[:half_heads]),
            added(block_grads[:, :, near], early_got[half_heads:]),
        ]
        return [added(proj_grad(normed_b[:, near]), proj_got), jnp.concatenate(early)]

    proj_last = proj_grad(last_columns(normed_b))
    proj_last, wide_got = lax.optimization_barrier((proj_last, wide_got))
    wide_far = proj_grad(normed_b[:, wide])
    wide_proj = swapped(wide_far, "ctx", 2)
    keep_last, send_last = pick_table([proj_last, early_last], [wide_far])
    low_last = swapped(send_last, "fsdp", 1)
    keep_last, grad_proj = lax.optimization_barrier((keep_last, grad_proj))
    slim_far = jnp.concatenate([proj_grad(normed_b[:, slim]), early_slim])
    normed_far = dot(grad_proj[:, half_rows:], w_qkv, 0, 0).astype(bf16)
    slim_far, wide_proj = lax.optimization_barrier((slim_far, wide_proj))
    low_last, wide_proj, normed_far = lax.optimization_barrier((low_last, wide_proj, normed_far))
    normed_got = swapped(normed_far, "ctx", 1)
    slim_got = swapped(slim_far, "ctx", 2)
    totals = chip_sums(256, wide_proj, wide_got)
    keep_three, send_three = pick_table(totals, [normed_got])
    low_last, keep_three, grad_proj = lax.optimization_barrier((low_last, keep_three, grad_proj))
    low_three = swapped(send_three, "fsdp", 1)
    tables_last = table_sums(keep_last, low_last)
    high_last = from_owners(tables_last)
    grad_normed_in = dot(grad_proj[:, :half_rows], w_qkv, 0, 0) + normed_got.astype(f32)
    inverse = inverse_rms(values_in)
    scaled = grad_normed_in * gains[0]
    input_grad = grad_middle + (
        inverse * scaled
        - values_in * inverse**3 * jnp.mean(scaled * values_in, axis=-1, keepdims=True)
    )
    grad_gain_one = jnp.sum(grad_normed_in * values_in * inverse, axis=0)
    low_three, high_last, slim_got, input_grad = lax.optimization_barrier(
        (low_three, high_last, slim_got, input_grad)
    )
    totals = chip_sums(0, slim_got[: 3 * half_heads], slim_got[3 * half_heads :])
    keep_one, send_one = pick_table(totals, [low_three])
    keep_one, low_three = lax.optimization_barrier((keep_one, low_three))
    tables_three = table_sums(keep_three, low_three)
    high_three = from_owners(tables_three)

    gain_terms = columns_here(jnp.stack([grad_gain_one, grad_gain_two]))
    small = jnp.concatenate([gain_terms.reshape(-1), scale_term])
    small = jnp.pad(small, (0, -small.shape[0] % 1024))
    keep_one, small = lax.optimization_barrier((keep_one, small))
    tables_one = table_sums(keep_one, swapped(send_one, "fsdp", 1))
    small = summed(small, "ctx")
    input_own, input_got = rows_apart(input_grad)
    tables_one, high_three, high_last, small, input_got = lax.optimization_barrier(
        (tables_one, high_three, high_last, small, input_got)
    )
    high_one = from_owners(tables_one)
    small = small + swapped(small, "fsdp", 1)
    owned_last = owner_sum(tables_last[0], high_last)
    owned_got = swapped(owned_last[:, :, tail:], "ctx", 2)
    high_one, small, owned_got = lax.optimization_barrier((high_one, small, owned_got))

    owned = [
        owner_sum(tables_one[0], high_one),
        owner_sum(tables_three[0], high_three),
        (owned_last[:, :, :tail].astype(f32) + owned_got.astype(f32)).astype(bf16),
    ]
    owned = jnp.concatenate(owned, axis=2).reshape(half_slots, head_dim, 2, column_count)
    kept = jnp.where(first_core, owned[:, :, 0], owned[:, :, 1])
    sent = swapped(jnp.where(first_core, owned[:, :, 1], owned[:, :, 0]), "ctx", 1)
    sent, small = lax.optimization_barrier((sent, small))
    small = small + swapped(small, "fsdp", 2)
    small = small + swapped(small, "fsdp", 4)
    gain_sums = small[: 2 * width].reshape(2, width)
    scale_sums = small[2 * width : 2 * width + head_dim]

    count = count[0].astype(f32)
    slot_sums = jnp.where(
        first_core, jnp.concatenate([kept, sent]), jnp.concatenate([sent, kept])
    ).astype(f32)
    new_master, new_first, new_second = adam_step(
        master, first_moment, second_moment, slot_sums / count, master_rate, decay_rate
    )
    new_gains, new_gain_first, new_gain_second = adam_step(
        norm_gains, gain_first, gain_second, gain_sums / count, gain_rate, 0.0
    )
    new_scale, new_scale_first, new_scale_second = adam_step(
        query_scale, scale_first, scale_second, scale_sums / count, scale_rate, 0.0
    )
    return (
        rows_home(block_own, block_got),
        rows_home(input_own, input_got),
        new_master,
        new_first,
        new_second,
        new_gains,
        new_gain_first,
        new_gain_second,
        new_scale,
        new_scale_first,
        new_scale_second,
    )


def on_device(*arguments):
    paired = (
        lax.axis_size("ctx") == 4
        and lax.axis_size("fsdp") == 8
        and arguments[0].shape[0] == 2
    )
    return (paired_layer if paired else general_layer)(*arguments)


def solution(mesh):
    in_specs = (
        P("fsdp", "ctx", None),
        P("fsdp", "ctx", None),
        P("fsdp"),
        P(),
        P("fsdp", None, "ctx"),
        P("fsdp", None, "ctx"),
        P("fsdp", None, "ctx"),
        P(),
        P(),
        P(),
        P(),
        P(),
        P(),
    )
    out_specs = (
        P("fsdp", "ctx", None),
        P("fsdp", "ctx", None),
        P("fsdp", None, "ctx"),
        P("fsdp", None, "ctx"),
        P("fsdp", None, "ctx"),
        P(),
        P(),
        P(),
        P(),
        P(),
        P(),
    )
    return jax.shard_map(
        on_device, mesh=mesh, in_specs=in_specs, out_specs=out_specs, check_vma=False
    )
```

```python
import functools
import math

import jax
import jax.numpy as jnp
from jax import lax
from jax.experimental import pallas as pl
from jax.experimental.pallas import tpu as pltpu
from jax.sharding import PartitionSpec as P

H = 16
FF = 1280
STEP = 10


norm_eps = 1e-06
beta_first = 0.9
beta_second = 0.95
adam_eps = 1e-08
decay_rate = 0.1
master_rate = 0.05
gain_rate = 2.0
scale_rate = 2.0
score_base = 1.442695041
masked_score = -1e30


def from_behind(block, axis, distance):
    devices = range(lax.axis_size(axis))
    route = [(i - distance, i) for i in devices if i - distance in devices]
    return lax.ppermute(block, axis, route)


def shifted(array, axis, by):
    count = lax.axis_size(axis)
    return lax.ppermute(array, axis, [(i, (i + by) % count) for i in range(count)])


def unit_rows(owners, slot_count):
    unit_count = owners.shape[0]
    unit_order = jnp.arange(unit_count, dtype=jnp.int32)
    same_owner = owners[:, None] == owners[None, :]
    earlier = unit_order[None, :] < unit_order[:, None]
    slot_rank = jnp.sum((same_owner & earlier).astype(jnp.int32), axis=1)
    return owners * slot_count + slot_rank


def inverse_rms(values):
    return lax.rsqrt(jnp.mean(values * values, axis=-1, keepdims=True) + norm_eps)


def norm_back(values, gain, grad_normed):
    inverse = inverse_rms(values)
    scaled = grad_normed * gain
    grad_values = inverse * scaled - values * inverse**3 * jnp.mean(
        scaled * values, axis=-1, keepdims=True
    )
    grad_gain = jnp.sum(grad_normed * values * inverse, axis=(0, 1))
    return (grad_values, grad_gain)


def adam_step(values, moment_one, moment_two, gradient, step_rate, weight_decay):
    moment_one = beta_first * moment_one + (1.0 - beta_first) * gradient
    moment_two = beta_second * moment_two + (1.0 - beta_second) * gradient * gradient
    first_hat = moment_one / (1.0 - beta_first**STEP)
    second_hat = moment_two / (1.0 - beta_second**STEP)
    values = values - step_rate * (
        first_hat / (jnp.sqrt(second_hat) + adam_eps) + weight_decay * values
    )
    return (values, moment_one, moment_two)


def general_layer(
    inputs,
    targets,
    valid_counts,
    owners,
    master,
    first_moment,
    second_moment,
    norm_gains,
    gain_first,
    gain_second,
    query_scale,
    scale_first,
    scale_second,
):
    seq_local, block_rows, width = inputs.shape
    slot_count, head_dim, column_count = master.shape
    ff_blocks = FF // head_dim
    ctx_size = lax.axis_size("ctx")
    ctx_index = lax.axis_index("ctx")
    slot_rows = unit_rows(owners, slot_count)
    owner_table = lax.all_gather(master.astype(jnp.bfloat16), "fsdp", axis=0, tiled=True)
    picked = owner_table[slot_rows]
    weights = lax.all_gather(picked, "ctx", axis=2, tiled=True)
    w_qkv = weights[0 : 3 * H]
    w_out = weights[3 * H : 4 * H]
    w_up = weights[4 * H : 4 * H + ff_blocks]
    w_down = weights[4 * H + ff_blocks :]
    values_in = inputs.astype(jnp.float32)
    normed_b = (values_in * inverse_rms(values_in) * norm_gains[0]).astype(jnp.bfloat16)
    projected = jnp.einsum("sbd,hed->shbe", normed_b, w_qkv, preferred_element_type=jnp.float32)
    query_pre = projected[:, 0:H]
    multiplier = jax.nn.softplus(query_scale) * (score_base / math.sqrt(head_dim))
    query_b = (query_pre * multiplier).astype(jnp.bfloat16)
    key_b = projected[:, H : 2 * H].astype(jnp.bfloat16)
    value_b = projected[:, 2 * H : 3 * H].astype(jnp.bfloat16)
    query_rows = ctx_index * block_rows + jnp.arange(block_rows, dtype=jnp.int32)
    last_row = ctx_index * block_rows + block_rows - 1
    start_state = (
        jnp.full(query_pre.shape[:3], masked_score, jnp.float32),
        jnp.zeros(query_pre.shape[:3], jnp.float32),
        jnp.zeros(query_pre.shape, jnp.float32),
    )
    key_part = lax.all_gather(key_b, "ctx", axis=2, tiled=True)
    value_part = lax.all_gather(value_b, "ctx", axis=2, tiled=True)
    key_count = key_part.shape[2]

    def update(current):
        run_max, run_sum, accum = current
        key_rows = jnp.arange(key_count, dtype=jnp.int32)
        allowed = query_rows[:, None] >= key_rows[None, :]
        scores = jnp.einsum(
            "shqe,shke->shqk", query_b, key_part, preferred_element_type=jnp.float32
        )
        scores = jnp.where(allowed, scores, masked_score)
        new_max = jnp.maximum(run_max, jnp.max(scores, axis=-1))
        attn_probs = jnp.where(allowed, jnp.exp(scores - new_max[..., None]), 0.0)
        run_sum = jnp.sum(attn_probs, axis=-1)
        accum = jnp.einsum(
            "shqk,shke->shqe",
            attn_probs.astype(jnp.bfloat16),
            value_part,
            preferred_element_type=jnp.float32,
        )
        return (new_max, run_sum, accum)

    run_max, run_sum, accum = lax.cond(
        jnp.int32(0) <= last_row, update, lambda current: current, start_state
    )
    attended = accum / run_sum[..., None]
    log_total = run_max + jnp.log(run_sum)
    attended_b = attended.astype(jnp.bfloat16)
    branch = jnp.einsum("shbe,hed->sbd", attended_b, w_out, preferred_element_type=jnp.float32)
    middle = values_in + branch
    normed_mid_b = (middle * inverse_rms(middle) * norm_gains[1]).astype(jnp.bfloat16)
    hidden = jnp.einsum("sbd,fed->sbfe", normed_mid_b, w_up, preferred_element_type=jnp.float32)
    active_b = jax.nn.silu(hidden).astype(jnp.bfloat16)
    block_out = middle + jnp.einsum(
        "sbfe,fed->sbd", active_b, w_down, preferred_element_type=jnp.float32
    )
    seq_length = block_rows * ctx_size
    counted = (query_rows[None, :] >= (seq_length - valid_counts)[:, None]).astype(jnp.float32)
    count_term = jnp.sum(counted)
    out_grad = 2.0 * (block_out - targets.astype(jnp.float32)) * counted[..., None]
    out_grad_b = out_grad.astype(jnp.bfloat16)
    grad_down = jnp.einsum(
        "sbfe,sbd->fed", active_b, out_grad_b, preferred_element_type=jnp.float32
    )
    grad_active = jnp.einsum(
        "sbd,fed->sbfe", out_grad_b, w_down, preferred_element_type=jnp.float32
    )
    sigma = jax.nn.sigmoid(hidden)
    grad_hidden_b = (grad_active * sigma * (1.0 + hidden * (1.0 - sigma))).astype(jnp.bfloat16)
    grad_up = jnp.einsum(
        "sbfe,sbd->fed", grad_hidden_b, normed_mid_b, preferred_element_type=jnp.float32
    )
    grad_normed_mid = jnp.einsum(
        "sbfe,fed->sbd", grad_hidden_b, w_up, preferred_element_type=jnp.float32
    )
    grad_middle_norm, grad_gain_two = norm_back(middle, norm_gains[1], grad_normed_mid)
    grad_middle = out_grad + grad_middle_norm
    grad_middle_b = grad_middle.astype(jnp.bfloat16)
    grad_out = jnp.einsum(
        "shbe,sbd->hed", attended_b, grad_middle_b, preferred_element_type=jnp.float32
    )
    grad_attended_b = jnp.einsum(
        "sbd,hed->shbe", grad_middle_b, w_out, preferred_element_type=jnp.float32
    ).astype(jnp.bfloat16)
    delta = jnp.sum(grad_attended_b.astype(jnp.float32) * attended, axis=-1)

    def block_grads(source, key_cur, value_cur, partial_grads):
        grad_key, grad_value, grad_query = partial_grads
        key_rows = source * block_rows + jnp.arange(block_rows, dtype=jnp.int32)
        allowed = query_rows[:, None] >= key_rows[None, :]
        scores = jnp.einsum("shqe,shke->shqk", query_b, key_cur, preferred_element_type=jnp.float32)
        scores = jnp.where(allowed, scores, masked_score)
        attn_probs = jnp.exp(scores - log_total[..., None])
        grad_value = grad_value + jnp.einsum(
            "shqk,shqe->shke",
            attn_probs.astype(jnp.bfloat16),
            grad_attended_b,
            preferred_element_type=jnp.float32,
        )
        grad_probs = jnp.einsum(
            "shqe,shke->shqk", grad_attended_b, value_cur, preferred_element_type=jnp.float32
        )
        grad_scores_b = (attn_probs * (grad_probs - delta[..., None])).astype(jnp.bfloat16)
        grad_query = grad_query + jnp.einsum(
            "shqk,shke->shqe", grad_scores_b, key_cur, preferred_element_type=jnp.float32
        )
        grad_key = grad_key + jnp.einsum(
            "shqk,shqe->shke", grad_scores_b, query_b, preferred_element_type=jnp.float32
        )
        return (grad_key, grad_value, grad_query)

    zero_heads = jnp.zeros(query_pre.shape, jnp.float32)

    def back_turn(which_turn, current):
        key_cur, value_cur, grad_key, grad_value, grad_query = current
        source = (ctx_index - which_turn) % ctx_size
        grad_key, grad_value, grad_query = lax.cond(
            source <= ctx_index,
            lambda parts: block_grads(source, key_cur, value_cur, parts),
            lambda parts: parts,
            (grad_key, grad_value, grad_query),
        )
        key_cur, value_cur = from_behind((key_cur, value_cur), "ctx", 1)
        grad_key, grad_value = (
            shifted(grad_key.astype(jnp.bfloat16), "ctx", 1).astype(grad_key.dtype),
            shifted(grad_value.astype(jnp.bfloat16), "ctx", 1).astype(grad_value.dtype),
        )
        return (key_cur, value_cur, grad_key, grad_value, grad_query)

    back_state = (key_b, value_b, zero_heads, zero_heads, zero_heads)
    back_state = lax.fori_loop(0, ctx_size, back_turn, back_state)
    grad_key, grad_value, grad_query = (back_state[2], back_state[3], back_state[4])
    grad_proj_b = jnp.concatenate([grad_query * multiplier, grad_key, grad_value], axis=1).astype(
        jnp.bfloat16
    )
    grad_qkv = jnp.einsum(
        "shbe,sbd->hed", grad_proj_b, normed_b, preferred_element_type=jnp.float32
    )
    grad_normed_in = jnp.einsum(
        "shbe,hed->sbd", grad_proj_b, w_qkv, preferred_element_type=jnp.float32
    )
    grad_input_norm, grad_gain_one = norm_back(values_in, norm_gains[0], grad_normed_in)
    input_grad = grad_middle + grad_input_norm
    scale_term = (
        jnp.sum(grad_query * query_pre, axis=(0, 1, 2))
        * (score_base / math.sqrt(head_dim))
        * jax.nn.sigmoid(query_scale)
    )
    unit_grads = jnp.concatenate([grad_qkv, grad_out, grad_up, grad_down], axis=0)
    owner_total = lax.axis_size("fsdp") * slot_count
    table_grads = (
        jnp.zeros((owner_total, head_dim, width), jnp.float32).at[slot_rows].set(unit_grads)
    )
    owned = lax.psum_scatter(
        table_grads.astype(jnp.bfloat16), "fsdp", scatter_dimension=0, tiled=True
    )
    slot_sums = lax.psum_scatter(owned, "ctx", scatter_dimension=2, tiled=True).astype(jnp.float32)
    gain_sums, scale_sums, count = lax.psum(
        (jnp.stack([grad_gain_one, grad_gain_two]), scale_term, count_term), ("ctx", "fsdp")
    )
    new_master, new_first, new_second = adam_step(
        master, first_moment, second_moment, slot_sums / count, master_rate, decay_rate
    )
    new_gains, new_gain_first, new_gain_second = adam_step(
        norm_gains, gain_first, gain_second, gain_sums / count, gain_rate, 0.0
    )
    new_scale, new_scale_first, new_scale_second = adam_step(
        query_scale, scale_first, scale_second, scale_sums / count, scale_rate, 0.0
    )
    return (
        block_out,
        input_grad,
        new_master,
        new_first,
        new_second,
        new_gains,
        new_gain_first,
        new_gain_second,
        new_scale,
        new_scale_first,
        new_scale_second,
    )


def swapped(array, axis, distance):
    return lax.ppermute(
        array, axis, [(i, i ^ distance) for i in range(lax.axis_size(axis))]
    )


def summed(array, axis):
    size = lax.axis_size(axis)
    if size & (size - 1):
        return lax.psum(array, axis)
    distance = 1
    while distance < size:
        array = array + swapped(array, axis, distance)
        distance *= 2
    return array


def dot(left, right, left_dim, right_dim):
    return lax.dot_general(
        left,
        right,
        (((left_dim,), (right_dim,)), ((), ())),
        preferred_element_type=jnp.float32,
    )


def copy_rows_kernel(sizes, offsets, width, bound_ref, place_ref, row_ref, *refs):
    sources = refs[: len(offsets)]
    outs = refs[-2 - len(sizes) : -2]
    rows, sems = refs[-2:]
    for number, (source, offset) in enumerate(zip(sources, offsets)):

        @pl.loop(bound_ref[number], bound_ref[number + 1])
        def copy_row(i, source=source, offset=offset):
            pltpu.make_async_copy(
                source.at[row_ref[i], :, pl.ds(offset, width)],
                rows.at[place_ref[i]],
                sems.at[len(sizes)],
            ).start()

    pltpu.make_async_copy(rows, rows, sems.at[len(sizes)]).wait()
    copies, start = [], 0
    for place, (out, size) in enumerate(zip(outs, sizes)):
        copies.append(
            pltpu.make_async_copy(rows.at[pl.ds(start, size)], out, sems.at[place])
        )
        start += size
    for copy in copies:
        copy.start()
    for copy in copies:
        copy.wait()


def copy_plan(pick_from, pick_row, source_count):
    number = jnp.arange(pick_from.shape[0], dtype=jnp.int32)
    before = pick_from[None, :] < pick_from[:, None]
    same = (pick_from[None, :] == pick_from[:, None]) & (number[None, :] < number[:, None])
    rank = jnp.sum((before | same).astype(jnp.int32), axis=1)
    here = rank[None, :] == number[:, None]
    place = jnp.sum(jnp.where(here, number[None, :], 0), axis=1)
    row = jnp.sum(jnp.where(here, pick_row[None, :], 0), axis=1)
    bounds = jnp.sum(
        (pick_from[None, :] < jnp.arange(source_count + 1)[:, None]).astype(jnp.int32), axis=1
    )
    return (bounds.astype(jnp.int32), place.astype(jnp.int32), row.astype(jnp.int32))


def copy_rows(sources, offsets, width, plan, sizes, events=()):
    rows = sources[0].shape[1]
    total = sum(sizes)
    return pl.pallas_call(
        functools.partial(copy_rows_kernel, tuple(sizes), tuple(offsets), width),
        out_shape=[jax.ShapeDtypeStruct((size, rows, width), sources[0].dtype) for size in sizes],
        grid_spec=pltpu.PrefetchScalarGridSpec(
            num_scalar_prefetch=3,
            grid=(1,),
            in_specs=[pl.BlockSpec(memory_space=pltpu.HBM)] * (len(sources) + len(events)),
            out_specs=[pl.BlockSpec(memory_space=pltpu.HBM)] * len(sizes),
            scratch_shapes=[
                pltpu.VMEM((total, rows, width), sources[0].dtype),
                pltpu.SemaphoreType.DMA((len(sizes) + 1,)),
            ],
        ),
        compiler_params=pltpu.CompilerParams(vmem_limit_bytes=40 * 1024 * 1024),
        cost_estimate=pl.CostEstimate(flops=0, bytes_accessed=1024, transcendentals=0),
        name="copy_rows",
    )(*plan, *sources, *events)


def place_pieces_kernel(places, count_outs, *refs):
    pieces = refs[: len(places)]
    outs = refs[-1 - count_outs : -1]
    sems = refs[-1]
    copies = []
    for number, (piece, place) in enumerate(zip(pieces, places)):
        first, count, begin, size, column, out, row = place
        copies.append(
            pltpu.make_async_copy(
                piece.at[pl.ds(first, count), :, pl.ds(begin, size)],
                outs[out].at[pl.ds(row, count), :, pl.ds(column, size)],
                sems.at[number],
            )
        )
    for copy in copies:
        copy.start()
    for copy in copies:
        copy.wait()


def place_pieces(pieces, places, shapes, events=()):
    return pl.pallas_call(
        functools.partial(place_pieces_kernel, tuple(places), len(shapes)),
        out_shape=[jax.ShapeDtypeStruct(shape, pieces[0].dtype) for shape in shapes],
        in_specs=[pl.BlockSpec(memory_space=pltpu.HBM)] * (len(pieces) + len(events)),
        out_specs=[pl.BlockSpec(memory_space=pltpu.VMEM)] * len(shapes),
        scratch_shapes=[pltpu.SemaphoreType.DMA((len(pieces),))],
        compiler_params=pltpu.CompilerParams(vmem_limit_bytes=40 * 1024 * 1024),
        cost_estimate=pl.CostEstimate(flops=0, bytes_accessed=1024, transcendentals=0),
        name="place_pieces",
    )(*pieces, *events)


def scores_of(blocks, key_rows, query, i):
    size = query.shape[1]
    parts = [(i * size, size)] + ([(0, i * size)] if i else [])
    return [dot(key_rows[first : first + count, :], query, 1, 0) for first, count in parts]


def attend_kernel(blocks, pair, order_ref, q_ref, k_ref, v_ref, out_ref, log_ref, *refs):
    key_rows, value_cols = refs[:pair], refs[pair:]
    head_dim = q_ref.shape[0] // pair
    size = q_ref.shape[1] // blocks
    at = [pl.multiple_of(order_ref[i] * size, size) for i in range(blocks)]
    heads = [slice(p * head_dim, (p + 1) * head_dim) for p in range(pair)]
    for i in range(blocks):
        here = slice(i * size, (i + 1) * size)
        for p in range(pair):
            key_rows[p][here, :] = k_ref[heads[p], pl.ds(at[i], size)].T
            value_cols[p][:, here] = v_ref[heads[p], pl.ds(at[i], size)]
    key_pos = lax.broadcasted_iota(jnp.int32, (size, size), 0)
    query_pos = lax.broadcasted_iota(jnp.int32, (size, size), 1)
    seen = key_pos <= query_pos

    def scores(i):
        return [
            scores_of(blocks, key_rows[p], q_ref[heads[p], pl.ds(at[i], size)], i)
            for p in range(pair)
        ]

    upcoming = scores(0)
    for i in range(blocks):
        current = upcoming
        if i + 1 < blocks:
            upcoming = scores(i + 1)
        past = i * size
        for p in range(pair):
            near, *far = current[p]
            near = jnp.where(seen, near, masked_score)
            top = jnp.max(near, axis=0, keepdims=True)
            for part in far:
                top = jnp.maximum(top, jnp.max(part, axis=0, keepdims=True))
            near = jnp.exp(near - top)
            total = jnp.sum(near, axis=0, keepdims=True)
            value = dot(
                value_cols[p][:, past : past + size], near.astype(jnp.bfloat16), 1, 0
            )
            for part in far:
                part = jnp.exp(part - top)
                total = total + jnp.sum(part, axis=0, keepdims=True)
                value = value + dot(value_cols[p][:, :past], part.astype(jnp.bfloat16), 1, 0)
            out_ref[heads[p], pl.ds(at[i], size)] = (value / total).astype(jnp.bfloat16)
            log_ref[p, :, pl.ds(at[i], size)] = top + jnp.log(total)


def attend(projected, order, heads, head_dim):
    tokens = projected.shape[1]
    blocks = order.shape[0]
    pair = 4
    rows = pair * head_dim

    def part(first):
        return pl.BlockSpec((rows, tokens), lambda h, order, first=first: (first // pair + h, 0))

    return pl.pallas_call(
        functools.partial(attend_kernel, blocks, pair),
        out_shape=[
            jax.ShapeDtypeStruct((heads * head_dim, tokens), jnp.bfloat16),
            jax.ShapeDtypeStruct((heads, 1, tokens), jnp.float32),
        ],
        grid_spec=pltpu.PrefetchScalarGridSpec(
            num_scalar_prefetch=1,
            grid=(heads // pair,),
            in_specs=[part(0), part(heads), part(2 * heads)],
            out_specs=[
                pl.BlockSpec((rows, tokens), lambda h, order: (h, 0)),
                pl.BlockSpec((pair, 1, tokens), lambda h, order: (h, 0, 0)),
            ],
            scratch_shapes=[pltpu.VMEM((tokens, head_dim), jnp.bfloat16)] * pair
            + [pltpu.VMEM((head_dim, tokens), jnp.bfloat16)] * pair,
        ),
        compiler_params=pltpu.CompilerParams(vmem_limit_bytes=48 * 1024 * 1024),
        cost_estimate=pl.CostEstimate(
            flops=heads * tokens * tokens * head_dim * 4,
            bytes_accessed=heads * head_dim * tokens * 8,
            transcendentals=heads * tokens * tokens,
        ),
        name="attend",
    )(order, projected, projected, projected)


def attend_back_kernel(
    blocks,
    pair,
    order_ref,
    q_ref,
    k_ref,
    v_ref,
    grad_ref,
    log_ref,
    scale_ref,
    *refs,
):
    scratch = refs[-5 * pair :]
    out_ref, term_ref = refs[-5 * pair - 2 : -5 * pair]
    key_rows, key_cols, value_rows, key_sum, value_sum = (
        scratch[n * pair : (n + 1) * pair] for n in range(5)
    )
    head_dim = q_ref.shape[0] // pair
    size = q_ref.shape[1] // blocks
    at = [pl.multiple_of(order_ref[i] * size, size) for i in range(blocks)]
    heads = [slice(p * head_dim, (p + 1) * head_dim) for p in range(pair)]
    for i in range(blocks):
        here = slice(i * size, (i + 1) * size)
        for p in range(pair):
            key = k_ref[heads[p], pl.ds(at[i], size)]
            key_rows[p][here, :] = key.T
            key_cols[p][:, here] = key
            value_rows[p][here, :] = v_ref[heads[p], pl.ds(at[i], size)].T
    for p in range(pair):
        key_sum[p][...] = jnp.zeros_like(key_sum[p])
        value_sum[p][...] = jnp.zeros_like(value_sum[p])
    key_pos = lax.broadcasted_iota(jnp.int32, (size, size), 0)
    query_pos = lax.broadcasted_iota(jnp.int32, (size, size), 1)
    seen = key_pos <= query_pos
    terms = [jnp.zeros((head_dim, 1), jnp.float32) for _ in range(pair)]

    def products(i):
        return [
            (
                scores_of(blocks, key_rows[p], q_ref[heads[p], pl.ds(at[i], size)], i),
                scores_of(blocks, value_rows[p], grad_ref[heads[p], pl.ds(at[i], size)], i),
            )
            for p in range(pair)
        ]

    upcoming = products(0)
    for i in range(blocks):
        current = upcoming
        if i + 1 < blocks:
            upcoming = products(i + 1)
        past = i * size
        spans = [slice(past, past + size)] + ([slice(0, past)] if i else [])
        for p in range(pair):
            query = q_ref[heads[p], pl.ds(at[i], size)]
            grad = grad_ref[heads[p], pl.ds(at[i], size)]
            log_total = log_ref[p, :, pl.ds(at[i], size)]
            scores, grads = current[p]
            probs = [jnp.exp(part - log_total) for part in scores]
            probs[0] = jnp.where(seen, probs[0], 0.0)
            delta = jnp.zeros((1, size), jnp.float32)
            for prob, grad_prob in zip(probs, grads):
                delta = delta + jnp.sum(prob * grad_prob, axis=0, keepdims=True)
            grad_query = jnp.zeros(query.shape, jnp.float32)
            for cols, prob, grad_prob in zip(spans, probs, grads):
                grad_score = (prob * (grad_prob - delta)).astype(jnp.bfloat16)
                value_sum[p][:, cols] += dot(grad, prob.astype(jnp.bfloat16), 1, 1)
                key_sum[p][:, cols] += dot(query, grad_score, 1, 1)
                grad_query = grad_query + dot(key_cols[p][:, cols], grad_score, 1, 0)
            terms[p] = terms[p] + jnp.sum(
                grad_query * query.astype(jnp.float32), axis=1, keepdims=True
            )
            out_ref[0, heads[p], pl.ds(at[i], size)] = (grad_query * scale_ref[...]).astype(
                jnp.bfloat16
            )
    for i in range(blocks):
        here = slice(i * size, (i + 1) * size)
        for p in range(pair):
            out_ref[1, heads[p], pl.ds(at[i], size)] = key_sum[p][:, here].astype(jnp.bfloat16)
            out_ref[2, heads[p], pl.ds(at[i], size)] = value_sum[p][:, here].astype(jnp.bfloat16)
    for p in range(pair):
        term_ref[p] = terms[p]


def attend_back(
    projected, grad_attended, log_total, multiplier, order, heads, head_dim, events=()
):
    tokens = projected.shape[1]
    blocks = order.shape[0]
    pair = 2
    rows = pair * head_dim

    def part(first):
        return pl.BlockSpec((rows, tokens), lambda h, order, first=first: (first // pair + h, 0))

    return pl.pallas_call(
        functools.partial(attend_back_kernel, blocks, pair),
        out_shape=[
            jax.ShapeDtypeStruct((3, heads * head_dim, tokens), jnp.bfloat16),
            jax.ShapeDtypeStruct((heads, head_dim, 1), jnp.float32),
        ],
        grid_spec=pltpu.PrefetchScalarGridSpec(
            num_scalar_prefetch=1,
            grid=(heads // pair,),
            in_specs=[
                part(0),
                part(heads),
                part(2 * heads),
                part(0),
                pl.BlockSpec((pair, 1, tokens), lambda h, order: (h, 0, 0)),
                pl.BlockSpec((head_dim, 1), lambda h, order: (0, 0)),
            ]
            + [pl.BlockSpec(memory_space=pltpu.HBM)] * len(events),
            out_specs=[
                pl.BlockSpec((3, rows, tokens), lambda h, order: (0, h, 0)),
                pl.BlockSpec((pair, head_dim, 1), lambda h, order: (h, 0, 0)),
            ],
            scratch_shapes=[pltpu.VMEM((tokens, head_dim), jnp.bfloat16)] * pair
            + [pltpu.VMEM((head_dim, tokens), jnp.bfloat16)] * pair
            + [pltpu.VMEM((tokens, head_dim), jnp.bfloat16)] * pair
            + [pltpu.VMEM((head_dim, tokens), jnp.float32)] * (2 * pair),
        ),
        compiler_params=pltpu.CompilerParams(vmem_limit_bytes=56 * 1024 * 1024),
        cost_estimate=pl.CostEstimate(
            flops=heads * tokens * tokens * head_dim * 10,
            bytes_accessed=heads * head_dim * tokens * 14,
            transcendentals=heads * tokens * tokens,
        ),
        name="attend_back",
    )(order, projected, projected, projected, grad_attended, log_total, multiplier, *events)


def paired_layer(
    inputs,
    targets,
    valid_counts,
    owners,
    master,
    first_moment,
    second_moment,
    norm_gains,
    gain_first,
    gain_second,
    query_scale,
    scale_first,
    scale_second,
):
    bf16 = jnp.bfloat16
    f32 = jnp.float32
    seq_local, block_rows, width = inputs.shape
    slot_count, head_dim, column_count = master.shape
    ff_blocks = FF // head_dim
    owner_count = lax.axis_size("fsdp")
    device = lax.axis_index("ctx")
    chip, core = device // 2, device % 2
    owner_here = lax.axis_index("fsdp")
    low_here = owner_here % 2
    high_here = owner_here // 2
    high_count = owner_count // 2
    high_distances = range(1, high_count)
    half_width = width // 2
    half_slots = slot_count // 2
    half_rows = seq_local * block_rows
    half_heads = H // 2
    half_blocks = ff_blocks // 2
    set_units = 4 * half_heads + 2 * half_blocks
    first_chip, first_core = chip == 0, core == 0

    def columns_here(array):
        return jnp.where(first_chip, array, jnp.roll(array, half_width, axis=-1))

    def sequence_rows(array):
        own = jnp.where(first_chip, array[0], array[1])
        got = swapped(jnp.where(first_chip, array[1], array[0]), "ctx", 2)
        return jnp.where(
            first_chip, jnp.concatenate([own, got]), jnp.concatenate([got, own])
        )

    def rows_apart(array):
        array = columns_here(array)
        first, last = array[:block_rows], array[block_rows:]
        other = jnp.where(first_chip, last, first).astype(bf16)
        return (jnp.where(first_chip, first, last), swapped(other, "ctx", 2))

    def rows_home(own, got):
        got = got.astype(f32)
        return jnp.where(first_chip, jnp.stack([own, got]), jnp.stack([got, own]))

    slot_rows = unit_rows(owners, slot_count)
    unit_total = owners.shape[0]
    kind_sizes = [H, H, H, H, ff_blocks, ff_blocks]
    kind_starts = [sum(kind_sizes[:i]) for i in range(6)]

    def unit_list(kinds, which):
        return jnp.concatenate(
            [
                kind_starts[k] + which * (kind_sizes[k] // 2) + jnp.arange(kind_sizes[k] // 2)
                for k in kinds
            ]
        ).astype(jnp.int32)

    wanted = jnp.concatenate(
        [unit_list(range(6), core), unit_list((4, 5), 1 - core)]
    )
    wanted_rows = slot_rows[wanted]
    wanted_owner, wanted_slot = wanted_rows // slot_count, wanted_rows % slot_count
    weight_from = 2 * (wanted_slot // half_slots != core) + (wanted_owner % 2 != low_here)
    weight_from = weight_from.astype(jnp.int32)
    weight_row = ((wanted_owner // 2) ^ high_here) * half_slots + wanted_slot % half_slots
    weight_plan = copy_plan(weight_from, weight_row, 4)
    weight_sizes = [3 * half_heads, half_heads + 2 * half_blocks, 2 * half_blocks]

    chunks = [(0, 256), (256, 256)]
    lead = 512
    tail = half_width - lead
    shard = master.astype(bf16)
    own_half = jnp.where(first_core, shard[:half_slots], shard[half_slots:])
    got_half = swapped(jnp.where(first_core, shard[half_slots:], shard[:half_slots]), "ctx", 1)
    shard = jnp.where(
        first_core,
        jnp.concatenate([own_half, got_half], axis=2),
        jnp.concatenate([got_half, own_half], axis=2),
    )
    shard, inputs, targets = lax.optimization_barrier((shard, inputs, targets))
    values_b = columns_here(sequence_rows(inputs))
    targets_b = columns_here(sequence_rows(targets))
    shard_last = shard[:, :, lead:]
    shards = [shard[:, :, start : start + size] for start, size in chunks]
    shards.append(jnp.concatenate([shard_last, swapped(shard_last, "ctx", 2)], axis=2))
    highs = []
    for number, part in enumerate(shards):
        if number:
            part, highs[-1] = lax.optimization_barrier((part, highs[-1]))
        highs.append(
            jnp.concatenate([part] + [swapped(part, "fsdp", 2 * d) for d in high_distances])
        )
    lows = [swapped(high, "fsdp", 1) for high in highs]
    own_units, rest_units, far_units = weight_sizes
    near_units = own_units + rest_units

    def pick_units(number, sizes, events):
        high, low = highs[number], lows[number]
        sources = [high, low, swapped(high, "ctx", 1), swapped(low, "ctx", 1)]
        return copy_rows(sources, [0] * 4, high.shape[2], weight_plan, sizes, events)

    lows[0], highs[1] = lax.optimization_barrier((lows[0], highs[1]))
    near_one, far_one = pick_units(
        0, [near_units, far_units], [shards[2], values_b, targets_b]
    )
    got_one = swapped(near_one, "ctx", 2)
    lows[1], far_one, highs[2] = lax.optimization_barrier((lows[1], far_one, highs[2]))
    qkv_two, rest_two, far_two = pick_units(1, weight_sizes, [])
    qkv_got = swapped(qkv_two, "ctx", 2)
    rest_two, qkv_got = lax.optimization_barrier((rest_two, qkv_got))
    rest_got = swapped(rest_two, "ctx", 2)
    lows[2], far_two, got_one = lax.optimization_barrier((lows[2], far_two, got_one))
    arrived = swapped(qkv_got[0, :16, :128], "ctx", 1)
    qkv_last, rest_last, far_last = pick_units(2, weight_sizes, [arrived])

    def columns_of(owns, gots, last):
        pieces = [(last, 0, tail, lead), (last, tail, tail, half_width + lead)]
        for (start, size), own, got in zip(chunks, owns, gots):
            pieces += [(own, 0, size, start), (got, 0, size, half_width + start)]
        return pieces

    def placed(pieces, from_end, count, out, row):
        return [
            (piece.shape[0] - from_end if from_end else 0, count, *columns, out, row)
            for piece, *columns in pieces
        ]

    qkv_pieces = columns_of([near_one, qkv_two], [got_one, qkv_got], qkv_last)
    rest_pieces = columns_of([near_one, rest_two], [got_one, rest_got], rest_last)
    far_pieces = columns_of(
        [far_one, far_two], [swapped(got, "ctx", 1) for got in (got_one, rest_got)], far_last
    )
    (w_qkv,) = place_pieces(
        [piece for piece, *_ in qkv_pieces],
        placed(qkv_pieces, 0, own_units, 0, 0),
        [(own_units, head_dim, width)],
    )
    w_qkv = w_qkv.reshape(-1, width)

    gains = columns_here(norm_gains)
    values_in = values_b.astype(f32)
    normed_own = (values_in * inverse_rms(values_in) * gains[0]).astype(bf16)
    normed_b = jnp.concatenate([normed_own, swapped(normed_own, "ctx", 1)])
    base = score_base / math.sqrt(head_dim)
    multiplier = jax.nn.softplus(query_scale) * base
    row_scale = jnp.concatenate(
        [jnp.tile(multiplier, half_heads), jnp.ones((2 * half_heads * head_dim,), f32)]
    )
    projected = (dot(w_qkv, normed_b, 1, 1) * row_scale[:, None]).astype(bf16)
    positions = jnp.arange(4, dtype=jnp.int32)
    order = jnp.where(positions % 2 == core, 0, 2) + positions // 2
    order = order.astype(jnp.int32)
    attended, log_total = attend(projected, order, half_heads, head_dim)
    count = summed(jnp.sum(valid_counts)[None], "fsdp")
    (w_out,) = place_pieces(
        [piece for piece, *_ in rest_pieces],
        placed(rest_pieces, rest_units, half_heads, 0, 0),
        [(half_heads, head_dim, width)],
        [log_total],
    )
    mlp_pieces, mlp_places = [], []
    for row, pieces in ((0, rest_pieces), (half_blocks, far_pieces)):
        for kind in range(2):
            mlp_pieces += [piece for piece, *_ in pieces]
            mlp_places += placed(pieces, (2 - kind) * half_blocks, half_blocks, kind, row)
    w_up, w_down = place_pieces(
        mlp_pieces, mlp_places, [(ff_blocks, head_dim, width)] * 2, [log_total]
    )
    w_out = w_out.reshape(-1, width)
    w_up = w_up.reshape(-1, width)
    w_down = w_down.reshape(-1, width)
    branch_far = dot(attended[:, half_rows:], w_out, 0, 0).astype(bf16)
    branch_got = swapped(branch_far, "ctx", 1)
    branch_own = dot(attended[:, :half_rows], w_out, 0, 0)
    middle = values_in + (branch_own + branch_got.astype(f32))
    normed_mid_b = (middle * inverse_rms(middle) * gains[1]).astype(bf16)
    hidden = dot(normed_mid_b, w_up, 1, 1)
    active_b = jax.nn.silu(hidden).astype(bf16)
    block_out = middle + dot(active_b, w_down, 1, 0)
    seq_length = 2 * half_rows
    row = jnp.arange(half_rows, dtype=jnp.int32)
    row_pos = (core + 2 * (row // block_rows)) * block_rows + row % block_rows
    valid = jnp.where(first_chip, valid_counts[0], valid_counts[1])
    counted = (row_pos >= seq_length - valid).astype(f32)

    (apart,) = lax.optimization_barrier((block_out,))
    block_own, block_got = rows_apart(apart)

    out_grad = 2.0 * (block_out - targets_b.astype(f32)) * counted[:, None]
    out_grad_b = out_grad.astype(bf16)
    grad_active = dot(out_grad_b, w_down, 1, 1)
    sigma = jax.nn.sigmoid(hidden)
    grad_hidden_b = (grad_active * sigma * (1.0 + hidden * (1.0 - sigma))).astype(bf16)
    grad_normed_mid = dot(grad_hidden_b, w_up, 1, 0)
    inverse = inverse_rms(middle)
    scaled = grad_normed_mid * gains[1]
    grad_middle = out_grad + (
        inverse * scaled
        - middle * inverse**3 * jnp.mean(scaled * middle, axis=-1, keepdims=True)
    )
    grad_gain_two = jnp.sum(grad_normed_mid * middle * inverse, axis=0)
    grad_middle_own = grad_middle.astype(bf16)
    grad_middle_got = swapped(grad_middle_own, "ctx", 1)
    far_blocks = half_blocks * head_dim
    wide = slice(half_width + 256, half_width + lead)
    slim = slice(half_width, half_width + 256)
    block_grads = []
    for left, right in ((grad_hidden_b, normed_mid_b), (active_b, out_grad_b)):
        got = swapped(dot(left[:, far_blocks:], right, 0, 0).astype(bf16), "ctx", 1)
        total = dot(left[:, :far_blocks], right, 0, 0) + got.astype(f32)
        block_grads.append(total.astype(bf16).reshape(half_blocks, head_dim, width))
    block_grads = jnp.concatenate(block_grads)
    grad_middle_got, block_grads = lax.optimization_barrier((grad_middle_got, block_grads))
    grad_middle_b = jnp.concatenate([grad_middle_own, grad_middle_got])
    grad_attended = dot(w_out, grad_middle_b, 1, 1).astype(bf16)
    head_grads = dot(attended, grad_middle_b, 1, 0).astype(bf16)
    head_grads = head_grads.reshape(half_heads, head_dim, width)

    def early_columns(columns):
        return jnp.concatenate([head_grads[:, :, columns], block_grads[:, :, columns]])

    early_wide, early_slim = early_columns(wide), early_columns(slim)
    wide_got = swapped(early_wide, "ctx", 2)

    def last_columns(array):
        return jnp.concatenate(
            [array[..., lead:half_width], array[..., half_width + lead :]], axis=-1
        )

    early_last = jnp.concatenate([last_columns(head_grads), last_columns(block_grads)])
    grad_proj, grad_scale = attend_back(
        projected,
        grad_attended,
        log_total,
        multiplier[:, None],
        order,
        half_heads,
        head_dim,
        [early_wide, early_slim, early_last, block_got],
    )
    grad_proj = grad_proj.reshape(-1, grad_proj.shape[2])
    scale_term = (
        jnp.sum(grad_scale[:, :, 0], axis=0) / multiplier * base * jax.nn.sigmoid(query_scale)
    )

    low_order = jnp.stack([low_here, 1 - low_here])
    table_slots = (
        (2 * (jnp.arange(high_count) ^ high_here)[None, :, None] + low_order[:, None, None])
        * slot_count
        + core * half_slots
        + jnp.arange(half_slots)[None, None, :]
    ).reshape(-1)
    holds = table_slots[:, None] == slot_rows[None, :]
    unit_order = jnp.arange(unit_total, dtype=jnp.int32)
    slot_unit = jnp.sum(jnp.where(holds, unit_order[None, :] + 1, 0), axis=1) - 1
    kind = jnp.where(
        slot_unit < 4 * H, slot_unit // H, 4 + (slot_unit - 4 * H) // ff_blocks
    )
    kind_size = jnp.where(kind < 4, H, ff_blocks)
    within = jnp.where(kind < 4, slot_unit % H, (slot_unit - 4 * H) % ff_blocks)
    other_set = (within // (kind_size // 2) != core).astype(jnp.int32)
    rank = within % (kind_size // 2)
    early = (kind >= 3).astype(jnp.int32)
    grad_row = rank + jnp.where(
        kind <= 3, kind % 3 * half_heads, half_heads + (kind - 4) * half_blocks
    )
    empty = slot_unit < 0
    grad_from = jnp.where(empty, 4, 2 * early + other_set).astype(jnp.int32)
    grad_row = jnp.where(empty, 0, grad_row).astype(jnp.int32)
    grad_plan = copy_plan(grad_from, grad_row, 5)
    zero = jnp.zeros((1, head_dim, 256), bf16)

    def pick_table(parts, events=()):
        sources = [side for part in parts for side in (part, swapped(part, "ctx", 1))]
        return copy_rows(
            [*sources, zero], [0] * 5, 256, grad_plan, [high_count * half_slots] * 2, events
        )

    def table_sums(keep, got):
        sums = []
        for d in range(high_count):
            rows = slice(d * half_slots, (d + 1) * half_slots)
            sums.append((keep[rows].astype(f32) + got[rows].astype(f32)).astype(bf16))
        return sums

    def from_owners(tables):
        return [swapped(tables[d], "fsdp", 2 * d) for d in high_distances]

    def owner_sum(table, got):
        total = table.astype(f32)
        for part in got:
            total = total + part.astype(f32)
        return total.astype(bf16)

    def proj_grad(columns):
        return dot(grad_proj, columns, 1, 0).astype(bf16).reshape(-1, head_dim, columns.shape[1])

    def chip_sums(start, proj_got, early_got):
        near = slice(start, start + 256)

        def added(own, got):
            return (own.astype(f32) + got.astype(f32)).astype(bf16)

        early = [
            added(head_grads[:, :, near], early_got[:half_heads]),
            added(block_grads[:, :, near], early_got[half_heads:]),
        ]
        return [added(proj_grad(normed_b[:, near]), proj_got), jnp.concatenate(early)]

    proj_last = proj_grad(last_columns(normed_b))
    proj_last, wide_got = lax.optimization_barrier((proj_last, wide_got))
    wide_far = proj_grad(normed_b[:, wide])
    wide_proj = swapped(wide_far, "ctx", 2)
    keep_last, send_last = pick_table([proj_last, early_last], [wide_far])
    low_last = swapped(send_last, "fsdp", 1)
    keep_last, grad_proj = lax.optimization_barrier((keep_last, grad_proj))
    slim_far = jnp.concatenate([proj_grad(normed_b[:, slim]), early_slim])
    normed_far = dot(grad_proj[:, half_rows:], w_qkv, 0, 0).astype(bf16)
    slim_far, wide_proj = lax.optimization_barrier((slim_far, wide_proj))
    low_last, wide_proj, normed_far, count = lax.optimization_barrier(
        (low_last, wide_proj, normed_far, count)
    )
    normed_got = swapped(normed_far, "ctx", 1)
    slim_got = swapped(slim_far, "ctx", 2)
    totals = chip_sums(256, wide_proj, wide_got)
    keep_three, send_three = pick_table(totals, [normed_got])
    low_last, keep_three, grad_proj = lax.optimization_barrier((low_last, keep_three, grad_proj))
    low_three = swapped(send_three, "fsdp", 1)
    tables_last = table_sums(keep_last, low_last)
    high_last = from_owners(tables_last)
    grad_normed_in = dot(grad_proj[:, :half_rows], w_qkv, 0, 0) + normed_got.astype(f32)
    inverse = inverse_rms(values_in)
    scaled = grad_normed_in * gains[0]
    input_grad = grad_middle + (
        inverse * scaled
        - values_in * inverse**3 * jnp.mean(scaled * values_in, axis=-1, keepdims=True)
    )
    grad_gain_one = jnp.sum(grad_normed_in * values_in * inverse, axis=0)
    low_three, high_last, slim_got, input_grad = lax.optimization_barrier(
        (low_three, high_last, slim_got, input_grad)
    )
    totals = chip_sums(0, slim_got[: 3 * half_heads], slim_got[3 * half_heads :])
    keep_one, send_one = pick_table(totals, [low_three])
    keep_one, low_three = lax.optimization_barrier((keep_one, low_three))
    tables_three = table_sums(keep_three, low_three)
    high_three = from_owners(tables_three)

    gain_terms = columns_here(jnp.stack([grad_gain_one, grad_gain_two]))
    small = jnp.concatenate([gain_terms.reshape(-1), scale_term])
    small = jnp.pad(small, (0, -small.shape[0] % 1024))
    keep_one, small = lax.optimization_barrier((keep_one, small))
    tables_one = table_sums(keep_one, swapped(send_one, "fsdp", 1))
    small = summed(small, "ctx")
    input_own, input_got = rows_apart(input_grad)
    tables_one, high_three, high_last, small, input_got = lax.optimization_barrier(
        (tables_one, high_three, high_last, small, input_got)
    )
    high_one = from_owners(tables_one)
    small = small + swapped(small, "fsdp", 1)
    owned_last = owner_sum(tables_last[0], high_last)
    owned_got = swapped(owned_last[:, :, tail:], "ctx", 2)
    high_one, small, owned_got = lax.optimization_barrier((high_one, small, owned_got))

    owned = [
        owner_sum(tables_one[0], high_one),
        owner_sum(tables_three[0], high_three),
        (owned_last[:, :, :tail].astype(f32) + owned_got.astype(f32)).astype(bf16),
    ]
    owned = jnp.concatenate(owned, axis=2).reshape(half_slots, head_dim, 2, column_count)
    kept = jnp.where(first_core, owned[:, :, 0], owned[:, :, 1])
    sent = swapped(jnp.where(first_core, owned[:, :, 1], owned[:, :, 0]), "ctx", 1)
    sent, small = lax.optimization_barrier((sent, small))
    small = small + swapped(small, "fsdp", 2)
    small = small + swapped(small, "fsdp", 4)
    gain_sums = small[: 2 * width].reshape(2, width)
    scale_sums = small[2 * width : 2 * width + head_dim]

    count = count[0].astype(f32)
    slot_sums = jnp.where(
        first_core, jnp.concatenate([kept, sent]), jnp.concatenate([sent, kept])
    ).astype(f32)
    new_master, new_first, new_second = adam_step(
        master, first_moment, second_moment, slot_sums / count, master_rate, decay_rate
    )
    new_gains, new_gain_first, new_gain_second = adam_step(
        norm_gains, gain_first, gain_second, gain_sums / count, gain_rate, 0.0
    )
    new_scale, new_scale_first, new_scale_second = adam_step(
        query_scale, scale_first, scale_second, scale_sums / count, scale_rate, 0.0
    )
    return (
        rows_home(block_own, block_got),
        rows_home(input_own, input_got),
        new_master,
        new_first,
        new_second,
        new_gains,
        new_gain_first,
        new_gain_second,
        new_scale,
        new_scale_first,
        new_scale_second,
    )


def on_device(*arguments):
    paired = (
        lax.axis_size("ctx") == 4
        and lax.axis_size("fsdp") == 8
        and arguments[0].shape[0] == 2
    )
    return (paired_layer if paired else general_layer)(*arguments)


def solution(mesh):
    in_specs = (
        P("fsdp", "ctx", None),
        P("fsdp", "ctx", None),
        P("fsdp"),
        P(),
        P("fsdp", None, "ctx"),
        P("fsdp", None, "ctx"),
        P("fsdp", None, "ctx"),
        P(),
        P(),
        P(),
        P(),
        P(),
        P(),
    )
    out_specs = (
        P("fsdp", "ctx", None),
        P("fsdp", "ctx", None),
        P("fsdp", None, "ctx"),
        P("fsdp", None, "ctx"),
        P("fsdp", None, "ctx"),
        P(),
        P(),
        P(),
        P(),
        P(),
        P(),
    )
    return jax.shard_map(
        on_device, mesh=mesh, in_specs=in_specs, out_specs=out_specs, check_vma=False
    )
```

```python
import functools
import math

import jax
import jax.numpy as jnp
from jax import lax
from jax.experimental import pallas as pl
from jax.experimental.pallas import tpu as pltpu
from jax.sharding import PartitionSpec as P

H = 16
FF = 1280
STEP = 10


norm_eps = 1e-06
beta_first = 0.9
beta_second = 0.95
adam_eps = 1e-08
decay_rate = 0.1
master_rate = 0.05
gain_rate = 2.0
scale_rate = 2.0
score_base = 1.442695041
masked_score = -1e30


def from_behind(block, axis, distance):
    devices = range(lax.axis_size(axis))
    route = [(i - distance, i) for i in devices if i - distance in devices]
    return lax.ppermute(block, axis, route)


def shifted(array, axis, by):
    count = lax.axis_size(axis)
    return lax.ppermute(array, axis, [(i, (i + by) % count) for i in range(count)])


def unit_rows(owners, slot_count):
    unit_count = owners.shape[0]
    unit_order = jnp.arange(unit_count, dtype=jnp.int32)
    same_owner = owners[:, None] == owners[None, :]
    earlier = unit_order[None, :] < unit_order[:, None]
    slot_rank = jnp.sum((same_owner & earlier).astype(jnp.int32), axis=1)
    return owners * slot_count + slot_rank


def inverse_rms(values):
    return lax.rsqrt(jnp.mean(values * values, axis=-1, keepdims=True) + norm_eps)


def norm_back(values, gain, grad_normed):
    inverse = inverse_rms(values)
    scaled = grad_normed * gain
    grad_values = inverse * scaled - values * inverse**3 * jnp.mean(
        scaled * values, axis=-1, keepdims=True
    )
    grad_gain = jnp.sum(grad_normed * values * inverse, axis=(0, 1))
    return (grad_values, grad_gain)


def adam_step(values, moment_one, moment_two, gradient, step_rate, weight_decay):
    moment_one = beta_first * moment_one + (1.0 - beta_first) * gradient
    moment_two = beta_second * moment_two + (1.0 - beta_second) * gradient * gradient
    first_hat = moment_one / (1.0 - beta_first**STEP)
    second_hat = moment_two / (1.0 - beta_second**STEP)
    values = values - step_rate * (
        first_hat / (jnp.sqrt(second_hat) + adam_eps) + weight_decay * values
    )
    return (values, moment_one, moment_two)


def general_layer(
    inputs,
    targets,
    valid_counts,
    owners,
    master,
    first_moment,
    second_moment,
    norm_gains,
    gain_first,
    gain_second,
    query_scale,
    scale_first,
    scale_second,
):
    seq_local, block_rows, width = inputs.shape
    slot_count, head_dim, column_count = master.shape
    ff_blocks = FF // head_dim
    ctx_size = lax.axis_size("ctx")
    ctx_index = lax.axis_index("ctx")
    slot_rows = unit_rows(owners, slot_count)
    owner_table = lax.all_gather(master.astype(jnp.bfloat16), "fsdp", axis=0, tiled=True)
    picked = owner_table[slot_rows]
    weights = lax.all_gather(picked, "ctx", axis=2, tiled=True)
    w_qkv = weights[0 : 3 * H]
    w_out = weights[3 * H : 4 * H]
    w_up = weights[4 * H : 4 * H + ff_blocks]
    w_down = weights[4 * H + ff_blocks :]
    values_in = inputs.astype(jnp.float32)
    normed_b = (values_in * inverse_rms(values_in) * norm_gains[0]).astype(jnp.bfloat16)
    projected = jnp.einsum("sbd,hed->shbe", normed_b, w_qkv, preferred_element_type=jnp.float32)
    query_pre = projected[:, 0:H]
    multiplier = jax.nn.softplus(query_scale) * (score_base / math.sqrt(head_dim))
    query_b = (query_pre * multiplier).astype(jnp.bfloat16)
    key_b = projected[:, H : 2 * H].astype(jnp.bfloat16)
    value_b = projected[:, 2 * H : 3 * H].astype(jnp.bfloat16)
    query_rows = ctx_index * block_rows + jnp.arange(block_rows, dtype=jnp.int32)
    last_row = ctx_index * block_rows + block_rows - 1
    start_state = (
        jnp.full(query_pre.shape[:3], masked_score, jnp.float32),
        jnp.zeros(query_pre.shape[:3], jnp.float32),
        jnp.zeros(query_pre.shape, jnp.float32),
    )
    key_part = lax.all_gather(key_b, "ctx", axis=2, tiled=True)
    value_part = lax.all_gather(value_b, "ctx", axis=2, tiled=True)
    key_count = key_part.shape[2]

    def update(current):
        run_max, run_sum, accum = current
        key_rows = jnp.arange(key_count, dtype=jnp.int32)
        allowed = query_rows[:, None] >= key_rows[None, :]
        scores = jnp.einsum(
            "shqe,shke->shqk", query_b, key_part, preferred_element_type=jnp.float32
        )
        scores = jnp.where(allowed, scores, masked_score)
        new_max = jnp.maximum(run_max, jnp.max(scores, axis=-1))
        attn_probs = jnp.where(allowed, jnp.exp(scores - new_max[..., None]), 0.0)
        run_sum = jnp.sum(attn_probs, axis=-1)
        accum = jnp.einsum(
            "shqk,shke->shqe",
            attn_probs.astype(jnp.bfloat16),
            value_part,
            preferred_element_type=jnp.float32,
        )
        return (new_max, run_sum, accum)

    run_max, run_sum, accum = lax.cond(
        jnp.int32(0) <= last_row, update, lambda current: current, start_state
    )
    attended = accum / run_sum[..., None]
    log_total = run_max + jnp.log(run_sum)
    attended_b = attended.astype(jnp.bfloat16)
    branch = jnp.einsum("shbe,hed->sbd", attended_b, w_out, preferred_element_type=jnp.float32)
    middle = values_in + branch
    normed_mid_b = (middle * inverse_rms(middle) * norm_gains[1]).astype(jnp.bfloat16)
    hidden = jnp.einsum("sbd,fed->sbfe", normed_mid_b, w_up, preferred_element_type=jnp.float32)
    active_b = jax.nn.silu(hidden).astype(jnp.bfloat16)
    block_out = middle + jnp.einsum(
        "sbfe,fed->sbd", active_b, w_down, preferred_element_type=jnp.float32
    )
    seq_length = block_rows * ctx_size
    counted = (query_rows[None, :] >= (seq_length - valid_counts)[:, None]).astype(jnp.float32)
    count_term = jnp.sum(counted)
    out_grad = 2.0 * (block_out - targets.astype(jnp.float32)) * counted[..., None]
    out_grad_b = out_grad.astype(jnp.bfloat16)
    grad_down = jnp.einsum(
        "sbfe,sbd->fed", active_b, out_grad_b, preferred_element_type=jnp.float32
    )
    grad_active = jnp.einsum(
        "sbd,fed->sbfe", out_grad_b, w_down, preferred_element_type=jnp.float32
    )
    sigma = jax.nn.sigmoid(hidden)
    grad_hidden_b = (grad_active * sigma * (1.0 + hidden * (1.0 - sigma))).astype(jnp.bfloat16)
    grad_up = jnp.einsum(
        "sbfe,sbd->fed", grad_hidden_b, normed_mid_b, preferred_element_type=jnp.float32
    )
    grad_normed_mid = jnp.einsum(
        "sbfe,fed->sbd", grad_hidden_b, w_up, preferred_element_type=jnp.float32
    )
    grad_middle_norm, grad_gain_two = norm_back(middle, norm_gains[1], grad_normed_mid)
    grad_middle = out_grad + grad_middle_norm
    grad_middle_b = grad_middle.astype(jnp.bfloat16)
    grad_out = jnp.einsum(
        "shbe,sbd->hed", attended_b, grad_middle_b, preferred_element_type=jnp.float32
    )
    grad_attended_b = jnp.einsum(
        "sbd,hed->shbe", grad_middle_b, w_out, preferred_element_type=jnp.float32
    ).astype(jnp.bfloat16)
    delta = jnp.sum(grad_attended_b.astype(jnp.float32) * attended, axis=-1)

    def block_grads(source, key_cur, value_cur, partial_grads):
        grad_key, grad_value, grad_query = partial_grads
        key_rows = source * block_rows + jnp.arange(block_rows, dtype=jnp.int32)
        allowed = query_rows[:, None] >= key_rows[None, :]
        scores = jnp.einsum("shqe,shke->shqk", query_b, key_cur, preferred_element_type=jnp.float32)
        scores = jnp.where(allowed, scores, masked_score)
        attn_probs = jnp.exp(scores - log_total[..., None])
        grad_value = grad_value + jnp.einsum(
            "shqk,shqe->shke",
            attn_probs.astype(jnp.bfloat16),
            grad_attended_b,
            preferred_element_type=jnp.float32,
        )
        grad_probs = jnp.einsum(
            "shqe,shke->shqk", grad_attended_b, value_cur, preferred_element_type=jnp.float32
        )
        grad_scores_b = (attn_probs * (grad_probs - delta[..., None])).astype(jnp.bfloat16)
        grad_query = grad_query + jnp.einsum(
            "shqk,shke->shqe", grad_scores_b, key_cur, preferred_element_type=jnp.float32
        )
        grad_key = grad_key + jnp.einsum(
            "shqk,shqe->shke", grad_scores_b, query_b, preferred_element_type=jnp.float32
        )
        return (grad_key, grad_value, grad_query)

    zero_heads = jnp.zeros(query_pre.shape, jnp.float32)

    def back_turn(which_turn, current):
        key_cur, value_cur, grad_key, grad_value, grad_query = current
        source = (ctx_index - which_turn) % ctx_size
        grad_key, grad_value, grad_query = lax.cond(
            source <= ctx_index,
            lambda parts: block_grads(source, key_cur, value_cur, parts),
            lambda parts: parts,
            (grad_key, grad_value, grad_query),
        )
        key_cur, value_cur = from_behind((key_cur, value_cur), "ctx", 1)
        grad_key, grad_value = (
            shifted(grad_key.astype(jnp.bfloat16), "ctx", 1).astype(grad_key.dtype),
            shifted(grad_value.astype(jnp.bfloat16), "ctx", 1).astype(grad_value.dtype),
        )
        return (key_cur, value_cur, grad_key, grad_value, grad_query)

    back_state = (key_b, value_b, zero_heads, zero_heads, zero_heads)
    back_state = lax.fori_loop(0, ctx_size, back_turn, back_state)
    grad_key, grad_value, grad_query = (back_state[2], back_state[3], back_state[4])
    grad_proj_b = jnp.concatenate([grad_query * multiplier, grad_key, grad_value], axis=1).astype(
        jnp.bfloat16
    )
    grad_qkv = jnp.einsum(
        "shbe,sbd->hed", grad_proj_b, normed_b, preferred_element_type=jnp.float32
    )
    grad_normed_in = jnp.einsum(
        "shbe,hed->sbd", grad_proj_b, w_qkv, preferred_element_type=jnp.float32
    )
    grad_input_norm, grad_gain_one = norm_back(values_in, norm_gains[0], grad_normed_in)
    input_grad = grad_middle + grad_input_norm
    scale_term = (
        jnp.sum(grad_query * query_pre, axis=(0, 1, 2))
        * (score_base / math.sqrt(head_dim))
        * jax.nn.sigmoid(query_scale)
    )
    unit_grads = jnp.concatenate([grad_qkv, grad_out, grad_up, grad_down], axis=0)
    owner_total = lax.axis_size("fsdp") * slot_count
    table_grads = (
        jnp.zeros((owner_total, head_dim, width), jnp.float32).at[slot_rows].set(unit_grads)
    )
    owned = lax.psum_scatter(
        table_grads.astype(jnp.bfloat16), "fsdp", scatter_dimension=0, tiled=True
    )
    slot_sums = lax.psum_scatter(owned, "ctx", scatter_dimension=2, tiled=True).astype(jnp.float32)
    gain_sums, scale_sums, count = lax.psum(
        (jnp.stack([grad_gain_one, grad_gain_two]), scale_term, count_term), ("ctx", "fsdp")
    )
    new_master, new_first, new_second = adam_step(
        master, first_moment, second_moment, slot_sums / count, master_rate, decay_rate
    )
    new_gains, new_gain_first, new_gain_second = adam_step(
        norm_gains, gain_first, gain_second, gain_sums / count, gain_rate, 0.0
    )
    new_scale, new_scale_first, new_scale_second = adam_step(
        query_scale, scale_first, scale_second, scale_sums / count, scale_rate, 0.0
    )
    return (
        block_out,
        input_grad,
        new_master,
        new_first,
        new_second,
        new_gains,
        new_gain_first,
        new_gain_second,
        new_scale,
        new_scale_first,
        new_scale_second,
    )


def swapped(array, axis, distance):
    return lax.ppermute(
        array, axis, [(i, i ^ distance) for i in range(lax.axis_size(axis))]
    )


def summed(array, axis):
    size = lax.axis_size(axis)
    if size & (size - 1):
        return lax.psum(array, axis)
    distance = 1
    while distance < size:
        array = array + swapped(array, axis, distance)
        distance *= 2
    return array


def dot(left, right, left_dim, right_dim):
    return lax.dot_general(
        left,
        right,
        (((left_dim,), (right_dim,)), ((), ())),
        preferred_element_type=jnp.float32,
    )


def copy_rows_kernel(sizes, offsets, width, bound_ref, place_ref, row_ref, *refs):
    sources = refs[: len(offsets)]
    outs = refs[-2 - len(sizes) : -2]
    rows, sems = refs[-2:]
    for number, (source, offset) in enumerate(zip(sources, offsets)):

        @pl.loop(bound_ref[number], bound_ref[number + 1])
        def copy_row(i, source=source, offset=offset):
            pltpu.make_async_copy(
                source.at[row_ref[i], :, pl.ds(offset, width)],
                rows.at[place_ref[i]],
                sems.at[len(sizes)],
            ).start()

    pltpu.make_async_copy(rows, rows, sems.at[len(sizes)]).wait()
    copies, start = [], 0
    for place, (out, size) in enumerate(zip(outs, sizes)):
        copies.append(
            pltpu.make_async_copy(rows.at[pl.ds(start, size)], out, sems.at[place])
        )
        start += size
    for copy in copies:
        copy.start()
    for copy in copies:
        copy.wait()


def copy_plan(pick_from, pick_row, source_count):
    number = jnp.arange(pick_from.shape[0], dtype=jnp.int32)
    before = pick_from[None, :] < pick_from[:, None]
    same = (pick_from[None, :] == pick_from[:, None]) & (number[None, :] < number[:, None])
    rank = jnp.sum((before | same).astype(jnp.int32), axis=1)
    here = rank[None, :] == number[:, None]
    place = jnp.sum(jnp.where(here, number[None, :], 0), axis=1)
    row = jnp.sum(jnp.where(here, pick_row[None, :], 0), axis=1)
    bounds = jnp.sum(
        (pick_from[None, :] < jnp.arange(source_count + 1)[:, None]).astype(jnp.int32), axis=1
    )
    return (bounds.astype(jnp.int32), place.astype(jnp.int32), row.astype(jnp.int32))


def copy_rows(sources, offsets, width, plan, sizes, events=()):
    rows = sources[0].shape[1]
    total = sum(sizes)
    return pl.pallas_call(
        functools.partial(copy_rows_kernel, tuple(sizes), tuple(offsets), width),
        out_shape=[jax.ShapeDtypeStruct((size, rows, width), sources[0].dtype) for size in sizes],
        grid_spec=pltpu.PrefetchScalarGridSpec(
            num_scalar_prefetch=3,
            grid=(1,),
            in_specs=[pl.BlockSpec(memory_space=pltpu.HBM)] * (len(sources) + len(events)),
            out_specs=[pl.BlockSpec(memory_space=pltpu.HBM)] * len(sizes),
            scratch_shapes=[
                pltpu.VMEM((total, rows, width), sources[0].dtype),
                pltpu.SemaphoreType.DMA((len(sizes) + 1,)),
            ],
        ),
        compiler_params=pltpu.CompilerParams(vmem_limit_bytes=40 * 1024 * 1024),
        cost_estimate=pl.CostEstimate(flops=0, bytes_accessed=1024, transcendentals=0),
        name="copy_rows",
    )(*plan, *sources, *events)


def place_pieces_kernel(places, count_outs, *refs):
    pieces = refs[: len(places)]
    outs = refs[-1 - count_outs : -1]
    sems = refs[-1]
    copies = []
    for number, (piece, place) in enumerate(zip(pieces, places)):
        first, count, begin, size, column, out, row = place
        copies.append(
            pltpu.make_async_copy(
                piece.at[pl.ds(first, count), :, pl.ds(begin, size)],
                outs[out].at[pl.ds(row, count), :, pl.ds(column, size)],
                sems.at[number],
            )
        )
    for copy in copies:
        copy.start()
    for copy in copies:
        copy.wait()


def place_pieces(pieces, places, shapes, events=()):
    return pl.pallas_call(
        functools.partial(place_pieces_kernel, tuple(places), len(shapes)),
        out_shape=[jax.ShapeDtypeStruct(shape, pieces[0].dtype) for shape in shapes],
        in_specs=[pl.BlockSpec(memory_space=pltpu.HBM)] * (len(pieces) + len(events)),
        out_specs=[pl.BlockSpec(memory_space=pltpu.VMEM)] * len(shapes),
        scratch_shapes=[pltpu.SemaphoreType.DMA((len(pieces),))],
        compiler_params=pltpu.CompilerParams(vmem_limit_bytes=40 * 1024 * 1024),
        cost_estimate=pl.CostEstimate(flops=0, bytes_accessed=1024, transcendentals=0),
        name="place_pieces",
    )(*pieces, *events)


def scores_of(blocks, key_rows, query, i):
    size = query.shape[1]
    parts = [(i * size, size)] + ([(0, i * size)] if i else [])
    return [dot(key_rows[first : first + count, :], query, 1, 0) for first, count in parts]


def attend_kernel(blocks, pair, order_ref, q_ref, k_ref, v_ref, out_ref, log_ref, *refs):
    key_rows, value_cols = refs[:pair], refs[pair:]
    head_dim = q_ref.shape[0] // pair
    size = q_ref.shape[1] // blocks
    at = [pl.multiple_of(order_ref[i] * size, size) for i in range(blocks)]
    heads = [slice(p * head_dim, (p + 1) * head_dim) for p in range(pair)]
    for i in range(blocks):
        here = slice(i * size, (i + 1) * size)
        for p in range(pair):
            key_rows[p][here, :] = k_ref[heads[p], pl.ds(at[i], size)].T
            value_cols[p][:, here] = v_ref[heads[p], pl.ds(at[i], size)]
    key_pos = lax.broadcasted_iota(jnp.int32, (size, size), 0)
    query_pos = lax.broadcasted_iota(jnp.int32, (size, size), 1)
    seen = key_pos <= query_pos

    def scores(i):
        return [
            scores_of(blocks, key_rows[p], q_ref[heads[p], pl.ds(at[i], size)], i)
            for p in range(pair)
        ]

    upcoming = scores(0)
    for i in range(blocks):
        current = upcoming
        if i + 1 < blocks:
            upcoming = scores(i + 1)
        past = i * size
        for p in range(pair):
            near, *far = current[p]
            near = jnp.where(seen, near, masked_score)
            top = jnp.max(near, axis=0, keepdims=True)
            for part in far:
                top = jnp.maximum(top, jnp.max(part, axis=0, keepdims=True))
            near = jnp.exp(near - top)
            total = jnp.sum(near, axis=0, keepdims=True)
            value = dot(
                value_cols[p][:, past : past + size], near.astype(jnp.bfloat16), 1, 0
            )
            for part in far:
                part = jnp.exp(part - top)
                total = total + jnp.sum(part, axis=0, keepdims=True)
                value = value + dot(value_cols[p][:, :past], part.astype(jnp.bfloat16), 1, 0)
            out_ref[heads[p], pl.ds(at[i], size)] = (value / total).astype(jnp.bfloat16)
            log_ref[p, :, pl.ds(at[i], size)] = top + jnp.log(total)


def attend(projected, order, heads, head_dim):
    tokens = projected.shape[1]
    blocks = order.shape[0]
    pair = 4
    rows = pair * head_dim

    def part(first):
        return pl.BlockSpec((rows, tokens), lambda h, order, first=first: (first // pair + h, 0))

    return pl.pallas_call(
        functools.partial(attend_kernel, blocks, pair),
        out_shape=[
            jax.ShapeDtypeStruct((heads * head_dim, tokens), jnp.bfloat16),
            jax.ShapeDtypeStruct((heads, 1, tokens), jnp.float32),
        ],
        grid_spec=pltpu.PrefetchScalarGridSpec(
            num_scalar_prefetch=1,
            grid=(heads // pair,),
            in_specs=[part(0), part(heads), part(2 * heads)],
            out_specs=[
                pl.BlockSpec((rows, tokens), lambda h, order: (h, 0)),
                pl.BlockSpec((pair, 1, tokens), lambda h, order: (h, 0, 0)),
            ],
            scratch_shapes=[pltpu.VMEM((tokens, head_dim), jnp.bfloat16)] * pair
            + [pltpu.VMEM((head_dim, tokens), jnp.bfloat16)] * pair,
        ),
        compiler_params=pltpu.CompilerParams(vmem_limit_bytes=48 * 1024 * 1024),
        cost_estimate=pl.CostEstimate(
            flops=heads * tokens * tokens * head_dim * 4,
            bytes_accessed=heads * head_dim * tokens * 8,
            transcendentals=heads * tokens * tokens,
        ),
        name="attend",
    )(order, projected, projected, projected)


def attend_back_kernel(
    blocks,
    pair,
    order_ref,
    q_ref,
    k_ref,
    v_ref,
    grad_ref,
    log_ref,
    scale_ref,
    *refs,
):
    scratch = refs[-5 * pair :]
    out_ref, term_ref = refs[-5 * pair - 2 : -5 * pair]
    key_rows, key_cols, value_rows, key_sum, value_sum = (
        scratch[n * pair : (n + 1) * pair] for n in range(5)
    )
    head_dim = q_ref.shape[0] // pair
    size = q_ref.shape[1] // blocks
    at = [pl.multiple_of(order_ref[i] * size, size) for i in range(blocks)]
    heads = [slice(p * head_dim, (p + 1) * head_dim) for p in range(pair)]
    for i in range(blocks):
        here = slice(i * size, (i + 1) * size)
        for p in range(pair):
            key = k_ref[heads[p], pl.ds(at[i], size)]
            key_rows[p][here, :] = key.T
            key_cols[p][:, here] = key
            value_rows[p][here, :] = v_ref[heads[p], pl.ds(at[i], size)].T
    for p in range(pair):
        key_sum[p][...] = jnp.zeros_like(key_sum[p])
        value_sum[p][...] = jnp.zeros_like(value_sum[p])
    key_pos = lax.broadcasted_iota(jnp.int32, (size, size), 0)
    query_pos = lax.broadcasted_iota(jnp.int32, (size, size), 1)
    seen = key_pos <= query_pos
    terms = [jnp.zeros((head_dim, 1), jnp.float32) for _ in range(pair)]

    def products(i):
        return [
            (
                scores_of(blocks, key_rows[p], q_ref[heads[p], pl.ds(at[i], size)], i),
                scores_of(blocks, value_rows[p], grad_ref[heads[p], pl.ds(at[i], size)], i),
            )
            for p in range(pair)
        ]

    upcoming = products(0)
    for i in range(blocks):
        current = upcoming
        if i + 1 < blocks:
            upcoming = products(i + 1)
        past = i * size
        spans = [slice(past, past + size)] + ([slice(0, past)] if i else [])
        for p in range(pair):
            query = q_ref[heads[p], pl.ds(at[i], size)]
            grad = grad_ref[heads[p], pl.ds(at[i], size)]
            log_total = log_ref[p, :, pl.ds(at[i], size)]
            scores, grads = current[p]
            probs = [jnp.exp(part - log_total) for part in scores]
            probs[0] = jnp.where(seen, probs[0], 0.0)
            delta = jnp.zeros((1, size), jnp.float32)
            for prob, grad_prob in zip(probs, grads):
                delta = delta + jnp.sum(prob * grad_prob, axis=0, keepdims=True)
            grad_query = jnp.zeros(query.shape, jnp.float32)
            for cols, prob, grad_prob in zip(spans, probs, grads):
                grad_score = (prob * (grad_prob - delta)).astype(jnp.bfloat16)
                value_sum[p][:, cols] += dot(grad, prob.astype(jnp.bfloat16), 1, 1)
                key_sum[p][:, cols] += dot(query, grad_score, 1, 1)
                grad_query = grad_query + dot(key_cols[p][:, cols], grad_score, 1, 0)
            terms[p] = terms[p] + jnp.sum(
                grad_query * query.astype(jnp.float32), axis=1, keepdims=True
            )
            out_ref[0, heads[p], pl.ds(at[i], size)] = (grad_query * scale_ref[...]).astype(
                jnp.bfloat16
            )
    for i in range(blocks):
        here = slice(i * size, (i + 1) * size)
        for p in range(pair):
            out_ref[1, heads[p], pl.ds(at[i], size)] = key_sum[p][:, here].astype(jnp.bfloat16)
            out_ref[2, heads[p], pl.ds(at[i], size)] = value_sum[p][:, here].astype(jnp.bfloat16)
    for p in range(pair):
        term_ref[p] = terms[p]


def attend_back(
    projected, grad_attended, log_total, multiplier, order, heads, head_dim, events=()
):
    tokens = projected.shape[1]
    blocks = order.shape[0]
    pair = 2
    rows = pair * head_dim

    def part(first):
        return pl.BlockSpec((rows, tokens), lambda h, order, first=first: (first // pair + h, 0))

    return pl.pallas_call(
        functools.partial(attend_back_kernel, blocks, pair),
        out_shape=[
            jax.ShapeDtypeStruct((3, heads * head_dim, tokens), jnp.bfloat16),
            jax.ShapeDtypeStruct((heads, head_dim, 1), jnp.float32),
        ],
        grid_spec=pltpu.PrefetchScalarGridSpec(
            num_scalar_prefetch=1,
            grid=(heads // pair,),
            in_specs=[
                part(0),
                part(heads),
                part(2 * heads),
                part(0),
                pl.BlockSpec((pair, 1, tokens), lambda h, order: (h, 0, 0)),
                pl.BlockSpec((head_dim, 1), lambda h, order: (0, 0)),
            ]
            + [pl.BlockSpec(memory_space=pltpu.HBM)] * len(events),
            out_specs=[
                pl.BlockSpec((3, rows, tokens), lambda h, order: (0, h, 0)),
                pl.BlockSpec((pair, head_dim, 1), lambda h, order: (h, 0, 0)),
            ],
            scratch_shapes=[pltpu.VMEM((tokens, head_dim), jnp.bfloat16)] * pair
            + [pltpu.VMEM((head_dim, tokens), jnp.bfloat16)] * pair
            + [pltpu.VMEM((tokens, head_dim), jnp.bfloat16)] * pair
            + [pltpu.VMEM((head_dim, tokens), jnp.float32)] * (2 * pair),
        ),
        compiler_params=pltpu.CompilerParams(vmem_limit_bytes=56 * 1024 * 1024),
        cost_estimate=pl.CostEstimate(
            flops=heads * tokens * tokens * head_dim * 10,
            bytes_accessed=heads * head_dim * tokens * 14,
            transcendentals=heads * tokens * tokens,
        ),
        name="attend_back",
    )(order, projected, projected, projected, grad_attended, log_total, multiplier, *events)


def paired_layer(
    inputs,
    targets,
    valid_counts,
    owners,
    master,
    first_moment,
    second_moment,
    norm_gains,
    gain_first,
    gain_second,
    query_scale,
    scale_first,
    scale_second,
):
    bf16 = jnp.bfloat16
    f32 = jnp.float32
    seq_local, block_rows, width = inputs.shape
    slot_count, head_dim, column_count = master.shape
    ff_blocks = FF // head_dim
    owner_count = lax.axis_size("fsdp")
    device = lax.axis_index("ctx")
    chip, core = device // 2, device % 2
    owner_here = lax.axis_index("fsdp")
    low_here = owner_here % 2
    high_here = owner_here // 2
    high_count = owner_count // 2
    high_distances = range(1, high_count)
    half_width = width // 2
    half_slots = slot_count // 2
    half_rows = seq_local * block_rows
    half_heads = H // 2
    half_blocks = ff_blocks // 2
    set_units = 4 * half_heads + 2 * half_blocks
    first_chip, first_core = chip == 0, core == 0

    def columns_here(array):
        return jnp.where(first_chip, array, jnp.roll(array, half_width, axis=-1))

    def sequence_rows(array):
        own = jnp.where(first_chip, array[0], array[1])
        got = swapped(jnp.where(first_chip, array[1], array[0]), "ctx", 2)
        return jnp.where(
            first_chip, jnp.concatenate([own, got]), jnp.concatenate([got, own])
        )

    def rows_apart(array):
        array = columns_here(array)
        first, last = array[:block_rows], array[block_rows:]
        other = jnp.where(first_chip, last, first).astype(bf16)
        return (jnp.where(first_chip, first, last), swapped(other, "ctx", 2))

    def rows_home(own, got):
        got = got.astype(f32)
        return jnp.where(first_chip, jnp.stack([own, got]), jnp.stack([got, own]))

    slot_rows = unit_rows(owners, slot_count)
    unit_total = owners.shape[0]
    kind_sizes = [H, H, H, H, ff_blocks, ff_blocks]
    kind_starts = [sum(kind_sizes[:i]) for i in range(6)]

    def unit_list(kinds, which):
        return jnp.concatenate(
            [
                kind_starts[k] + which * (kind_sizes[k] // 2) + jnp.arange(kind_sizes[k] // 2)
                for k in kinds
            ]
        ).astype(jnp.int32)

    wanted = jnp.concatenate(
        [unit_list(range(6), core), unit_list((4, 5), 1 - core)]
    )
    wanted_rows = slot_rows[wanted]
    wanted_owner, wanted_slot = wanted_rows // slot_count, wanted_rows % slot_count
    weight_from = 2 * (wanted_slot // half_slots != core) + (wanted_owner % 2 != low_here)
    weight_from = weight_from.astype(jnp.int32)
    weight_row = ((wanted_owner // 2) ^ high_here) * half_slots + wanted_slot % half_slots
    weight_plan = copy_plan(weight_from, weight_row, 4)
    weight_sizes = [3 * half_heads, half_heads + 2 * half_blocks, 2 * half_blocks]

    chunks = [(0, 256), (256, 256)]
    lead = 512
    tail = half_width - lead
    shard = master.astype(bf16)
    own_half = jnp.where(first_core, shard[:half_slots], shard[half_slots:])
    got_half = swapped(jnp.where(first_core, shard[half_slots:], shard[:half_slots]), "ctx", 1)
    shard = jnp.where(
        first_core,
        jnp.concatenate([own_half, got_half], axis=2),
        jnp.concatenate([got_half, own_half], axis=2),
    )
    shard, inputs, targets = lax.optimization_barrier((shard, inputs, targets))
    values_b = columns_here(sequence_rows(inputs))
    targets_b = columns_here(sequence_rows(targets))
    shard_last = shard[:, :, lead:]
    shards = [shard[:, :, start : start + size] for start, size in chunks]
    shards.append(jnp.concatenate([shard_last, swapped(shard_last, "ctx", 2)], axis=2))
    highs = []
    for number, part in enumerate(shards):
        if number:
            part, highs[-1] = lax.optimization_barrier((part, highs[-1]))
        highs.append(
            jnp.concatenate([part] + [swapped(part, "fsdp", 2 * d) for d in high_distances])
        )
    lows = [swapped(high, "fsdp", 1) for high in highs]
    own_units, rest_units, far_units = weight_sizes
    near_units = own_units + rest_units

    def pick_units(number, sizes, events):
        high, low = highs[number], lows[number]
        sources = [high, low, swapped(high, "ctx", 1), swapped(low, "ctx", 1)]
        return copy_rows(sources, [0] * 4, high.shape[2], weight_plan, sizes, events)

    lows[0], highs[1] = lax.optimization_barrier((lows[0], highs[1]))
    near_one, far_one = pick_units(
        0, [near_units, far_units], [shards[2], values_b, targets_b]
    )
    got_one = swapped(near_one, "ctx", 2)
    lows[1], far_one, highs[2] = lax.optimization_barrier((lows[1], far_one, highs[2]))
    qkv_two, rest_two, far_two = pick_units(1, weight_sizes, [])
    qkv_got = swapped(qkv_two, "ctx", 2)
    rest_two, qkv_got = lax.optimization_barrier((rest_two, qkv_got))
    rest_got = swapped(rest_two, "ctx", 2)
    lows[2], far_two, got_one = lax.optimization_barrier((lows[2], far_two, got_one))
    arrived = swapped(qkv_got[0, :16, :128], "ctx", 1)
    qkv_last, rest_last, far_last = pick_units(2, weight_sizes, [arrived])

    def columns_of(owns, gots, last):
        pieces = [(last, 0, tail, lead), (last, tail, tail, half_width + lead)]
        for (start, size), own, got in zip(chunks, owns, gots):
            pieces += [(own, 0, size, start), (got, 0, size, half_width + start)]
        return pieces

    def placed(pieces, from_end, count, out, row):
        return [
            (piece.shape[0] - from_end if from_end else 0, count, *columns, out, row)
            for piece, *columns in pieces
        ]

    qkv_pieces = columns_of([near_one, qkv_two], [got_one, qkv_got], qkv_last)
    rest_pieces = columns_of([near_one, rest_two], [got_one, rest_got], rest_last)
    far_pieces = columns_of(
        [far_one, far_two], [swapped(got, "ctx", 1) for got in (got_one, rest_got)], far_last
    )
    (w_qkv,) = place_pieces(
        [piece for piece, *_ in qkv_pieces],
        placed(qkv_pieces, 0, own_units, 0, 0),
        [(own_units, head_dim, width)],
    )
    w_qkv = w_qkv.reshape(-1, width)

    gains = columns_here(norm_gains)
    values_in = values_b.astype(f32)
    normed_own = (values_in * inverse_rms(values_in) * gains[0]).astype(bf16)
    normed_b = jnp.concatenate([normed_own, swapped(normed_own, "ctx", 1)])
    base = score_base / math.sqrt(head_dim)
    multiplier = jax.nn.softplus(query_scale) * base
    row_scale = jnp.concatenate(
        [jnp.tile(multiplier, half_heads), jnp.ones((2 * half_heads * head_dim,), f32)]
    )
    projected = (dot(w_qkv, normed_b, 1, 1) * row_scale[:, None]).astype(bf16)
    positions = jnp.arange(4, dtype=jnp.int32)
    order = jnp.where(positions % 2 == core, 0, 2) + positions // 2
    order = order.astype(jnp.int32)
    attended, log_total = attend(projected, order, half_heads, head_dim)
    partial = jnp.sum(valid_counts).astype(f32)[None]
    (w_out,) = place_pieces(
        [piece for piece, *_ in rest_pieces],
        placed(rest_pieces, rest_units, half_heads, 0, 0),
        [(half_heads, head_dim, width)],
        [log_total],
    )
    mlp_pieces, mlp_places = [], []
    for row, pieces in ((0, rest_pieces), (half_blocks, far_pieces)):
        for kind in range(2):
            mlp_pieces += [piece for piece, *_ in pieces]
            mlp_places += placed(pieces, (2 - kind) * half_blocks, half_blocks, kind, row)
    w_up, w_down = place_pieces(
        mlp_pieces, mlp_places, [(ff_blocks, head_dim, width)] * 2, [log_total]
    )
    w_out = w_out.reshape(-1, width)
    w_up = w_up.reshape(-1, width)
    w_down = w_down.reshape(-1, width)
    branch_far = dot(attended[:, half_rows:], w_out, 0, 0).astype(bf16)
    branch_got = swapped(branch_far, "ctx", 1)
    branch_own = dot(attended[:, :half_rows], w_out, 0, 0)
    middle = values_in + (branch_own + branch_got.astype(f32))
    normed_mid_b = (middle * inverse_rms(middle) * gains[1]).astype(bf16)
    hidden = dot(normed_mid_b, w_up, 1, 1)
    active_b = jax.nn.silu(hidden).astype(bf16)
    block_out = middle + dot(active_b, w_down, 1, 0)
    seq_length = 2 * half_rows
    row = jnp.arange(half_rows, dtype=jnp.int32)
    row_pos = (core + 2 * (row // block_rows)) * block_rows + row % block_rows
    valid = jnp.where(first_chip, valid_counts[0], valid_counts[1])
    counted = (row_pos >= seq_length - valid).astype(f32)

    (apart,) = lax.optimization_barrier((block_out,))
    block_own, block_got = rows_apart(apart)

    out_grad = 2.0 * (block_out - targets_b.astype(f32)) * counted[:, None]
    out_grad_b = out_grad.astype(bf16)
    grad_active = dot(out_grad_b, w_down, 1, 1)
    sigma = jax.nn.sigmoid(hidden)
    grad_hidden_b = (grad_active * sigma * (1.0 + hidden * (1.0 - sigma))).astype(bf16)
    grad_normed_mid = dot(grad_hidden_b, w_up, 1, 0)
    inverse = inverse_rms(middle)
    scaled = grad_normed_mid * gains[1]
    grad_middle = out_grad + (
        inverse * scaled
        - middle * inverse**3 * jnp.mean(scaled * middle, axis=-1, keepdims=True)
    )
    grad_gain_two = jnp.sum(grad_normed_mid * middle * inverse, axis=0)
    grad_middle_own = grad_middle.astype(bf16)
    grad_middle_got = swapped(grad_middle_own, "ctx", 1)
    far_blocks = half_blocks * head_dim
    wide = slice(half_width + 256, half_width + lead)
    slim = slice(half_width, half_width + 256)
    block_grads = []
    for left, right in ((grad_hidden_b, normed_mid_b), (active_b, out_grad_b)):
        got = swapped(dot(left[:, far_blocks:], right, 0, 0).astype(bf16), "ctx", 1)
        total = dot(left[:, :far_blocks], right, 0, 0) + got.astype(f32)
        block_grads.append(total.astype(bf16).reshape(half_blocks, head_dim, width))
    block_grads = jnp.concatenate(block_grads)
    grad_middle_got, block_grads = lax.optimization_barrier((grad_middle_got, block_grads))
    grad_middle_b = jnp.concatenate([grad_middle_own, grad_middle_got])
    grad_attended = dot(w_out, grad_middle_b, 1, 1).astype(bf16)
    head_grads = dot(attended, grad_middle_b, 1, 0).astype(bf16)
    head_grads = head_grads.reshape(half_heads, head_dim, width)

    def early_columns(columns):
        return jnp.concatenate([head_grads[:, :, columns], block_grads[:, :, columns]])

    early_wide, early_slim = early_columns(wide), early_columns(slim)
    wide_got = swapped(early_wide, "ctx", 2)

    def last_columns(array):
        return jnp.concatenate(
            [array[..., lead:half_width], array[..., half_width + lead :]], axis=-1
        )

    early_last = jnp.concatenate([last_columns(head_grads), last_columns(block_grads)])
    grad_proj, grad_scale = attend_back(
        projected,
        grad_attended,
        log_total,
        multiplier[:, None],
        order,
        half_heads,
        head_dim,
        [early_wide, early_slim, early_last, block_got],
    )
    grad_proj = grad_proj.reshape(-1, grad_proj.shape[2])
    scale_term = (
        jnp.sum(grad_scale[:, :, 0], axis=0) / multiplier * base * jax.nn.sigmoid(query_scale)
    )

    low_order = jnp.stack([low_here, 1 - low_here])
    table_slots = (
        (2 * (jnp.arange(high_count) ^ high_here)[None, :, None] + low_order[:, None, None])
        * slot_count
        + core * half_slots
        + jnp.arange(half_slots)[None, None, :]
    ).reshape(-1)
    holds = table_slots[:, None] == slot_rows[None, :]
    unit_order = jnp.arange(unit_total, dtype=jnp.int32)
    slot_unit = jnp.sum(jnp.where(holds, unit_order[None, :] + 1, 0), axis=1) - 1
    kind = jnp.where(
        slot_unit < 4 * H, slot_unit // H, 4 + (slot_unit - 4 * H) // ff_blocks
    )
    kind_size = jnp.where(kind < 4, H, ff_blocks)
    within = jnp.where(kind < 4, slot_unit % H, (slot_unit - 4 * H) % ff_blocks)
    other_set = (within // (kind_size // 2) != core).astype(jnp.int32)
    rank = within % (kind_size // 2)
    early = (kind >= 3).astype(jnp.int32)
    grad_row = rank + jnp.where(
        kind <= 3, kind % 3 * half_heads, half_heads + (kind - 4) * half_blocks
    )
    empty = slot_unit < 0
    grad_from = jnp.where(empty, 4, 2 * early + other_set).astype(jnp.int32)
    grad_row = jnp.where(empty, 0, grad_row).astype(jnp.int32)
    grad_plan = copy_plan(grad_from, grad_row, 5)
    zero = jnp.zeros((1, head_dim, 256), bf16)

    def pick_table(parts, events=()):
        sources = [side for part in parts for side in (part, swapped(part, "ctx", 1))]
        return copy_rows(
            [*sources, zero], [0] * 5, 256, grad_plan, [high_count * half_slots] * 2, events
        )

    def table_sums(keep, got):
        sums = []
        for d in range(high_count):
            rows = slice(d * half_slots, (d + 1) * half_slots)
            sums.append((keep[rows].astype(f32) + got[rows].astype(f32)).astype(bf16))
        return sums

    def from_owners(tables):
        return [swapped(tables[d], "fsdp", 2 * d) for d in high_distances]

    def owner_sum(table, got):
        total = table.astype(f32)
        for part in got:
            total = total + part.astype(f32)
        return total.astype(bf16)

    def proj_grad(columns):
        return dot(grad_proj, columns, 1, 0).astype(bf16).reshape(-1, head_dim, columns.shape[1])

    def chip_sums(start, proj_got, early_got):
        near = slice(start, start + 256)

        def added(own, got):
            return (own.astype(f32) + got.astype(f32)).astype(bf16)

        early = [
            added(head_grads[:, :, near], early_got[:half_heads]),
            added(block_grads[:, :, near], early_got[half_heads:]),
        ]
        return [added(proj_grad(normed_b[:, near]), proj_got), jnp.concatenate(early)]

    proj_last = proj_grad(last_columns(normed_b))
    proj_last, wide_got = lax.optimization_barrier((proj_last, wide_got))
    wide_far = proj_grad(normed_b[:, wide])
    wide_proj = swapped(wide_far, "ctx", 2)
    keep_last, send_last = pick_table([proj_last, early_last], [wide_far])
    low_last = swapped(send_last, "fsdp", 1)
    keep_last, grad_proj, partial = lax.optimization_barrier((keep_last, grad_proj, partial))
    partial = partial + swapped(partial, "fsdp", 2)
    slim_far = jnp.concatenate([proj_grad(normed_b[:, slim]), early_slim])
    normed_far = dot(grad_proj[:, half_rows:], w_qkv, 0, 0).astype(bf16)
    slim_far, wide_proj = lax.optimization_barrier((slim_far, wide_proj))
    low_last, wide_proj, normed_far, partial = lax.optimization_barrier(
        (low_last, wide_proj, normed_far, partial)
    )
    partial = partial + swapped(partial, "fsdp", 4)
    normed_got = swapped(normed_far, "ctx", 1)
    slim_got = swapped(slim_far, "ctx", 2)
    totals = chip_sums(256, wide_proj, wide_got)
    keep_three, send_three = pick_table(totals, [normed_got, partial])
    low_last, keep_three, grad_proj = lax.optimization_barrier((low_last, keep_three, grad_proj))
    low_three = swapped(send_three, "fsdp", 1)
    tables_last = table_sums(keep_last, low_last)
    high_last = from_owners(tables_last)
    grad_normed_in = dot(grad_proj[:, :half_rows], w_qkv, 0, 0) + normed_got.astype(f32)
    inverse = inverse_rms(values_in)
    scaled = grad_normed_in * gains[0]
    input_grad = grad_middle + (
        inverse * scaled
        - values_in * inverse**3 * jnp.mean(scaled * values_in, axis=-1, keepdims=True)
    )
    grad_gain_one = jnp.sum(grad_normed_in * values_in * inverse, axis=0)
    low_three, high_last, slim_got, input_grad = lax.optimization_barrier(
        (low_three, high_last, slim_got, input_grad)
    )
    totals = chip_sums(0, slim_got[: 3 * half_heads], slim_got[3 * half_heads :])
    keep_one, send_one = pick_table(totals, [low_three])
    keep_one, low_three = lax.optimization_barrier((keep_one, low_three))
    tables_three = table_sums(keep_three, low_three)
    high_three = from_owners(tables_three)

    gain_terms = columns_here(jnp.stack([grad_gain_one, grad_gain_two]))
    small = jnp.concatenate([gain_terms.reshape(-1), scale_term])
    small = jnp.pad(small, (0, -small.shape[0] % 1024))
    keep_one, small = lax.optimization_barrier((keep_one, small))
    tables_one = table_sums(keep_one, swapped(send_one, "fsdp", 1))
    small = summed(small, "ctx")
    filled = 2 * width + head_dim
    small = jnp.concatenate([small[:filled], partial, small[filled + 1 :]])
    input_own, input_got = rows_apart(input_grad)
    tables_one, high_three, high_last, small, input_got = lax.optimization_barrier(
        (tables_one, high_three, high_last, small, input_got)
    )
    high_one = from_owners(tables_one)
    small = small + swapped(small, "fsdp", 1)
    owned_last = owner_sum(tables_last[0], high_last)
    owned_got = swapped(owned_last[:, :, tail:], "ctx", 2)
    high_one, small, owned_got = lax.optimization_barrier((high_one, small, owned_got))
    count = small[filled]

    owned = [
        owner_sum(tables_one[0], high_one),
        owner_sum(tables_three[0], high_three),
        (owned_last[:, :, :tail].astype(f32) + owned_got.astype(f32)).astype(bf16),
    ]
    owned = jnp.concatenate(owned, axis=2).reshape(half_slots, head_dim, 2, column_count)
    kept = jnp.where(first_core, owned[:, :, 0], owned[:, :, 1])
    sent = swapped(jnp.where(first_core, owned[:, :, 1], owned[:, :, 0]), "ctx", 1)
    sent, small = lax.optimization_barrier((sent, small))
    small = small + swapped(small, "fsdp", 2)
    small = small + swapped(small, "fsdp", 4)
    gain_sums = small[: 2 * width].reshape(2, width)
    scale_sums = small[2 * width : 2 * width + head_dim]

    slot_sums = jnp.where(
        first_core, jnp.concatenate([kept, sent]), jnp.concatenate([sent, kept])
    ).astype(f32)
    new_master, new_first, new_second = adam_step(
        master, first_moment, second_moment, slot_sums / count, master_rate, decay_rate
    )
    new_gains, new_gain_first, new_gain_second = adam_step(
        norm_gains, gain_first, gain_second, gain_sums / count, gain_rate, 0.0
    )
    new_scale, new_scale_first, new_scale_second = adam_step(
        query_scale, scale_first, scale_second, scale_sums / count, scale_rate, 0.0
    )
    return (
        rows_home(block_own, block_got),
        rows_home(input_own, input_got),
        new_master,
        new_first,
        new_second,
        new_gains,
        new_gain_first,
        new_gain_second,
        new_scale,
        new_scale_first,
        new_scale_second,
    )


def on_device(*arguments):
    paired = (
        lax.axis_size("ctx") == 4
        and lax.axis_size("fsdp") == 8
        and arguments[0].shape[0] == 2
    )
    return (paired_layer if paired else general_layer)(*arguments)


def solution(mesh):
    in_specs = (
        P("fsdp", "ctx", None),
        P("fsdp", "ctx", None),
        P("fsdp"),
        P(),
        P("fsdp", None, "ctx"),
        P("fsdp", None, "ctx"),
        P("fsdp", None, "ctx"),
        P(),
        P(),
        P(),
        P(),
        P(),
        P(),
    )
    out_specs = (
        P("fsdp", "ctx", None),
        P("fsdp", "ctx", None),
        P("fsdp", None, "ctx"),
        P("fsdp", None, "ctx"),
        P("fsdp", None, "ctx"),
        P(),
        P(),
        P(),
        P(),
        P(),
        P(),
    )
    return jax.shard_map(
        on_device, mesh=mesh, in_specs=in_specs, out_specs=out_specs, check_vma=False
    )
```
